32 devices in a mesh: dp: 4 (over x, core), seq: 4 (over z), head: 2 (over y).
Axes of the slice: x: 2, y: 2, z: 4, core: 2. Of those that a mesh axis runs over, the one named last changes fastest.
Arguments:
- hidden_in: bfloat16 [4096, 1024], P(('dp', 'seq')), may hold values from -6 to 6
- segment_ids: int32 [4, 1024], P('dp'), may hold values from 0 to 2, as said below
- gain_mix: bfloat16 [2, 1024], replicated, may hold values from 0.5 to 1.5
- w_zx: bfloat16 [2, 1024, 2, 1536], P(None, None, None, 'head'), may hold values from -0.1875 to 0.1875
- w_bc: bfloat16 [2, 1024, 256], replicated, may hold values from -0.1875 to 0.1875
- w_dt: bfloat16 [2, 1024, 24], P(None, None, 'head'), may hold values from -0.1875 to 0.1875
- conv_x: bfloat16 [2, 4, 24, 64], P(None, None, 'head'), may hold values from -3 to 3
- conv_bc: bfloat16 [2, 4, 256], replicated, may hold values from -3 to 3
- ssm_head: float32 [2, 3, 24], P(None, None, 'head'), may hold values from -6 to 2
- w_q: bfloat16 [2, 1024, 512], P(None, None, 'head'), may hold values from -0.1875 to 0.1875
- w_kv: bfloat16 [2, 1024, 2, 128], P(None, None, 'head'), may hold values from -0.1875 to 0.1875
- w_o: bfloat16 [2, 512, 1024], P(None, 'head'), may hold values from -1 to 1
- w_out: bfloat16 [2, 1536, 1024], P(None, 'head'), may hold values from -0.15625 to 0.15625
- gain_ff: bfloat16 [2, 1024], replicated, may hold values from 0.5 to 1.5
- w_gu: bfloat16 [2, 1024, 2, 2048], P(None, None, None, 'head'), may hold values from -0.1875 to 0.1875
- w_down: bfloat16 [2, 2048, 1024], P(None, 'head'), may hold values from -0.125 to 0.125
- cotangent: bfloat16 [4096, 1024], P(('dp', 'seq')), may hold values from -6 to 6
Outputs:
- block_out: bfloat16 [4096, 1024], P(('dp', 'seq'))
- grad_in: float32 [4096, 1024], P(('dp', 'seq'))
- grad_gain_mix: float32 [2, 1024], P(None, ('dp', 'seq'))
- grad_w_zx: float32 [2, 1024, 2, 1536], P(None, ('dp', 'seq'), None, 'head')
- grad_w_bc: float32 [2, 1024, 256], P(None, None, ('dp', 'seq', 'head'))
- grad_w_dt: float32 [2, 1024, 24], P(None, ('dp', 'seq'), 'head')
- grad_conv_x: float32 [2, 4, 24, 64], P(None, None, 'head', ('dp', 'seq'))
- grad_conv_bc: float32 [2, 4, 256], P(None, None, ('dp', 'seq', 'head'))
- grad_ssm_head: float32 [2, 3, 24], P(None, None, 'head')
- grad_w_q: float32 [2, 1024, 512], P(None, ('dp', 'seq'), 'head')
- grad_w_kv: float32 [2, 1024, 2, 128], P(None, ('dp', 'seq'), 'head')
- grad_w_o: float32 [2, 512, 1024], P(None, 'head', ('dp', 'seq'))
- grad_w_out: float32 [2, 1536, 1024], P(None, 'head', ('dp', 'seq'))
- grad_gain_ff: float32 [2, 1024], P(None, ('dp', 'seq'))
- grad_w_gu: float32 [2, 1024, 2, 2048], P(None, ('dp', 'seq'), None, 'head')
- grad_w_down: float32 [2, 2048, 1024], P(None, 'head', ('dp', 'seq'))
The draws below stay inside these ranges and needn't reach their ends.
Inputs may be any that keep to these rules, and one draw needn't show every extreme that they name: `segment_ids`: never falling along a sequence; every sequence holds documents 0, 1 and 2.
All inputs are finite; a program needn't handle non-finite values.
Results may differ from the reference program's by a relative error of at most 0.03.
Values may be sent and summed in bfloat16 or wider, within the bound.
A program may use at most 320 MiB of HBM per device.

```python
import math
import jax
import jax.numpy as jnp
from jax import lax

D = 1024
MH = 24
HP = 64
NS = 128
CONV = 4
QH = 8
KVH = 2
HD = 64
FF = 2048
LAYERS = 2
BLOCK = 64
TOK_DEV = 256
DSSM = 1536
LENGTH = 1024
TOKENS = 4096
QBLOCK = 256
N_DP = 4


def draw_segment_ids(key, part):
    key = jax.random.fold_in(key, 5)
    first_key, second_key = jax.random.split(key)
    quarter = max(TOK_DEV // 4, 1)
    head_length = jax.random.randint(first_key, (N_DP, 1), quarter, 2 * quarter)
    tail_length = jax.random.randint(second_key, (N_DP, 1), quarter, 2 * quarter)
    positions = jnp.arange(LENGTH)[None, :]
    return (positions >= head_length).astype(jnp.int32) + (positions >= LENGTH - tail_length).astype(jnp.int32)


def draw_ssm_head(key, part):
    key = jax.random.fold_in(key, 11)
    first_key, second_key, third_key = jax.random.split(key, 3)
    step_base = jnp.exp(jax.random.uniform(first_key, (LAYERS, MH), jnp.float32, math.log(0.005), math.log(0.1)))
    step_bias = jnp.log(jnp.expm1(step_base))
    rate_log = jax.random.uniform(second_key, (LAYERS, MH), jnp.float32, math.log(0.02), math.log(4.0))
    skip_factor = jax.random.uniform(third_key, (LAYERS, MH), jnp.float32, 0.5, 1.5)
    return jnp.stack([step_bias, rate_log, skip_factor], axis=1)


def levels(rng, extent, shards, low, top_value):
    level, own = 1.0, jax.random.fold_in(rng, 6)
    for dim, parts in shards:
        heights = jnp.exp(jax.random.uniform(jax.random.fold_in(own, dim), (parts,), jnp.float32, low / len(shards), top_value / len(shards)))
        level = level * jnp.repeat(heights, extent[dim] // parts).reshape([-1 if axis == dim else 1 for axis in range(len(extent))])
    return level


def bell_draw(rng, extent, spread, reach, cuts=(), kind=jnp.bfloat16):
    level = levels(rng, extent, cuts, -0.22, 0.18) if cuts else 1.0
    entries = jax.random.normal(rng, extent, jnp.float32) * spread * level
    return jnp.minimum(jnp.maximum(entries, -reach), reach).astype(kind)


def setup_inputs(seed: int = 0) -> dict:
    arg_keys = jax.random.split(jax.random.key(seed), 18)
    hidden_in = bell_draw(arg_keys[0], (TOKENS, D), 1.0, 6.0, ((0, 16),))
    segment_ids = draw_segment_ids(jax.random.fold_in(arg_keys[17], 71), 0)
    gain_mix = jnp.clip(1.0 + 0.1 * jax.random.normal(arg_keys[2], (LAYERS, D), jnp.float32), 0.5, 1.5).astype(jnp.bfloat16)
    w_zx = bell_draw(arg_keys[3], (LAYERS, D, 2, DSSM), D ** -0.5, 0.1875, ((3, 2),))
    w_bc = bell_draw(arg_keys[4], (LAYERS, D, 2 * NS), D ** -0.5, 0.1875)
    w_dt = bell_draw(arg_keys[5], (LAYERS, D, MH), D ** -0.5, 0.1875, ((2, 2),))
    conv_x = bell_draw(arg_keys[6], (LAYERS, CONV, MH, HP), CONV ** -0.5, 3.0, ((2, 2),))
    conv_bc = bell_draw(arg_keys[7], (LAYERS, CONV, 2 * NS), CONV ** -0.5, 3.0)
    ssm_head = draw_ssm_head(jax.random.fold_in(arg_keys[17], 71), 0)
    w_q = bell_draw(arg_keys[9], (LAYERS, D, QH * HD), D ** -0.5, 0.1875, ((2, 2),))
    w_kv = bell_draw(arg_keys[10], (LAYERS, D, KVH, 2 * HD), D ** -0.5, 0.1875, ((2, 2),))
    w_o = bell_draw(arg_keys[11], (LAYERS, QH * HD, D), (QH * HD // 16) ** -0.5, 1.0, ((1, 2),))
    w_out = bell_draw(arg_keys[12], (LAYERS, DSSM, D), DSSM ** -0.5, 0.15625, ((1, 2),))
    gain_ff = jnp.clip(1.0 + 0.1 * jax.random.normal(arg_keys[13], (LAYERS, D), jnp.float32), 0.5, 1.5).astype(jnp.bfloat16)
    w_gu = bell_draw(arg_keys[14], (LAYERS, D, 2, FF), D ** -0.5, 0.1875, ((3, 2),))
    w_down = bell_draw(arg_keys[15], (LAYERS, FF, D), FF ** -0.5, 0.125, ((1, 2),))
    cotangent = bell_draw(arg_keys[16], (TOKENS, D), 1.0, 6.0, ((0, 16),))
    return {"hidden_in": hidden_in, "segment_ids": segment_ids, "gain_mix": gain_mix, "w_zx": w_zx, "w_bc": w_bc, "w_dt": w_dt, "conv_x": conv_x, "conv_bc": conv_bc, "ssm_head": ssm_head, "w_q": w_q, "w_kv": w_kv, "w_o": w_o, "w_out": w_out, "gain_ff": gain_ff, "w_gu": w_gu, "w_down": w_down, "cotangent": cotangent}


@jax.custom_vjp
def low(v):
    return lax.optimization_barrier(v.astype(jnp.bfloat16)).astype(jnp.float32)

@jax.custom_vjp
def low_back(v):
    return v

def low_keep(v):
    return (low(v), None)

def low_pass(kept, grad):
    return (grad,)

def back_keep(v):
    return (v, None)

def back_low(kept, grad):
    return (low(grad),)
low.defvjp(low_keep, low_pass)
low_back.defvjp(back_keep, back_low)
highest = lax.Precision.HIGHEST
norm_eps = 1e-05
masked_score = -1e+30

def matmul(left, right):
    return jnp.dot(left, right, precision=highest)

def rms_scaled(hidden, gain):
    return hidden * lax.rsqrt(lax.optimization_barrier(jnp.mean(hidden * hidden, axis=-1, keepdims=True)) + norm_eps) * gain

def conv_silu(stacked, weights, doc_ids):
    row_count = stacked.shape[0]
    running_sum = stacked * weights[0]
    for offset in range(1, CONV):
        shifted = jnp.concatenate([jnp.zeros((offset, stacked.shape[1]), jnp.float32), stacked[:row_count - offset]], axis=0)
        earlier = jnp.concatenate([jnp.full((offset,), -1, jnp.int32), doc_ids[:row_count - offset]])
        same_doc = (earlier == doc_ids).astype(jnp.float32)[:, None]
        running_sum = running_sum + shifted * same_doc * weights[offset]
    return jax.nn.silu(running_sum)

def block_step(carry_in, inputs):
    memory, last_doc = carry_in
    values, b_rows, c_rows, step_sizes, log_decay, doc_ids = inputs
    running = jnp.cumsum(log_decay, axis=0)
    gaps_log = running[:, None, :] - running[None, :, :]
    ordered = jnp.arange(BLOCK)[:, None] >= jnp.arange(BLOCK)[None, :]
    linked = ordered & (doc_ids[:, None] == doc_ids[None, :])
    decays = jnp.exp(jnp.where(linked[:, :, None], gaps_log, 0.0)) * linked[:, :, None].astype(jnp.float32)
    intersection = jnp.dot(c_rows, b_rows.T, precision=highest)
    mixing = decays * intersection[:, :, None] * step_sizes[None, :, :]
    outputs = jnp.einsum('tsh,shp->thp', mixing, values, precision=highest)
    carried = (doc_ids == last_doc).astype(jnp.float32)[:, None] * jnp.exp(running)
    outputs = outputs + carried[:, :, None] * jnp.einsum('tn,hpn->thp', c_rows, memory, precision=highest)
    fading = jnp.exp(running[-1][None, :] - running) * (doc_ids == doc_ids[-1]).astype(jnp.float32)[:, None] * step_sizes
    memory = carried[-1][:, None, None] * memory + jnp.einsum('sh,shp,sn->hpn', fading, values, b_rows, precision=highest)
    return ((memory, doc_ids[-1]), outputs)

def ssm_scan(values, b_rows, c_rows, step_sizes, log_decay, doc_ids, start_memory, start_doc):
    block_count = values.shape[0] // BLOCK

    def into_blocks(tensor):
        return tensor.reshape((block_count, BLOCK) + tensor.shape[1:])
    final, scanned = lax.scan(jax.checkpoint(block_step), (start_memory, start_doc), (into_blocks(values), into_blocks(b_rows), into_blocks(c_rows), into_blocks(step_sizes), into_blocks(log_decay), into_blocks(doc_ids)))
    return (final, scanned.reshape(values.shape))

def mamba_part(normed, doc_ids, w_zx, w_bc, w_dt, conv_x, conv_bc, ssm_head):
    length_all = normed.shape[0]
    zx_proj = low(low_back(matmul(normed, w_zx.reshape(D, 2 * DSSM))))
    gate_in = zx_proj[:, :DSSM]
    bc_proj = low(matmul(normed, w_bc))
    dt_raw = low(low_back(matmul(normed, w_dt)))
    stacked = jnp.concatenate([zx_proj[:, DSSM:], bc_proj], axis=1)
    taps_all = jnp.concatenate([conv_x.reshape(CONV, DSSM), conv_bc], axis=1)
    mixed = conv_silu(stacked, taps_all, doc_ids)
    values = mixed[:, :DSSM].reshape(length_all, MH, HP)
    b_rows = mixed[:, DSSM:DSSM + NS]
    c_rows = mixed[:, DSSM + NS:]
    step_sizes = jax.nn.softplus(dt_raw + ssm_head[0])
    log_decay = -jnp.exp(ssm_head[1]) * step_sizes
    _, scanned = ssm_scan(values, b_rows, c_rows, step_sizes, log_decay, doc_ids, jnp.zeros((MH, HP, NS), jnp.float32), jnp.array(-1, jnp.int32))
    ssm_out = scanned + ssm_head[2][None, :, None] * values
    return low(ssm_out.reshape(length_all, DSSM) * jax.nn.silu(gate_in))

def attention_part(normed, doc_ids, w_q, w_kv):
    length_all = normed.shape[0]
    group_size = QH // KVH
    queries = low(low_back(matmul(normed, w_q)))
    keyvals = low(low_back(matmul(normed, w_kv.reshape(D, KVH * 2 * HD)))).reshape(length_all, KVH, 2, HD)
    keys_all = keyvals[:, :, 0]
    vals_all = keyvals[:, :, 1]
    positions = jnp.arange(length_all)
    score_scale = HD ** (-0.5)

    def one_block(start):
        start = start.astype(jnp.int32)
        block_q = lax.dynamic_slice_in_dim(queries, start, QBLOCK, 0).reshape(QBLOCK, KVH, group_size, HD)
        query_pos = start + jnp.arange(QBLOCK).astype(jnp.int32)
        query_doc = lax.dynamic_slice_in_dim(doc_ids, start, QBLOCK, 0)
        allowed = (positions[None, :] <= query_pos[:, None]) & (doc_ids[None, :] == query_doc[:, None])
        scores = low_back(jnp.einsum('tgrd,kgd->grtk', block_q, keys_all, precision=highest) * score_scale)
        scores = jnp.where(allowed[None, None], scores, masked_score)
        weights_soft = low(jax.nn.softmax(scores, axis=-1))
        mixed = jnp.einsum('grtk,kgd->tgrd', weights_soft, vals_all, precision=highest)
        return low(low_back(mixed.reshape(QBLOCK, QH * HD)))
    starts = (jnp.arange(length_all // QBLOCK) * QBLOCK).astype(jnp.int32)
    blocks = lax.map(jax.checkpoint(one_block), starts)
    return blocks.reshape(length_all, QH * HD)

def block_layer(hidden, doc_ids, params):
    gain_mix, w_zx, w_bc, w_dt, conv_x, conv_bc, ssm_head, w_q, w_kv, w_o, w_out, gain_ff, w_gu, w_down = params
    normed = low(rms_scaled(hidden, gain_mix))
    gated = mamba_part(normed, doc_ids, w_zx, w_bc, w_dt, conv_x, conv_bc, ssm_head)
    attended = attention_part(normed, doc_ids, w_q, w_kv)
    branch = low_back(matmul(gated, w_out) + matmul(attended, w_o))
    middle = hidden + branch
    normed_ff = low(rms_scaled(middle, gain_ff))
    gate_up = low(low_back(matmul(normed_ff, w_gu.reshape(D, 2 * FF))))
    inner_act = low(jax.nn.silu(gate_up[:, :FF]) * gate_up[:, FF:])
    return middle + low_back(matmul(inner_act, w_down))

def forward_pass(hidden, params, doc_ids):
    for layer_index in range(LAYERS):
        if layer_index > 0:
            hidden = low(hidden)
        hidden = block_layer(hidden, doc_ids, tuple((weight[layer_index] for weight in params)))
    return hidden

def reference(hidden_in, segment_ids, gain_mix, w_zx, w_bc, w_dt, conv_x, conv_bc, ssm_head, w_q, w_kv, w_o, w_out, gain_ff, w_gu, w_down, cotangent):
    params = tuple((weight.astype(jnp.float32) for weight in (gain_mix, w_zx, w_bc, w_dt, conv_x, conv_bc, ssm_head, w_q, w_kv, w_o, w_out, gain_ff, w_gu, w_down)))
    inputs_all = hidden_in.astype(jnp.float32).reshape(N_DP, LENGTH, D)
    cots_all = cotangent.astype(jnp.float32).reshape(N_DP, LENGTH, D)

    def per_sequence(accum, item):
        sequence_in, sequence_cot, doc_ids = item

        def forward_one(hidden, weights):
            return forward_pass(hidden, weights, doc_ids)
        output, pullback = jax.vjp(forward_one, sequence_in, params)
        grad_hidden, grad_params = pullback(sequence_cot)
        accum = jax.tree.map(jnp.add, accum, grad_params)
        return (accum, (output.astype(jnp.bfloat16), grad_hidden))
    start_grads = tuple((jnp.zeros_like(weight) for weight in params))
    grads, (outputs, grad_inputs) = lax.scan(per_sequence, start_grads, (inputs_all, cots_all, segment_ids))
    return (outputs.reshape(TOKENS, D), grad_inputs.reshape(TOKENS, D), grads[0], grads[1], grads[2], grads[3], grads[4], grads[5], grads[6], grads[7], grads[8], grads[9], grads[10], grads[11], grads[12], grads[13])
```

```python
import functools

import jax
import jax.numpy as jnp
from jax import lax
from jax.experimental import pallas as pl
from jax.experimental.pallas import tpu as pltpu
from jax.sharding import PartitionSpec as P

NS = 128
HD = 64
RIM = 16

highest = lax.Precision.HIGHEST
norm_eps = 1e-05
masked_score = -1e30
bf16 = jnp.bfloat16
f32 = jnp.float32
VMEM_LIMIT = 56 * 1024 * 1024


def nn(left, right):
    return jnp.dot(left, right, preferred_element_type=f32)


def tn(left, right):
    return lax.dot_general(left, right, (((0,), (0,)), ((), ())), preferred_element_type=f32)


def nt(left, right):
    return lax.dot_general(left, right, (((1,), (1,)), ((), ())), preferred_element_type=f32)


def exact(left, right, contract=(1, 0)):
    return lax.dot_general(
        left,
        right,
        (((contract[0],), (contract[1],)), ((), ())),
        precision=highest,
        preferred_element_type=f32,
    )


def sigmoid(v):
    return 1.0 / (1.0 + jnp.exp(-v))


def softplus(v):
    return jnp.maximum(v, 0.0) + jnp.log(1.0 + jnp.exp(-jnp.abs(v)))


def head_map(heads, width):
    rows = lax.broadcasted_iota(jnp.int32, (128, heads * width), 0)
    columns = lax.broadcasted_iota(jnp.int32, (128, heads * width), 1)
    return (columns // width == rows).astype(f32)


def call(kernel, outs, scratch=(), **extra):
    return pl.pallas_call(
        kernel,
        out_shape=[jax.ShapeDtypeStruct(shape, kind) for shape, kind in outs],
        scratch_shapes=list(scratch),
        compiler_params=pltpu.CompilerParams(vmem_limit_bytes=VMEM_LIMIT),
        **extra,
    )


def rms_scaled(hidden, gain):
    return hidden * lax.rsqrt(jnp.mean(hidden * hidden, axis=-1, keepdims=True) + norm_eps) * gain


def project_kernel(h_ref, gain_ref, wzx_ref, wbc_ref, wdt_ref, wq_ref, wkv_ref,
                   normed_ref, gate_ref, stack_ref, dt_ref, q_ref, kv_ref):
    d_local = gate_ref.shape[1]
    normed_ref[...] = rms_scaled(h_ref[...], gain_ref[...]).astype(bf16)
    normed = normed_ref[...]
    q_ref[...] = nn(normed, wq_ref[...]).astype(bf16)
    kv_ref[...] = nn(normed, wkv_ref[...]).astype(bf16)
    dt_ref[...] = nn(normed, wdt_ref[...]).astype(bf16).astype(f32)
    stack_ref[:, d_local:] = nn(normed, wbc_ref[...]).astype(bf16)
    gate_ref[...] = nn(normed, wzx_ref[:, :d_local]).astype(bf16)
    stack_ref[:, :d_local] = nn(normed, wzx_ref[:, d_local:]).astype(bf16)


def ssm_scalars(dt_ref, heads_ref):
    rows = dt_ref.shape[0]
    raw = dt_ref[...] + heads_ref[0:1, :]
    step = softplus(raw)
    log_decay = -jnp.exp(heads_ref[1:2, :]) * step
    place_t = lax.broadcasted_iota(jnp.int32, (rows, rows), 0)
    place_s = lax.broadcasted_iota(jnp.int32, (rows, rows), 1)
    lower = (place_s <= place_t).astype(f32)
    running = exact(lower, log_decay)
    running_t = jnp.transpose(running)
    return raw, step, log_decay, running, running_t, place_t >= place_s


def spread(scalars, mapping):
    return exact(scalars, mapping)


def mix_local_kernel(heads, ext_ref, dt_ref, dcol_ref, dloc_ref, drow_ref, taps_ref, heads_ref,
                     q_ref, kv_ref,
                     y_ref, pre_ref, state_ref, dec_ref, crow_ref, att_ref, lse_ref, ext):
    rows = dt_ref.shape[0]
    d_local = y_ref.shape[1]
    ext[...] = ext_ref[...].astype(f32)
    pre = ext[RIM:RIM + rows, :] * taps_ref[0:1, :]
    for k in range(1, 4):
        pre = pre + ext[RIM - k:RIM - k + rows, :] * dcol_ref[:, k:k + 1] * taps_ref[k:k + 1, :]
    pre_ref[...] = pre
    raw, step, log_decay, running, running_t, ordered = ssm_scalars(dt_ref, heads_ref)
    mapping = head_map(heads, d_local // heads)
    last = running[rows - 1:rows, :]
    fade = jnp.exp(last - running) * dcol_ref[:, 5:6]
    dec = jnp.exp(running) * dcol_ref[:, 4:5]
    dec_ref[...] = dec
    mixed = pre_ref[...] * sigmoid(pre_ref[...])
    values = mixed[:, :d_local]
    b_rows = mixed[:, d_local:d_local + NS].astype(bf16)
    c_rows = mixed[:, d_local + NS:].astype(bf16)
    crow_ref[...] = c_rows
    stepped = values * spread(step, mapping)
    state_ref[...] = tn((stepped * spread(fade, mapping)).astype(bf16), b_rows)
    y_ref[...] = values * spread(heads_ref[2:3, :] + jnp.zeros((8, 128), f32), mapping)[0:1, :]
    linked = ordered & (dcol_ref[:, 0:1] == dloc_ref[0:1, :])
    cb = jnp.where(linked, nt(c_rows, b_rows), 0.0)
    stepped = stepped.astype(bf16)
    lane = lax.broadcasted_iota(jnp.int32, (rows, 128), 1)
    for pair in range(heads // 2):
        span = slice(pair * 128, pair * 128 + 128)
        sides = []
        for h in (2 * pair, 2 * pair + 1):
            gap = running[:, h:h + 1] - running_t[h:h + 1, :]
            mixing = (jnp.exp(jnp.minimum(gap, 0.0)) * cb).astype(bf16)
            sides.append(nn(mixing, stepped[:, span]))
        y_ref[:, span] += jnp.where(lane < 64, sides[0], sides[1])
    allowed = score_mask(dcol_ref, drow_ref)
    keyvals = kv_ref[...]
    keys, vals = keyvals[:, :HD], keyvals[:, HD:]
    totals = jnp.zeros((rows, 128), f32)
    for h in range(q_ref.shape[1] // HD):
        query = q_ref[:, h * HD:(h + 1) * HD] * jnp.asarray(HD ** -0.5, bf16)
        scores = jnp.where(allowed, nt(query, keys), masked_score)
        peak = jnp.max(scores, axis=1, keepdims=True)
        expo = jnp.exp(scores - peak)
        total = jnp.sum(expo, axis=1, keepdims=True)
        probs = (expo * (1.0 / total)).astype(bf16)
        att_ref[:, h * HD:(h + 1) * HD] = nn(probs, vals).astype(bf16)
        totals = jnp.where(lane == h, peak + jnp.log(total), totals)
    lse_ref[...] = totals


def score_mask(dcol_ref, drow_ref):
    rows, length = dcol_ref.shape[0], drow_ref.shape[1]
    query_pos = lax.broadcasted_iota(jnp.int32, (rows, length), 0) + lax.axis_index("seq") * rows
    key_pos = lax.broadcasted_iota(jnp.int32, (rows, length), 1)
    return (key_pos <= query_pos) & (dcol_ref[:, 0:1] == drow_ref[0:1, :])


def mix_finish_kernel(heads, y_ref, dec_ref, crow_ref, gate_ref, mem_ref, att_ref, wout_ref, wo_ref,
                      gated_ref, part_ref):
    d_local = y_ref.shape[1]
    mapping = head_map(heads, d_local // heads)
    carried = spread(dec_ref[...], mapping) * nt(crow_ref[...], mem_ref[...])
    gate = gate_ref[...].astype(f32)
    gated_ref[...] = ((y_ref[...] + carried) * (gate * sigmoid(gate))).astype(bf16)
    part_ref[...] = (nn(gated_ref[...], wout_ref[...]) + nn(att_ref[...], wo_ref[...])).astype(bf16)


def back_push_kernel(heads, branch_ref, wout_ref, wo_ref, gate_ref, dec_ref, crow_ref, q_ref, kv_ref,
                     att_ref, lse_ref, dcol_ref, drow_ref,
                     gg_ref, push_ref, dq_ref, dkv_ref, acc):
    d_local = gg_ref.shape[1]
    rows = gg_ref.shape[0]
    mapping = head_map(heads, d_local // heads)
    branch = branch_ref[...]
    gg_ref[...] = nt(branch, wout_ref[...])
    gate = gate_ref[...].astype(f32)
    grad_ssm = gg_ref[...] * (gate * sigmoid(gate))
    push_ref[...] = tn((grad_ssm * spread(dec_ref[...], mapping)).astype(bf16), crow_ref[...])
    grad_att = nt(branch, wo_ref[...])
    allowed = score_mask(dcol_ref, drow_ref)
    keyvals = kv_ref[...]
    keys, vals = keyvals[:, :HD], keyvals[:, HD:]
    scale = jnp.asarray(HD ** -0.5, bf16)
    for h in range(q_ref.shape[1] // HD):
        span = slice(h * HD, (h + 1) * HD)
        query = q_ref[:, span] * scale
        grad = grad_att[:, span].astype(bf16)
        delta = jnp.sum(grad.astype(f32) * att_ref[:, span].astype(f32), axis=1, keepdims=True)
        scores = jnp.where(allowed, nt(query, keys), masked_score)
        probs = jnp.exp(scores - lse_ref[:, h:h + 1])
        low = probs.astype(bf16)
        grad_scores = (probs * (nt(grad, vals) - delta)).astype(bf16)
        dq_ref[:, span] = (nn(grad_scores, keys) * HD ** -0.5).astype(bf16)
        dk = tn(grad_scores, query)
        dv = tn(low, grad)
        if h == 0:
            acc[:, :HD] = dk
            acc[:, HD:] = dv
        else:
            acc[:, :HD] += dk
            acc[:, HD:] += dv
    dkv_ref[...] = acc[...].astype(bf16)


def back_ssm_kernel(heads, ext_ref, pre_ref, dt_ref, dcol_ref, dloc_ref, taps_ref, heads_ref, gate_ref,
                    gg_ref, mem_ref, gmem_ref,
                    dgate_ref, dext_ref, draw_ref, dtaps_ref, dheads_ref, ext, dy_s, dxs_s, u_s, pad):
    rows = dt_ref.shape[0]
    d_local = gate_ref.shape[1]
    width = pre_ref.shape[1]
    mapping = head_map(heads, d_local // heads)
    raw, step, log_decay, running, running_t, ordered = ssm_scalars(dt_ref, heads_ref)
    last = running[rows - 1:rows, :]
    fade = spread(jnp.exp(last - running) * dcol_ref[:, 5:6], mapping)
    dec = jnp.exp(running) * dcol_ref[:, 4:5]
    steps = spread(step, mapping)
    skip = spread(heads_ref[2:3, :] + jnp.zeros((8, 128), f32), mapping)[0:1, :]
    pre_v = pre_ref[:, :d_local]
    values = pre_v * sigmoid(pre_v)
    pre_n = pre_ref[:, d_local:]
    maps = (pre_n * sigmoid(pre_n)).astype(bf16)
    b_rows, c_rows = maps[:, :NS], maps[:, NS:]
    stepped = (values * steps).astype(bf16)
    gate = gate_ref[...].astype(f32)
    gate_sig = sigmoid(gate)
    grad_ssm = gg_ref[...] * (gate * gate_sig)
    dy_s[...] = grad_ssm.astype(bf16)
    memory = mem_ref[...]
    gmem = gmem_ref[...]
    decs = spread(dec, mapping)
    carried = decs * nt(c_rows, memory)
    back = fade * nt(b_rows, gmem)
    linked = ordered & (dcol_ref[:, 0:1] == dloc_ref[0:1, :])
    cb = jnp.where(linked, nt(c_rows, b_rows), 0.0)
    dcb = jnp.zeros((rows, rows), f32)
    lane = lax.broadcasted_iota(jnp.int32, (rows, 128), 1)
    for pair in range(heads // 2):
        span = slice(pair * 128, pair * 128 + 128)
        stepped_p = stepped[:, span]
        dy_p = dy_s[:, span]
        ys, dxs = [], []
        for side, h in enumerate((2 * pair, 2 * pair + 1)):
            gap = running[:, h:h + 1] - running_t[h:h + 1, :]
            decay = jnp.exp(jnp.minimum(gap, 0.0))
            mixing = (decay * cb).astype(bf16)
            ys.append(nn(mixing, stepped_p))
            dxs.append(tn(mixing, dy_p))
            half = jnp.where((lane < 64) == (side == 0), dy_p, jnp.zeros_like(dy_p))
            dcb = dcb + nt(half, stepped_p) * decay
        u_s[:, span] = jnp.where(lane < 64, ys[0], ys[1])
        dxs_s[:, span] = jnp.where(lane < 64, dxs[0], dxs[1])
    dy_low = dy_s[...].astype(f32)
    stepped_f = stepped.astype(f32)
    scanned = u_s[...] + carried
    dxs_all = dxs_s[...] + back
    drun = exact(dy_low * scanned - stepped_f * dxs_all, mapping, (1, 1))
    ssm_out = scanned + skip * values
    dgate_ref[...] = (gg_ref[...] * ssm_out * (gate_sig * (1.0 + gate * (1.0 - gate_sig)))).astype(bf16)
    gstep = exact(values * dxs_all, mapping, (1, 1))
    ones = jnp.ones((8, 128), f32)
    moved = exact(ones, gmem.astype(f32) * memory.astype(f32), (1, 1))
    end = exact(jnp.sum(stepped_f * back, axis=0, keepdims=True) + jnp.zeros((8, 1), f32), mapping, (1, 1))
    end = end + exact(moved, mapping, (1, 1)) * dec[rows - 1:rows, :]
    upper = (lax.broadcasted_iota(jnp.int32, (rows, rows), 1)
             >= lax.broadcasted_iota(jnp.int32, (rows, rows), 0)).astype(f32)
    dlog = exact(upper, drun) + end[0:1, :]
    draw = (gstep - jnp.exp(heads_ref[1:2, :]) * dlog) * sigmoid(raw)
    draw_ref[...] = draw.astype(bf16)
    dskip = exact(jnp.sum(grad_ssm * values, axis=0, keepdims=True) + jnp.zeros((8, 1), f32), mapping, (1, 1))
    dheads_ref[...] = jnp.zeros((8, 128), f32)
    dheads_ref[0:1, :] = jnp.sum(draw, axis=0, keepdims=True)
    dheads_ref[1:2, :] = jnp.sum(dlog * log_decay, axis=0, keepdims=True)
    dheads_ref[2:3, :] = dskip[0:1, :]
    dcb = jnp.where(linked, dcb, 0.0).astype(bf16)
    dc = nn(dcb, b_rows) + nn((dy_low * decs).astype(bf16), memory)
    db = tn(dcb, c_rows) + nn((stepped_f * fade).astype(bf16), gmem)
    dvalues = steps * dxs_all + skip * grad_ssm

    pad[0:8, :] = jnp.zeros((8, width), f32)
    pad[8 + rows:, :] = jnp.zeros((8, width), f32)
    sig = sigmoid(pre_v)
    pad[8:8 + rows, :d_local] = dvalues * (sig * (1.0 + pre_v * (1.0 - sig)))
    sig = sigmoid(pre_n)
    slope = sig * (1.0 + pre_n * (1.0 - sig))
    pad[8:8 + rows, d_local:d_local + NS] = db * slope[:, :NS]
    pad[8:8 + rows, d_local + NS:] = dc * slope[:, NS:]
    ext[...] = ext_ref[...].astype(f32)
    dpre = pad[8:8 + rows, :]
    total = pad[0:8 + rows, :] * taps_ref[0:1, :]
    dext_ref[...] = total
    dtaps_ref[...] = jnp.zeros((8, width), f32)
    dtaps_ref[0:1, :] = jnp.sum(dpre * ext[RIM:RIM + rows, :], axis=0, keepdims=True)
    for k in range(1, 4):
        masked = dpre * dcol_ref[:, k:k + 1]
        pad[8:8 + rows, :] = masked
        dtaps_ref[k:k + 1, :] = jnp.sum(masked * ext[RIM - k:RIM - k + rows, :], axis=0, keepdims=True)
        dext_ref[...] += pad[k:k + 8 + rows, :] * taps_ref[k:k + 1, :]


def wgrad_kernel(terms, *refs):
    out_ref = refs[-1]
    at = 0
    for i, count in enumerate(terms):
        left = refs[at][...]
        at += 1
        for right in refs[at:at + count]:
            begin = right_offset(refs, terms, at, right)
            out_ref[:, begin:begin + right.shape[1]] = tn(left, right[...]).astype(out_ref.dtype)
        at += count


def right_offset(refs, terms, at, right):
    begin, place = 0, 0
    for count in terms:
        place += 1
        for ref in refs[place:place + count]:
            if ref is right:
                return begin
            begin += ref.shape[1]
        place += count
    return begin


def weight_grads(groups, blocks=8):
    operands, specs, columns, terms = [], [], 0, []
    for left, rights in groups:
        rows, width = left.shape
        operands.append(left)
        specs.append(pl.BlockSpec((rows, width // blocks), lambda i: (0, i)))
        for right in rights:
            operands.append(right)
            specs.append(pl.BlockSpec(right.shape, lambda i: (0, 0)))
            columns += right.shape[1]
        terms.append(len(rights))
    return pl.pallas_call(
        functools.partial(wgrad_kernel, tuple(terms)),
        grid=(blocks,),
        in_specs=specs,
        out_specs=pl.BlockSpec((width // blocks, columns), lambda i: (i, 0)),
        out_shape=jax.ShapeDtypeStruct((width, columns), bf16),
        compiler_params=pltpu.CompilerParams(vmem_limit_bytes=VMEM_LIMIT),
    )(*operands)


def pass_states(state, dec_last, heads, backward):
    count = lax.axis_size("seq")
    place = lax.axis_index("seq")
    states = lax.all_gather(state.astype(bf16), "seq")
    decays = lax.all_gather(dec_last, "seq")
    total = jnp.zeros(state.shape, f32)
    size = state.shape[0] // heads
    order = range(count) if not backward else range(count - 1, -1, -1)
    for source in order:
        ahead = source > place if backward else source < place
        decay = jnp.repeat(decays[source][:heads], size)[:, None]
        total = jnp.where(ahead, decay * total + states[source].astype(f32), total)
    return total.astype(bf16)


def from_behind(value, steps):
    count = lax.axis_size("seq")
    initial, last = (max(0, -steps), min(count, count - steps))
    return lax.ppermute(value, "seq", [(source, source + steps) for source in range(initial, last)])


def layer_forward(hidden, weights, context):
    dcol, dloc, drow = context
    rows, model_width = hidden.shape
    heads = weights["heads"]
    d_local = weights["out"].shape[0]
    ff_local = weights["down"].shape[0]
    width = d_local + 2 * NS
    normed, gate, stack, dt, queries, keyvals = call(
        project_kernel,
        [((rows, model_width), bf16), ((rows, d_local), bf16), ((rows, width), bf16),
         ((rows, 128), f32), ((rows, weights["q"].shape[1]), bf16), ((rows, 128), bf16)],
    )(hidden, weights["gain_mix"], weights["zx"], weights["bc"], weights["dt"], weights["q"], weights["kv"])
    ext = jnp.concatenate([from_behind(stack[rows - RIM:], 1), stack], axis=0)
    keyvals_all = lax.all_gather(keyvals, "seq", axis=0, tiled=True)
    local, pre, state, dec, crow, att, lse = call(
        functools.partial(mix_local_kernel, heads),
        [((rows, d_local), f32), ((rows, width), f32), ((d_local, NS), f32), ((rows, 128), f32),
         ((rows, NS), bf16), ((rows, weights["q"].shape[1]), bf16), ((rows, 128), f32)],
        [pltpu.VMEM((rows + RIM, width), f32)],
    )(ext, dt, dcol, dloc, drow, weights["taps"], weights["head_vals"], queries, keyvals_all)
    memory = pass_states(state, dec[-1], heads, False)
    gated, part = call(
        functools.partial(mix_finish_kernel, heads),
        [((rows, d_local), bf16), ((rows, model_width), bf16)],
    )(local, dec, crow, gate, memory, att, weights["out"], weights["o"])
    middle = hidden + lax.psum(part, "head").astype(f32)
    normed_ff = rms_scaled(middle, weights["gain_ff"]).astype(bf16)
    gate_up = nn(normed_ff, weights["gu"]).astype(bf16)
    inner = (jax.nn.silu(gate_up[:, :ff_local].astype(f32)) * gate_up[:, ff_local:].astype(f32)).astype(bf16)
    output = middle + lax.psum(nn(inner, weights["down"]).astype(bf16), "head").astype(f32)
    saved = (hidden, normed, gate, ext, pre, dt, queries, keyvals_all, dec, crow, att, lse, memory,
             gated, middle, normed_ff, gate_up, inner)
    return output, saved


def layer_backward(grad_out, weights, saved, context):
    dcol, dloc, drow = context
    (hidden, normed, gate, ext, pre, dt, queries, keyvals_all, dec, crow, att, lse, memory,
     gated, middle, normed_ff, gate_up, inner) = saved
    rows, model_width = hidden.shape
    heads = weights["heads"]
    d_local = gate.shape[1]
    ff_local = inner.shape[1]
    width = d_local + 2 * NS
    grad_ff = grad_out.astype(bf16)
    grad_inner = nt(grad_ff, weights["down"])
    gate_f = gate_up[:, :ff_local].astype(f32)
    up_f = gate_up[:, ff_local:].astype(f32)
    sig = jax.nn.sigmoid(gate_f)
    grad_gu = jnp.concatenate(
        [grad_inner * up_f * (sig * (1.0 + gate_f * (1.0 - sig))), grad_inner * gate_f * sig], axis=1
    ).astype(bf16)
    grad_nff = lax.psum(nt(grad_gu, weights["gu"]).astype(bf16), "head").astype(f32)
    ff_grads = weight_grads([(grad_ff, [inner]), (normed_ff, [grad_gu])])
    ff_sum = lax.psum_scatter(ff_grads, ("dp", "seq"), scatter_dimension=0, tiled=True)
    _, pull = jax.vjp(rms_scaled, middle, weights["gain_ff"])
    grad_middle, g_gain_ff = pull(grad_nff)
    grad_middle = grad_middle + grad_out
    branch = grad_middle.astype(bf16)
    gg, push, dq, dkv = call(
        functools.partial(back_push_kernel, heads),
        [((rows, d_local), f32), ((d_local, NS), f32), (queries.shape, bf16), (keyvals_all.shape, bf16)],
        [pltpu.VMEM(keyvals_all.shape, f32)],
    )(branch, weights["out"], weights["o"], gate, dec, crow, queries, keyvals_all, att, lse, dcol, drow)
    gmem = pass_states(push, dec[-1], heads, True)
    grad_kv = lax.psum_scatter(dkv, "seq", scatter_dimension=0, tiled=True)
    dgate, dext, draw, dtaps, dheads = call(
        functools.partial(back_ssm_kernel, heads),
        [((rows, d_local), bf16), ((rows + 8, width), f32), ((rows, 128), bf16), ((8, width), f32),
         ((8, 128), f32)],
        [pltpu.VMEM((rows + RIM, width), f32), pltpu.VMEM((rows, d_local), bf16),
         pltpu.VMEM((rows, d_local), f32), pltpu.VMEM((rows, d_local), f32),
         pltpu.VMEM((rows + 16, width), f32)],
    )(ext, pre, dt, dcol, dloc, weights["taps"], weights["head_vals"], gate, gg, memory, gmem)
    rim = from_behind(dext[:8], -1)
    dstack = dext[8:] + jnp.concatenate([jnp.zeros((rows - 8, width), f32), rim], axis=0)
    dx = dstack[:, :d_local].astype(bf16)
    dbc = dstack[:, d_local:].astype(bf16)
    grad_normed = (
        nt(dgate, weights["zx"][:, :d_local]) + nt(dx, weights["zx"][:, d_local:]) + nt(dbc, weights["bc"])
        + nt(draw, weights["dt"]) + nt(dq, weights["q"]) + nt(grad_kv, weights["kv"])
    )
    grad_normed = lax.psum(grad_normed.astype(bf16), "head").astype(f32)
    mix_grads = weight_grads([(normed, [dgate, dx, dq, grad_kv, draw]), (branch, [gated, att])])
    mix_sum = lax.psum_scatter(mix_grads, ("dp", "seq"), scatter_dimension=0, tiled=True)
    _, pull = jax.vjp(rms_scaled, hidden, weights["gain_mix"])
    grad_hidden, g_gain_mix = pull(grad_normed)
    grad_hidden = grad_hidden + grad_middle
    g_bc = jnp.concatenate(
        [tn(dbc, normed), jnp.pad(jnp.transpose(dtaps[:4, d_local:]), ((0, 0), (0, 124)))], axis=1
    )
    shards = lax.axis_size("dp") * lax.axis_size("seq")
    taps = dtaps[:4, :d_local].reshape(4, heads, shards, -1)
    small = jnp.concatenate(
        [g_gain_mix.reshape(shards, -1), g_gain_ff.reshape(shards, -1),
         jnp.transpose(taps, (2, 0, 1, 3)).reshape(shards, -1),
         jnp.broadcast_to(dheads[:3, :heads].reshape(1, -1), (shards, 3 * heads))], axis=1
    )
    return grad_hidden, ff_sum, mix_sum, g_bc, small


def on_device(hidden_in, segment_ids, gain_mix, w_zx, w_bc, w_dt, conv_x, conv_bc, ssm_head, w_q, w_kv,
              w_o, w_out, gain_ff, w_gu, w_down, cotangent):
    rows, model_width = hidden_in.shape
    taps_count = conv_x.shape[1]
    place = lax.axis_index("seq")
    offset = place * rows
    doc_all = segment_ids[0]
    padded = jnp.concatenate([jnp.full((taps_count - 1,), -1, jnp.int32), doc_all])
    doc_ext = lax.dynamic_slice_in_dim(padded, offset, rows + taps_count - 1)
    docs = doc_ext[taps_count - 1:]
    columns = [docs.astype(f32)]
    for k in range(1, taps_count):
        columns.append((doc_ext[taps_count - 1 - k:taps_count - 1 - k + rows] == docs).astype(f32))
    columns.append((docs == doc_ext[taps_count - 2]).astype(f32))
    columns.append((docs == docs[-1]).astype(f32))
    dcol = jnp.pad(jnp.stack(columns, axis=1), ((0, 0), (0, 128 - len(columns))))
    dloc = jnp.broadcast_to(docs.astype(f32)[None], (8, rows))
    drow = jnp.broadcast_to(doc_all.astype(f32)[None], (8, doc_all.shape[0]))
    context = (dcol, dloc, drow)
    layers = gain_mix.shape[0]
    heads = ssm_head.shape[2]
    d_local = w_zx.shape[3]
    all_weights = []
    for l in range(layers):
        all_weights.append(dict(
            heads=heads,
            gain_mix=gain_mix[l][None].astype(f32),
            gain_ff=gain_ff[l][None].astype(f32),
            zx=w_zx[l].reshape(model_width, -1),
            bc=w_bc[l],
            dt=jnp.pad(w_dt[l], ((0, 0), (0, 128 - heads))),
            q=w_q[l],
            kv=w_kv[l].reshape(model_width, -1),
            o=w_o[l],
            out=w_out[l],
            gu=w_gu[l].reshape(model_width, -1),
            down=w_down[l],
            taps=jnp.pad(jnp.concatenate([conv_x[l].reshape(taps_count, -1), conv_bc[l]], axis=1).astype(f32),
                         ((0, 8 - taps_count), (0, 0))),
            head_vals=jnp.pad(ssm_head[l], ((0, 5), (0, 128 - heads))),
        ))
    hidden = hidden_in.astype(f32)
    saved = []
    output = hidden
    for l in range(layers):
        output, kept = layer_forward(hidden, all_weights[l], context)
        saved.append(kept)
        hidden = output.astype(bf16).astype(f32)
    block_out = output.astype(bf16)
    gradient = cotangent.astype(f32)
    parts = [None] * layers
    for l in reversed(range(layers)):
        gradient, *parts[l] = layer_backward(gradient, all_weights[l], saved[l], context)
    g_bc = lax.psum_scatter(jnp.concatenate([p[2] for p in parts], axis=1), ("dp", "seq", "head"),
                            scatter_dimension=0, tiled=True)
    small = lax.psum_scatter(jnp.concatenate([p[3] for p in parts], axis=1), ("dp", "seq"),
                             scatter_dimension=0, tiled=True)
    ff_local = w_down.shape[1]
    q_width = w_q.shape[2]
    part = model_width // (lax.axis_size("dp") * lax.axis_size("seq"))

    def both(pieces):
        return jnp.stack(pieces, axis=0).astype(f32)

    def cut(index, begin, size):
        return [p[index][:, begin:begin + size] for p in parts]

    down = both([jnp.transpose(a) for a in cut(0, 0, ff_local)])
    gu = both(cut(0, ff_local, 2 * ff_local)).reshape(layers, part, 2, ff_local)
    at = 2 * d_local
    zx = both(cut(1, 0, at)).reshape(layers, part, 2, d_local)
    q = both(cut(1, at, q_width))
    at += q_width
    kv = both(cut(1, at, 128)).reshape(layers, part, 1, 128)
    at += 128
    dt = both(cut(1, at, heads))
    at += 128
    out = both([jnp.transpose(a) for a in cut(1, at, d_local)])
    at += d_local
    o = both([jnp.transpose(a) for a in cut(1, at, q_width)])
    g_bc = g_bc.reshape(g_bc.shape[0], layers, -1)
    w_bc_grad = jnp.transpose(g_bc[:, :, :model_width], (1, 2, 0))
    conv_bc_grad = jnp.transpose(g_bc[:, :, model_width:model_width + taps_count], (1, 2, 0))
    small = small.reshape(layers, -1)
    gain_a = small[:, :part]
    gain_b = small[:, part:2 * part]
    taps_end = 2 * part + taps_count * d_local // (model_width // part)
    conv_x_grad = small[:, 2 * part:taps_end].reshape(layers, taps_count, heads, -1)
    head_grad = small[:, taps_end:].reshape(layers, 3, heads)
    return (block_out, gradient, gain_a, zx, w_bc_grad, dt, conv_x_grad, conv_bc_grad, head_grad, q, kv,
            o, out, gain_b, gu, down)


def solution(mesh):
    in_specs = (
        P(("dp", "seq"), None),
        P("dp", None),
        P(),
        P(None, None, None, "head"),
        P(),
        P(None, None, "head"),
        P(None, None, "head", None),
        P(),
        P(None, None, "head"),
        P(None, None, "head"),
        P(None, None, "head", None),
        P(None, "head", None),
        P(None, "head", None),
        P(),
        P(None, None, None, "head"),
        P(None, "head", None),
        P(("dp", "seq"), None),
    )
    out_specs = (
        P(("dp", "seq"), None),
        P(("dp", "seq"), None),
        P(None, ("dp", "seq")),
        P(None, ("dp", "seq"), None, "head"),
        P(None, None, ("dp", "seq", "head")),
        P(None, ("dp", "seq"), "head"),
        P(None, None, "head", ("dp", "seq")),
        P(None, None, ("dp", "seq", "head")),
        P(None, None, "head"),
        P(None, ("dp", "seq"), "head"),
        P(None, ("dp", "seq"), "head", None),
        P(None, "head", ("dp", "seq")),
        P(None, "head", ("dp", "seq")),
        P(None, ("dp", "seq")),
        P(None, ("dp", "seq"), None, "head"),
        P(None, "head", ("dp", "seq")),
    )
    return jax.shard_map(
        on_device, mesh=mesh, in_specs=in_specs, out_specs=out_specs, check_vma=False
    )
```

```python
import functools

import jax
import jax.numpy as jnp
from jax import lax
from jax.experimental import pallas as pl
from jax.experimental.pallas import tpu as pltpu
from jax.sharding import PartitionSpec as P

NS = 128
HD = 64
RIM = 16

highest = lax.Precision.HIGHEST
norm_eps = 1e-05
masked_score = -1e30
bf16 = jnp.bfloat16
f32 = jnp.float32
VMEM_LIMIT = 56 * 1024 * 1024


def nn(left, right):
    return jnp.dot(left, right, preferred_element_type=f32)


def tn(left, right):
    return lax.dot_general(left, right, (((0,), (0,)), ((), ())), preferred_element_type=f32)


def nt(left, right):
    return lax.dot_general(left, right, (((1,), (1,)), ((), ())), preferred_element_type=f32)


def exact(left, right, contract=(1, 0)):
    return lax.dot_general(
        left,
        right,
        (((contract[0],), (contract[1],)), ((), ())),
        precision=highest,
        preferred_element_type=f32,
    )


def sigmoid(v):
    return 1.0 / (1.0 + jnp.exp(-v))


def softplus(v):
    return jnp.maximum(v, 0.0) + jnp.log(1.0 + jnp.exp(-jnp.abs(v)))


def head_map(heads, width):
    rows = lax.broadcasted_iota(jnp.int32, (128, heads * width), 0)
    columns = lax.broadcasted_iota(jnp.int32, (128, heads * width), 1)
    return (columns // width == rows).astype(f32)


def call(kernel, outs, scratch=(), **extra):
    return pl.pallas_call(
        kernel,
        out_shape=[jax.ShapeDtypeStruct(shape, kind) for shape, kind in outs],
        scratch_shapes=list(scratch),
        compiler_params=pltpu.CompilerParams(vmem_limit_bytes=VMEM_LIMIT),
        **extra,
    )


def rms_scaled(hidden, gain):
    return hidden * lax.rsqrt(jnp.mean(hidden * hidden, axis=-1, keepdims=True) + norm_eps) * gain


def project_kernel(h_ref, gain_ref, wzx_ref, wbc_ref, wdt_ref, wq_ref, wkv_ref,
                   normed_ref, gate_ref, stack_ref, dt_ref, q_ref, kv_ref):
    d_local = gate_ref.shape[1]
    normed_ref[...] = rms_scaled(h_ref[...], gain_ref[...]).astype(bf16)
    normed = normed_ref[...]
    q_ref[...] = nn(normed, wq_ref[...]).astype(bf16)
    kv_ref[...] = nn(normed, wkv_ref[...]).astype(bf16)
    dt_ref[...] = nn(normed, wdt_ref[...]).astype(bf16).astype(f32)
    stack_ref[:, d_local:] = nn(normed, wbc_ref[...]).astype(bf16)
    gate_ref[...] = nn(normed, wzx_ref[:, :d_local]).astype(bf16)
    stack_ref[:, :d_local] = nn(normed, wzx_ref[:, d_local:]).astype(bf16)


def ssm_scalars(dt_ref, heads_ref):
    rows = dt_ref.shape[0]
    raw = dt_ref[...] + heads_ref[0:1, :]
    step = softplus(raw)
    log_decay = -jnp.exp(heads_ref[1:2, :]) * step
    place_t = lax.broadcasted_iota(jnp.int32, (rows, rows), 0)
    place_s = lax.broadcasted_iota(jnp.int32, (rows, rows), 1)
    lower = (place_s <= place_t).astype(f32)
    running = exact(lower, log_decay)
    running_t = jnp.transpose(running)
    return raw, step, log_decay, running, running_t, place_t >= place_s


def spread(scalars, mapping):
    return exact(scalars, mapping)


def mix_local_kernel(heads, ext_ref, dt_ref, dcol_ref, dloc_ref, drow_ref, taps_ref, heads_ref,
                     q_ref, kv_ref,
                     y_ref, pre_ref, state_ref, dec_ref, crow_ref, att_ref, lse_ref, ext):
    rows = dt_ref.shape[0]
    d_local = y_ref.shape[1]
    ext[...] = ext_ref[...].astype(f32)
    pre = ext[RIM:RIM + rows, :] * taps_ref[0:1, :]
    for k in range(1, 4):
        pre = pre + ext[RIM - k:RIM - k + rows, :] * dcol_ref[:, k:k + 1] * taps_ref[k:k + 1, :]
    pre_ref[...] = pre
    raw, step, log_decay, running, running_t, ordered = ssm_scalars(dt_ref, heads_ref)
    mapping = head_map(heads, d_local // heads)
    last = running[rows - 1:rows, :]
    fade = jnp.exp(last - running) * dcol_ref[:, 5:6]
    dec = jnp.exp(running) * dcol_ref[:, 4:5]
    dec_ref[...] = dec
    mixed = pre_ref[...] * sigmoid(pre_ref[...])
    values = mixed[:, :d_local]
    b_rows = mixed[:, d_local:d_local + NS].astype(bf16)
    c_rows = mixed[:, d_local + NS:].astype(bf16)
    crow_ref[...] = c_rows
    stepped = values * spread(step, mapping)
    state_ref[...] = tn((stepped * spread(fade, mapping)).astype(bf16), b_rows)
    y_ref[...] = values * spread(heads_ref[2:3, :] + jnp.zeros((8, 128), f32), mapping)[0:1, :]
    linked = ordered & (dcol_ref[:, 0:1] == dloc_ref[0:1, :])
    cb = jnp.where(linked, nt(c_rows, b_rows), 0.0)
    stepped = stepped.astype(bf16)
    lane = lax.broadcasted_iota(jnp.int32, (rows, 128), 1)
    for pair in range(heads // 2):
        span = slice(pair * 128, pair * 128 + 128)
        sides = []
        for h in (2 * pair, 2 * pair + 1):
            gap = running[:, h:h + 1] - running_t[h:h + 1, :]
            mixing = (jnp.exp(jnp.minimum(gap, 0.0)) * cb).astype(bf16)
            sides.append(nn(mixing, stepped[:, span]))
        y_ref[:, span] += jnp.where(lane < 64, sides[0], sides[1])
    allowed = score_mask(dcol_ref, drow_ref)
    keyvals = kv_ref[...]
    keys, vals = keyvals[:, :HD], keyvals[:, HD:]
    totals = jnp.zeros((rows, 128), f32)
    for h in range(q_ref.shape[1] // HD):
        query = q_ref[:, h * HD:(h + 1) * HD] * jnp.asarray(HD ** -0.5, bf16)
        scores = jnp.where(allowed, nt(query, keys), masked_score)
        peak = jnp.max(scores, axis=1, keepdims=True)
        expo = jnp.exp(scores - peak)
        total = jnp.sum(expo, axis=1, keepdims=True)
        probs = (expo * (1.0 / total)).astype(bf16)
        att_ref[:, h * HD:(h + 1) * HD] = nn(probs, vals).astype(bf16)
        totals = jnp.where(lane == h, peak + jnp.log(total), totals)
    lse_ref[...] = totals


def score_mask(dcol_ref, drow_ref):
    rows, length = dcol_ref.shape[0], drow_ref.shape[1]
    query_pos = lax.broadcasted_iota(jnp.int32, (rows, length), 0) + lax.axis_index("seq") * rows
    key_pos = lax.broadcasted_iota(jnp.int32, (rows, length), 1)
    return (key_pos <= query_pos) & (dcol_ref[:, 0:1] == drow_ref[0:1, :])


def mix_finish_kernel(heads, y_ref, dec_ref, crow_ref, gate_ref, mem_ref, att_ref, wout_ref, wo_ref,
                      gated_ref, part_ref):
    d_local = y_ref.shape[1]
    mapping = head_map(heads, d_local // heads)
    carried = spread(dec_ref[...], mapping) * nt(crow_ref[...], mem_ref[...])
    gate = gate_ref[...].astype(f32)
    gated_ref[...] = ((y_ref[...] + carried) * (gate * sigmoid(gate))).astype(bf16)
    part_ref[...] = (nn(gated_ref[...], wout_ref[...]) + nn(att_ref[...], wo_ref[...])).astype(bf16)


def back_push_kernel(heads, branch_ref, wout_ref, wo_ref, gate_ref, dec_ref, crow_ref, q_ref, kv_ref,
                     att_ref, lse_ref, dcol_ref, drow_ref,
                     gg_ref, push_ref, dq_ref, dkv_ref, acc):
    d_local = gg_ref.shape[1]
    rows = gg_ref.shape[0]
    mapping = head_map(heads, d_local // heads)
    branch = branch_ref[...]
    gg_ref[...] = nt(branch, wout_ref[...])
    gate = gate_ref[...].astype(f32)
    grad_ssm = gg_ref[...] * (gate * sigmoid(gate))
    push_ref[...] = tn((grad_ssm * spread(dec_ref[...], mapping)).astype(bf16), crow_ref[...])
    grad_att = nt(branch, wo_ref[...])
    allowed = score_mask(dcol_ref, drow_ref)
    keyvals = kv_ref[...]
    keys, vals = keyvals[:, :HD], keyvals[:, HD:]
    scale = jnp.asarray(HD ** -0.5, bf16)
    for h in range(q_ref.shape[1] // HD):
        span = slice(h * HD, (h + 1) * HD)
        query = q_ref[:, span] * scale
        grad = grad_att[:, span].astype(bf16)
        delta = jnp.sum(grad.astype(f32) * att_ref[:, span].astype(f32), axis=1, keepdims=True)
        scores = jnp.where(allowed, nt(query, keys), masked_score)
        probs = jnp.exp(scores - lse_ref[:, h:h + 1])
        low = probs.astype(bf16)
        grad_scores = (probs * (nt(grad, vals) - delta)).astype(bf16)
        dq_ref[:, span] = (nn(grad_scores, keys) * HD ** -0.5).astype(bf16)
        dk = tn(grad_scores, query)
        dv = tn(low, grad)
        if h == 0:
            acc[:, :HD] = dk
            acc[:, HD:] = dv
        else:
            acc[:, :HD] += dk
            acc[:, HD:] += dv
    dkv_ref[...] = acc[...].astype(bf16)


def back_ssm_kernel(heads, ext_ref, pre_ref, dt_ref, dcol_ref, dloc_ref, taps_ref, heads_ref, gate_ref,
                    gg_ref, mem_ref, gmem_ref,
                    dgate_ref, dext_ref, draw_ref, dtaps_ref, dheads_ref, ext, dy_s, dxs_s, u_s, pad):
    rows = dt_ref.shape[0]
    d_local = gate_ref.shape[1]
    width = pre_ref.shape[1]
    mapping = head_map(heads, d_local // heads)
    raw, step, log_decay, running, running_t, ordered = ssm_scalars(dt_ref, heads_ref)
    last = running[rows - 1:rows, :]
    fade = spread(jnp.exp(last - running) * dcol_ref[:, 5:6], mapping)
    dec = jnp.exp(running) * dcol_ref[:, 4:5]
    steps = spread(step, mapping)
    skip = spread(heads_ref[2:3, :] + jnp.zeros((8, 128), f32), mapping)[0:1, :]
    pre_v = pre_ref[:, :d_local]
    values = pre_v * sigmoid(pre_v)
    pre_n = pre_ref[:, d_local:]
    maps = (pre_n * sigmoid(pre_n)).astype(bf16)
    b_rows, c_rows = maps[:, :NS], maps[:, NS:]
    stepped = (values * steps).astype(bf16)
    gate = gate_ref[...].astype(f32)
    gate_sig = sigmoid(gate)
    grad_ssm = gg_ref[...] * (gate * gate_sig)
    dy_s[...] = grad_ssm.astype(bf16)
    memory = mem_ref[...]
    gmem = gmem_ref[...]
    decs = spread(dec, mapping)
    carried = decs * nt(c_rows, memory)
    back = fade * nt(b_rows, gmem)
    linked = ordered & (dcol_ref[:, 0:1] == dloc_ref[0:1, :])
    cb = jnp.where(linked, nt(c_rows, b_rows), 0.0)
    dcb = jnp.zeros((rows, rows), f32)
    lane = lax.broadcasted_iota(jnp.int32, (rows, 128), 1)
    for pair in range(heads // 2):
        span = slice(pair * 128, pair * 128 + 128)
        stepped_p = stepped[:, span]
        dy_p = dy_s[:, span]
        ys, dxs = [], []
        for side, h in enumerate((2 * pair, 2 * pair + 1)):
            gap = running[:, h:h + 1] - running_t[h:h + 1, :]
            decay = jnp.exp(jnp.minimum(gap, 0.0))
            mixing = (decay * cb).astype(bf16)
            ys.append(nn(mixing, stepped_p))
            dxs.append(tn(mixing, dy_p))
            half = jnp.where((lane < 64) == (side == 0), dy_p, jnp.zeros_like(dy_p))
            dcb = dcb + nt(half, stepped_p) * decay
        u_s[:, span] = jnp.where(lane < 64, ys[0], ys[1])
        dxs_s[:, span] = jnp.where(lane < 64, dxs[0], dxs[1])
    dy_low = dy_s[...].astype(f32)
    stepped_f = stepped.astype(f32)
    scanned = u_s[...] + carried
    dxs_all = dxs_s[...] + back
    drun = exact(dy_low * scanned - stepped_f * dxs_all, mapping, (1, 1))
    ssm_out = scanned + skip * values
    dgate_ref[...] = (gg_ref[...] * ssm_out * (gate_sig * (1.0 + gate * (1.0 - gate_sig)))).astype(bf16)
    gstep = exact(values * dxs_all, mapping, (1, 1))
    ones = jnp.ones((8, 128), f32)
    moved = exact(ones, gmem.astype(f32) * memory.astype(f32), (1, 1))
    end = exact(jnp.sum(stepped_f * back, axis=0, keepdims=True) + jnp.zeros((8, 1), f32), mapping, (1, 1))
    end = end + exact(moved, mapping, (1, 1)) * dec[rows - 1:rows, :]
    upper = (lax.broadcasted_iota(jnp.int32, (rows, rows), 1)
             >= lax.broadcasted_iota(jnp.int32, (rows, rows), 0)).astype(f32)
    dlog = exact(upper, drun) + end[0:1, :]
    draw = (gstep - jnp.exp(heads_ref[1:2, :]) * dlog) * sigmoid(raw)
    draw_ref[...] = draw.astype(bf16)
    dskip = exact(jnp.sum(grad_ssm * values, axis=0, keepdims=True) + jnp.zeros((8, 1), f32), mapping, (1, 1))
    dheads_ref[...] = jnp.zeros((8, 128), f32)
    dheads_ref[0:1, :] = jnp.sum(draw, axis=0, keepdims=True)
    dheads_ref[1:2, :] = jnp.sum(dlog * log_decay, axis=0, keepdims=True)
    dheads_ref[2:3, :] = dskip[0:1, :]
    dcb = jnp.where(linked, dcb, 0.0).astype(bf16)
    dc = nn(dcb, b_rows) + nn((dy_low * decs).astype(bf16), memory)
    db = tn(dcb, c_rows) + nn((stepped_f * fade).astype(bf16), gmem)
    dvalues = steps * dxs_all + skip * grad_ssm

    pad[0:8, :] = jnp.zeros((8, width), f32)
    pad[8 + rows:, :] = jnp.zeros((8, width), f32)
    sig = sigmoid(pre_v)
    pad[8:8 + rows, :d_local] = dvalues * (sig * (1.0 + pre_v * (1.0 - sig)))
    sig = sigmoid(pre_n)
    slope = sig * (1.0 + pre_n * (1.0 - sig))
    pad[8:8 + rows, d_local:d_local + NS] = db * slope[:, :NS]
    pad[8:8 + rows, d_local + NS:] = dc * slope[:, NS:]
    ext[...] = ext_ref[...].astype(f32)
    dpre = pad[8:8 + rows, :]
    total = pad[0:8 + rows, :] * taps_ref[0:1, :]
    dext_ref[...] = total
    dtaps_ref[...] = jnp.zeros((8, width), f32)
    dtaps_ref[0:1, :] = jnp.sum(dpre * ext[RIM:RIM + rows, :], axis=0, keepdims=True)
    for k in range(1, 4):
        masked = dpre * dcol_ref[:, k:k + 1]
        pad[8:8 + rows, :] = masked
        dtaps_ref[k:k + 1, :] = jnp.sum(masked * ext[RIM - k:RIM - k + rows, :], axis=0, keepdims=True)
        dext_ref[...] += pad[k:k + 8 + rows, :] * taps_ref[k:k + 1, :]


def wgrad_kernel(terms, *refs):
    out_ref = refs[-1]
    at = 0
    for i, count in enumerate(terms):
        left = refs[at][...]
        at += 1
        for right in refs[at:at + count]:
            begin = right_offset(refs, terms, at, right)
            out_ref[:, begin:begin + right.shape[1]] = tn(left, right[...]).astype(out_ref.dtype)
        at += count


def right_offset(refs, terms, at, right):
    begin, place = 0, 0
    for count in terms:
        place += 1
        for ref in refs[place:place + count]:
            if ref is right:
                return begin
            begin += ref.shape[1]
        place += count
    return begin


def weight_grads(groups, blocks=8):
    operands, specs, columns, terms = [], [], 0, []
    for left, rights in groups:
        rows, width = left.shape
        operands.append(left)
        specs.append(pl.BlockSpec((rows, width // blocks), lambda i: (0, i)))
        for right in rights:
            operands.append(right)
            specs.append(pl.BlockSpec(right.shape, lambda i: (0, 0)))
            columns += right.shape[1]
        terms.append(len(rights))
    return pl.pallas_call(
        functools.partial(wgrad_kernel, tuple(terms)),
        grid=(blocks,),
        in_specs=specs,
        out_specs=pl.BlockSpec((width // blocks, columns), lambda i: (i, 0)),
        out_shape=jax.ShapeDtypeStruct((width, columns), bf16),
        compiler_params=pltpu.CompilerParams(vmem_limit_bytes=VMEM_LIMIT),
    )(*operands)


def pass_states(state, dec_last, heads, backward):
    count = lax.axis_size("seq")
    place = lax.axis_index("seq")
    states = lax.all_gather(state.astype(bf16), "seq")
    decays = lax.all_gather(dec_last, "seq")
    total = jnp.zeros(state.shape, f32)
    size = state.shape[0] // heads
    order = range(count) if not backward else range(count - 1, -1, -1)
    for source in order:
        ahead = source > place if backward else source < place
        decay = jnp.repeat(decays[source][:heads], size)[:, None]
        total = jnp.where(ahead, decay * total + states[source].astype(f32), total)
    return total.astype(bf16)


def from_behind(value, steps):
    count = lax.axis_size("seq")
    initial, last = (max(0, -steps), min(count, count - steps))
    return lax.ppermute(value, "seq", [(source, source + steps) for source in range(initial, last)])


MESH_ID = pl.DeviceIdType.MESH
CHUNK = 128


def remote(src, dst, send, recv, axis, target):
    return pltpu.make_async_remote_copy(
        src_ref=src, dst_ref=dst, send_sem=send, recv_sem=recv,
        device_id={axis: target}, device_id_type=MESH_ID,
    )


def meet(count, later_sends):
    place = lax.axis_index("seq")
    barrier = pltpu.get_barrier_semaphore()
    for j in range(1, count):
        here = place - j if not later_sends else place + j

        @pl.when((here >= 0) & (here < count))
        def _():
            pl.semaphore_signal(barrier, inc=1, device_id={"seq": here}, device_id_type=MESH_ID)
    heads_axis = lax.axis_size("head")
    partner = lax.rem(lax.axis_index("head") + 1, heads_axis)
    pl.semaphore_signal(barrier, inc=1, device_id={"head": partner}, device_id_type=MESH_ID)
    waits = (place if later_sends else count - 1 - place) + 1
    pl.semaphore_wait(barrier, waits)
    return partner


def layer_forward_kernel(heads, h_ref, gain_mix_ref, gain_ff_ref, wzx_ref, wbc_ref, wdt_ref, wq_ref, wkv_ref,
                         taps_ref, heads_ref, dcol_ref, dloc_ref, drow_ref,
                         wo_hbm, wout_hbm, wgu_hbm, wdown_hbm,
                         h_out, normed_ref, gate_ref, stack_ref, rim_ref, pre_ref, dt_ref, q_ref, kvall_ref,
                         att_ref, lse_ref, mem_ref, gated_ref, middle_ref, nff_ref, gu_ref, inner_ref,
                         ext, y, wo_ref, wout_ref, wgu_ref, wdown_ref, rim_in, kv_in, chain_in, chain_out,
                         part_out, part_in, down_out, down_in,
                         load_sem, kv_send, kv_recv, rim_send, rim_recv, chain_send, chain_recv,
                         part_send, part_recv, down_send, down_recv):
    rows = dt_ref.shape[0]
    d_local = gate_ref.shape[1]
    ff_local = inner_ref.shape[1]
    count = lax.axis_size("seq")
    place = lax.axis_index("seq")
    loads = [
        pltpu.make_async_copy(src, dst, load_sem.at[i])
        for i, (src, dst) in enumerate(((wout_hbm, wout_ref), (wo_hbm, wo_ref), (wgu_hbm, wgu_ref),
                                        (wdown_hbm, wdown_ref)))
    ]
    for load in loads:
        load.start()
    partner = meet(count, False)

    normed_ref[...] = rms_scaled(h_ref[...].astype(f32), gain_mix_ref[...]).astype(bf16)
    normed = normed_ref[...]
    own = pl.ds(pl.multiple_of(place * rows, rows), rows)
    for j in range(count):
        @pl.when(j > place)
        def _():
            kv_in[j * rows:(j + 1) * rows, :] = jnp.zeros((rows, 2 * HD), bf16)
    kv_in[own, :] = nn(normed, wkv_ref[...]).astype(bf16)
    kv_copies = [
        remote(kv_in.at[own], kv_in.at[own], kv_send.at[j - 1], kv_recv.at[j - 1], "seq", place + j)
        for j in range(1, count)
    ]
    for j in range(1, count):
        @pl.when(place + j < count)
        def _():
            kv_copies[j - 1].start()
    stack_ref[:, d_local:] = nn(normed, wbc_ref[...]).astype(bf16)
    stack_ref[:, :d_local] = nn(normed, wzx_ref[:, d_local:]).astype(bf16)
    rim_copy = remote(stack_ref.at[pl.ds(rows - RIM, RIM)], rim_in, rim_send, rim_recv, "seq", place + 1)

    @pl.when(place + 1 < count)
    def _():
        rim_copy.start()

    @pl.when(place == 0)
    def _():
        rim_in[...] = jnp.zeros(rim_in.shape, bf16)
        chain_in[...] = jnp.zeros(chain_in.shape, bf16)
    dt_ref[...] = nn(normed, wdt_ref[...]).astype(bf16).astype(f32)
    gate_ref[...] = nn(normed, wzx_ref[:, :d_local]).astype(bf16)
    q_ref[...] = nn(normed, wq_ref[...]).astype(bf16)
    raw, step, log_decay, running, running_t, ordered = ssm_scalars(dt_ref, heads_ref)
    mapping = head_map(heads, d_local // heads)
    last = running[rows - 1:rows, :]
    fade = jnp.exp(last - running) * dcol_ref[:, 5:6]
    dec = jnp.exp(running) * dcol_ref[:, 4:5]
    ends = jnp.exp(running_t[:, rows - 1:rows]) * dcol_ref[rows - 1:rows, 4:5] + jnp.zeros((128, NS), f32)
    ends = exact(mapping, ends, (0, 0))
    steps = spread(step, mapping)
    ext[RIM:, :] = stack_ref[...].astype(f32)

    @pl.when(place > 0)
    def _():
        rim_copy.wait_recv()
    rim_ref[...] = rim_in[...]
    ext[0:RIM, :] = rim_in[...].astype(f32)
    pre = ext[RIM:RIM + rows, :] * taps_ref[0:1, :]
    for k in range(1, 4):
        pre = pre + ext[RIM - k:RIM - k + rows, :] * dcol_ref[:, k:k + 1] * taps_ref[k:k + 1, :]
    pre_ref[...] = pre
    mixed = pre_ref[...] * sigmoid(pre_ref[...])
    values = mixed[:, :d_local]
    b_rows = mixed[:, d_local:d_local + NS].astype(bf16)
    c_rows = mixed[:, d_local + NS:].astype(bf16)
    stepped = values * steps
    state = tn((stepped * spread(fade, mapping)).astype(bf16), b_rows)
    y[...] = values * spread(heads_ref[2:3, :] + jnp.zeros((8, 128), f32), mapping)[0:1, :]
    linked = ordered & (dcol_ref[:, 0:1] == dloc_ref[0:1, :])
    cb = jnp.where(linked, nt(c_rows, b_rows), 0.0)
    stepped = stepped.astype(bf16)
    lane = lax.broadcasted_iota(jnp.int32, (rows, 128), 1)

    for j in range(1, count):
        @pl.when(place - j >= 0)
        def _():
            kv_copies[j - 1].wait_recv()
    allowed = score_mask(dcol_ref, drow_ref)
    keyvals = kv_in[...]
    kvall_ref[...] = keyvals
    keys, vals = keyvals[:, :HD], keyvals[:, HD:]
    totals = jnp.zeros((rows, 128), f32)
    pairs = heads // 2
    query_heads = q_ref.shape[1] // HD
    chain_copies = []
    for pair in range(pairs):
        span = slice(pair * 128, pair * 128 + 128)
        copy = remote(chain_out.at[pl.ds(pair * 128, 128)], chain_in.at[pl.ds(pair * 128, 128)],
                      chain_send.at[pair], chain_recv.at[pair], "seq", place + 1)
        chain_copies.append(copy)

        @pl.when(place > 0)
        def _():
            copy.wait_recv()
        chain_out[span, :] = (ends[span] * chain_in[span, :].astype(f32) + state[span]).astype(bf16)

        @pl.when(place + 1 < count)
        def _():
            copy.start()
        sides = []
        for h in (2 * pair, 2 * pair + 1):
            gap = running[:, h:h + 1] - running_t[h:h + 1, :]
            mixing = (jnp.exp(jnp.minimum(gap, 0.0)) * cb).astype(bf16)
            sides.append(nn(mixing, stepped[:, span]))
        y[:, span] += jnp.where(lane < 64, sides[0], sides[1])
        for h in range(query_heads * pair // pairs, query_heads * (pair + 1) // pairs):
            query = q_ref[:, h * HD:(h + 1) * HD] * jnp.asarray(HD ** -0.5, bf16)
            scores = jnp.where(allowed, nt(query, keys), masked_score)
            peak = jnp.max(scores, axis=1, keepdims=True)
            expo = jnp.exp(scores - peak)
            total = jnp.sum(expo, axis=1, keepdims=True)
            probs = (expo * (1.0 / total)).astype(bf16)
            att_ref[:, h * HD:(h + 1) * HD] = nn(probs, vals).astype(bf16)
            totals = jnp.where(lane == h, peak + jnp.log(total), totals)
    lse_ref[...] = totals
    mem_ref[...] = chain_in[...]
    decs = spread(dec, mapping)
    carried = decs * nt(c_rows, mem_ref[...])
    gate = gate_ref[...].astype(f32)
    gated_ref[...] = ((y[...] + carried) * (gate * sigmoid(gate))).astype(bf16)
    loads[0].wait()
    loads[1].wait()
    chunks = [pl.ds(begin, CHUNK) for begin in range(0, rows, CHUNK)]
    part_copies, down_copies = [], []
    for i, chunk in enumerate(chunks):
        part_out[chunk, :] = (nn(gated_ref[chunk, :], wout_ref[...])
                              + nn(att_ref[chunk, :], wo_ref[...])).astype(bf16)
        copy = remote(part_out.at[chunk], part_in.at[chunk], part_send.at[i], part_recv.at[i], "head", partner)
        copy.start()
        part_copies.append(copy)
    loads[2].wait()
    loads[3].wait()
    for i, chunk in enumerate(chunks):
        part_copies[i].wait_recv()
        middle_ref[chunk, :] = h_ref[chunk, :].astype(f32) + (
            part_out[chunk, :].astype(f32) + part_in[chunk, :].astype(f32))
        nff_ref[chunk, :] = rms_scaled(middle_ref[chunk, :], gain_ff_ref[...]).astype(bf16)
        gu_ref[chunk, :] = nn(nff_ref[chunk, :], wgu_ref[...]).astype(bf16)
        gate = gu_ref[chunk, :ff_local].astype(f32)
        inner_ref[chunk, :] = (gate * sigmoid(gate) * gu_ref[chunk, ff_local:].astype(f32)).astype(bf16)
        down_out[chunk, :] = nn(inner_ref[chunk, :], wdown_ref[...]).astype(bf16)
        copy = remote(down_out.at[chunk], down_in.at[chunk], down_send.at[i], down_recv.at[i], "head", partner)
        copy.start()
        down_copies.append(copy)
    for i, chunk in enumerate(chunks):
        down_copies[i].wait_recv()
        h_out[chunk, :] = (middle_ref[chunk, :] + (
            down_out[chunk, :].astype(f32) + down_in[chunk, :].astype(f32))).astype(bf16)
    for i in range(len(chunks)):
        part_copies[i].wait_send()
        down_copies[i].wait_send()

    @pl.when(place + 1 < count)
    def _():
        rim_copy.wait_send()
        for copy in chain_copies:
            copy.wait_send()
    for j in range(1, count):
        @pl.when(place + j < count)
        def _():
            kv_copies[j - 1].wait_send()


VM = pl.BlockSpec(memory_space=pltpu.VMEM)
ANY = pl.BlockSpec(memory_space=pl.ANY)
DMA = pltpu.SemaphoreType.DMA


def layer_forward(hidden, w, context):
    dcol, dloc, drow = context
    rows, model_width = hidden.shape
    heads = w["heads"]
    d_local = w["out"].shape[0]
    ff_local = w["down"].shape[0]
    q_width = w["q"].shape[1]
    width = d_local + 2 * NS
    count = lax.axis_size("seq")
    length = count * rows
    parts = rows // CHUNK
    outs = [
        ((rows, model_width), bf16), ((rows, model_width), bf16), ((rows, d_local), bf16), ((rows, width), bf16),
        ((RIM, width), bf16), ((rows, width), f32), ((rows, 128), f32), ((rows, q_width), bf16),
        ((length, 2 * HD), bf16), ((rows, q_width), bf16), ((rows, 128), f32), ((d_local, NS), bf16),
        ((rows, d_local), bf16), ((rows, model_width), f32), ((rows, model_width), bf16),
        ((rows, 2 * ff_local), bf16), ((rows, ff_local), bf16),
    ]
    full = (rows, model_width)
    result = pl.pallas_call(
        functools.partial(layer_forward_kernel, heads),
        out_shape=[jax.ShapeDtypeStruct(shape, kind) for shape, kind in outs],
        in_specs=[VM] * 13 + [ANY] * 4,
        out_specs=[VM] * len(outs),
        scratch_shapes=[
            pltpu.VMEM((rows + RIM, width), f32), pltpu.VMEM((rows, d_local), f32),
            pltpu.VMEM(w["o"].shape, bf16), pltpu.VMEM(w["out"].shape, bf16),
            pltpu.VMEM(w["gu"].shape, bf16), pltpu.VMEM(w["down"].shape, bf16),
            pltpu.VMEM((RIM, width), bf16), pltpu.VMEM((length, 2 * HD), bf16),
            pltpu.VMEM((d_local, NS), bf16), pltpu.VMEM((d_local, NS), bf16),
            pltpu.VMEM(full, bf16), pltpu.VMEM(full, bf16), pltpu.VMEM(full, bf16), pltpu.VMEM(full, bf16),
            DMA((4,)), DMA((count - 1,)), DMA((count - 1,)), DMA, DMA, DMA((heads // 2,)), DMA((heads // 2,)),
            DMA((parts,)), DMA((parts,)), DMA((parts,)), DMA((parts,)),
        ],
        compiler_params=pltpu.CompilerParams(
            vmem_limit_bytes=VMEM_LIMIT, collective_id=0, has_side_effects=True),
    )(hidden, w["gain_mix"], w["gain_ff"], w["zx"], w["bc"], w["dt"], w["q"], w["kv"], w["taps"],
      w["head_vals"], dcol, dloc, drow, w["o"], w["out"], w["gu"], w["down"])
    names = ("out", "normed", "gate", "stack", "rim", "pre", "dt", "q", "kv", "att", "lse", "memory",
             "gated", "middle", "nff", "gu", "inner")
    saved = dict(zip(names, result))
    saved["hidden"] = hidden
    return saved.pop("out"), saved


def layer_backward(grad_out, weights, saved, context):
    dcol, dloc, drow = context
    hidden, normed, gate, pre, dt = (saved[name] for name in ("hidden", "normed", "gate", "pre", "dt"))
    queries, keyvals_all, att, lse, memory = (saved[name] for name in ("q", "kv", "att", "lse", "memory"))
    gated, middle, normed_ff, gate_up, inner = (saved[name] for name in ("gated", "middle", "nff", "gu", "inner"))
    hidden = hidden.astype(f32)
    ext = jnp.concatenate([saved["rim"], saved["stack"]], axis=0)
    step = jax.nn.softplus(dt + weights["head_vals"][0:1])
    dec = jnp.exp(jnp.cumsum(-jnp.exp(weights["head_vals"][1:2]) * step, axis=0)) * dcol[:, 4:5]
    crow = pre[:, pre.shape[1] - NS:]
    crow = (crow * jax.nn.sigmoid(crow)).astype(bf16)
    rows, model_width = hidden.shape
    heads = weights["heads"]
    d_local = gate.shape[1]
    ff_local = inner.shape[1]
    width = d_local + 2 * NS
    grad_ff = grad_out.astype(bf16)
    grad_inner = nt(grad_ff, weights["down"])
    gate_f = gate_up[:, :ff_local].astype(f32)
    up_f = gate_up[:, ff_local:].astype(f32)
    sig = jax.nn.sigmoid(gate_f)
    grad_gu = jnp.concatenate(
        [grad_inner * up_f * (sig * (1.0 + gate_f * (1.0 - sig))), grad_inner * gate_f * sig], axis=1
    ).astype(bf16)
    grad_nff = lax.psum(nt(grad_gu, weights["gu"]).astype(bf16), "head").astype(f32)
    ff_grads = weight_grads([(grad_ff, [inner]), (normed_ff, [grad_gu])])
    ff_sum = lax.psum_scatter(ff_grads, ("dp", "seq"), scatter_dimension=0, tiled=True)
    _, pull = jax.vjp(rms_scaled, middle, weights["gain_ff"])
    grad_middle, g_gain_ff = pull(grad_nff)
    grad_middle = grad_middle + grad_out
    branch = grad_middle.astype(bf16)
    gg, push, dq, dkv = call(
        functools.partial(back_push_kernel, heads),
        [((rows, d_local), f32), ((d_local, NS), f32), (queries.shape, bf16), (keyvals_all.shape, bf16)],
        [pltpu.VMEM(keyvals_all.shape, f32)],
    )(branch, weights["out"], weights["o"], gate, dec, crow, queries, keyvals_all, att, lse, dcol, drow)
    gmem = pass_states(push, dec[-1], heads, True)
    grad_kv = lax.psum_scatter(dkv, "seq", scatter_dimension=0, tiled=True)
    dgate, dext, draw, dtaps, dheads = call(
        functools.partial(back_ssm_kernel, heads),
        [((rows, d_local), bf16), ((rows + 8, width), f32), ((rows, 128), bf16), ((8, width), f32),
         ((8, 128), f32)],
        [pltpu.VMEM((rows + RIM, width), f32), pltpu.VMEM((rows, d_local), bf16),
         pltpu.VMEM((rows, d_local), f32), pltpu.VMEM((rows, d_local), f32),
         pltpu.VMEM((rows + 16, width), f32)],
    )(ext, pre, dt, dcol, dloc, weights["taps"], weights["head_vals"], gate, gg, memory, gmem)
    rim = from_behind(dext[:8], -1)
    dstack = dext[8:] + jnp.concatenate([jnp.zeros((rows - 8, width), f32), rim], axis=0)
    dx = dstack[:, :d_local].astype(bf16)
    dbc = dstack[:, d_local:].astype(bf16)
    grad_normed = (
        nt(dgate, weights["zx"][:, :d_local]) + nt(dx, weights["zx"][:, d_local:]) + nt(dbc, weights["bc"])
        + nt(draw, weights["dt"]) + nt(dq, weights["q"]) + nt(grad_kv, weights["kv"])
    )
    grad_normed = lax.psum(grad_normed.astype(bf16), "head").astype(f32)
    mix_grads = weight_grads([(normed, [dgate, dx, dq, grad_kv, draw]), (branch, [gated, att])])
    mix_sum = lax.psum_scatter(mix_grads, ("dp", "seq"), scatter_dimension=0, tiled=True)
    _, pull = jax.vjp(rms_scaled, hidden, weights["gain_mix"])
    grad_hidden, g_gain_mix = pull(grad_normed)
    grad_hidden = grad_hidden + grad_middle
    g_bc = jnp.concatenate(
        [tn(dbc, normed), jnp.pad(jnp.transpose(dtaps[:4, d_local:]), ((0, 0), (0, 124)))], axis=1
    )
    shards = lax.axis_size("dp") * lax.axis_size("seq")
    taps = dtaps[:4, :d_local].reshape(4, heads, shards, -1)
    small = jnp.concatenate(
        [g_gain_mix.reshape(shards, -1), g_gain_ff.reshape(shards, -1),
         jnp.transpose(taps, (2, 0, 1, 3)).reshape(shards, -1),
         jnp.broadcast_to(dheads[:3, :heads].reshape(1, -1), (shards, 3 * heads))], axis=1
    )
    return grad_hidden, ff_sum, mix_sum, g_bc, small


def on_device(hidden_in, segment_ids, gain_mix, w_zx, w_bc, w_dt, conv_x, conv_bc, ssm_head, w_q, w_kv,
              w_o, w_out, gain_ff, w_gu, w_down, cotangent):
    rows, model_width = hidden_in.shape
    taps_count = conv_x.shape[1]
    place = lax.axis_index("seq")
    offset = place * rows
    doc_all = segment_ids[0]
    padded = jnp.concatenate([jnp.full((taps_count - 1,), -1, jnp.int32), doc_all])
    doc_ext = lax.dynamic_slice_in_dim(padded, offset, rows + taps_count - 1)
    docs = doc_ext[taps_count - 1:]
    columns = [docs.astype(f32)]
    for k in range(1, taps_count):
        columns.append((doc_ext[taps_count - 1 - k:taps_count - 1 - k + rows] == docs).astype(f32))
    columns.append((docs == doc_ext[taps_count - 2]).astype(f32))
    columns.append((docs == docs[-1]).astype(f32))
    dcol = jnp.pad(jnp.stack(columns, axis=1), ((0, 0), (0, 128 - len(columns))))
    dloc = jnp.broadcast_to(docs.astype(f32)[None], (8, rows))
    drow = jnp.broadcast_to(doc_all.astype(f32)[None], (8, doc_all.shape[0]))
    context = (dcol, dloc, drow)
    layers = gain_mix.shape[0]
    heads = ssm_head.shape[2]
    d_local = w_zx.shape[3]
    all_weights = []
    for l in range(layers):
        all_weights.append(dict(
            heads=heads,
            gain_mix=gain_mix[l][None].astype(f32),
            gain_ff=gain_ff[l][None].astype(f32),
            zx=w_zx[l].reshape(model_width, -1),
            bc=w_bc[l],
            dt=jnp.pad(w_dt[l], ((0, 0), (0, 128 - heads))),
            q=w_q[l],
            kv=w_kv[l].reshape(model_width, -1),
            o=w_o[l],
            out=w_out[l],
            gu=w_gu[l].reshape(model_width, -1),
            down=w_down[l],
            taps=jnp.pad(jnp.concatenate([conv_x[l].reshape(taps_count, -1), conv_bc[l]], axis=1).astype(f32),
                         ((0, 8 - taps_count), (0, 0))),
            head_vals=jnp.pad(ssm_head[l], ((0, 5), (0, 128 - heads))),
        ))
    hidden = hidden_in
    saved = []
    for l in range(layers):
        hidden, kept = layer_forward(hidden, all_weights[l], context)
        saved.append(kept)
    block_out = hidden
    gradient = cotangent.astype(f32)
    parts = [None] * layers
    for l in reversed(range(layers)):
        gradient, *parts[l] = layer_backward(gradient, all_weights[l], saved[l], context)
    g_bc = lax.psum_scatter(jnp.concatenate([p[2] for p in parts], axis=1), ("dp", "seq", "head"),
                            scatter_dimension=0, tiled=True)
    small = lax.psum_scatter(jnp.concatenate([p[3] for p in parts], axis=1), ("dp", "seq"),
                             scatter_dimension=0, tiled=True)
    ff_local = w_down.shape[1]
    q_width = w_q.shape[2]
    part = model_width // (lax.axis_size("dp") * lax.axis_size("seq"))

    def both(pieces):
        return jnp.stack(pieces, axis=0).astype(f32)

    def cut(index, begin, size):
        return [p[index][:, begin:begin + size] for p in parts]

    down = both([jnp.transpose(a) for a in cut(0, 0, ff_local)])
    gu = both(cut(0, ff_local, 2 * ff_local)).reshape(layers, part, 2, ff_local)
    at = 2 * d_local
    zx = both(cut(1, 0, at)).reshape(layers, part, 2, d_local)
    q = both(cut(1, at, q_width))
    at += q_width
    kv = both(cut(1, at, 128)).reshape(layers, part, 1, 128)
    at += 128
    dt = both(cut(1, at, heads))
    at += 128
    out = both([jnp.transpose(a) for a in cut(1, at, d_local)])
    at += d_local
    o = both([jnp.transpose(a) for a in cut(1, at, q_width)])
    g_bc = g_bc.reshape(g_bc.shape[0], layers, -1)
    w_bc_grad = jnp.transpose(g_bc[:, :, :model_width], (1, 2, 0))
    conv_bc_grad = jnp.transpose(g_bc[:, :, model_width:model_width + taps_count], (1, 2, 0))
    small = small.reshape(layers, -1)
    gain_a = small[:, :part]
    gain_b = small[:, part:2 * part]
    taps_end = 2 * part + taps_count * d_local // (model_width // part)
    conv_x_grad = small[:, 2 * part:taps_end].reshape(layers, taps_count, heads, -1)
    head_grad = small[:, taps_end:].reshape(layers, 3, heads)
    return (block_out, gradient, gain_a, zx, w_bc_grad, dt, conv_x_grad, conv_bc_grad, head_grad, q, kv,
            o, out, gain_b, gu, down)


def solution(mesh):
    in_specs = (
        P(("dp", "seq"), None),
        P("dp", None),
        P(),
        P(None, None, None, "head"),
        P(),
        P(None, None, "head"),
        P(None, None, "head", None),
        P(),
        P(None, None, "head"),
        P(None, None, "head"),
        P(None, None, "head", None),
        P(None, "head", None),
        P(None, "head", None),
        P(),
        P(None, None, None, "head"),
        P(None, "head", None),
        P(("dp", "seq"), None),
    )
    out_specs = (
        P(("dp", "seq"), None),
        P(("dp", "seq"), None),
        P(None, ("dp", "seq")),
        P(None, ("dp", "seq"), None, "head"),
        P(None, None, ("dp", "seq", "head")),
        P(None, ("dp", "seq"), "head"),
        P(None, None, "head", ("dp", "seq")),
        P(None, None, ("dp", "seq", "head")),
        P(None, None, "head"),
        P(None, ("dp", "seq"), "head"),
        P(None, ("dp", "seq"), "head", None),
        P(None, "head", ("dp", "seq")),
        P(None, "head", ("dp", "seq")),
        P(None, ("dp", "seq")),
        P(None, ("dp", "seq"), None, "head"),
        P(None, "head", ("dp", "seq")),
    )
    return jax.shard_map(
        on_device, mesh=mesh, in_specs=in_specs, out_specs=out_specs, check_vma=False
    )
```

```python
import functools

import jax
import jax.numpy as jnp
from jax import lax
from jax.experimental import pallas as pl
from jax.experimental.pallas import tpu as pltpu
from jax.sharding import PartitionSpec as P

NS = 128
HD = 64
RIM = 16

highest = lax.Precision.HIGHEST
norm_eps = 1e-05
masked_score = -1e30
bf16 = jnp.bfloat16
f32 = jnp.float32
VMEM_LIMIT = 61 * 1024 * 1024


def nn(left, right):
    return jnp.dot(left, right, preferred_element_type=f32)


def tn(left, right):
    return lax.dot_general(left, right, (((0,), (0,)), ((), ())), preferred_element_type=f32)


def nt(left, right):
    return lax.dot_general(left, right, (((1,), (1,)), ((), ())), preferred_element_type=f32)


def exact(left, right, contract=(1, 0)):
    return lax.dot_general(
        left,
        right,
        (((contract[0],), (contract[1],)), ((), ())),
        precision=highest,
        preferred_element_type=f32,
    )


def sigmoid(v):
    return 1.0 / (1.0 + jnp.exp(-v))


def softplus(v):
    return jnp.maximum(v, 0.0) + jnp.log(1.0 + jnp.exp(-jnp.abs(v)))


def head_map(heads, width):
    rows = lax.broadcasted_iota(jnp.int32, (128, heads * width), 0)
    columns = lax.broadcasted_iota(jnp.int32, (128, heads * width), 1)
    return (columns // width == rows).astype(f32)


def rms_scaled(hidden, gain):
    return hidden * lax.rsqrt(jnp.mean(hidden * hidden, axis=-1, keepdims=True) + norm_eps) * gain


def ssm_scalars(dt_ref, heads_ref):
    rows = dt_ref.shape[0]
    raw = dt_ref[...] + heads_ref[0:1, :]
    step = softplus(raw)
    log_decay = -jnp.exp(heads_ref[1:2, :]) * step
    place_t = lax.broadcasted_iota(jnp.int32, (rows, rows), 0)
    place_s = lax.broadcasted_iota(jnp.int32, (rows, rows), 1)
    lower = (place_s <= place_t).astype(f32)
    running = exact(lower, log_decay)
    running_t = jnp.transpose(running)
    return raw, step, log_decay, running, running_t, place_t >= place_s


def spread(scalars, mapping):
    return exact(scalars, mapping)


def score_mask(dcol_ref, drow_ref):
    rows, length = dcol_ref.shape[0], drow_ref.shape[1]
    query_pos = lax.broadcasted_iota(jnp.int32, (rows, length), 0) + lax.axis_index("seq") * rows
    key_pos = lax.broadcasted_iota(jnp.int32, (rows, length), 1)
    return (key_pos <= query_pos) & (dcol_ref[:, 0:1] == drow_ref[0:1, :])


MESH_ID = pl.DeviceIdType.MESH
CHUNK = 128


def remote(src, dst, send, recv, axis, target):
    return pltpu.make_async_remote_copy(
        src_ref=src, dst_ref=dst, send_sem=send, recv_sem=recv,
        device_id={axis: target}, device_id_type=MESH_ID,
    )


def meet(count, later_sends):
    place = lax.axis_index("seq")
    barrier = pltpu.get_barrier_semaphore()
    for j in range(1, count):
        here = place - j if not later_sends else place + j

        @pl.when((here >= 0) & (here < count))
        def _():
            pl.semaphore_signal(barrier, inc=1, device_id={"seq": here}, device_id_type=MESH_ID)
    heads_axis = lax.axis_size("head")
    partner = lax.rem(lax.axis_index("head") + 1, heads_axis)
    pl.semaphore_signal(barrier, inc=1, device_id={"head": partner}, device_id_type=MESH_ID)
    waits = (place if later_sends else count - 1 - place) + 1
    pl.semaphore_wait(barrier, waits)
    return partner


def layer_forward_kernel(heads, layer, h_ref, gain_mix_ref, gain_ff_ref, wdt_ref,
                         taps_ref, heads_ref, dcol_ref, dloc_ref, drow_ref,
                         wkv_hbm, wbc_hbm, wx_hbm, wz_hbm, wq_hbm, wout_hbm, wo_hbm, wg_hbm, wu_hbm, wdown_hbm,
                         h_out, normed_ref, gate_ref, stack_ref, rim_ref, pre_ref, dt_ref, q_ref, kvall_ref,
                         att_ref, lse_ref, mem_ref, gated_ref, middle_ref, nff_ref, gu_ref, inner_ref,
                         ext, y, wkv_ref, wbc_ref, wzx_ref, wq_ref, wo_ref, wout_ref, wgu_ref, wdown_ref, rim_in, kv_in, chain_in, chain_out,
                         part_out, part_in, down_out, down_in,
                         load_sem, kv_send, kv_recv, rim_send, rim_recv, chain_send, chain_recv,
                         part_send, part_recv, down_send, down_recv):
    rows = dt_ref.shape[0]
    d_local = gate_ref.shape[1]
    ff_local = inner_ref.shape[1]
    count = lax.axis_size("seq")
    place = lax.axis_index("seq")
    loads = {}
    for name, src, dst in (
        ("kv", wkv_hbm, wkv_ref), ("bc", wbc_hbm, wbc_ref), ("x", wx_hbm, wzx_ref.at[:, pl.ds(d_local, d_local)]),
        ("z", wz_hbm, wzx_ref.at[:, pl.ds(0, d_local)]), ("q", wq_hbm, wq_ref), ("out", wout_hbm, wout_ref),
        ("o", wo_hbm, wo_ref), ("g", wg_hbm, wgu_ref.at[:, pl.ds(0, ff_local)]),
        ("u", wu_hbm, wgu_ref.at[:, pl.ds(ff_local, ff_local)]), ("down", wdown_hbm, wdown_ref),
    ):
        loads[name] = pltpu.make_async_copy(src.at[layer], dst, load_sem.at[len(loads)])
    for load in loads.values():
        load.start()
    partner = meet(count, False)

    normed_ref[...] = rms_scaled(h_ref[...].astype(f32), gain_mix_ref[...]).astype(bf16)
    normed = normed_ref[...]
    own = pl.ds(pl.multiple_of(place * rows, rows), rows)
    for j in range(count):
        @pl.when(j > place)
        def _():
            kv_in[j * rows:(j + 1) * rows, :] = jnp.zeros((rows, 2 * HD), bf16)
    loads["kv"].wait()
    kv_in[own, :] = nn(normed, wkv_ref[...]).astype(bf16)
    kv_copies = [
        remote(kv_in.at[own], kv_in.at[own], kv_send.at[j - 1], kv_recv.at[j - 1], "seq", place + j)
        for j in range(1, count)
    ]
    for j in range(1, count):
        @pl.when(place + j < count)
        def _():
            kv_copies[j - 1].start()
    loads["bc"].wait()
    stack_ref[:, d_local:] = nn(normed, wbc_ref[...]).astype(bf16)
    loads["x"].wait()
    stack_ref[:, :d_local] = nn(normed, wzx_ref[:, d_local:]).astype(bf16)
    rim_copy = remote(stack_ref.at[pl.ds(rows - RIM, RIM)], rim_in, rim_send, rim_recv, "seq", place + 1)

    @pl.when(place + 1 < count)
    def _():
        rim_copy.start()

    @pl.when(place == 0)
    def _():
        rim_in[...] = jnp.zeros(rim_in.shape, bf16)
        chain_in[...] = jnp.zeros(chain_in.shape, bf16)
    dt_ref[...] = nn(normed, wdt_ref[...]).astype(bf16).astype(f32)
    loads["z"].wait()
    gate_ref[...] = nn(normed, wzx_ref[:, :d_local]).astype(bf16)
    loads["q"].wait()
    q_ref[...] = nn(normed, wq_ref[...]).astype(bf16)
    raw, step, log_decay, running, running_t, ordered = ssm_scalars(dt_ref, heads_ref)
    mapping = head_map(heads, d_local // heads)
    last = running[rows - 1:rows, :]
    fade = jnp.exp(last - running) * dcol_ref[:, 5:6]
    dec = jnp.exp(running) * dcol_ref[:, 4:5]
    ends = jnp.exp(running_t[:, rows - 1:rows]) * dcol_ref[rows - 1:rows, 4:5] + jnp.zeros((128, NS), f32)
    ends = exact(mapping, ends, (0, 0))
    steps = spread(step, mapping)
    ext[RIM:, :] = stack_ref[...].astype(f32)

    @pl.when(place > 0)
    def _():
        rim_copy.wait_recv()
    rim_ref[...] = rim_in[...]
    ext[0:RIM, :] = rim_in[...].astype(f32)
    pre = ext[RIM:RIM + rows, :] * taps_ref[0:1, :]
    for k in range(1, 4):
        pre = pre + ext[RIM - k:RIM - k + rows, :] * dcol_ref[:, k:k + 1] * taps_ref[k:k + 1, :]
    pre_ref[...] = pre
    mixed = pre_ref[...] * sigmoid(pre_ref[...])
    values = mixed[:, :d_local]
    b_rows = mixed[:, d_local:d_local + NS].astype(bf16)
    c_rows = mixed[:, d_local + NS:].astype(bf16)
    stepped = values * steps
    state = tn((stepped * spread(fade, mapping)).astype(bf16), b_rows)
    y[...] = values * spread(heads_ref[2:3, :] + jnp.zeros((8, 128), f32), mapping)[0:1, :]
    linked = ordered & (dcol_ref[:, 0:1] == dloc_ref[0:1, :])
    cb = jnp.where(linked, nt(c_rows, b_rows), 0.0)
    stepped = stepped.astype(bf16)
    lane = lax.broadcasted_iota(jnp.int32, (rows, 128), 1)

    for j in range(1, count):
        @pl.when(place - j >= 0)
        def _():
            kv_copies[j - 1].wait_recv()
    allowed = score_mask(dcol_ref, drow_ref)
    keyvals = kv_in[...]
    kvall_ref[...] = keyvals
    keys, vals = keyvals[:, :HD], keyvals[:, HD:]
    totals = jnp.zeros((rows, 128), f32)
    pairs = heads // 2
    query_heads = q_ref.shape[1] // HD
    chain_copies = []
    for pair in range(pairs):
        span = slice(pair * 128, pair * 128 + 128)
        copy = remote(chain_out.at[pl.ds(pair * 128, 128)], chain_in.at[pl.ds(pair * 128, 128)],
                      chain_send.at[pair], chain_recv.at[pair], "seq", place + 1)
        chain_copies.append(copy)

        @pl.when(place > 0)
        def _():
            copy.wait_recv()
        chain_out[span, :] = (ends[span] * chain_in[span, :].astype(f32) + state[span]).astype(bf16)

        @pl.when(place + 1 < count)
        def _():
            copy.start()
        sides = []
        for h in (2 * pair, 2 * pair + 1):
            gap = running[:, h:h + 1] - running_t[h:h + 1, :]
            mixing = (jnp.exp(jnp.minimum(gap, 0.0)) * cb).astype(bf16)
            sides.append(nn(mixing, stepped[:, span]))
        y[:, span] += jnp.where(lane < 64, sides[0], sides[1])
        for h in range(query_heads * pair // pairs, query_heads * (pair + 1) // pairs):
            query = q_ref[:, h * HD:(h + 1) * HD] * jnp.asarray(HD ** -0.5, bf16)
            scores = jnp.where(allowed, nt(query, keys), masked_score)
            peak = jnp.max(scores, axis=1, keepdims=True)
            expo = jnp.exp(scores - peak)
            total = jnp.sum(expo, axis=1, keepdims=True)
            probs = (expo * (1.0 / total)).astype(bf16)
            att_ref[:, h * HD:(h + 1) * HD] = nn(probs, vals).astype(bf16)
            totals = jnp.where(lane == h, peak + jnp.log(total), totals)
    lse_ref[...] = totals
    mem_ref[...] = chain_in[...]
    decs = spread(dec, mapping)
    carried = decs * nt(c_rows, mem_ref[...])
    gate = gate_ref[...].astype(f32)
    gated_ref[...] = ((y[...] + carried) * (gate * sigmoid(gate))).astype(bf16)
    loads["out"].wait()
    loads["o"].wait()
    chunks = [pl.ds(begin, CHUNK) for begin in range(0, rows, CHUNK)]
    part_copies, down_copies = [], []
    for i, chunk in enumerate(chunks):
        part_out[chunk, :] = (nn(gated_ref[chunk, :], wout_ref[...])
                              + nn(att_ref[chunk, :], wo_ref[...])).astype(bf16)
        copy = remote(part_out.at[chunk], part_in.at[chunk], part_send.at[i], part_recv.at[i], "head", partner)
        copy.start()
        part_copies.append(copy)
    loads["g"].wait()
    loads["u"].wait()
    loads["down"].wait()
    for i, chunk in enumerate(chunks):
        part_copies[i].wait_recv()
        middle_ref[chunk, :] = h_ref[chunk, :].astype(f32) + (
            part_out[chunk, :].astype(f32) + part_in[chunk, :].astype(f32))
        nff_ref[chunk, :] = rms_scaled(middle_ref[chunk, :], gain_ff_ref[...]).astype(bf16)
        gu_ref[chunk, :] = nn(nff_ref[chunk, :], wgu_ref[...]).astype(bf16)
        gate = gu_ref[chunk, :ff_local].astype(f32)
        inner_ref[chunk, :] = (gate * sigmoid(gate) * gu_ref[chunk, ff_local:].astype(f32)).astype(bf16)
        down_out[chunk, :] = nn(inner_ref[chunk, :], wdown_ref[...]).astype(bf16)
        copy = remote(down_out.at[chunk], down_in.at[chunk], down_send.at[i], down_recv.at[i], "head", partner)
        copy.start()
        down_copies.append(copy)
    for i, chunk in enumerate(chunks):
        down_copies[i].wait_recv()
        h_out[chunk, :] = (middle_ref[chunk, :] + (
            down_out[chunk, :].astype(f32) + down_in[chunk, :].astype(f32))).astype(bf16)
    for i in range(len(chunks)):
        part_copies[i].wait_send()
        down_copies[i].wait_send()

    @pl.when(place + 1 < count)
    def _():
        rim_copy.wait_send()
        for copy in chain_copies:
            copy.wait_send()
    for j in range(1, count):
        @pl.when(place + j < count)
        def _():
            kv_copies[j - 1].wait_send()


VM = pl.BlockSpec(memory_space=pltpu.VMEM)
ANY = pl.BlockSpec(memory_space=pl.ANY)
DMA = pltpu.SemaphoreType.DMA


def layer_forward(layer, hidden, w, context):
    dcol, dloc, drow = context
    rows, model_width = hidden.shape
    heads = w["heads"]
    d_local = w["out"].shape[1]
    ff_local = w["down"].shape[1]
    q_width = w["q"].shape[2]
    width = d_local + 2 * NS
    count = lax.axis_size("seq")
    length = count * rows
    parts = rows // CHUNK
    outs = [
        ((rows, model_width), bf16), ((rows, model_width), bf16), ((rows, d_local), bf16), ((rows, width), bf16),
        ((RIM, width), bf16), ((rows, width), f32), ((rows, 128), f32), ((rows, q_width), bf16),
        ((length, 2 * HD), bf16), ((rows, q_width), bf16), ((rows, 128), f32), ((d_local, NS), bf16),
        ((rows, d_local), bf16), ((rows, model_width), f32), ((rows, model_width), bf16),
        ((rows, 2 * ff_local), bf16), ((rows, ff_local), bf16),
    ]
    full = (rows, model_width)
    result = pl.pallas_call(
        functools.partial(layer_forward_kernel, heads, layer),
        out_shape=[jax.ShapeDtypeStruct(shape, kind) for shape, kind in outs],
        in_specs=[VM] * 9 + [ANY] * 10,
        out_specs=[VM] * len(outs),
        scratch_shapes=[
            pltpu.VMEM((rows + RIM, width), f32), pltpu.VMEM((rows, d_local), f32),
            pltpu.VMEM((model_width, 2 * HD), bf16), pltpu.VMEM((model_width, 2 * NS), bf16),
            pltpu.VMEM((model_width, 2 * d_local), bf16), pltpu.VMEM((model_width, q_width), bf16),
            pltpu.VMEM((q_width, model_width), bf16), pltpu.VMEM((d_local, model_width), bf16),
            pltpu.VMEM((model_width, 2 * ff_local), bf16), pltpu.VMEM((ff_local, model_width), bf16),
            pltpu.VMEM((RIM, width), bf16), pltpu.VMEM((length, 2 * HD), bf16),
            pltpu.VMEM((d_local, NS), bf16), pltpu.VMEM((d_local, NS), bf16),
            pltpu.VMEM(full, bf16), pltpu.VMEM(full, bf16), pltpu.VMEM(full, bf16), pltpu.VMEM(full, bf16),
            DMA((10,)), DMA((count - 1,)), DMA((count - 1,)), DMA, DMA, DMA((heads // 2,)), DMA((heads // 2,)),
            DMA((parts,)), DMA((parts,)), DMA((parts,)), DMA((parts,)),
        ],
        compiler_params=pltpu.CompilerParams(
            vmem_limit_bytes=VMEM_LIMIT, collective_id=layer, has_side_effects=True),
    )(hidden, w["gain_mix"][layer], w["gain_ff"][layer], w["dt"][layer], w["taps"][layer], w["head_vals"][layer],
      dcol, dloc, drow, w["kv"], w["bc"], w["x"], w["z"], w["q"], w["out"], w["o"], w["g"], w["u"], w["down"])
    names = ("out", "normed", "gate", "stack", "rim", "pre", "dt", "q", "kv", "att", "lse", "memory",
             "gated", "middle", "nff", "gu", "inner")
    saved = dict(zip(names, result))
    saved["hidden"] = hidden
    return saved.pop("out"), saved


def norm_back(hidden, gain, grad):
    inverse = lax.rsqrt(jnp.mean(hidden * hidden, axis=-1, keepdims=True) + norm_eps)
    scaled = grad * gain
    lean = jnp.mean(scaled * hidden, axis=-1, keepdims=True)
    grad_gain = jnp.sum(grad * hidden * inverse, axis=0, keepdims=True)
    return inverse * (scaled - hidden * (inverse * inverse * lean)), grad_gain


def store_blocks(compute, slots, out, sems):
    columns = out.shape[1]

    def copy(i, slot):
        rows = pl.ds(pl.multiple_of(i * 256, 256), 256)
        return pltpu.make_async_copy(slots.at[slot, :, pl.ds(0, columns)], out.at[rows], sems.at[slot])
    blocks = out.shape[0] // 256

    def one(i, carry):
        slot = lax.rem(i, 2)

        @pl.when(i >= 2)
        def _():
            copy(i - 2, slot).wait()
        compute(pl.ds(pl.multiple_of(i * 256, 256), 256), slot)
        copy(i, slot).start()
        return carry
    lax.fori_loop(0, blocks, one, 0)
    for i in range(max(0, blocks - 2), blocks):
        copy(i, i % 2).wait()


def layer_backward_kernel(heads, layer, grad_ref, h_ref, normed_ref, gate_ref, stack_ref, rim_ref, pre_ref, dt_ref,
                          q_ref, kv_ref, att_ref, lse_ref, mem_ref, gated_ref, middle_ref, nff_ref, gu_ref,
                          inner_ref, gain_mix_ref, gain_ff_ref, wdt_ref,
                          taps_ref, heads_ref, dcol_ref, dloc_ref, drow_ref,
                          wdown_hbm, wg_hbm, wu_hbm, wout_hbm, wo_hbm, wz_hbm, wx_hbm, wbc_hbm, wq_hbm, wkv_hbm,
                          g_out, gff_out, gmix_out, gbc_out, dtaps_ref, dheads_ref, gains_ref,
                          wdown_ref, wide_ref, wout_ref, wo_ref, wbc_ref, wq_ref, wkv_ref,
                          gff, dgu, one_out, one_in, two_out, two_in, gmid, branch, gg, datt, dy_s, dxs_s, u_s,
                          decay_s, probs_s, acc, dkv_out, dkv_in, chain_in, chain_out, rim_in,
                          ext, pad, dext, dgate, dstack, dq, dkv, draw_s,
                          load_sem, one_send, one_recv, two_send, two_recv, chain_send, chain_recv,
                          rim_send, rim_recv, kv_send, kv_recv, gblk, grad_sem):
    rows = dt_ref.shape[0]
    d_local = gate_ref.shape[1]
    ff_local = inner_ref.shape[1]
    q_width = q_ref.shape[1]
    model_width = h_ref.shape[1]
    width = pre_ref.shape[1]
    length = kv_ref.shape[0]
    count = lax.axis_size("seq")
    place = lax.axis_index("seq")
    wgu_ref = wide_ref.at[:, pl.ds(0, 2 * ff_local)]
    wzx_ref = wide_ref.at[:, pl.ds(0, 2 * d_local)]
    loads = {}
    for name, src, dst in (
        ("down", wdown_hbm, wdown_ref), ("g", wg_hbm, wide_ref.at[:, pl.ds(0, ff_local)]),
        ("u", wu_hbm, wide_ref.at[:, pl.ds(ff_local, ff_local)]), ("out", wout_hbm, wout_ref),
        ("o", wo_hbm, wo_ref), ("bc", wbc_hbm, wbc_ref), ("q", wq_hbm, wq_ref), ("kv", wkv_hbm, wkv_ref),
        ("z", wz_hbm, wide_ref.at[:, pl.ds(0, d_local)]), ("x", wx_hbm, wide_ref.at[:, pl.ds(d_local, d_local)]),
    ):
        loads[name] = pltpu.make_async_copy(src.at[layer], dst, load_sem.at[len(loads)])
    for name in ("down", "g", "u", "out", "o", "bc", "q", "kv"):
        loads[name].start()
    partner = meet(count, True)
    chunks = [pl.ds(begin, CHUNK) for begin in range(0, rows, CHUNK)]

    gff[...] = grad_ref[...].astype(bf16)
    loads["down"].wait()
    loads["g"].wait()
    loads["u"].wait()
    one_copies, two_copies = [], []
    for i, chunk in enumerate(chunks):
        grad_inner = nt(gff[chunk, :], wdown_ref[...])
        gate = gu_ref[chunk, :ff_local].astype(f32)
        up = gu_ref[chunk, ff_local:].astype(f32)
        sig = sigmoid(gate)
        dgu[chunk, :ff_local] = (grad_inner * up * (sig * (1.0 + gate * (1.0 - sig)))).astype(bf16)
        dgu[chunk, ff_local:] = (grad_inner * (gate * sig)).astype(bf16)
        one_out[chunk, :] = nt(dgu[chunk, :], wgu_ref[...]).astype(bf16)
        copy = remote(one_out.at[chunk], one_in.at[chunk], one_send.at[i], one_recv.at[i], "head", partner)
        copy.start()
        one_copies.append(copy)
    loads["z"].start()
    loads["x"].start()

    @pl.when(place == count - 1)
    def _():
        rim_in[...] = jnp.zeros(rim_in.shape, f32)
        chain_in[...] = jnp.zeros(chain_in.shape, bf16)
    for j in range(1, count):
        @pl.when(place + j >= count)
        def _():
            dkv_in[(j - 1) * rows:j * rows, :] = jnp.zeros((rows, 2 * HD), bf16)

    def ff_weights(block, slot):
        gblk[slot, :, :ff_local] = tn(gff[:, block], inner_ref[...]).astype(bf16)
        gblk[slot, :, ff_local:3 * ff_local] = tn(nff_ref[:, block], dgu[...]).astype(bf16)
    store_blocks(ff_weights, gblk, gff_out, grad_sem)

    raw, step, log_decay, running, running_t, ordered = ssm_scalars(dt_ref, heads_ref)
    mapping = head_map(heads, d_local // heads)
    last = running[rows - 1:rows, :]
    fade = spread(jnp.exp(last - running) * dcol_ref[:, 5:6], mapping)
    dec = jnp.exp(running) * dcol_ref[:, 4:5]
    decs = spread(dec, mapping)
    ends = jnp.exp(running_t[:, rows - 1:rows]) * dcol_ref[rows - 1:rows, 4:5] + jnp.zeros((128, NS), f32)
    ends = exact(mapping, ends, (0, 0))
    steps = spread(step, mapping)
    skip = spread(heads_ref[2:3, :] + jnp.zeros((8, 128), f32), mapping)[0:1, :]
    pre_v = pre_ref[:, :d_local]
    values = pre_v * sigmoid(pre_v)
    pre_n = pre_ref[:, d_local:]
    maps = (pre_n * sigmoid(pre_n)).astype(bf16)
    b_rows, c_rows = maps[:, :NS], maps[:, NS:]
    stepped = (values * steps).astype(bf16)
    linked = ordered & (dcol_ref[:, 0:1] == dloc_ref[0:1, :])
    cb = jnp.where(linked, nt(c_rows, b_rows), 0.0)
    lane = lax.broadcasted_iota(jnp.int32, (rows, 128), 1)
    pairs = heads // 2
    for pair in range(pairs):
        span = slice(pair * 128, pair * 128 + 128)
        sides = []
        for h in (2 * pair, 2 * pair + 1):
            at = slice(h * rows, (h + 1) * rows)
            gap = running[:, h:h + 1] - running_t[h:h + 1, :]
            decay = jnp.exp(jnp.minimum(gap, 0.0))
            decay_s[:, at] = decay.astype(bf16)
            mixing = (decay_s[:, at].astype(f32) * cb).astype(bf16)
            sides.append(nn(mixing, stepped[:, span]))
        u_s[:, span] = jnp.where(lane < 64, sides[0], sides[1])
    allowed = score_mask(dcol_ref, drow_ref)
    keyvals = kv_ref[...]
    keys, vals = keyvals[:, :HD], keyvals[:, HD:]
    scale = jnp.asarray(HD ** -0.5, bf16)
    query_heads = q_width // HD
    for h in range(query_heads):
        query = q_ref[:, h * HD:(h + 1) * HD] * scale
        scores = jnp.where(allowed, nt(query, keys), masked_score)
        probs_s[:, h * length:(h + 1) * length] = jnp.exp(scores - lse_ref[:, h:h + 1]).astype(bf16)
    ext[0:RIM, :] = rim_ref[...].astype(f32)
    ext[RIM:, :] = stack_ref[...].astype(f32)
    gate = gate_ref[...].astype(f32)
    gate_sig = sigmoid(gate)
    gate_act = gate * gate_sig
    loads["out"].wait()
    loads["o"].wait()
    gains_ref[...] = jnp.zeros(gains_ref.shape, f32)
    for i, chunk in enumerate(chunks):
        one_copies[i].wait_recv()
        grad = one_out[chunk, :].astype(f32) + one_in[chunk, :].astype(f32)
        moved, gain = norm_back(middle_ref[chunk, :], gain_ff_ref[...], grad)
        gains_ref[1:2, :] += gain
        gmid[chunk, :] = grad_ref[chunk, :] + moved
        branch[chunk, :] = gmid[chunk, :].astype(bf16)
        gg[chunk, :] = nt(branch[chunk, :], wout_ref[...])
        datt[chunk, :] = nt(branch[chunk, :], wo_ref[...]).astype(bf16)
    grad_ssm = gg[...] * gate_act
    dy_s[...] = grad_ssm.astype(bf16)
    push = tn((grad_ssm * decs).astype(bf16), c_rows)
    dcb = jnp.zeros((rows, rows), f32)
    chain_copies = []
    for pair in range(pairs):
        span = slice(pair * 128, pair * 128 + 128)
        copy = remote(chain_out.at[pl.ds(pair * 128, 128)], chain_in.at[pl.ds(pair * 128, 128)],
                      chain_send.at[pair], chain_recv.at[pair], "seq", place - 1)
        chain_copies.append(copy)

        @pl.when(place < count - 1)
        def _():
            copy.wait_recv()
        chain_out[span, :] = (ends[span] * chain_in[span, :].astype(f32) + push[span]).astype(bf16)

        @pl.when(place > 0)
        def _():
            copy.start()
        stepped_p = stepped[:, span]
        dy_p = dy_s[:, span]
        dxs = []
        for side, h in enumerate((2 * pair, 2 * pair + 1)):
            at = slice(h * rows, (h + 1) * rows)
            decay = decay_s[:, at].astype(f32)
            dxs.append(tn((decay * cb).astype(bf16), dy_p))
            half = jnp.where((lane < 64) == (side == 0), dy_p, jnp.zeros_like(dy_p))
            dcb = dcb + nt(half, stepped_p) * decay
        dxs_s[:, span] = jnp.where(lane < 64, dxs[0], dxs[1])
        for h in range(query_heads * pair // pairs, query_heads * (pair + 1) // pairs):
            part = slice(h * HD, (h + 1) * HD)
            query = q_ref[:, part] * scale
            grad = datt[:, part]
            delta = jnp.sum(grad.astype(f32) * att_ref[:, part].astype(f32), axis=1, keepdims=True)
            probs = probs_s[:, h * length:(h + 1) * length]
            grad_scores = (probs.astype(f32) * (nt(grad, vals) - delta)).astype(bf16)
            dq[:, part] = (nn(grad_scores, keys) * HD ** -0.5).astype(bf16)
            dk = tn(grad_scores, query)
            dv = tn(probs, grad)
            if h == 0:
                acc[:, :HD] = dk
                acc[:, HD:] = dv
            else:
                acc[:, :HD] += dk
                acc[:, HD:] += dv
    dkv_out[...] = acc[...].astype(bf16)
    kv_copies = []
    for j in range(1, count):
        target = jnp.maximum(place - j, 0)
        theirs = pl.ds(pl.multiple_of(target * rows, rows), rows)
        copy = remote(dkv_out.at[theirs], dkv_in.at[pl.ds((j - 1) * rows, rows)], kv_send.at[j - 1],
                      kv_recv.at[j - 1], "seq", place - j)
        kv_copies.append(copy)

        @pl.when(place >= j)
        def _():
            copy.start()
    memory = mem_ref[...]
    gmem = chain_in[...]
    carried = decs * nt(c_rows, memory)
    back = fade * nt(b_rows, gmem)
    dy_low = dy_s[...].astype(f32)
    stepped_f = stepped.astype(f32)
    dxs_all = dxs_s[...] + back
    dxs_s[...] = dxs_all
    dcb = jnp.where(linked, dcb, 0.0).astype(bf16)
    dc = nn(dcb, b_rows) + nn((dy_low * decs).astype(bf16), memory)
    db = tn(dcb, c_rows) + nn((stepped_f * fade).astype(bf16), gmem)
    dvalues = steps * dxs_all + skip * grad_ssm
    pad[0:8, :] = jnp.zeros((8, width), f32)
    pad[8 + rows:, :] = jnp.zeros((8, width), f32)
    sig = sigmoid(pre_v)
    pad[8:8 + rows, :d_local] = dvalues * (sig * (1.0 + pre_v * (1.0 - sig)))
    sig = sigmoid(pre_n)
    slope = sig * (1.0 + pre_n * (1.0 - sig))
    pad[8:8 + rows, d_local:d_local + NS] = db * slope[:, :NS]
    pad[8:8 + rows, d_local + NS:] = dc * slope[:, NS:]
    dpre = pad[8:8 + rows, :]
    dext[...] = pad[0:8 + rows, :] * taps_ref[0:1, :]
    dtaps_ref[...] = jnp.zeros((8, width), f32)
    dtaps_ref[0:1, :] = jnp.sum(dpre * ext[RIM:RIM + rows, :], axis=0, keepdims=True)
    for k in range(1, 4):
        masked = dpre * dcol_ref[:, k:k + 1]
        pad[8:8 + rows, :] = masked
        dtaps_ref[k:k + 1, :] = jnp.sum(masked * ext[RIM - k:RIM - k + rows, :], axis=0, keepdims=True)
        dext[...] += pad[k:k + 8 + rows, :] * taps_ref[k:k + 1, :]
    rim_copy = remote(dext.at[pl.ds(0, 8)], rim_in, rim_send, rim_recv, "seq", place - 1)

    @pl.when(place > 0)
    def _():
        rim_copy.start()
    scanned = u_s[...] + carried
    drun = exact(dy_low * scanned - stepped_f * dxs_all, mapping, (1, 1))
    ssm_out = scanned + skip * values
    dgate[...] = (gg[...] * ssm_out * (gate_sig * (1.0 + gate * (1.0 - gate_sig)))).astype(bf16)
    gstep = exact(values * dxs_all, mapping, (1, 1))
    ones = jnp.ones((8, 128), f32)
    moved = exact(ones, gmem.astype(f32) * memory.astype(f32), (1, 1))
    end = exact(jnp.sum(stepped_f * back, axis=0, keepdims=True) + jnp.zeros((8, 1), f32), mapping, (1, 1))
    end = end + exact(moved, mapping, (1, 1)) * dec[rows - 1:rows, :]
    upper = (lax.broadcasted_iota(jnp.int32, (rows, rows), 1)
             >= lax.broadcasted_iota(jnp.int32, (rows, rows), 0)).astype(f32)
    dlog = exact(upper, drun) + end[0:1, :]
    draw = (gstep - jnp.exp(heads_ref[1:2, :]) * dlog) * sigmoid(raw)
    draw_s[...] = draw.astype(bf16)
    dskip = exact(jnp.sum(grad_ssm * values, axis=0, keepdims=True) + jnp.zeros((8, 1), f32), mapping, (1, 1))
    dheads_ref[...] = jnp.zeros((8, 128), f32)
    dheads_ref[0:1, :] = jnp.sum(draw, axis=0, keepdims=True)
    dheads_ref[1:2, :] = jnp.sum(dlog * log_decay, axis=0, keepdims=True)
    dheads_ref[2:3, :] = dskip[0:1, :]
    for name in ("z", "x", "bc", "q", "kv"):
        loads[name].wait()

    for j in range(1, count):
        @pl.when(place + j < count)
        def _():
            kv_copies[j - 1].wait_recv()
    own = pl.ds(pl.multiple_of(place * rows, rows), rows)
    total = acc[own, :]
    for j in range(1, count):
        total = total + dkv_in[(j - 1) * rows:j * rows, :].astype(f32)
    dkv[...] = total.astype(bf16)

    for i, chunk in enumerate(chunks):
        if i == len(chunks) - 1:
            @pl.when(place < count - 1)
            def _():
                rim_copy.wait_recv()
            dext[rows:rows + 8, :] += rim_in[...]
        dstack[chunk, :] = dext[8 + i * CHUNK:8 + (i + 1) * CHUNK, :].astype(bf16)
        two_out[chunk, :] = (
            nt(dgate[chunk, :], wzx_ref[:, :d_local]) + nt(dstack[chunk, :d_local], wzx_ref[:, d_local:])
            + nt(dstack[chunk, d_local:], wbc_ref[...]) + nt(draw_s[chunk, :], wdt_ref[...])
            + nt(dq[chunk, :], wq_ref[...]) + nt(dkv[chunk, :], wkv_ref[...])
        ).astype(bf16)
        copy = remote(two_out.at[chunk], two_in.at[chunk], two_send.at[i], two_recv.at[i], "head", partner)
        copy.start()
        two_copies.append(copy)

    def mix_weights(block, slot):
        left = normed_ref[:, block]
        at = 0
        for right in (dgate[...], dstack[:, :d_local], dq[...], dkv[...], draw_s[...]):
            gblk[slot, :, at:at + right.shape[1]] = tn(left, right).astype(bf16)
            at += right.shape[1]
        left = branch[:, block]
        for right in (gated_ref[...], att_ref[...]):
            gblk[slot, :, at:at + right.shape[1]] = tn(left, right).astype(bf16)
            at += right.shape[1]
        gbc_out[:, block] = tn(dstack[:, d_local:], normed_ref[:, block]).astype(bf16)
    store_blocks(mix_weights, gblk, gmix_out, grad_sem)

    for i, chunk in enumerate(chunks):
        two_copies[i].wait_recv()
        grad = two_out[chunk, :].astype(f32) + two_in[chunk, :].astype(f32)
        moved, gain = norm_back(h_ref[chunk, :].astype(f32), gain_mix_ref[...], grad)
        gains_ref[0:1, :] += gain
        g_out[chunk, :] = gmid[chunk, :] + moved
    for i in range(len(chunks)):
        one_copies[i].wait_send()
        two_copies[i].wait_send()

    @pl.when(place > 0)
    def _():
        rim_copy.wait_send()
        for copy in chain_copies:
            copy.wait_send()
    for j in range(1, count):
        @pl.when(place >= j)
        def _():
            kv_copies[j - 1].wait_send()


def layer_backward(layer, grad, w, saved, context):
    dcol, dloc, drow = context
    rows, model_width = grad.shape
    heads = w["heads"]
    d_local = w["out"].shape[1]
    ff_local = w["down"].shape[1]
    q_width = w["q"].shape[2]
    width = d_local + 2 * NS
    count = lax.axis_size("seq")
    length = count * rows
    parts = rows // CHUNK
    mix_width = 3 * d_local + 2 * q_width + 256
    outs = [
        ((rows, model_width), f32), ((model_width, 3 * ff_local), bf16), ((model_width, mix_width), bf16),
        ((2 * NS, model_width), bf16), ((8, width), f32), ((8, 128), f32), ((8, model_width), f32),
    ]
    full = (rows, model_width)
    state = (d_local, NS)
    names = ("hidden", "normed", "gate", "stack", "rim", "pre", "dt", "q", "kv", "att", "lse", "memory",
             "gated", "middle", "nff", "gu", "inner")

    def vm(shape, kind):
        return pltpu.VMEM(shape, kind)
    return pl.pallas_call(
        functools.partial(layer_backward_kernel, heads, layer),
        out_shape=[jax.ShapeDtypeStruct(shape, kind) for shape, kind in outs],
        in_specs=[VM] * 26 + [ANY] * 10,
        out_specs=[VM, ANY, ANY] + [VM] * 4,
        scratch_shapes=[
            vm((ff_local, model_width), bf16), vm((model_width, 2 * max(d_local, ff_local)), bf16),
            vm((d_local, model_width), bf16), vm((q_width, model_width), bf16), vm((model_width, 2 * NS), bf16),
            vm((model_width, q_width), bf16), vm((model_width, 2 * HD), bf16),
            vm(full, bf16), vm((rows, 2 * ff_local), bf16), vm(full, bf16), vm(full, bf16), vm(full, bf16),
            vm(full, bf16), vm(full, f32), vm(full, bf16), vm((rows, d_local), f32), vm((rows, q_width), bf16),
            vm((rows, d_local), bf16), vm((rows, d_local), f32), vm((rows, d_local), f32),
            vm((rows, heads * rows), bf16),
            vm((rows, q_width // HD * length), bf16), vm((length, 2 * HD), f32), vm((length, 2 * HD), bf16),
            vm(((count - 1) * rows, 2 * HD), bf16), vm(state, bf16), vm(state, bf16), vm((8, width), f32),
            vm((rows + RIM, width), f32), vm((rows + 16, width), f32), vm((rows + 8, width), f32),
            vm((rows, d_local), bf16), vm((rows, width), bf16), vm((rows, q_width), bf16),
            vm((rows, 2 * HD), bf16), vm((rows, 128), bf16),
            DMA((10,)), DMA((parts,)), DMA((parts,)), DMA((parts,)), DMA((parts,)), DMA((heads // 2,)),
            DMA((heads // 2,)), DMA, DMA, DMA((count - 1,)), DMA((count - 1,)),
            vm((2, 256, max(3 * ff_local, mix_width)), bf16), DMA((2,)),
        ],
        compiler_params=pltpu.CompilerParams(
            vmem_limit_bytes=VMEM_LIMIT, collective_id=2 + layer, has_side_effects=True),
    )(grad, *[saved[name] for name in names], w["gain_mix"][layer], w["gain_ff"][layer], w["dt"][layer],
      w["taps"][layer], w["head_vals"][layer], dcol, dloc, drow, w["down"], w["g"], w["u"], w["out"], w["o"],
      w["z"], w["x"], w["bc"], w["q"], w["kv"])


def pack_small(dtaps, dheads, gains, heads, d_local):
    shards = lax.axis_size("dp") * lax.axis_size("seq")
    taps = dtaps[:4, :d_local].reshape(4, heads, shards, -1)
    return jnp.concatenate(
        [gains[0].reshape(shards, -1), gains[1].reshape(shards, -1),
         jnp.transpose(taps, (2, 0, 1, 3)).reshape(shards, -1),
         jnp.broadcast_to(dheads[:3, :heads].reshape(1, -1), (shards, 3 * heads))], axis=1
    )


UNITS = 4


def add_rows(out, terms):
    rows = out.shape[0]
    size = min(64, rows)

    def one(i, carry):
        part = pl.ds(pl.multiple_of(i * size, size), size)
        total = terms[0][part, :].astype(f32)
        for term in terms[1:]:
            total = total + term[part, :].astype(f32)
        out[part, :] = total.astype(out.dtype)
        return carry
    lax.fori_loop(0, rows // size, one, 0)


def reduce_kernel(arrays, *refs):
    grads = refs[:arrays]
    outs = refs[arrays:2 * arrays]
    (own, first, second, right_in, left_in, load_sem, first_send, first_recv, second_send, second_recv,
     line_send, right_recv, left_recv) = refs[2 * arrays:]
    others = grads[0].shape[0]
    span = grads[0].shape[2]
    count = lax.axis_size("seq")
    shard = span // count
    spot = lax.axis_index("dp")
    place = lax.axis_index("seq")
    core = lax.rem(spot, 2)
    group = spot // 2
    barrier = pltpu.get_barrier_semaphore()
    sibling = spot + 1 - 2 * core
    pl.semaphore_signal(barrier, inc=1, device_id={"dp": sibling}, device_id_type=MESH_ID)
    peers = [lax.rem(group + k, others) * 2 + core for k in range(1, others)]
    for peer in peers:
        pl.semaphore_signal(barrier, inc=1, device_id={"dp": peer}, device_id_type=MESH_ID)

    @pl.when(place > 0)
    def _():
        pl.semaphore_signal(barrier, inc=1, device_id={"seq": place - 1}, device_id_type=MESH_ID)

    @pl.when(place < count - 1)
    def _():
        pl.semaphore_signal(barrier, inc=1, device_id={"seq": place + 1}, device_id_type=MESH_ID)
    waits = others + 2 - (place == 0).astype(jnp.int32) - (place == count - 1).astype(jnp.int32)
    pl.semaphore_wait(barrier, waits)

    units = []
    for a in range(arrays):
        columns = grads[a].shape[3] // UNITS
        for u in range(UNITS):
            units.append((a, pl.ds(u * columns, columns)))
    loads, firsts, seconds = [], [], []
    for n, (a, columns) in enumerate(units):
        loads.append(pltpu.make_async_copy(grads[a].at[:, core, :, columns], own.at[n], load_sem.at[n]))
        firsts.append(remote(grads[a].at[:, 1 - core, :, columns], first.at[n], first_send.at[n],
                             first_recv.at[n], "dp", sibling))
        loads[n].start()
        firsts[n].start()
    for n in range(len(units)):
        loads[n].wait()
        firsts[n].wait_recv()
        copies = []
        for k, peer in enumerate(peers):
            theirs = lax.rem(group + k + 1, others)
            add_rows(own.at[n, theirs], [own.at[n, theirs], first.at[n, theirs]])
            copy = remote(own.at[n, theirs], second.at[n, k], second_send.at[n, k], second_recv.at[n, k], "dp", peer)
            copy.start()
            copies.append(copy)
        seconds.append(copies)
    lines = []
    for n, (a, columns) in enumerate(units):
        for copy in seconds[n]:
            copy.wait_recv()
        total = own.at[n, group]
        add_rows(total, [total, first.at[n, group]] + [second.at[n, k] for k in range(others - 1)])
        copies = []
        for j in range(count):
            rows = pl.ds(j * shard, shard)
            right = remote(total.at[rows], right_in.at[n, rows], line_send.at[n, j], right_recv.at[n, j],
                           "seq", place + 1)
            left = remote(total.at[rows], left_in.at[n, rows], line_send.at[n, j], left_recv.at[n, j],
                          "seq", place - 1)

            @pl.when(place < j)
            def _():
                @pl.when(place > 0)
                def _():
                    right.wait_recv()
                    add_rows(total.at[rows], [total.at[rows], right_in.at[n, rows]])
                right.start()

            @pl.when(place > j)
            def _():
                @pl.when(place < count - 1)
                def _():
                    left.wait_recv()
                    add_rows(total.at[rows], [total.at[rows], left_in.at[n, rows]])
                left.start()
            copies.append((right, left))
        lines.append(copies)
    for n, (a, columns) in enumerate(units):
        total = own.at[n, group]
        for j in range(count):
            right, left = lines[n][j]
            rows = pl.ds(j * shard, shard)

            @pl.when(place == j)
            def _():
                terms = [total.at[rows]]
                if j > 0:
                    right.wait_recv()
                    terms.append(right_in.at[n, rows])
                if j < count - 1:
                    left.wait_recv()
                    terms.append(left_in.at[n, rows])
                add_rows(outs[a].at[:, columns], terms)
    for n in range(len(units)):
        firsts[n].wait_send()
        for copy in seconds[n]:
            copy.wait_send()
        for j in range(count):
            right, left = lines[n][j]

            @pl.when(place < j)
            def _():
                right.wait_send()

            @pl.when(place > j)
            def _():
                left.wait_send()


def reduce_grads(arrays):
    count = lax.axis_size("seq")
    others = lax.axis_size("dp") // 2
    rows = arrays[0].shape[0]
    span = rows // (2 * others)
    shard = span // count
    columns = arrays[0].shape[1] // UNITS
    total = len(arrays) * UNITS
    views = [a.reshape(others, 2, span, a.shape[1]) for a in arrays]
    return pl.pallas_call(
        functools.partial(reduce_kernel, len(arrays)),
        out_shape=[jax.ShapeDtypeStruct((shard, a.shape[1]), f32) for a in arrays],
        in_specs=[ANY] * len(arrays),
        out_specs=[VM] * len(arrays),
        scratch_shapes=[
            pltpu.VMEM((total, others, span, columns), bf16), pltpu.VMEM((total, others, span, columns), bf16),
            pltpu.VMEM((total, others - 1, span, columns), bf16),
            pltpu.VMEM((total, span, columns), bf16), pltpu.VMEM((total, span, columns), bf16),
            DMA((total,)), DMA((total,)), DMA((total,)), DMA((total, others - 1)), DMA((total, others - 1)),
            DMA((total, count)), DMA((total, count)), DMA((total, count)),
        ],
        compiler_params=pltpu.CompilerParams(
            vmem_limit_bytes=VMEM_LIMIT, collective_id=9, has_side_effects=True),
        cost_estimate=pl.CostEstimate(flops=0, bytes_accessed=400 * 1024 * 1024, transcendentals=0),
    )(*views)


def on_device(hidden_in, segment_ids, gain_mix, w_zx, w_bc, w_dt, conv_x, conv_bc, ssm_head, w_q, w_kv,
              w_o, w_out, gain_ff, w_gu, w_down, cotangent):
    rows, model_width = hidden_in.shape
    taps_count = conv_x.shape[1]
    place = lax.axis_index("seq")
    offset = place * rows
    doc_all = segment_ids[0]
    padded = jnp.concatenate([jnp.full((taps_count - 1,), -1, jnp.int32), doc_all])
    doc_ext = lax.dynamic_slice_in_dim(padded, offset, rows + taps_count - 1)
    docs = doc_ext[taps_count - 1:]
    columns = [docs.astype(f32)]
    for k in range(1, taps_count):
        columns.append((doc_ext[taps_count - 1 - k:taps_count - 1 - k + rows] == docs).astype(f32))
    columns.append((docs == doc_ext[taps_count - 2]).astype(f32))
    columns.append((docs == docs[-1]).astype(f32))
    dcol = jnp.pad(jnp.stack(columns, axis=1), ((0, 0), (0, 128 - len(columns))))
    dloc = jnp.broadcast_to(docs.astype(f32)[None], (8, rows))
    drow = jnp.broadcast_to(doc_all.astype(f32)[None], (8, doc_all.shape[0]))
    context = (dcol, dloc, drow)
    layers = gain_mix.shape[0]
    heads = ssm_head.shape[2]
    d_local = w_zx.shape[3]
    w = dict(
        heads=heads,
        gain_mix=gain_mix[:, None].astype(f32),
        gain_ff=gain_ff[:, None].astype(f32),
        z=w_zx[:, :, 0, :],
        x=w_zx[:, :, 1, :],
        bc=w_bc,
        dt=jnp.pad(w_dt, ((0, 0), (0, 0), (0, 128 - heads))),
        q=w_q,
        kv=w_kv.reshape(layers, model_width, -1),
        o=w_o,
        out=w_out,
        g=w_gu[:, :, 0, :],
        u=w_gu[:, :, 1, :],
        down=w_down,
        taps=jnp.pad(jnp.concatenate([conv_x.reshape(layers, taps_count, -1), conv_bc], axis=2).astype(f32),
                     ((0, 0), (0, 8 - taps_count), (0, 0))),
        head_vals=jnp.pad(ssm_head, ((0, 0), (0, 5), (0, 128 - heads))),
    )
    hidden = hidden_in
    saved = []
    for l in range(layers):
        hidden, kept = layer_forward(l, hidden, w, context)
        saved.append(kept)
    block_out = hidden
    gradient = cotangent.astype(f32)
    wide, narrow, small = [], [None] * layers, [None] * layers
    for l in reversed(range(layers)):
        gradient, ff_grads, mix_grads, g_bc, dtaps, dheads, gains = layer_backward(
            l, gradient, w, saved[l], context)
        wide = [ff_grads, mix_grads] + wide
        narrow[l] = jnp.concatenate(
            [g_bc, jnp.pad(jnp.transpose(dtaps[:4, d_local:]), ((0, 0), (0, 124))).astype(bf16)], axis=1)
        small[l] = pack_small(dtaps, dheads, gains, heads, d_local)
    g_bc = lax.psum_scatter(jnp.concatenate(narrow, axis=1), ("dp", "seq", "head"),
                            scatter_dimension=0, tiled=True)
    small = jnp.concatenate(small, axis=1)
    shards, used = small.shape
    room = -(-used // 1024) * 1024
    small = jnp.pad(small, ((0, 0), (0, room - used))).reshape(shards * (room // 128), 128)
    small = lax.psum_scatter(small, ("dp", "seq"), scatter_dimension=0, tiled=True)
    small = small.reshape(-1)[:used]
    summed = reduce_grads(wide)
    parts = [(summed[2 * l], summed[2 * l + 1]) for l in range(layers)]
    ff_local = w_down.shape[1]
    q_width = w_q.shape[2]
    part = model_width // (lax.axis_size("dp") * lax.axis_size("seq"))

    def both(pieces):
        return jnp.stack(pieces, axis=0).astype(f32)

    def cut(index, begin, size):
        return [p[index][:, begin:begin + size] for p in parts]

    down = both([jnp.transpose(a) for a in cut(0, 0, ff_local)])
    gu = both(cut(0, ff_local, 2 * ff_local)).reshape(layers, part, 2, ff_local)
    at = 2 * d_local
    zx = both(cut(1, 0, at)).reshape(layers, part, 2, d_local)
    q = both(cut(1, at, q_width))
    at += q_width
    kv = both(cut(1, at, 128)).reshape(layers, part, 1, 128)
    at += 128
    dt = both(cut(1, at, heads))
    at += 128
    out = both([jnp.transpose(a) for a in cut(1, at, d_local)])
    at += d_local
    o = both([jnp.transpose(a) for a in cut(1, at, q_width)])
    g_bc = g_bc.astype(f32).reshape(g_bc.shape[0], layers, -1)
    w_bc_grad = jnp.transpose(g_bc[:, :, :model_width], (1, 2, 0))
    conv_bc_grad = jnp.transpose(g_bc[:, :, model_width:model_width + taps_count], (1, 2, 0))
    small = small.reshape(layers, -1)
    gain_a = small[:, :part]
    gain_b = small[:, part:2 * part]
    taps_end = 2 * part + taps_count * d_local // (model_width // part)
    conv_x_grad = small[:, 2 * part:taps_end].reshape(layers, taps_count, heads, -1)
    head_grad = small[:, taps_end:].reshape(layers, 3, heads)
    return (block_out, gradient, gain_a, zx, w_bc_grad, dt, conv_x_grad, conv_bc_grad, head_grad, q, kv,
            o, out, gain_b, gu, down)


def solution(mesh):
    in_specs = (
        P(("dp", "seq"), None),
        P("dp", None),
        P(),
        P(None, None, None, "head"),
        P(),
        P(None, None, "head"),
        P(None, None, "head", None),
        P(),
        P(None, None, "head"),
        P(None, None, "head"),
        P(None, None, "head", None),
        P(None, "head", None),
        P(None, "head", None),
        P(),
        P(None, None, None, "head"),
        P(None, "head", None),
        P(("dp", "seq"), None),
    )
    out_specs = (
        P(("dp", "seq"), None),
        P(("dp", "seq"), None),
        P(None, ("dp", "seq")),
        P(None, ("dp", "seq"), None, "head"),
        P(None, None, ("dp", "seq", "head")),
        P(None, ("dp", "seq"), "head"),
        P(None, None, "head", ("dp", "seq")),
        P(None, None, ("dp", "seq", "head")),
        P(None, None, "head"),
        P(None, ("dp", "seq"), "head"),
        P(None, ("dp", "seq"), "head", None),
        P(None, "head", ("dp", "seq")),
        P(None, "head", ("dp", "seq")),
        P(None, ("dp", "seq")),
        P(None, ("dp", "seq"), None, "head"),
        P(None, "head", ("dp", "seq")),
    )
    return jax.shard_map(
        on_device, mesh=mesh, in_specs=in_specs, out_specs=out_specs, check_vma=False
    )
```

```python
import functools

import jax
import jax.numpy as jnp
from jax import lax
from jax.experimental import pallas as pl
from jax.experimental.pallas import tpu as pltpu
from jax.sharding import PartitionSpec as P

NS = 128
HD = 64
RIM = 16

highest = lax.Precision.HIGHEST
norm_eps = 1e-05
masked_score = -1e30
bf16 = jnp.bfloat16
f32 = jnp.float32
VMEM_LIMIT = 63 * 1024 * 1024


def nn(left, right):
    return jnp.dot(left, right, preferred_element_type=f32)


def tn(left, right):
    return lax.dot_general(left, right, (((0,), (0,)), ((), ())), preferred_element_type=f32)


def nt(left, right):
    return lax.dot_general(left, right, (((1,), (1,)), ((), ())), preferred_element_type=f32)


def exact(left, right, contract=(1, 0)):
    return lax.dot_general(
        left,
        right,
        (((contract[0],), (contract[1],)), ((), ())),
        precision=highest,
        preferred_element_type=f32,
    )


def sigmoid(v):
    return 1.0 / (1.0 + jnp.exp(-v))


def softplus(v):
    return jnp.maximum(v, 0.0) + jnp.log(1.0 + jnp.exp(-jnp.abs(v)))


def head_map(heads, width):
    rows = lax.broadcasted_iota(jnp.int32, (128, heads * width), 0)
    columns = lax.broadcasted_iota(jnp.int32, (128, heads * width), 1)
    return (columns // width == rows).astype(f32)


def rms_scaled(hidden, gain):
    return hidden * lax.rsqrt(jnp.mean(hidden * hidden, axis=-1, keepdims=True) + norm_eps) * gain


def ssm_scalars(dt_ref, heads_ref):
    rows = dt_ref.shape[0]
    raw = dt_ref[...] + heads_ref[0:1, :]
    step = softplus(raw)
    log_decay = -jnp.exp(heads_ref[1:2, :]) * step
    place_t = lax.broadcasted_iota(jnp.int32, (rows, rows), 0)
    place_s = lax.broadcasted_iota(jnp.int32, (rows, rows), 1)
    lower = (place_s <= place_t).astype(f32)
    running = exact(lower, log_decay)
    running_t = jnp.transpose(running)
    return raw, step, log_decay, running, running_t, place_t >= place_s


def spread(scalars, mapping):
    return exact(scalars, mapping)


def score_mask(dcol_ref, drow_ref):
    rows, length = dcol_ref.shape[0], drow_ref.shape[1]
    query_pos = lax.broadcasted_iota(jnp.int32, (rows, length), 0) + lax.axis_index("seq") * rows
    key_pos = lax.broadcasted_iota(jnp.int32, (rows, length), 1)
    return (key_pos <= query_pos) & (dcol_ref[:, 0:1] == drow_ref[0:1, :])


MESH_ID = pl.DeviceIdType.MESH
CHUNK = 128


def remote(src, dst, send, recv, axis, target):
    return pltpu.make_async_remote_copy(
        src_ref=src, dst_ref=dst, send_sem=send, recv_sem=recv,
        device_id={axis: target}, device_id_type=MESH_ID,
    )


def meet(count, later_sends, extra=None):
    place = lax.axis_index("seq")
    barrier = pltpu.get_barrier_semaphore()
    for j in range(1, count if extra is None else 1):
        here = place - j if not later_sends else place + j

        @pl.when((here >= 0) & (here < count))
        def _():
            pl.semaphore_signal(barrier, inc=1, device_id={"seq": here}, device_id_type=MESH_ID)
    heads_axis = lax.axis_size("head")
    partner = lax.rem(lax.axis_index("head") + 1, heads_axis)
    pl.semaphore_signal(barrier, inc=1, device_id={"head": partner}, device_id_type=MESH_ID)
    waits = (place if later_sends else count - 1 - place) + 1
    if extra is not None:
        waits = extra() + 1
    pl.semaphore_wait(barrier, waits)
    return partner


VM = pl.BlockSpec(memory_space=pltpu.VMEM)
ANY = pl.BlockSpec(memory_space=pl.ANY)
DMA = pltpu.SemaphoreType.DMA
UNITS = 4


def add_rows(out, terms):
    rows = out.shape[0]
    size = min(64, rows)

    def one(i, carry):
        part = pl.ds(pl.multiple_of(i * size, size), size)
        total = terms[0][part, :].astype(f32)
        for term in terms[1:]:
            total = total + term[part, :].astype(f32)
        out[part, :] = total.astype(out.dtype)
        return carry
    lax.fori_loop(0, rows // size, one, 0)


def dp_spot():
    spot = lax.axis_index("dp")
    return lax.rem(spot, 2), spot // 2, lax.axis_size("dp") // 2


def greet_sums():
    barrier = pltpu.get_barrier_semaphore()
    core, group, others = dp_spot()
    count = lax.axis_size("seq")
    place = lax.axis_index("seq")
    targets = [{"dp": group * 2 + 1 - core}]
    targets += [{"dp": lax.rem(group + k, others) * 2 + core} for k in range(1, others)]
    targets += [{"seq": lax.rem(place + k, count)} for k in range(1, count)]
    for target in targets:
        pl.semaphore_signal(barrier, inc=1, device_id=target, device_id_type=MESH_ID)
    return len(targets)


class CrossSum:
    def __init__(self, ranges, buffers, sems):
        self.ranges = ranges
        self.own, self.first, self.second = buffers
        self.load_sem, self.first_send, self.first_recv, self.second_send, self.second_recv = sems
        self.core, self.group, self.others = dp_spot()
        self.loads, self.firsts, self.seconds = [], [], []

    def start(self):
        span = self.own.shape[2]
        for n, (grad, columns) in enumerate(self.ranges):
            self.firsts.append([])
            self.loads.append([])
            for g in range(self.others):
                theirs = pl.ds(pl.multiple_of((2 * g + 1 - self.core) * span, span), span)
                mine = pl.ds(pl.multiple_of((2 * g + self.core) * span, span), span)
                self.firsts[n].append(remote(
                    grad.at[theirs, columns], self.first.at[n, g], self.first_send.at[n, g],
                    self.first_recv.at[n, g], "dp", self.group * 2 + 1 - self.core))
                self.loads[n].append(pltpu.make_async_copy(
                    grad.at[mine, columns], self.own.at[n, g], self.load_sem.at[n, g]))
                self.firsts[n][g].start()
                self.loads[n][g].start()

    def step_a(self, n):
        for g in range(self.others):
            self.loads[n][g].wait()
            self.firsts[n][g].wait_recv()
        copies = []
        for k in range(1, self.others):
            peer = lax.rem(self.group + k, self.others)
            theirs = self.own.at[n, peer]
            add_rows(theirs, [theirs, self.first.at[n, peer]])
            copies.append(remote(
                theirs, self.second.at[n, k - 1], self.second_send.at[n, k - 1], self.second_recv.at[n, k - 1],
                "dp", peer * 2 + self.core))
            copies[-1].start()
        self.seconds.append(copies)

    def step_b(self, n, out):
        for copy in self.seconds[n]:
            copy.wait_recv()
        add_rows(out, [self.own.at[n, self.group], self.first.at[n, self.group]]
                 + [self.second.at[n, k] for k in range(self.others - 1)])

    def finish(self):
        for n in range(len(self.ranges)):
            for copy in self.firsts[n] + self.seconds[n]:
                copy.wait_send()


class LineSum:
    def __init__(self, pieces, received, send_sem, recv_sem):
        self.pieces = pieces
        self.received, self.send_sem, self.recv_sem = received, send_sem, recv_sem
        self.count = lax.axis_size("seq")
        self.place = lax.axis_index("seq")
        self.shard = received.shape[2]
        self.copies = [[] for _ in pieces]

    def rows(self, shard):
        return pl.ds(pl.multiple_of(shard * self.shard, self.shard), self.shard)

    def pass_on(self, n, bit):
        step = 2 ** bit
        side = lax.rem(lax.div(self.place, step), 2)
        target = self.place + step - 2 * step * side
        low = lax.rem(target, 2 * step)
        copies = []
        slot = self.count - self.count // step
        for m in range(self.count // (2 * step)):
            copies.append(remote(
                self.pieces[n].at[self.rows(low + 2 * step * m)], self.received.at[n, slot + m],
                self.send_sem.at[n, slot + m], self.recv_sem.at[n, slot + m], "seq", target))
            copies[-1].start()
        self.copies[n].append(copies)

    def take_in(self, n, bit):
        step = 2 ** bit
        low = lax.rem(self.place, 2 * step)
        slot = self.count - self.count // step
        for m, copy in enumerate(self.copies[n][bit]):
            copy.wait_recv()
            rows = self.pieces[n].at[self.rows(low + 2 * step * m)]
            if 2 * step == self.count:
                return [rows, self.received.at[n, slot + m]]
            add_rows(rows, [rows, self.received.at[n, slot + m]])

    def step_c(self, n):
        self.pass_on(n, 0)

    def step_d(self, n):
        bit = 1
        while 2 ** bit < self.count:
            self.take_in(n, bit - 1)
            self.pass_on(n, bit)
            bit += 1

    def step_e(self, n, write):
        write(n, self.take_in(n, len(self.copies[n]) - 1))

    def finish(self):
        for steps in self.copies:
            for copies in steps:
                for copy in copies:
                    copy.wait_send()


def cut_columns(refs):
    ranges = []
    for ref in refs:
        size = ref.shape[1] // UNITS
        ranges += [(ref, pl.ds(u * size, size)) for u in range(UNITS)]
    return ranges


def cross_scratch(ranges, span, columns):
    others = lax.axis_size("dp") // 2
    size = columns // UNITS
    peers = max(others - 1, 1)
    return [
        pltpu.VMEM((ranges, others, span, size), bf16), pltpu.VMEM((ranges, others, span, size), bf16),
        pltpu.VMEM((ranges, peers, span, size), bf16), DMA((ranges, others)), DMA((ranges, others)),
        DMA((ranges, others)), DMA((ranges, peers)), DMA((ranges, peers)),
    ]


def line_scratch(ranges, span, columns):
    count = lax.axis_size("seq")
    return [pltpu.VMEM((ranges, count - 1, span // count, columns // UNITS), bf16),
            DMA((ranges, count - 1)), DMA((ranges, count - 1))]


CROSS_REFS = 8
LINE_REFS = 3


def last_sum_kernel(widths, *refs):
    grads, half, done = refs[:2], refs[2], refs[3]
    kinds = len(widths[0]) + len(widths[1])
    outs = refs[4:4 + kinds]
    scratch = refs[4 + kinds:]
    partners = greet_sums()
    pl.semaphore_wait(pltpu.get_barrier_semaphore(), partners)
    halves, early_half = scratch[:2]
    for n, (_, columns) in enumerate(cut_columns([half])):
        early_half[n] = half[:, columns]
    early = LineSum([early_half.at[n] for n in range(UNITS)], *scratch[2:5])
    cross = CrossSum(cut_columns(grads), scratch[5:8], scratch[8:13])
    total = len(cross.ranges)
    line = LineSum([halves.at[n] for n in range(total)], *scratch[13:])
    cross.start()
    for n in range(UNITS):
        early.step_c(n)
    pieces = []
    which = 0
    for a in range(2):
        at = 0
        for width in widths[a]:
            pieces.append((a, at, width, outs[which]))
            at += width
            which += 1

    def write(layer, array, n, terms):
        size = terms[0].shape[1]
        begin = n % UNITS * size
        for a, at, width, out in pieces:
            low, high = max(at, begin), min(at + width, begin + size)
            if a == array and low < high:
                add_rows(out.at[layer, :, pl.ds(low - at, high - low)],
                         [term.at[:, pl.ds(low - begin, high - low)] for term in terms])

    def write_early(n, terms):
        write(1, 1, n, terms)

    def write_line(n, terms):
        write(0, n // UNITS, n, terms)
    for n in range(total):
        cross.step_a(n)
        if n < UNITS:
            early.step_d(n)
    for a, at, width, out in pieces:
        if a == 0:
            out[1] = done[:, at:at + width]
    for n in range(total + 2):
        if n < total:
            cross.step_b(n, halves.at[n])
            line.step_c(n)
        if 1 <= n <= total:
            line.step_d(n - 1)
        if n < UNITS:
            early.step_e(n, write_early)
        if n >= 2:
            line.step_e(n - 2, write_line)
    early.finish()
    cross.finish()
    line.finish()


def last_sum(grads, half, done, widths):
    columns = grads[0].shape[1]
    span = half.shape[0]
    shard = span // lax.axis_size("seq")
    total = 2 * UNITS
    return pl.pallas_call(
        functools.partial(last_sum_kernel, widths),
        out_shape=[jax.ShapeDtypeStruct((2, shard, width), f32) for width in widths[0] + widths[1]],
        in_specs=[ANY] * 2 + [VM] * 2,
        out_specs=[VM] * (len(widths[0]) + len(widths[1])),
        scratch_shapes=[pltpu.VMEM((total, span, columns // UNITS), bf16),
                        pltpu.VMEM((UNITS, span, columns // UNITS), bf16), *line_scratch(UNITS, span, columns),
                        *cross_scratch(total, span, columns), *line_scratch(total, span, columns)],
        compiler_params=pltpu.CompilerParams(
            vmem_limit_bytes=VMEM_LIMIT, collective_id=9, has_side_effects=True),
        cost_estimate=pl.CostEstimate(flops=0, bytes_accessed=400 * 1024 * 1024, transcendentals=0),
    )(*grads, half, done)


def unpack(pairs, out):
    def one(i, carry):
        rows = pl.ds(pl.multiple_of(i * 128, 128), 128)
        out[rows, :] = pairs[rows].reshape(128, out.shape[1])
        return carry
    lax.fori_loop(0, out.shape[0] // 128, one, 0)


def layer_forward_kernel(heads, layer, layers, h_ref, gain_mix_ref, gain_ff_ref, wdt_ref,
                         taps_ref, heads_ref, dcol_ref, dloc_ref, drow_ref,
                         wkv_hbm, wbc_hbm, zx_hbm, wq_hbm, wout_hbm, wo_hbm, gu_hbm, wdown_hbm, *refs):
    ready = layer > 0
    follows = layer + 1 < layers
    refs = list(refs)
    zx_ready = refs.pop(0) if ready else None
    (h_out, normed_ref, gate_ref, stack_ref, rim_ref, pre_ref, dt_ref, q_ref, kvall_ref,
     att_ref, lse_ref, mem_ref, gated_ref, middle_ref, nff_ref, gu_ref, inner_ref, gu_out) = refs[:18]
    refs = refs[18:]
    zx_out = None if ready else refs.pop(0)
    zx_next = refs.pop(0) if follows else None
    (ext, y, wkv_ref, wbc_ref, wzx_ref, wq_ref, wo_ref, wout_ref, wgu_ref, wdown_ref, raw_zx, raw_gu,
     rim_in, kv_in, chain_in, chain_out, part_out, part_in, down_out, down_in,
     load_sem, kv_send, kv_recv, rim_send, rim_recv, chain_send, chain_recv,
     part_send, part_recv, down_send, down_recv) = refs
    rows = dt_ref.shape[0]
    d_local = gate_ref.shape[1]
    ff_local = inner_ref.shape[1]
    count = lax.axis_size("seq")
    place = lax.axis_index("seq")
    loads = {}
    plan = [("kv", wkv_hbm.at[layer], wkv_ref), ("bc", wbc_hbm.at[layer], wbc_ref)]
    plan.append(("zx", zx_ready, wzx_ref) if ready else ("zx", zx_hbm.at[layer], raw_zx))
    plan += [("q", wq_hbm.at[layer], wq_ref), ("out", wout_hbm.at[layer], wout_ref), ("o", wo_hbm.at[layer], wo_ref),
             ("gu", gu_hbm.at[layer], raw_gu), ("down", wdown_hbm.at[layer], wdown_ref)]
    later = [("gu_store", wgu_ref, gu_out)]
    if not ready:
        later.append(("zx_store", wzx_ref, zx_out))
    if follows:
        later += [("next", zx_hbm.at[layer + 1], raw_zx), ("next_store", wzx_ref, zx_next)]
    for name, src, dst in plan + later:
        loads[name] = pltpu.make_async_copy(src, dst, load_sem.at[len(loads)])
    for name, src, dst in plan:
        loads[name].start()
    partner = meet(count, False)

    normed_ref[...] = rms_scaled(h_ref[...].astype(f32), gain_mix_ref[...]).astype(bf16)
    normed = normed_ref[...]
    own = pl.ds(pl.multiple_of(place * rows, rows), rows)
    for j in range(count):
        @pl.when(j > place)
        def _():
            kv_in[j * rows:(j + 1) * rows, :] = jnp.zeros((rows, 2 * HD), bf16)
    loads["kv"].wait()
    kv_in[own, :] = nn(normed, wkv_ref[...]).astype(bf16)
    kv_copies = [
        remote(kv_in.at[own], kv_in.at[own], kv_send.at[j - 1], kv_recv.at[j - 1], "seq", place + j)
        for j in range(1, count)
    ]
    for j in range(1, count):
        @pl.when(place + j < count)
        def _():
            kv_copies[j - 1].start()
    loads["bc"].wait()
    stack_ref[:, d_local:] = nn(normed, wbc_ref[...]).astype(bf16)
    loads["zx"].wait()
    if not ready:
        unpack(raw_zx, wzx_ref)
        loads["zx_store"].start()
    if follows:
        loads["next"].start()
    stack_ref[:, :d_local] = nn(normed, wzx_ref[:, d_local:]).astype(bf16)
    rim_copy = remote(stack_ref.at[pl.ds(rows - RIM, RIM)], rim_in, rim_send, rim_recv, "seq", place + 1)

    @pl.when(place + 1 < count)
    def _():
        rim_copy.start()

    @pl.when(place == 0)
    def _():
        rim_in[...] = jnp.zeros(rim_in.shape, bf16)
        chain_in[...] = jnp.zeros(chain_in.shape, bf16)
    dt_ref[...] = nn(normed, wdt_ref[...]).astype(bf16).astype(f32)
    gate_ref[...] = nn(normed, wzx_ref[:, :d_local]).astype(bf16)
    loads["q"].wait()
    q_ref[...] = nn(normed, wq_ref[...]).astype(bf16)
    raw, step, log_decay, running, running_t, ordered = ssm_scalars(dt_ref, heads_ref)
    mapping = head_map(heads, d_local // heads)
    last = running[rows - 1:rows, :]
    fade = jnp.exp(last - running) * dcol_ref[:, 5:6]
    dec = jnp.exp(running) * dcol_ref[:, 4:5]
    ends = jnp.exp(running_t[:, rows - 1:rows]) * dcol_ref[rows - 1:rows, 4:5] + jnp.zeros((128, NS), f32)
    ends = exact(mapping, ends, (0, 0))
    steps = spread(step, mapping)
    ext[RIM:, :] = stack_ref[...].astype(f32)

    @pl.when(place > 0)
    def _():
        rim_copy.wait_recv()
    rim_ref[...] = rim_in[...]
    ext[0:RIM, :] = rim_in[...].astype(f32)
    pre = ext[RIM:RIM + rows, :] * taps_ref[0:1, :]
    for k in range(1, 4):
        pre = pre + ext[RIM - k:RIM - k + rows, :] * dcol_ref[:, k:k + 1] * taps_ref[k:k + 1, :]
    pre_ref[...] = pre
    mixed = pre_ref[...] * sigmoid(pre_ref[...])
    values = mixed[:, :d_local]
    b_rows = mixed[:, d_local:d_local + NS].astype(bf16)
    c_rows = mixed[:, d_local + NS:].astype(bf16)
    stepped = values * steps
    state = tn((stepped * spread(fade, mapping)).astype(bf16), b_rows)
    y[...] = values * spread(heads_ref[2:3, :] + jnp.zeros((8, 128), f32), mapping)[0:1, :]
    linked = ordered & (dcol_ref[:, 0:1] == dloc_ref[0:1, :])
    cb = jnp.where(linked, nt(c_rows, b_rows), 0.0)
    stepped = stepped.astype(bf16)
    lane = lax.broadcasted_iota(jnp.int32, (rows, 128), 1)

    for j in range(1, count):
        @pl.when(place - j >= 0)
        def _():
            kv_copies[j - 1].wait_recv()
    allowed = score_mask(dcol_ref, drow_ref)
    keyvals = kv_in[...]
    kvall_ref[...] = keyvals
    keys, vals = keyvals[:, :HD], keyvals[:, HD:]
    totals = jnp.zeros((rows, 128), f32)
    pairs = heads // 2
    query_heads = q_ref.shape[1] // HD
    chain_copies = []
    for pair in range(pairs):
        span = slice(pair * 128, pair * 128 + 128)
        copy = remote(chain_out.at[pl.ds(pair * 128, 128)], chain_in.at[pl.ds(pair * 128, 128)],
                      chain_send.at[pair], chain_recv.at[pair], "seq", place + 1)
        chain_copies.append(copy)

        @pl.when(place > 0)
        def _():
            copy.wait_recv()
        chain_out[span, :] = (ends[span] * chain_in[span, :].astype(f32) + state[span]).astype(bf16)

        @pl.when(place + 1 < count)
        def _():
            copy.start()
        sides = []
        for h in (2 * pair, 2 * pair + 1):
            gap = running[:, h:h + 1] - running_t[h:h + 1, :]
            mixing = (jnp.exp(jnp.minimum(gap, 0.0)) * cb).astype(bf16)
            sides.append(nn(mixing, stepped[:, span]))
        y[:, span] += jnp.where(lane < 64, sides[0], sides[1])
        for h in range(query_heads * pair // pairs, query_heads * (pair + 1) // pairs):
            query = q_ref[:, h * HD:(h + 1) * HD] * jnp.asarray(HD ** -0.5, bf16)
            scores = jnp.where(allowed, nt(query, keys), masked_score)
            peak = jnp.max(scores, axis=1, keepdims=True)
            expo = jnp.exp(scores - peak)
            total = jnp.sum(expo, axis=1, keepdims=True)
            probs = (expo * (1.0 / total)).astype(bf16)
            att_ref[:, h * HD:(h + 1) * HD] = nn(probs, vals).astype(bf16)
            totals = jnp.where(lane == h, peak + jnp.log(total), totals)
    lse_ref[...] = totals
    mem_ref[...] = chain_in[...]
    decs = spread(dec, mapping)
    carried = decs * nt(c_rows, mem_ref[...])
    gate = gate_ref[...].astype(f32)
    gated_ref[...] = ((y[...] + carried) * (gate * sigmoid(gate))).astype(bf16)
    loads["out"].wait()
    loads["o"].wait()
    chunks = [pl.ds(begin, CHUNK) for begin in range(0, rows, CHUNK)]
    part_copies, down_copies = [], []
    for i, chunk in enumerate(chunks):
        part_out[chunk, :] = (nn(gated_ref[chunk, :], wout_ref[...])
                              + nn(att_ref[chunk, :], wo_ref[...])).astype(bf16)
        copy = remote(part_out.at[chunk], part_in.at[chunk], part_send.at[i], part_recv.at[i], "head", partner)
        copy.start()
        part_copies.append(copy)
    loads["gu"].wait()
    unpack(raw_gu, wgu_ref)
    loads["gu_store"].start()
    loads["down"].wait()
    for i, chunk in enumerate(chunks):
        part_copies[i].wait_recv()
        middle_ref[chunk, :] = h_ref[chunk, :].astype(f32) + (
            part_out[chunk, :].astype(f32) + part_in[chunk, :].astype(f32))
        nff_ref[chunk, :] = rms_scaled(middle_ref[chunk, :], gain_ff_ref[...]).astype(bf16)
        gu_ref[chunk, :] = nn(nff_ref[chunk, :], wgu_ref[...]).astype(bf16)
        gate = gu_ref[chunk, :ff_local].astype(f32)
        inner_ref[chunk, :] = (gate * sigmoid(gate) * gu_ref[chunk, ff_local:].astype(f32)).astype(bf16)
        down_out[chunk, :] = nn(inner_ref[chunk, :], wdown_ref[...]).astype(bf16)
        copy = remote(down_out.at[chunk], down_in.at[chunk], down_send.at[i], down_recv.at[i], "head", partner)
        copy.start()
        down_copies.append(copy)
    if not ready:
        loads["zx_store"].wait()
    if follows:
        loads["next"].wait()
        unpack(raw_zx, wzx_ref)
        loads["next_store"].start()
    for i, chunk in enumerate(chunks):
        down_copies[i].wait_recv()
        h_out[chunk, :] = (middle_ref[chunk, :] + (
            down_out[chunk, :].astype(f32) + down_in[chunk, :].astype(f32))).astype(bf16)
    loads["gu_store"].wait()
    if follows:
        loads["next_store"].wait()
    for i in range(len(chunks)):
        part_copies[i].wait_send()
        down_copies[i].wait_send()

    @pl.when(place + 1 < count)
    def _():
        rim_copy.wait_send()
        for copy in chain_copies:
            copy.wait_send()
    for j in range(1, count):
        @pl.when(place + j < count)
        def _():
            kv_copies[j - 1].wait_send()


def layer_forward(layer, hidden, zx, w, context):
    dcol, dloc, drow = context
    rows, model_width = hidden.shape
    heads = w["heads"]
    layers = w["out"].shape[0]
    d_local = w["out"].shape[1]
    ff_local = w["down"].shape[1]
    q_width = w["q"].shape[2]
    width = d_local + 2 * NS
    count = lax.axis_size("seq")
    length = count * rows
    parts = rows // CHUNK
    wide = ((model_width, 2 * d_local), bf16)
    outs = [
        ((rows, model_width), bf16), ((rows, model_width), bf16), ((rows, d_local), bf16), ((rows, width), bf16),
        ((RIM, width), bf16), ((rows, width), f32), ((rows, 128), f32), ((rows, q_width), bf16),
        ((length, 2 * HD), bf16), ((rows, q_width), bf16), ((rows, 128), f32), ((d_local, NS), bf16),
        ((rows, d_local), bf16), ((rows, model_width), f32), ((rows, model_width), bf16),
        ((rows, 2 * ff_local), bf16), ((rows, ff_local), bf16), ((model_width, 2 * ff_local), bf16),
    ]
    kept = len(outs) - 1
    outs += [wide] * ((layer == 0) + (layer + 1 < layers))
    full = (rows, model_width)
    given = [] if layer == 0 else [zx]
    result = pl.pallas_call(
        functools.partial(layer_forward_kernel, heads, layer, layers),
        out_shape=[jax.ShapeDtypeStruct(shape, kind) for shape, kind in outs],
        in_specs=[VM] * 9 + [ANY] * (8 + len(given)),
        out_specs=[VM] * kept + [ANY] * (len(outs) - kept),
        scratch_shapes=[
            pltpu.VMEM((rows + RIM, width), f32), pltpu.VMEM((rows, d_local), f32),
            pltpu.VMEM((model_width, 2 * HD), bf16), pltpu.VMEM((model_width, 2 * NS), bf16),
            pltpu.VMEM((model_width, 2 * d_local), bf16), pltpu.VMEM((model_width, q_width), bf16),
            pltpu.VMEM((q_width, model_width), bf16), pltpu.VMEM((d_local, model_width), bf16),
            pltpu.VMEM((model_width, 2 * ff_local), bf16), pltpu.VMEM((ff_local, model_width), bf16),
            pltpu.VMEM((model_width, 2, d_local), bf16), pltpu.VMEM((model_width, 2, ff_local), bf16),
            pltpu.VMEM((RIM, width), bf16), pltpu.VMEM((length, 2 * HD), bf16),
            pltpu.VMEM((d_local, NS), bf16), pltpu.VMEM((d_local, NS), bf16),
            pltpu.VMEM(full, bf16), pltpu.VMEM(full, bf16), pltpu.VMEM(full, bf16), pltpu.VMEM(full, bf16),
            DMA((12,)), DMA((count - 1,)), DMA((count - 1,)), DMA, DMA, DMA((heads // 2,)), DMA((heads // 2,)),
            DMA((parts,)), DMA((parts,)), DMA((parts,)), DMA((parts,)),
        ],
        compiler_params=pltpu.CompilerParams(
            vmem_limit_bytes=VMEM_LIMIT, collective_id=layer, has_side_effects=True),
    )(hidden, w["gain_mix"][layer], w["gain_ff"][layer], w["dt"][layer], w["taps"][layer], w["head_vals"][layer],
      dcol, dloc, drow, w["kv"], w["bc"], w["zx"], w["q"], w["out"], w["o"], w["gu"], w["down"], *given)
    names = ("out", "normed", "gate", "stack", "rim", "pre", "dt", "q", "kv", "att", "lse", "memory",
             "gated", "middle", "nff", "gu", "inner", "w_gu")
    saved = dict(zip(names, result))
    saved["hidden"] = hidden
    extra = list(result[len(names):])
    saved["w_zx"] = extra.pop(0) if layer == 0 else zx
    return saved.pop("out"), (extra.pop(0) if extra else None), saved


def norm_back(hidden, gain, grad):
    inverse = lax.rsqrt(jnp.mean(hidden * hidden, axis=-1, keepdims=True) + norm_eps)
    scaled = grad * gain
    lean = jnp.mean(scaled * hidden, axis=-1, keepdims=True)
    grad_gain = jnp.sum(grad * hidden * inverse, axis=0, keepdims=True)
    return inverse * (scaled - hidden * (inverse * inverse * lean)), grad_gain


def store_blocks(compute, slots, out, sems):
    size = slots.shape[1]
    columns = out.shape[1]
    blocks = out.shape[0] // size

    def rows(i):
        return pl.ds(pl.multiple_of(i * size, size), size)

    def copy(i, slot):
        return pltpu.make_async_copy(slots.at[slot, :, pl.ds(0, columns)], out.at[rows(i)], sems.at[slot])

    def one(i, carry):
        slot = lax.rem(i, 2)

        @pl.when(i >= 2)
        def _():
            copy(i - 2, slot).wait()
        compute(rows(i), slot)
        copy(i, slot).start()
        return carry
    lax.fori_loop(0, blocks, one, 0)
    for i in range(max(0, blocks - 2), blocks):
        copy(i, i % 2).wait()


def layer_backward_kernel(heads, layer, schedule, grad_ref, h_ref, normed_ref, gate_ref, stack_ref, rim_ref, pre_ref, dt_ref,
                          q_ref, kv_ref, att_ref, lse_ref, mem_ref, gated_ref, middle_ref, nff_ref, gu_ref,
                          inner_ref, gain_mix_ref, gain_ff_ref, wdt_ref,
                          taps_ref, heads_ref, dcol_ref, dloc_ref, drow_ref,
                          wdown_hbm, wgu_hbm, wout_hbm, wo_hbm, wzx_hbm, wbc_hbm, wq_hbm, wkv_hbm, *refs):
    refs = list(refs)
    own_sum = schedule["own"]
    source = None if own_sum else refs.pop(0)
    half_in = None if own_sum else refs.pop(0)
    if not own_sum:
        line_refs, refs = refs[-LINE_REFS - 1:], refs[:-LINE_REFS - 1]
    cross_refs, refs = refs[-CROSS_REFS:], refs[:-CROSS_REFS]
    summed_ref = None if own_sum else refs.pop(0)
    (g_out, gff_out, gmix_out, gbc_out, small_ref, half_ref,
     wdown_ref, wide_ref, wout_ref, wo_ref, wbc_ref, wq_ref, wkv_ref,
     gff, dgu, one_out, one_in, two_out, two_in, gmid, branch, gg, datt, dy_s, dxs_s, u_s,
     decay_s, probs_s, acc, dkv_out, dkv_in, chain_in, chain_out, rim_in,
     ext, pad, dext, dgate, dstack, dq, dkv, draw_s,
     load_sem, one_send, one_recv, two_send, two_recv, chain_send, chain_recv,
     rim_send, rim_recv, kv_send, kv_recv, gblk, grad_sem) = refs
    rows = dt_ref.shape[0]
    d_local = gate_ref.shape[1]
    ff_local = inner_ref.shape[1]
    q_width = q_ref.shape[1]
    model_width = h_ref.shape[1]
    width = pre_ref.shape[1]
    length = kv_ref.shape[0]
    count = lax.axis_size("seq")
    place = lax.axis_index("seq")
    wgu_ref = wide_ref.at[:, pl.ds(0, 2 * ff_local)]
    wzx_ref = wide_ref.at[:, pl.ds(0, 2 * d_local)]
    loads = {}
    for name, src, dst in (
        ("down", wdown_hbm.at[layer], wdown_ref), ("gu", wgu_hbm, wgu_ref), ("out", wout_hbm.at[layer], wout_ref),
        ("o", wo_hbm.at[layer], wo_ref), ("bc", wbc_hbm.at[layer], wbc_ref), ("q", wq_hbm.at[layer], wq_ref),
        ("kv", wkv_hbm.at[layer], wkv_ref), ("zx", wzx_hbm, wzx_ref),
    ):
        loads[name] = pltpu.make_async_copy(src, dst, load_sem.at[len(loads)])
    for name in ("down", "gu", "out", "o", "bc", "q", "kv"):
        loads[name].start()
    partner = meet(count, True, greet_sums)
    cross = CrossSum(cut_columns([gff_out if own_sum else source]), cross_refs[:3], cross_refs[3:])
    ranges = [columns for _, columns in cut_columns([half_ref])]
    steps_of = {"a": cross.step_a, "b": lambda n: cross.step_b(n, half_ref.at[:, ranges[n]])}
    if not own_sum:
        fetches = [pltpu.make_async_copy(half_in.at[:, columns], line_refs[0].at[n], load_sem.at[len(loads) + n])
                   for n, (_, columns) in enumerate(cut_columns([half_in]))]
        for fetch in fetches:
            fetch.start()
        for fetch in fetches:
            fetch.wait()
        line = LineSum([line_refs[0].at[n] for n in range(UNITS)], *line_refs[1:])

        def write(n, terms):
            size = terms[0].shape[1]
            add_rows(summed_ref.at[:, pl.ds(n * size, size)], terms)
        steps_of.update({"c": line.step_c, "d": line.step_d, "e": lambda n: line.step_e(n, write)})

    def pump(spot):
        for step in schedule.get(spot, ()):
            if step == "start":
                cross.start()
            elif step == "finish":
                cross.finish()
                if not own_sum:
                    line.finish()
            else:
                steps_of[step[0]](int(step[1]))
    pump("begin")
    chunks = [pl.ds(begin, CHUNK) for begin in range(0, rows, CHUNK)]

    gff[...] = grad_ref[...].astype(bf16)
    loads["down"].wait()
    loads["gu"].wait()
    one_copies, two_copies = [], []
    for i, chunk in enumerate(chunks):
        grad_inner = nt(gff[chunk, :], wdown_ref[...])
        gate = gu_ref[chunk, :ff_local].astype(f32)
        up = gu_ref[chunk, ff_local:].astype(f32)
        sig = sigmoid(gate)
        dgu[chunk, :ff_local] = (grad_inner * up * (sig * (1.0 + gate * (1.0 - sig)))).astype(bf16)
        dgu[chunk, ff_local:] = (grad_inner * (gate * sig)).astype(bf16)
        one_out[chunk, :] = nt(dgu[chunk, :], wgu_ref[...]).astype(bf16)
        copy = remote(one_out.at[chunk], one_in.at[chunk], one_send.at[i], one_recv.at[i], "head", partner)
        copy.start()
        one_copies.append(copy)
    loads["zx"].start()

    @pl.when(place == count - 1)
    def _():
        rim_in[...] = jnp.zeros(rim_in.shape, f32)
        chain_in[...] = jnp.zeros(chain_in.shape, bf16)
    for j in range(1, count):
        @pl.when(place + j >= count)
        def _():
            dkv_in[(j - 1) * rows:j * rows, :] = jnp.zeros((rows, 2 * HD), bf16)

    pump("ff0")

    def ff_weights(block, slot):
        gblk[slot, :, :ff_local] = tn(gff[:, block], inner_ref[...]).astype(bf16)
        gblk[slot, :, ff_local:3 * ff_local] = tn(nff_ref[:, block], dgu[...]).astype(bf16)
    store_blocks(ff_weights, gblk, gff_out, grad_sem)
    pump("ff")

    raw, step, log_decay, running, running_t, ordered = ssm_scalars(dt_ref, heads_ref)
    mapping = head_map(heads, d_local // heads)
    last = running[rows - 1:rows, :]
    fade = spread(jnp.exp(last - running) * dcol_ref[:, 5:6], mapping)
    dec = jnp.exp(running) * dcol_ref[:, 4:5]
    decs = spread(dec, mapping)
    ends = jnp.exp(running_t[:, rows - 1:rows]) * dcol_ref[rows - 1:rows, 4:5] + jnp.zeros((128, NS), f32)
    ends = exact(mapping, ends, (0, 0))
    steps = spread(step, mapping)
    skip = spread(heads_ref[2:3, :] + jnp.zeros((8, 128), f32), mapping)[0:1, :]
    pre_v = pre_ref[:, :d_local]
    values = pre_v * sigmoid(pre_v)
    pre_n = pre_ref[:, d_local:]
    maps = (pre_n * sigmoid(pre_n)).astype(bf16)
    b_rows, c_rows = maps[:, :NS], maps[:, NS:]
    stepped = (values * steps).astype(bf16)
    linked = ordered & (dcol_ref[:, 0:1] == dloc_ref[0:1, :])
    cb = jnp.where(linked, nt(c_rows, b_rows), 0.0)
    lane = lax.broadcasted_iota(jnp.int32, (rows, 128), 1)
    pairs = heads // 2
    for pair in range(pairs):
        span = slice(pair * 128, pair * 128 + 128)
        sides = []
        for h in (2 * pair, 2 * pair + 1):
            at = slice(h * rows, (h + 1) * rows)
            gap = running[:, h:h + 1] - running_t[h:h + 1, :]
            decay = jnp.exp(jnp.minimum(gap, 0.0))
            decay_s[:, at] = decay.astype(bf16)
            mixing = (decay_s[:, at].astype(f32) * cb).astype(bf16)
            sides.append(nn(mixing, stepped[:, span]))
        u_s[:, span] = jnp.where(lane < 64, sides[0], sides[1])
    allowed = score_mask(dcol_ref, drow_ref)
    keyvals = kv_ref[...]
    keys, vals = keyvals[:, :HD], keyvals[:, HD:]
    scale = jnp.asarray(HD ** -0.5, bf16)
    query_heads = q_width // HD
    for h in range(query_heads):
        query = q_ref[:, h * HD:(h + 1) * HD] * scale
        scores = jnp.where(allowed, nt(query, keys), masked_score)
        probs_s[:, h * length:(h + 1) * length] = jnp.exp(scores - lse_ref[:, h:h + 1]).astype(bf16)
    ext[0:RIM, :] = rim_ref[...].astype(f32)
    ext[RIM:, :] = stack_ref[...].astype(f32)
    gate = gate_ref[...].astype(f32)
    gate_sig = sigmoid(gate)
    gate_act = gate * gate_sig
    loads["out"].wait()
    loads["o"].wait()
    dtaps_ref = small_ref.at[pl.ds(0, 8)]
    gains_ref = small_ref.at[pl.ds(8, 8)]
    dheads_ref = small_ref.at[pl.ds(16, 8)]
    gains_ref[...] = jnp.zeros(gains_ref.shape, f32)
    for i, chunk in enumerate(chunks):
        pump("one%d" % i)
        one_copies[i].wait_recv()
        grad = one_out[chunk, :].astype(f32) + one_in[chunk, :].astype(f32)
        moved, gain = norm_back(middle_ref[chunk, :], gain_ff_ref[...], grad)
        gains_ref[1:2, :] += gain
        gmid[chunk, :] = grad_ref[chunk, :] + moved
        branch[chunk, :] = gmid[chunk, :].astype(bf16)
        gg[chunk, :] = nt(branch[chunk, :], wout_ref[...])
        datt[chunk, :] = nt(branch[chunk, :], wo_ref[...]).astype(bf16)
    grad_ssm = gg[...] * gate_act
    dy_s[...] = grad_ssm.astype(bf16)
    push = tn((grad_ssm * decs).astype(bf16), c_rows)
    dcb = jnp.zeros((rows, rows), f32)
    chain_copies = []
    for pair in range(pairs):
        pump("pair%d" % pair)
        span = slice(pair * 128, pair * 128 + 128)
        copy = remote(chain_out.at[pl.ds(pair * 128, 128)], chain_in.at[pl.ds(pair * 128, 128)],
                      chain_send.at[pair], chain_recv.at[pair], "seq", place - 1)
        chain_copies.append(copy)

        @pl.when(place < count - 1)
        def _():
            copy.wait_recv()
        chain_out[span, :] = (ends[span] * chain_in[span, :].astype(f32) + push[span]).astype(bf16)

        @pl.when(place > 0)
        def _():
            copy.start()
        stepped_p = stepped[:, span]
        dy_p = dy_s[:, span]
        dxs = []
        for side, h in enumerate((2 * pair, 2 * pair + 1)):
            at = slice(h * rows, (h + 1) * rows)
            decay = decay_s[:, at].astype(f32)
            dxs.append(tn((decay * cb).astype(bf16), dy_p))
            half = jnp.where((lane < 64) == (side == 0), dy_p, jnp.zeros_like(dy_p))
            dcb = dcb + nt(half, stepped_p) * decay
        dxs_s[:, span] = jnp.where(lane < 64, dxs[0], dxs[1])
        for h in range(query_heads * pair // pairs, query_heads * (pair + 1) // pairs):
            part = slice(h * HD, (h + 1) * HD)
            query = q_ref[:, part] * scale
            grad = datt[:, part]
            delta = jnp.sum(grad.astype(f32) * att_ref[:, part].astype(f32), axis=1, keepdims=True)
            probs = probs_s[:, h * length:(h + 1) * length]
            grad_scores = (probs.astype(f32) * (nt(grad, vals) - delta)).astype(bf16)
            dq[:, part] = (nn(grad_scores, keys) * HD ** -0.5).astype(bf16)
            dk = tn(grad_scores, query)
            dv = tn(probs, grad)
            if h == 0:
                acc[:, :HD] = dk
                acc[:, HD:] = dv
            else:
                acc[:, :HD] += dk
                acc[:, HD:] += dv
    dkv_out[...] = acc[...].astype(bf16)
    kv_copies = []
    for j in range(1, count):
        target = jnp.maximum(place - j, 0)
        theirs = pl.ds(pl.multiple_of(target * rows, rows), rows)
        copy = remote(dkv_out.at[theirs], dkv_in.at[pl.ds((j - 1) * rows, rows)], kv_send.at[j - 1],
                      kv_recv.at[j - 1], "seq", place - j)
        kv_copies.append(copy)

        @pl.when(place >= j)
        def _():
            copy.start()
    pump("post")
    memory = mem_ref[...]
    gmem = chain_in[...]
    carried = decs * nt(c_rows, memory)
    back = fade * nt(b_rows, gmem)
    dy_low = dy_s[...].astype(f32)
    stepped_f = stepped.astype(f32)
    dxs_all = dxs_s[...] + back
    dxs_s[...] = dxs_all
    dcb = jnp.where(linked, dcb, 0.0).astype(bf16)
    dc = nn(dcb, b_rows) + nn((dy_low * decs).astype(bf16), memory)
    db = tn(dcb, c_rows) + nn((stepped_f * fade).astype(bf16), gmem)
    dvalues = steps * dxs_all + skip * grad_ssm
    pad[0:8, :] = jnp.zeros((8, width), f32)
    pad[8 + rows:, :] = jnp.zeros((8, width), f32)
    sig = sigmoid(pre_v)
    pad[8:8 + rows, :d_local] = dvalues * (sig * (1.0 + pre_v * (1.0 - sig)))
    sig = sigmoid(pre_n)
    slope = sig * (1.0 + pre_n * (1.0 - sig))
    pad[8:8 + rows, d_local:d_local + NS] = db * slope[:, :NS]
    pad[8:8 + rows, d_local + NS:] = dc * slope[:, NS:]
    dpre = pad[8:8 + rows, :]
    dext[...] = pad[0:8 + rows, :] * taps_ref[0:1, :]
    dtaps_ref[...] = jnp.zeros((8, width), f32)
    dtaps_ref[0:1, :] = jnp.sum(dpre * ext[RIM:RIM + rows, :], axis=0, keepdims=True)
    for k in range(1, 4):
        masked = dpre * dcol_ref[:, k:k + 1]
        pad[8:8 + rows, :] = masked
        dtaps_ref[k:k + 1, :] = jnp.sum(masked * ext[RIM - k:RIM - k + rows, :], axis=0, keepdims=True)
        dext[...] += pad[k:k + 8 + rows, :] * taps_ref[k:k + 1, :]
    rim_copy = remote(dext.at[pl.ds(0, 8)], rim_in, rim_send, rim_recv, "seq", place - 1)

    @pl.when(place > 0)
    def _():
        rim_copy.start()
    scanned = u_s[...] + carried
    drun = exact(dy_low * scanned - stepped_f * dxs_all, mapping, (1, 1))
    ssm_out = scanned + skip * values
    dgate[...] = (gg[...] * ssm_out * (gate_sig * (1.0 + gate * (1.0 - gate_sig)))).astype(bf16)
    gstep = exact(values * dxs_all, mapping, (1, 1))
    ones = jnp.ones((8, 128), f32)
    moved = exact(ones, gmem.astype(f32) * memory.astype(f32), (1, 1))
    end = exact(jnp.sum(stepped_f * back, axis=0, keepdims=True) + jnp.zeros((8, 1), f32), mapping, (1, 1))
    end = end + exact(moved, mapping, (1, 1)) * dec[rows - 1:rows, :]
    upper = (lax.broadcasted_iota(jnp.int32, (rows, rows), 1)
             >= lax.broadcasted_iota(jnp.int32, (rows, rows), 0)).astype(f32)
    dlog = exact(upper, drun) + end[0:1, :]
    draw = (gstep - jnp.exp(heads_ref[1:2, :]) * dlog) * sigmoid(raw)
    draw_s[...] = draw.astype(bf16)
    dskip = exact(jnp.sum(grad_ssm * values, axis=0, keepdims=True) + jnp.zeros((8, 1), f32), mapping, (1, 1))
    dheads_ref[...] = jnp.zeros(dheads_ref.shape, f32)
    dheads_ref[0:1, :128] = jnp.sum(draw, axis=0, keepdims=True)
    dheads_ref[1:2, :128] = jnp.sum(dlog * log_decay, axis=0, keepdims=True)
    dheads_ref[2:3, :128] = dskip[0:1, :]
    for name in ("zx", "bc", "q", "kv"):
        loads[name].wait()

    for j in range(1, count):
        @pl.when(place + j < count)
        def _():
            kv_copies[j - 1].wait_recv()
    pump("two")
    own = pl.ds(pl.multiple_of(place * rows, rows), rows)
    total = acc[own, :]
    for j in range(1, count):
        total = total + dkv_in[(j - 1) * rows:j * rows, :].astype(f32)
    dkv[...] = total.astype(bf16)

    for i, chunk in enumerate(chunks):
        if i == len(chunks) - 1:
            @pl.when(place < count - 1)
            def _():
                rim_copy.wait_recv()
            dext[rows:rows + 8, :] += rim_in[...]
        dstack[chunk, :] = dext[8 + i * CHUNK:8 + (i + 1) * CHUNK, :].astype(bf16)
        two_out[chunk, :] = (
            nt(dgate[chunk, :], wzx_ref[:, :d_local]) + nt(dstack[chunk, :d_local], wzx_ref[:, d_local:])
            + nt(dstack[chunk, d_local:], wbc_ref[...]) + nt(draw_s[chunk, :], wdt_ref[...])
            + nt(dq[chunk, :], wq_ref[...]) + nt(dkv[chunk, :], wkv_ref[...])
        ).astype(bf16)
        copy = remote(two_out.at[chunk], two_in.at[chunk], two_send.at[i], two_recv.at[i], "head", partner)
        copy.start()
        two_copies.append(copy)

    gbc_out[:, model_width:] = jnp.transpose(jnp.concatenate(
        [dtaps_ref[:, d_local:], jnp.zeros((120, 2 * NS), f32)], axis=0)).astype(bf16)
    pump("mix")

    def mix_weights(block, slot):
        left = normed_ref[:, block]
        at = 0
        for right in (dgate[...], dstack[:, :d_local], dq[...], dkv[...], draw_s[...]):
            gblk[slot, :, at:at + right.shape[1]] = tn(left, right).astype(bf16)
            at += right.shape[1]
        left = branch[:, block]
        for right in (gated_ref[...], att_ref[...]):
            gblk[slot, :, at:at + right.shape[1]] = tn(left, right).astype(bf16)
            at += right.shape[1]
        gbc_out[:, block] = tn(dstack[:, d_local:], normed_ref[:, block]).astype(bf16)
    store_blocks(mix_weights, gblk, gmix_out, grad_sem)

    for i, chunk in enumerate(chunks):
        pump("last%d" % i)
        two_copies[i].wait_recv()
        grad = two_out[chunk, :].astype(f32) + two_in[chunk, :].astype(f32)
        moved, gain = norm_back(h_ref[chunk, :].astype(f32), gain_mix_ref[...], grad)
        gains_ref[0:1, :] += gain
        g_out[chunk, :] = gmid[chunk, :] + moved
    pump("end")
    for i in range(len(chunks)):
        one_copies[i].wait_send()
        two_copies[i].wait_send()

    @pl.when(place > 0)
    def _():
        rim_copy.wait_send()
        for copy in chain_copies:
            copy.wait_send()
    for j in range(1, count):
        @pl.when(place >= j)
        def _():
            kv_copies[j - 1].wait_send()


SCHEDULES = (
    {"own": False, "begin": ("start", "c0", "c1", "c2", "c3"), "ff0": ("a0", "a1", "a2", "a3"), "ff": ("d0", "d1"),
     "one0": ("d2",), "one1": ("d3",), "mix": ("b0", "b1"), "last0": ("e0", "e1", "e2", "e3", "b2"),
     "end": ("b3", "finish")},
    {"own": True, "ff": ("start",), "one0": ("a0", "a1"), "one1": ("a2", "a3"), "mix": ("b0",), "last0": ("b1", "b2"),
     "end": ("b3", "finish")},
)


def layer_backward(layer, grad, waiting, w, saved, context):
    dcol, dloc, drow = context
    rows, model_width = grad.shape
    heads = w["heads"]
    d_local = w["out"].shape[1]
    ff_local = w["down"].shape[1]
    q_width = w["q"].shape[2]
    width = d_local + 2 * NS
    count = lax.axis_size("seq")
    length = count * rows
    parts = rows // CHUNK
    mix_width = 3 * d_local + 2 * q_width + 256
    schedule = SCHEDULES[1 if waiting is None else 0]
    given = [] if waiting is None else list(waiting)
    outs = [
        ((rows, model_width), f32), ((model_width, 3 * ff_local), bf16), ((model_width, mix_width), bf16),
        ((2 * NS, model_width + 128), bf16), ((24, max(width, model_width)), f32),
    ]
    span = model_width // lax.axis_size("dp")
    if waiting is not None:
        outs.insert(0, ((span // count, 3 * ff_local), f32))
    outs.append(((span, 3 * ff_local if waiting is None else mix_width), bf16))
    full = (rows, model_width)
    state = (d_local, NS)
    names = ("hidden", "normed", "gate", "stack", "rim", "pre", "dt", "q", "kv", "att", "lse", "memory",
             "gated", "middle", "nff", "gu", "inner")

    def vm(shape, kind):
        return pltpu.VMEM(shape, kind)
    return pl.pallas_call(
        functools.partial(layer_backward_kernel, heads, layer, schedule),
        out_shape=[jax.ShapeDtypeStruct(shape, kind) for shape, kind in outs],
        in_specs=[VM] * 26 + [ANY] * (8 + len(given)),
        out_specs=[VM] * (len(outs) - 5) + [ANY, ANY] + [VM] * 3,
        scratch_shapes=[
            vm((ff_local, model_width), bf16), vm((model_width, 2 * max(d_local, ff_local)), bf16),
            vm((d_local, model_width), bf16), vm((q_width, model_width), bf16), vm((model_width, 2 * NS), bf16),
            vm((model_width, q_width), bf16), vm((model_width, 2 * HD), bf16),
            vm(full, bf16), vm((rows, 2 * ff_local), bf16), vm(full, bf16), vm(full, bf16), vm(full, bf16),
            vm(full, bf16), vm(full, f32), vm(full, bf16), vm((rows, d_local), f32), vm((rows, q_width), bf16),
            vm((rows, d_local), bf16), vm((rows, d_local), f32), vm((rows, d_local), f32),
            vm((rows, heads * rows), bf16),
            vm((rows, q_width // HD * length), bf16), vm((length, 2 * HD), f32), vm((length, 2 * HD), bf16),
            vm(((count - 1) * rows, 2 * HD), bf16), vm(state, bf16), vm(state, bf16), vm((8, width), f32),
            vm((rows + RIM, width), f32), vm((rows + 16, width), f32), vm((rows + 8, width), f32),
            vm((rows, d_local), bf16), vm((rows, width), bf16), vm((rows, q_width), bf16),
            vm((rows, 2 * HD), bf16), vm((rows, 128), bf16),
            DMA((8 + UNITS,)), DMA((parts,)), DMA((parts,)), DMA((parts,)), DMA((parts,)), DMA((heads // 2,)),
            DMA((heads // 2,)), DMA, DMA, DMA((count - 1,)), DMA((count - 1,)),
            vm((2, 128, max(3 * ff_local, mix_width)), bf16), DMA((2,)),
            *cross_scratch(UNITS, span, outs[-1][0][1]),
            *([] if waiting is None else
              [vm((UNITS, span, 3 * ff_local // UNITS), bf16), *line_scratch(UNITS, span, 3 * ff_local)]),
        ],
        compiler_params=pltpu.CompilerParams(
            vmem_limit_bytes=VMEM_LIMIT, collective_id=2 + layer, has_side_effects=True),
    )(grad, *[saved[name] for name in names], w["gain_mix"][layer], w["gain_ff"][layer], w["dt"][layer],
      w["taps"][layer], w["head_vals"][layer], dcol, dloc, drow, w["down"], saved["w_gu"], w["out"], w["o"],
      saved["w_zx"], w["bc"], w["q"], w["kv"], *given)


def on_device(hidden_in, segment_ids, gain_mix, w_zx, w_bc, w_dt, conv_x, conv_bc, ssm_head, w_q, w_kv,
              w_o, w_out, gain_ff, w_gu, w_down, cotangent):
    rows, model_width = hidden_in.shape
    taps_count = conv_x.shape[1]
    place = lax.axis_index("seq")
    offset = place * rows
    doc_all = segment_ids[0]
    padded = jnp.concatenate([jnp.full((taps_count - 1,), -1, jnp.int32), doc_all])
    doc_ext = lax.dynamic_slice_in_dim(padded, offset, rows + taps_count - 1)
    docs = doc_ext[taps_count - 1:]
    columns = [docs.astype(f32)]
    for k in range(1, taps_count):
        columns.append((doc_ext[taps_count - 1 - k:taps_count - 1 - k + rows] == docs).astype(f32))
    columns.append((docs == doc_ext[taps_count - 2]).astype(f32))
    columns.append((docs == docs[-1]).astype(f32))
    dcol = jnp.pad(jnp.stack(columns, axis=1), ((0, 0), (0, 128 - len(columns))))
    dloc = jnp.broadcast_to(docs.astype(f32)[None], (8, rows))
    drow = jnp.broadcast_to(doc_all.astype(f32)[None], (8, doc_all.shape[0]))
    context = (dcol, dloc, drow)
    layers = gain_mix.shape[0]
    heads = ssm_head.shape[2]
    d_local = w_zx.shape[3]
    w = dict(
        heads=heads,
        gain_mix=gain_mix[:, None].astype(f32),
        gain_ff=gain_ff[:, None].astype(f32),
        zx=w_zx,
        bc=w_bc,
        dt=jnp.pad(w_dt, ((0, 0), (0, 0), (0, 128 - heads))),
        q=w_q,
        kv=w_kv.reshape(layers, model_width, -1),
        o=w_o,
        out=w_out,
        gu=w_gu,
        down=w_down,
        taps=jnp.pad(jnp.concatenate([conv_x.reshape(layers, taps_count, -1), conv_bc], axis=2).astype(f32),
                     ((0, 0), (0, 8 - taps_count), (0, 0))),
        head_vals=jnp.pad(ssm_head, ((0, 0), (0, 5), (0, 128 - heads))),
    )
    hidden = hidden_in
    saved = []
    zx = None
    for l in range(layers):
        hidden, zx, kept = layer_forward(l, hidden, zx, w, context)
        saved.append(kept)
    block_out = hidden
    gradient = cotangent.astype(f32)
    narrow, small = [None] * layers, [None] * layers
    waiting = None
    for l in reversed(range(layers)):
        *summed, gradient, ff_grads, mix_grads, narrow[l], small[l], half = layer_backward(
            l, gradient, waiting, w, saved[l], context)
        waiting = (mix_grads, half)
    g_bc = lax.psum_scatter(jnp.concatenate(narrow, axis=1), ("dp", "seq", "head"), scatter_dimension=0, tiled=True)
    small = [lax.psum(a, ("dp", "seq")) for a in small]
    shards = lax.axis_size("dp") * lax.axis_size("seq")
    shard = lax.axis_index("dp") * lax.axis_size("seq") + place
    ff_local = w_down.shape[1]
    q_width = w_q.shape[2]
    part = model_width // shards
    down, gu, zx, q, kv, dt, out, o = last_sum(
        (ff_grads, mix_grads), half, summed[0],
        ((ff_local, 2 * ff_local), (2 * d_local, q_width, 128, 128, d_local, q_width)))
    down, out, o = (jnp.transpose(a, (0, 2, 1)) for a in (down, out, o))
    gu = gu.reshape(layers, part, 2, ff_local)
    zx = zx.reshape(layers, part, 2, d_local)
    kv = kv.reshape(layers, part, 1, 128)
    dt = dt[:, :, :heads]
    g_bc = g_bc.astype(f32).reshape(g_bc.shape[0], layers, -1)
    w_bc_grad = jnp.transpose(g_bc[:, :, :model_width], (1, 2, 0))
    conv_bc_grad = jnp.transpose(g_bc[:, :, model_width:model_width + taps_count], (1, 2, 0))
    small = jnp.stack(small, axis=0)
    gain_a = lax.dynamic_slice_in_dim(small[:, 8, :model_width], shard * part, part, 1)
    gain_b = lax.dynamic_slice_in_dim(small[:, 9, :model_width], shard * part, part, 1)
    taps = small[:, :taps_count, :d_local].reshape(layers, taps_count, heads, -1)
    taps_part = taps.shape[3] // shards
    conv_x_grad = lax.dynamic_slice_in_dim(taps, shard * taps_part, taps_part, 3)
    head_grad = small[:, 16:19, :heads]
    return (block_out, gradient, gain_a, zx, w_bc_grad, dt, conv_x_grad, conv_bc_grad, head_grad, q, kv,
            o, out, gain_b, gu, down)


def solution(mesh):
    in_specs = (
        P(("dp", "seq"), None),
        P("dp", None),
        P(),
        P(None, None, None, "head"),
        P(),
        P(None, None, "head"),
        P(None, None, "head", None),
        P(),
        P(None, None, "head"),
        P(None, None, "head"),
        P(None, None, "head", None),
        P(None, "head", None),
        P(None, "head", None),
        P(),
        P(None, None, None, "head"),
        P(None, "head", None),
        P(("dp", "seq"), None),
    )
    out_specs = (
        P(("dp", "seq"), None),
        P(("dp", "seq"), None),
        P(None, ("dp", "seq")),
        P(None, ("dp", "seq"), None, "head"),
        P(None, None, ("dp", "seq", "head")),
        P(None, ("dp", "seq"), "head"),
        P(None, None, "head", ("dp", "seq")),
        P(None, None, ("dp", "seq", "head")),
        P(None, None, "head"),
        P(None, ("dp", "seq"), "head"),
        P(None, ("dp", "seq"), "head", None),
        P(None, "head", ("dp", "seq")),
        P(None, "head", ("dp", "seq")),
        P(None, ("dp", "seq")),
        P(None, ("dp", "seq"), None, "head"),
        P(None, "head", ("dp", "seq")),
    )
    return jax.shard_map(
        on_device, mesh=mesh, in_specs=in_specs, out_specs=out_specs, check_vma=False
    )
```

```python
import functools

import jax
import jax.numpy as jnp
from jax import lax
from jax.experimental import pallas as pl
from jax.experimental.pallas import tpu as pltpu
from jax.sharding import PartitionSpec as P

NS = 128
HD = 64
RIM = 16

norm_eps = 1e-05
masked_score = -1e30
bf16 = jnp.bfloat16
f32 = jnp.float32
VMEM_LIMIT = 63 * 1024 * 1024


def nn(left, right):
    return jnp.dot(left, right, preferred_element_type=f32)


def tn(left, right):
    return lax.dot_general(left, right, (((0,), (0,)), ((), ())), preferred_element_type=f32)


def nt(left, right):
    return lax.dot_general(left, right, (((1,), (1,)), ((), ())), preferred_element_type=f32)


def split(v, terms):
    parts = []
    for _ in range(terms):
        parts.append(v.astype(bf16))
        v = v - parts[-1].astype(f32)
    return parts


def sigmoid(v):
    return 0.5 * jnp.tanh(0.5 * v) + 0.5


def softplus(v):
    return jnp.maximum(v, 0.0) + jnp.log(1.0 + jnp.exp(-jnp.abs(v)))


def head_map(heads, width):
    rows = lax.rem(lax.broadcasted_iota(jnp.int32, (256, heads * width), 0), 128)
    columns = lax.broadcasted_iota(jnp.int32, (256, heads * width), 1)
    return (columns // width == rows).astype(bf16)


def spread(scalars, mapping):
    return nn(jnp.concatenate(split(scalars, 2), axis=1), mapping)


def spread_rows(scalars, mapping):
    return tn(mapping, jnp.concatenate(split(scalars, 2), axis=0))


def gather(columns, mapping):
    high, low = split(columns, 2)
    return nt(high, mapping[:128]) + nt(low, mapping[:128])


def triangle_sum(triangle, v):
    width = v.shape[1]
    sums = nn(triangle, jnp.concatenate(split(v, 3), axis=1))
    return sums[:, :width] + sums[:, width:2 * width] + sums[:, 2 * width:]


def rms_scaled(hidden, gain):
    return hidden * lax.rsqrt(jnp.mean(hidden * hidden, axis=-1, keepdims=True) + norm_eps) * gain


def ssm_scalars(dt_ref, heads_ref):
    rows = dt_ref.shape[0]
    raw = dt_ref[...] + heads_ref[0:1, :]
    step = softplus(raw)
    log_decay = -jnp.exp(heads_ref[1:2, :]) * step
    place_t = lax.broadcasted_iota(jnp.int32, (rows, rows), 0)
    place_s = lax.broadcasted_iota(jnp.int32, (rows, rows), 1)
    running = triangle_sum((place_s <= place_t).astype(bf16), log_decay)
    running_t = jnp.transpose(running)
    return raw, step, log_decay, running, running_t, place_t >= place_s


def score_mask(dcol_ref, drow_ref):
    rows, length = dcol_ref.shape[0], drow_ref.shape[1]
    query_pos = lax.broadcasted_iota(jnp.int32, (rows, length), 0) + lax.axis_index("seq") * rows
    key_pos = lax.broadcasted_iota(jnp.int32, (rows, length), 1)
    return (key_pos <= query_pos) & (dcol_ref[:, 0:1] == drow_ref[0:1, :])


MESH_ID = pl.DeviceIdType.MESH
CHUNK = 128


def remote(src, dst, send, recv, axis, target):
    return pltpu.make_async_remote_copy(
        src_ref=src, dst_ref=dst, send_sem=send, recv_sem=recv,
        device_id={axis: target}, device_id_type=MESH_ID,
    )


def meet(count, later_sends, extra=None):
    place = lax.axis_index("seq")
    barrier = pltpu.get_barrier_semaphore()
    for j in range(1, count if extra is None else 1):
        here = place - j if not later_sends else place + j

        @pl.when((here >= 0) & (here < count))
        def _():
            pl.semaphore_signal(barrier, inc=1, device_id={"seq": here}, device_id_type=MESH_ID)
    heads_axis = lax.axis_size("head")
    partner = lax.rem(lax.axis_index("head") + 1, heads_axis)
    pl.semaphore_signal(barrier, inc=1, device_id={"head": partner}, device_id_type=MESH_ID)
    waits = (place if later_sends else count - 1 - place) + 1
    if extra is not None:
        waits = extra() + 1
    pl.semaphore_wait(barrier, waits)
    return partner


VM = pl.BlockSpec(memory_space=pltpu.VMEM)
ANY = pl.BlockSpec(memory_space=pl.ANY)
DMA = pltpu.SemaphoreType.DMA
UNITS = 4


def add_rows(out, terms):
    rows = out.shape[0]
    size = min(64, rows)

    def one(i, carry):
        part = pl.ds(pl.multiple_of(i * size, size), size)
        total = terms[0][part, :].astype(f32)
        for term in terms[1:]:
            total = total + term[part, :].astype(f32)
        out[part, :] = total.astype(out.dtype)
        return carry
    lax.fori_loop(0, rows // size, one, 0)


def dp_spot():
    spot = lax.axis_index("dp")
    return lax.rem(spot, 2), spot // 2, lax.axis_size("dp") // 2


def greet_sums():
    barrier = pltpu.get_barrier_semaphore()
    core, group, others = dp_spot()
    count = lax.axis_size("seq")
    place = lax.axis_index("seq")
    targets = [{"dp": group * 2 + 1 - core}]
    targets += [{"dp": lax.rem(group + k, others) * 2 + core} for k in range(1, others)]
    targets += [{"seq": lax.rem(place + k, count)} for k in range(1, count)]
    for target in targets:
        pl.semaphore_signal(barrier, inc=1, device_id=target, device_id_type=MESH_ID)
    return len(targets)


class CrossSum:
    def __init__(self, ranges, buffers, sems):
        self.ranges = ranges
        self.own, self.first, self.second = buffers
        self.load_sem, self.first_send, self.first_recv, self.second_send, self.second_recv = sems
        self.core, self.group, self.others = dp_spot()
        self.loads, self.firsts, self.seconds = [], [], []

    def start(self):
        span = self.own.shape[2]
        for n, (grad, columns) in enumerate(self.ranges):
            self.firsts.append([])
            self.loads.append([])
            for g in range(self.others):
                theirs = pl.ds(pl.multiple_of((2 * g + 1 - self.core) * span, span), span)
                mine = pl.ds(pl.multiple_of((2 * g + self.core) * span, span), span)
                self.firsts[n].append(remote(
                    grad.at[theirs, columns], self.first.at[n, g], self.first_send.at[n, g],
                    self.first_recv.at[n, g], "dp", self.group * 2 + 1 - self.core))
                self.loads[n].append(pltpu.make_async_copy(
                    grad.at[mine, columns], self.own.at[n, g], self.load_sem.at[n, g]))
                self.firsts[n][g].start()
                self.loads[n][g].start()

    def step_a(self, n):
        for g in range(self.others):
            self.loads[n][g].wait()
            self.firsts[n][g].wait_recv()
        copies = []
        for k in range(1, self.others):
            peer = lax.rem(self.group + k, self.others)
            theirs = self.own.at[n, peer]
            add_rows(theirs, [theirs, self.first.at[n, peer]])
            copies.append(remote(
                theirs, self.second.at[n, k - 1], self.second_send.at[n, k - 1], self.second_recv.at[n, k - 1],
                "dp", peer * 2 + self.core))
            copies[-1].start()
        self.seconds.append(copies)

    def step_b(self, n, out):
        for copy in self.seconds[n]:
            copy.wait_recv()
        add_rows(out, [self.own.at[n, self.group], self.first.at[n, self.group]]
                 + [self.second.at[n, k] for k in range(self.others - 1)])

    def finish(self):
        for n in range(len(self.ranges)):
            for copy in self.firsts[n] + self.seconds[n]:
                copy.wait_send()


class LineSum:
    def __init__(self, pieces, received, send_sem, recv_sem):
        self.pieces = pieces
        self.received, self.send_sem, self.recv_sem = received, send_sem, recv_sem
        self.count = lax.axis_size("seq")
        self.place = lax.axis_index("seq")
        self.shard = received.shape[2]
        self.copies = [[] for _ in pieces]

    def rows(self, shard):
        return pl.ds(pl.multiple_of(shard * self.shard, self.shard), self.shard)

    def pass_on(self, n, bit):
        step = 2 ** bit
        side = lax.rem(lax.div(self.place, step), 2)
        target = self.place + step - 2 * step * side
        low = lax.rem(target, 2 * step)
        copies = []
        slot = self.count - self.count // step
        for m in range(self.count // (2 * step)):
            copies.append(remote(
                self.pieces[n].at[self.rows(low + 2 * step * m)], self.received.at[n, slot + m],
                self.send_sem.at[n, slot + m], self.recv_sem.at[n, slot + m], "seq", target))
            copies[-1].start()
        self.copies[n].append(copies)

    def take_in(self, n, bit):
        step = 2 ** bit
        low = lax.rem(self.place, 2 * step)
        slot = self.count - self.count // step
        for m, copy in enumerate(self.copies[n][bit]):
            copy.wait_recv()
            rows = self.pieces[n].at[self.rows(low + 2 * step * m)]
            if 2 * step == self.count:
                return [rows, self.received.at[n, slot + m]]
            add_rows(rows, [rows, self.received.at[n, slot + m]])

    def step_c(self, n):
        self.pass_on(n, 0)

    def step_d(self, n):
        bit = 1
        while 2 ** bit < self.count:
            self.take_in(n, bit - 1)
            self.pass_on(n, bit)
            bit += 1

    def step_e(self, n, write):
        write(n, self.take_in(n, len(self.copies[n]) - 1))

    def finish(self):
        for steps in self.copies:
            for copies in steps:
                for copy in copies:
                    copy.wait_send()


def cut_columns(refs):
    ranges = []
    for ref in refs:
        size = ref.shape[1] // UNITS
        ranges += [(ref, pl.ds(u * size, size)) for u in range(UNITS)]
    return ranges


def cross_scratch(ranges, span, columns):
    others = lax.axis_size("dp") // 2
    size = columns // UNITS
    peers = max(others - 1, 1)
    return [
        pltpu.VMEM((ranges, others, span, size), bf16), pltpu.VMEM((ranges, others, span, size), bf16),
        pltpu.VMEM((ranges, peers, span, size), bf16), DMA((ranges, others)), DMA((ranges, others)),
        DMA((ranges, others)), DMA((ranges, peers)), DMA((ranges, peers)),
    ]


def line_scratch(ranges, span, columns):
    count = lax.axis_size("seq")
    return [pltpu.VMEM((ranges, count - 1, span // count, columns // UNITS), bf16),
            DMA((ranges, count - 1)), DMA((ranges, count - 1))]


CROSS_REFS = 8
LINE_REFS = 3


def last_sum_kernel(widths, *refs):
    grads, half, done = refs[:2], refs[2], refs[3]
    kinds = len(widths[0]) + len(widths[1])
    outs = refs[4:4 + kinds]
    scratch = refs[4 + kinds:]
    partners = greet_sums()
    pl.semaphore_wait(pltpu.get_barrier_semaphore(), partners)
    halves, early_half = scratch[:2]
    for n, (_, columns) in enumerate(cut_columns([half])):
        early_half[n] = half[:, columns]
    early = LineSum([early_half.at[n] for n in range(UNITS)], *scratch[2:5])
    cross = CrossSum(cut_columns(grads), scratch[5:8], scratch[8:13])
    total = len(cross.ranges)
    line = LineSum([halves.at[n] for n in range(total)], *scratch[13:])
    cross.start()
    for n in range(UNITS):
        early.step_c(n)
    pieces = []
    which = 0
    for a in range(2):
        at = 0
        for width in widths[a]:
            if width < 0:
                pieces += [(a, at, -width, outs[which], 0), (a, at - width, -width, outs[which], 1)]
                at -= 2 * width
            else:
                pieces.append((a, at, width, outs[which], None))
                at += width
            which += 1

    def place_of(out, layer, side, columns):
        return out.at[layer, :, columns] if side is None else out.at[layer, :, side, columns]

    def write(layer, array, n, terms):
        size = terms[0].shape[1]
        begin = n % UNITS * size
        for a, at, width, out, side in pieces:
            low, high = max(at, begin), min(at + width, begin + size)
            if a == array and low < high:
                add_rows(place_of(out, layer, side, pl.ds(low - at, high - low)),
                         [term.at[:, pl.ds(low - begin, high - low)] for term in terms])

    def write_early(n, terms):
        write(1, 1, n, terms)

    def write_line(n, terms):
        write(0, n // UNITS, n, terms)
    for n in range(total):
        cross.step_a(n)
        if n < UNITS:
            early.step_d(n)
    for a, at, width, out, side in pieces:
        if a == 0:
            place_of(out, 1, side, pl.ds(0, width))[...] = done[:, at:at + width]
    for n in range(total + 2):
        if n < total:
            cross.step_b(n, halves.at[n])
            line.step_c(n)
        if 1 <= n <= total:
            line.step_d(n - 1)
        if n < UNITS:
            early.step_e(n, write_early)
        if n >= 2:
            line.step_e(n - 2, write_line)
    early.finish()
    cross.finish()
    line.finish()


def last_sum(grads, half, done, widths):
    columns = grads[0].shape[1]
    span = half.shape[0]
    shard = span // lax.axis_size("seq")
    total = 2 * UNITS
    return pl.pallas_call(
        functools.partial(last_sum_kernel, widths),
        out_shape=[jax.ShapeDtypeStruct((2, shard, width) if width > 0 else (2, shard, 2, -width), f32)
                   for width in widths[0] + widths[1]],
        in_specs=[ANY] * 2 + [VM] * 2,
        out_specs=[VM] * (len(widths[0]) + len(widths[1])),
        scratch_shapes=[pltpu.VMEM((total, span, columns // UNITS), bf16),
                        pltpu.VMEM((UNITS, span, columns // UNITS), bf16), *line_scratch(UNITS, span, columns),
                        *cross_scratch(total, span, columns), *line_scratch(total, span, columns)],
        compiler_params=pltpu.CompilerParams(
            vmem_limit_bytes=VMEM_LIMIT, collective_id=9, has_side_effects=True),
        cost_estimate=pl.CostEstimate(flops=0, bytes_accessed=400 * 1024 * 1024, transcendentals=0),
    )(*grads, half, done)


def unpack(pairs, out):
    def one(i, carry):
        rows = pl.ds(pl.multiple_of(i * 128, 128), 128)
        out[rows, :] = pairs[rows].reshape(128, out.shape[1])
        return carry
    lax.fori_loop(0, out.shape[0] // 128, one, 0)


def find_documents(seg_ref, dcol_ref, dloc_ref, drow_ref, column):
    place = lax.axis_index("seq")
    rows = dcol_ref.shape[0]
    drow_ref[...] = jnp.broadcast_to(seg_ref[...].astype(f32), drow_ref.shape)
    here = drow_ref[0:1, pl.ds(pl.multiple_of(place * rows, 128), rows)]
    dloc_ref[...] = jnp.broadcast_to(here, dloc_ref.shape)
    behind = drow_ref[0:1, pl.ds(pl.multiple_of(jnp.maximum(place * rows - 128, 0), 128), 128)]
    behind = jnp.where(place > 0, behind, -1.0)
    column[0:8, :] = jnp.transpose(jnp.broadcast_to(behind, (128, 128)))[120:, :]
    column[8:, :] = jnp.transpose(jnp.broadcast_to(here, (128, rows)))
    lane = lax.broadcasted_iota(jnp.int32, (rows, 128), 1)
    docs = column[8:, :]
    result = jnp.where(lane == 0, docs, 0.0)
    tests = [column[8 - k:8 - k + rows, :] for k in range(1, 4)] + [column[7:8, :], column[7 + rows:8 + rows, :]]
    for i, test in enumerate(tests):
        result = jnp.where(lane == i + 1, (docs == test).astype(f32), result)
    dcol_ref[...] = result


def layer_forward_kernel(heads, layer, layers, h_ref, gain_mix_ref, gain_ff_ref, wdt_ref,
                         taps_ref, heads_ref, *refs):
    refs = list(refs)
    seg_ref = refs.pop(0) if layer == 0 else None
    dcol_ref, dloc_ref, drow_ref = (None,) * 3 if layer == 0 else [refs.pop(0) for _ in range(3)]
    (wkv_hbm, wbc_hbm, zx_hbm, wq_hbm, wout_hbm, wo_hbm, gu_hbm, wdown_hbm) = refs[:8]
    refs = refs[8:]
    ready = layer > 0
    follows = layer + 1 < layers
    zx_ready = refs.pop(0) if ready else None
    (h_out, normed_ref, gate_ref, stack_ref, rim_ref, pre_ref, dt_ref, q_ref, kvall_ref,
     att_ref, lse_ref, mem_ref, gated_ref, middle_ref, nff_ref, gu_ref, inner_ref, gu_out) = refs[:18]
    refs = refs[18:]
    if not ready:
        dcol_ref, dloc_ref, drow_ref = [refs.pop(0) for _ in range(3)]
    zx_out = None if ready else refs.pop(0)
    zx_next = refs.pop(0) if follows else None
    column = refs.pop() if not ready else None
    (ext, y, wkv_ref, wbc_ref, wzx_ref, wq_ref, wo_ref, wout_ref, wgu_ref, wdown_ref, raw_zx, raw_gu,
     rim_in, kv_in, chain_in, chain_out, part_out, part_in, down_out, down_in,
     load_sem, kv_send, kv_recv, rim_send, rim_recv, chain_send, chain_recv,
     part_send, part_recv, down_send, down_recv) = refs
    rows = dt_ref.shape[0]
    d_local = gate_ref.shape[1]
    ff_local = inner_ref.shape[1]
    count = lax.axis_size("seq")
    place = lax.axis_index("seq")
    loads = {}
    plan = [("kv", wkv_hbm.at[layer], wkv_ref), ("bc", wbc_hbm.at[layer], wbc_ref)]
    plan.append(("zx", zx_ready, wzx_ref) if ready else ("zx", zx_hbm.at[layer], raw_zx))
    plan += [("q", wq_hbm.at[layer], wq_ref), ("out", wout_hbm.at[layer], wout_ref), ("o", wo_hbm.at[layer], wo_ref),
             ("gu", gu_hbm.at[layer], raw_gu), ("down", wdown_hbm.at[layer], wdown_ref)]
    later = [("gu_store", wgu_ref, gu_out)]
    if not ready:
        later.append(("zx_store", wzx_ref, zx_out))
    if follows:
        later += [("next", zx_hbm.at[layer + 1], raw_zx), ("next_store", wzx_ref, zx_next)]
    for name, src, dst in plan + later:
        loads[name] = pltpu.make_async_copy(src, dst, load_sem.at[len(loads)])
    for name, src, dst in plan:
        loads[name].start()
    partner = meet(count, False)

    if not ready:
        find_documents(seg_ref, dcol_ref, dloc_ref, drow_ref, column)
    normed_ref[...] = rms_scaled(h_ref[...].astype(f32), gain_mix_ref[...]).astype(bf16)
    normed = normed_ref[...]
    own = pl.ds(pl.multiple_of(place * rows, rows), rows)
    for j in range(count):
        @pl.when(j > place)
        def _():
            kv_in[j * rows:(j + 1) * rows, :] = jnp.zeros((rows, 2 * HD), bf16)
    loads["kv"].wait()
    kv_in[own, :] = nn(normed, wkv_ref[...]).astype(bf16)
    kv_copies = [
        remote(kv_in.at[own], kv_in.at[own], kv_send.at[j - 1], kv_recv.at[j - 1], "seq", place + j)
        for j in range(1, count)
    ]
    for j in range(1, count):
        @pl.when(place + j < count)
        def _():
            kv_copies[j - 1].start()
    loads["bc"].wait()
    stack_ref[:, d_local:] = nn(normed, wbc_ref[...]).astype(bf16)
    loads["zx"].wait()
    if not ready:
        unpack(raw_zx, wzx_ref)
        loads["zx_store"].start()
    if follows:
        loads["next"].start()
    stack_ref[:, :d_local] = nn(normed, wzx_ref[:, d_local:]).astype(bf16)
    rim_copy = remote(stack_ref.at[pl.ds(rows - RIM, RIM)], rim_in, rim_send, rim_recv, "seq", place + 1)

    @pl.when(place + 1 < count)
    def _():
        rim_copy.start()

    @pl.when(place == 0)
    def _():
        rim_in[...] = jnp.zeros(rim_in.shape, bf16)
        chain_in[...] = jnp.zeros(chain_in.shape, bf16)
    dt_ref[...] = nn(normed, wdt_ref[...]).astype(bf16).astype(f32)
    gate_ref[...] = nn(normed, wzx_ref[:, :d_local]).astype(bf16)
    loads["q"].wait()
    q_ref[...] = nn(normed, wq_ref[...]).astype(bf16)
    raw, step, log_decay, running, running_t, ordered = ssm_scalars(dt_ref, heads_ref)
    mapping = head_map(heads, d_local // heads)
    last = running[rows - 1:rows, :]
    fade = jnp.exp(last - running) * dcol_ref[:, 5:6]
    dec = jnp.exp(running) * dcol_ref[:, 4:5]
    ends = jnp.exp(running_t[:, rows - 1:rows]) * dcol_ref[rows - 1:rows, 4:5] + jnp.zeros((128, NS), f32)
    ends = spread_rows(ends, mapping)
    steps = spread(step, mapping)
    ext[RIM:, :] = stack_ref[...].astype(f32)

    @pl.when(place > 0)
    def _():
        rim_copy.wait_recv()
    rim_ref[...] = rim_in[...]
    ext[0:RIM, :] = rim_in[...].astype(f32)
    pre = ext[RIM:RIM + rows, :] * taps_ref[0:1, :]
    for k in range(1, 4):
        pre = pre + ext[RIM - k:RIM - k + rows, :] * dcol_ref[:, k:k + 1] * taps_ref[k:k + 1, :]
    pre_ref[...] = pre
    mixed = pre_ref[...] * sigmoid(pre_ref[...])
    values = mixed[:, :d_local]
    b_rows = mixed[:, d_local:d_local + NS].astype(bf16)
    c_rows = mixed[:, d_local + NS:].astype(bf16)
    stepped = values * steps
    state = tn((stepped * spread(fade, mapping)).astype(bf16), b_rows)
    y[...] = values * spread(heads_ref[2:3, :] + jnp.zeros((8, 128), f32), mapping)[0:1, :]
    linked = ordered & (dcol_ref[:, 0:1] == dloc_ref[0:1, :])
    cb = jnp.where(linked, nt(c_rows, b_rows), 0.0)
    stepped = stepped.astype(bf16)
    lane = lax.broadcasted_iota(jnp.int32, (rows, 128), 1)

    for j in range(1, count):
        @pl.when(place - j >= 0)
        def _():
            kv_copies[j - 1].wait_recv()
    allowed = score_mask(dcol_ref, drow_ref)
    keyvals = kv_in[...]
    kvall_ref[...] = keyvals
    keys, vals = keyvals[:, :HD], keyvals[:, HD:]
    totals = jnp.zeros((rows, 128), f32)
    pairs = heads // 2
    query_heads = q_ref.shape[1] // HD
    chain_copies = []
    for pair in range(pairs):
        span = slice(pair * 128, pair * 128 + 128)
        copy = remote(chain_out.at[pl.ds(pair * 128, 128)], chain_in.at[pl.ds(pair * 128, 128)],
                      chain_send.at[pair], chain_recv.at[pair], "seq", place + 1)
        chain_copies.append(copy)

        @pl.when(place > 0)
        def _():
            copy.wait_recv()
        chain_out[span, :] = (ends[span] * chain_in[span, :].astype(f32) + state[span]).astype(bf16)

        @pl.when(place + 1 < count)
        def _():
            copy.start()
        sides = []
        for h in (2 * pair, 2 * pair + 1):
            gap = running[:, h:h + 1] - running_t[h:h + 1, :]
            mixing = (jnp.exp(jnp.minimum(gap, 0.0)) * cb).astype(bf16)
            sides.append(nn(mixing, stepped[:, span]))
        y[:, span] += jnp.where(lane < 64, sides[0], sides[1])
        for h in range(query_heads * pair // pairs, query_heads * (pair + 1) // pairs):
            query = q_ref[:, h * HD:(h + 1) * HD] * jnp.asarray(HD ** -0.5, bf16)
            scores = jnp.where(allowed, nt(query, keys), masked_score)
            peak = jnp.max(scores, axis=1, keepdims=True)
            expo = jnp.exp(scores - peak)
            total = jnp.sum(expo, axis=1, keepdims=True)
            probs = (expo * (1.0 / total)).astype(bf16)
            att_ref[:, h * HD:(h + 1) * HD] = nn(probs, vals).astype(bf16)
            totals = jnp.where(lane == h, peak + jnp.log(total), totals)
    lse_ref[...] = totals
    mem_ref[...] = chain_in[...]
    decs = spread(dec, mapping)
    carried = decs * nt(c_rows, mem_ref[...])
    gate = gate_ref[...].astype(f32)
    gated_ref[...] = ((y[...] + carried) * (gate * sigmoid(gate))).astype(bf16)
    loads["out"].wait()
    loads["o"].wait()
    chunks = [pl.ds(begin, CHUNK) for begin in range(0, rows, CHUNK)]
    part_copies, down_copies = [], []
    for i, chunk in enumerate(chunks):
        part_out[chunk, :] = (nn(gated_ref[chunk, :], wout_ref[...])
                              + nn(att_ref[chunk, :], wo_ref[...])).astype(bf16)
        copy = remote(part_out.at[chunk], part_in.at[chunk], part_send.at[i], part_recv.at[i], "head", partner)
        copy.start()
        part_copies.append(copy)
    loads["gu"].wait()
    unpack(raw_gu, wgu_ref)
    loads["gu_store"].start()
    loads["down"].wait()
    for i, chunk in enumerate(chunks):
        part_copies[i].wait_recv()
        middle_ref[chunk, :] = h_ref[chunk, :].astype(f32) + (
            part_out[chunk, :].astype(f32) + part_in[chunk, :].astype(f32))
        nff_ref[chunk, :] = rms_scaled(middle_ref[chunk, :], gain_ff_ref[...]).astype(bf16)
        gu_ref[chunk, :] = nn(nff_ref[chunk, :], wgu_ref[...]).astype(bf16)
        gate = gu_ref[chunk, :ff_local].astype(f32)
        inner_ref[chunk, :] = (gate * sigmoid(gate) * gu_ref[chunk, ff_local:].astype(f32)).astype(bf16)
        down_out[chunk, :] = nn(inner_ref[chunk, :], wdown_ref[...]).astype(bf16)
        copy = remote(down_out.at[chunk], down_in.at[chunk], down_send.at[i], down_recv.at[i], "head", partner)
        copy.start()
        down_copies.append(copy)
    if not ready:
        loads["zx_store"].wait()
    if follows:
        loads["next"].wait()
        unpack(raw_zx, wzx_ref)
        loads["next_store"].start()
    for i, chunk in enumerate(chunks):
        down_copies[i].wait_recv()
        h_out[chunk, :] = (middle_ref[chunk, :] + (
            down_out[chunk, :].astype(f32) + down_in[chunk, :].astype(f32))).astype(bf16)
    loads["gu_store"].wait()
    if follows:
        loads["next_store"].wait()
    for i in range(len(chunks)):
        part_copies[i].wait_send()
        down_copies[i].wait_send()

    @pl.when(place + 1 < count)
    def _():
        rim_copy.wait_send()
        for copy in chain_copies:
            copy.wait_send()
    for j in range(1, count):
        @pl.when(place + j < count)
        def _():
            kv_copies[j - 1].wait_send()


def layer_forward(layer, hidden, zx, w, context):
    rows, model_width = hidden.shape
    heads = w["heads"]
    layers = w["out"].shape[0]
    d_local = w["out"].shape[1]
    ff_local = w["down"].shape[1]
    q_width = w["q"].shape[2]
    width = d_local + 2 * NS
    count = lax.axis_size("seq")
    length = count * rows
    parts = rows // CHUNK
    wide = ((model_width, 2 * d_local), bf16)
    outs = [
        ((rows, model_width), bf16), ((rows, model_width), bf16), ((rows, d_local), bf16), ((rows, width), bf16),
        ((RIM, width), bf16), ((rows, width), f32), ((rows, 128), f32), ((rows, q_width), bf16),
        ((length, 2 * HD), bf16), ((rows, q_width), bf16), ((rows, 128), f32), ((d_local, NS), bf16),
        ((rows, d_local), bf16), ((rows, model_width), f32), ((rows, model_width), bf16),
        ((rows, 2 * ff_local), bf16), ((rows, ff_local), bf16), ((model_width, 2 * ff_local), bf16),
    ]
    kept = len(outs) - 1
    documents = [((rows, 128), f32), ((8, rows), f32), ((8, length), f32)] if layer == 0 else []
    outs += documents
    outs += [wide] * ((layer == 0) + (layer + 1 < layers))
    full = (rows, model_width)
    given = [] if layer == 0 else [zx]
    result = pl.pallas_call(
        functools.partial(layer_forward_kernel, heads, layer, layers),
        out_shape=[jax.ShapeDtypeStruct(shape, kind) for shape, kind in outs],
        in_specs=[VM] * (6 + len(context)) + [ANY] * (8 + len(given)),
        out_specs=[VM] * kept + [ANY] + [VM] * len(documents) + [ANY] * (len(outs) - kept - 1 - len(documents)),
        scratch_shapes=[
            pltpu.VMEM((rows + RIM, width), f32), pltpu.VMEM((rows, d_local), f32),
            pltpu.VMEM((model_width, 2 * HD), bf16), pltpu.VMEM((model_width, 2 * NS), bf16),
            pltpu.VMEM((model_width, 2 * d_local), bf16), pltpu.VMEM((model_width, q_width), bf16),
            pltpu.VMEM((q_width, model_width), bf16), pltpu.VMEM((d_local, model_width), bf16),
            pltpu.VMEM((model_width, 2 * ff_local), bf16), pltpu.VMEM((ff_local, model_width), bf16),
            pltpu.VMEM((model_width, 2, d_local), bf16), pltpu.VMEM((model_width, 2, ff_local), bf16),
            pltpu.VMEM((RIM, width), bf16), pltpu.VMEM((length, 2 * HD), bf16),
            pltpu.VMEM((d_local, NS), bf16), pltpu.VMEM((d_local, NS), bf16),
            pltpu.VMEM(full, bf16), pltpu.VMEM(full, bf16), pltpu.VMEM(full, bf16), pltpu.VMEM(full, bf16),
            DMA((12,)), DMA((count - 1,)), DMA((count - 1,)), DMA, DMA, DMA((heads // 2,)), DMA((heads // 2,)),
            DMA((parts,)), DMA((parts,)), DMA((parts,)), DMA((parts,)),
            *([pltpu.VMEM((rows + 8, 128), f32)] if layer == 0 else []),
        ],
        compiler_params=pltpu.CompilerParams(
            vmem_limit_bytes=VMEM_LIMIT, collective_id=layer, has_side_effects=True),
    )(hidden, w["gain_mix"][layer], w["gain_ff"][layer], w["dt"][layer], w["taps"][layer], w["head_vals"][layer],
      *context, w["kv"], w["bc"], w["zx"], w["q"], w["out"], w["o"], w["gu"], w["down"], *given)
    names = ("out", "normed", "gate", "stack", "rim", "pre", "dt", "q", "kv", "att", "lse", "memory",
             "gated", "middle", "nff", "gu", "inner", "w_gu")
    saved = dict(zip(names, result))
    saved["hidden"] = hidden
    extra = list(result[len(names):])
    if layer == 0:
        context = [extra.pop(0) for _ in range(3)]
    saved["w_zx"] = extra.pop(0) if layer == 0 else zx
    return saved.pop("out"), (extra.pop(0) if extra else None), context, saved


def norm_back(hidden, gain, grad):
    inverse = lax.rsqrt(jnp.mean(hidden * hidden, axis=-1, keepdims=True) + norm_eps)
    scaled = grad * gain
    lean = jnp.mean(scaled * hidden, axis=-1, keepdims=True)
    grad_gain = jnp.sum(grad * hidden * inverse, axis=0, keepdims=True)
    return inverse * (scaled - hidden * (inverse * inverse * lean)), grad_gain


def store_blocks(compute, slots, out, sems):
    size = slots.shape[1]
    columns = out.shape[1]
    blocks = out.shape[0] // size

    def rows(i):
        return pl.ds(pl.multiple_of(i * size, size), size)

    def copy(i, slot):
        return pltpu.make_async_copy(slots.at[slot, :, pl.ds(0, columns)], out.at[rows(i)], sems.at[slot])

    def one(i, carry):
        slot = lax.rem(i, 2)

        @pl.when(i >= 2)
        def _():
            copy(i - 2, slot).wait()
        compute(rows(i), slot)
        copy(i, slot).start()
        return carry
    lax.fori_loop(0, blocks, one, 0)
    for i in range(max(0, blocks - 2), blocks):
        copy(i, i % 2).wait()


def layer_backward_kernel(heads, layer, schedule, grad_ref, h_ref, normed_ref, gate_ref, stack_ref, rim_ref, pre_ref, dt_ref,
                          q_ref, kv_ref, att_ref, lse_ref, mem_ref, gated_ref, middle_ref, nff_ref, gu_ref,
                          inner_ref, gain_mix_ref, gain_ff_ref, wdt_ref,
                          taps_ref, heads_ref, dcol_ref, dloc_ref, drow_ref,
                          wdown_hbm, wgu_hbm, wout_hbm, wo_hbm, wzx_hbm, wbc_hbm, wq_hbm, wkv_hbm, *refs):
    refs = list(refs)
    own_sum = schedule["own"]
    source = None if own_sum else refs.pop(0)
    half_in = None if own_sum else refs.pop(0)
    if not own_sum:
        line_refs, refs = refs[-LINE_REFS - 1:], refs[:-LINE_REFS - 1]
    cross_refs, refs = refs[-CROSS_REFS:], refs[:-CROSS_REFS]
    summed_ref = None if own_sum else refs.pop(0)
    (g_out, gff_out, gmix_out, gbc_out, small_ref, half_ref,
     wdown_ref, wide_ref, wout_ref, wo_ref, wbc_ref, wq_ref, wkv_ref,
     gff, dgu, one_out, one_in, two_out, two_in, gmid, branch, gg, datt, dy_s, dxs_s, u_s,
     decay_s, probs_s, acc, dkv_out, dkv_in, chain_in, chain_out, rim_in,
     ext, pad, dext, dgate, dstack, dq, dkv, draw_s,
     load_sem, one_send, one_recv, two_send, two_recv, chain_send, chain_recv,
     rim_send, rim_recv, kv_send, kv_recv, gblk, grad_sem) = refs
    rows = dt_ref.shape[0]
    d_local = gate_ref.shape[1]
    ff_local = inner_ref.shape[1]
    q_width = q_ref.shape[1]
    model_width = h_ref.shape[1]
    width = pre_ref.shape[1]
    length = kv_ref.shape[0]
    count = lax.axis_size("seq")
    place = lax.axis_index("seq")
    wgu_ref = wide_ref.at[:, pl.ds(0, 2 * ff_local)]
    wzx_ref = wide_ref.at[:, pl.ds(0, 2 * d_local)]
    loads = {}
    for name, src, dst in (
        ("down", wdown_hbm.at[layer], wdown_ref), ("gu", wgu_hbm, wgu_ref), ("out", wout_hbm.at[layer], wout_ref),
        ("o", wo_hbm.at[layer], wo_ref), ("bc", wbc_hbm.at[layer], wbc_ref), ("q", wq_hbm.at[layer], wq_ref),
        ("kv", wkv_hbm.at[layer], wkv_ref), ("zx", wzx_hbm, wzx_ref),
    ):
        loads[name] = pltpu.make_async_copy(src, dst, load_sem.at[len(loads)])
    for name in ("down", "gu", "out", "o", "bc", "q", "kv"):
        loads[name].start()
    partner = meet(count, True, greet_sums)
    cross = CrossSum(cut_columns([gff_out if own_sum else source]), cross_refs[:3], cross_refs[3:])
    ranges = [columns for _, columns in cut_columns([half_ref])]
    steps_of = {"a": cross.step_a, "b": lambda n: cross.step_b(n, half_ref.at[:, ranges[n]])}
    if not own_sum:
        fetches = [pltpu.make_async_copy(half_in.at[:, columns], line_refs[0].at[n], load_sem.at[len(loads) + n])
                   for n, (_, columns) in enumerate(cut_columns([half_in]))]
        for fetch in fetches:
            fetch.start()
        for fetch in fetches:
            fetch.wait()
        line = LineSum([line_refs[0].at[n] for n in range(UNITS)], *line_refs[1:])

        def write(n, terms):
            size = terms[0].shape[1]
            add_rows(summed_ref.at[:, pl.ds(n * size, size)], terms)
        steps_of.update({"c": line.step_c, "d": line.step_d, "e": lambda n: line.step_e(n, write)})

    def pump(spot):
        for step in schedule.get(spot, ()):
            if step == "start":
                cross.start()
            elif step == "finish":
                cross.finish()
                if not own_sum:
                    line.finish()
            else:
                steps_of[step[0]](int(step[1]))
    pump("begin")
    chunks = [pl.ds(begin, CHUNK) for begin in range(0, rows, CHUNK)]

    gff[...] = grad_ref[...].astype(bf16)
    loads["down"].wait()
    loads["gu"].wait()
    one_copies, two_copies = [], []
    for i, chunk in enumerate(chunks):
        grad_inner = nt(gff[chunk, :], wdown_ref[...])
        gate = gu_ref[chunk, :ff_local].astype(f32)
        up = gu_ref[chunk, ff_local:].astype(f32)
        sig = sigmoid(gate)
        dgu[chunk, :ff_local] = (grad_inner * up * (sig * (1.0 + gate * (1.0 - sig)))).astype(bf16)
        dgu[chunk, ff_local:] = (grad_inner * (gate * sig)).astype(bf16)
        one_out[chunk, :] = nt(dgu[chunk, :], wgu_ref[...]).astype(bf16)
        copy = remote(one_out.at[chunk], one_in.at[chunk], one_send.at[i], one_recv.at[i], "head", partner)
        copy.start()
        one_copies.append(copy)
    loads["zx"].start()

    @pl.when(place == count - 1)
    def _():
        rim_in[...] = jnp.zeros(rim_in.shape, f32)
        chain_in[...] = jnp.zeros(chain_in.shape, bf16)
    for j in range(1, count):
        @pl.when(place + j >= count)
        def _():
            dkv_in[(j - 1) * rows:j * rows, :] = jnp.zeros((rows, 2 * HD), bf16)

    pump("ff0")

    def ff_weights(block, slot):
        gblk[slot, :, :ff_local] = tn(gff[:, block], inner_ref[...]).astype(bf16)
        gblk[slot, :, ff_local:3 * ff_local] = tn(nff_ref[:, block], dgu[...]).astype(bf16)
    store_blocks(ff_weights, gblk, gff_out, grad_sem)
    pump("ff")

    raw, step, log_decay, running, running_t, ordered = ssm_scalars(dt_ref, heads_ref)
    mapping = head_map(heads, d_local // heads)
    last = running[rows - 1:rows, :]
    fade = spread(jnp.exp(last - running) * dcol_ref[:, 5:6], mapping)
    dec = jnp.exp(running) * dcol_ref[:, 4:5]
    decs = spread(dec, mapping)
    ends = jnp.exp(running_t[:, rows - 1:rows]) * dcol_ref[rows - 1:rows, 4:5] + jnp.zeros((128, NS), f32)
    ends = spread_rows(ends, mapping)
    steps = spread(step, mapping)
    skip = spread(heads_ref[2:3, :] + jnp.zeros((8, 128), f32), mapping)[0:1, :]
    pre_v = pre_ref[:, :d_local]
    values = pre_v * sigmoid(pre_v)
    pre_n = pre_ref[:, d_local:]
    maps = (pre_n * sigmoid(pre_n)).astype(bf16)
    b_rows, c_rows = maps[:, :NS], maps[:, NS:]
    stepped = (values * steps).astype(bf16)
    linked = ordered & (dcol_ref[:, 0:1] == dloc_ref[0:1, :])
    cb = jnp.where(linked, nt(c_rows, b_rows), 0.0)
    lane = lax.broadcasted_iota(jnp.int32, (rows, 128), 1)
    pairs = heads // 2
    for pair in range(pairs):
        span = slice(pair * 128, pair * 128 + 128)
        sides = []
        for h in (2 * pair, 2 * pair + 1):
            at = slice(h * rows, (h + 1) * rows)
            gap = running[:, h:h + 1] - running_t[h:h + 1, :]
            decay = jnp.exp(jnp.minimum(gap, 0.0))
            decay_s[:, at] = decay.astype(bf16)
            mixing = (decay_s[:, at].astype(f32) * cb).astype(bf16)
            sides.append(nn(mixing, stepped[:, span]))
        u_s[:, span] = jnp.where(lane < 64, sides[0], sides[1])
    allowed = score_mask(dcol_ref, drow_ref)
    keyvals = kv_ref[...]
    keys, vals = keyvals[:, :HD], keyvals[:, HD:]
    scale = jnp.asarray(HD ** -0.5, bf16)
    query_heads = q_width // HD
    for h in range(query_heads):
        query = q_ref[:, h * HD:(h + 1) * HD] * scale
        scores = jnp.where(allowed, nt(query, keys), masked_score)
        probs_s[:, h * length:(h + 1) * length] = jnp.exp(scores - lse_ref[:, h:h + 1]).astype(bf16)
    ext[0:RIM, :] = rim_ref[...].astype(f32)
    ext[RIM:, :] = stack_ref[...].astype(f32)
    gate = gate_ref[...].astype(f32)
    gate_sig = sigmoid(gate)
    gate_act = gate * gate_sig
    loads["out"].wait()
    loads["o"].wait()
    dtaps_ref = small_ref.at[pl.ds(0, 8)]
    gains_ref = small_ref.at[pl.ds(8, 8)]
    dheads_ref = small_ref.at[pl.ds(16, 8)]
    gains_ref[...] = jnp.zeros(gains_ref.shape, f32)
    for i, chunk in enumerate(chunks):
        pump("one%d" % i)
        one_copies[i].wait_recv()
        grad = one_out[chunk, :].astype(f32) + one_in[chunk, :].astype(f32)
        moved, gain = norm_back(middle_ref[chunk, :], gain_ff_ref[...], grad)
        gains_ref[1:2, :] += gain
        gmid[chunk, :] = grad_ref[chunk, :].astype(f32) + moved
        branch[chunk, :] = gmid[chunk, :].astype(bf16)
        gg[chunk, :] = nt(branch[chunk, :], wout_ref[...])
        datt[chunk, :] = nt(branch[chunk, :], wo_ref[...]).astype(bf16)
    grad_ssm = gg[...] * gate_act
    dy_s[...] = grad_ssm.astype(bf16)
    push = tn((grad_ssm * decs).astype(bf16), c_rows)
    dcb = jnp.zeros((rows, rows), f32)
    chain_copies = []
    for pair in range(pairs):
        pump("pair%d" % pair)
        span = slice(pair * 128, pair * 128 + 128)
        copy = remote(chain_out.at[pl.ds(pair * 128, 128)], chain_in.at[pl.ds(pair * 128, 128)],
                      chain_send.at[pair], chain_recv.at[pair], "seq", place - 1)
        chain_copies.append(copy)

        @pl.when(place < count - 1)
        def _():
            copy.wait_recv()
        chain_out[span, :] = (ends[span] * chain_in[span, :].astype(f32) + push[span]).astype(bf16)

        @pl.when(place > 0)
        def _():
            copy.start()
        stepped_p = stepped[:, span]
        dy_p = dy_s[:, span]
        dxs = []
        for side, h in enumerate((2 * pair, 2 * pair + 1)):
            at = slice(h * rows, (h + 1) * rows)
            decay = decay_s[:, at].astype(f32)
            dxs.append(tn((decay * cb).astype(bf16), dy_p))
            half = jnp.where((lane < 64) == (side == 0), dy_p, jnp.zeros_like(dy_p))
            dcb = dcb + nt(half, stepped_p) * decay
        dxs_s[:, span] = jnp.where(lane < 64, dxs[0], dxs[1])
        for h in range(query_heads * pair // pairs, query_heads * (pair + 1) // pairs):
            part = slice(h * HD, (h + 1) * HD)
            query = q_ref[:, part] * scale
            grad = datt[:, part]
            delta = jnp.sum(grad.astype(f32) * att_ref[:, part].astype(f32), axis=1, keepdims=True)
            probs = probs_s[:, h * length:(h + 1) * length]
            grad_scores = (probs.astype(f32) * (nt(grad, vals) - delta)).astype(bf16)
            dq[:, part] = (nn(grad_scores, keys) * HD ** -0.5).astype(bf16)
            dk = tn(grad_scores, query)
            dv = tn(probs, grad)
            if h == 0:
                acc[:, :HD] = dk
                acc[:, HD:] = dv
            else:
                acc[:, :HD] += dk
                acc[:, HD:] += dv
    dkv_out[...] = acc[...].astype(bf16)
    kv_copies = []
    for j in range(1, count):
        target = jnp.maximum(place - j, 0)
        theirs = pl.ds(pl.multiple_of(target * rows, rows), rows)
        copy = remote(dkv_out.at[theirs], dkv_in.at[pl.ds((j - 1) * rows, rows)], kv_send.at[j - 1],
                      kv_recv.at[j - 1], "seq", place - j)
        kv_copies.append(copy)

        @pl.when(place >= j)
        def _():
            copy.start()
    pump("post")
    memory = mem_ref[...]
    gmem = chain_in[...]
    carried = decs * nt(c_rows, memory)
    back = fade * nt(b_rows, gmem)
    dy_low = dy_s[...].astype(f32)
    stepped_f = stepped.astype(f32)
    dxs_all = dxs_s[...] + back
    dxs_s[...] = dxs_all
    dcb = jnp.where(linked, dcb, 0.0).astype(bf16)
    dc = nn(dcb, b_rows) + nn((dy_low * decs).astype(bf16), memory)
    db = tn(dcb, c_rows) + nn((stepped_f * fade).astype(bf16), gmem)
    dvalues = steps * dxs_all + skip * grad_ssm
    pad[0:8, :] = jnp.zeros((8, width), f32)
    pad[8 + rows:, :] = jnp.zeros((8, width), f32)
    sig = sigmoid(pre_v)
    pad[8:8 + rows, :d_local] = dvalues * (sig * (1.0 + pre_v * (1.0 - sig)))
    sig = sigmoid(pre_n)
    slope = sig * (1.0 + pre_n * (1.0 - sig))
    pad[8:8 + rows, d_local:d_local + NS] = db * slope[:, :NS]
    pad[8:8 + rows, d_local + NS:] = dc * slope[:, NS:]
    dpre = pad[8:8 + rows, :]
    dext[...] = pad[0:8 + rows, :] * taps_ref[0:1, :]
    dtaps_ref[...] = jnp.zeros((8, width), f32)
    dtaps_ref[0:1, :] = jnp.sum(dpre * ext[RIM:RIM + rows, :], axis=0, keepdims=True)
    for k in range(1, 4):
        masked = dpre * dcol_ref[:, k:k + 1]
        pad[8:8 + rows, :] = masked
        dtaps_ref[k:k + 1, :] = jnp.sum(masked * ext[RIM - k:RIM - k + rows, :], axis=0, keepdims=True)
        dext[...] += pad[k:k + 8 + rows, :] * taps_ref[k:k + 1, :]
    rim_copy = remote(dext.at[pl.ds(0, 8)], rim_in, rim_send, rim_recv, "seq", place - 1)

    @pl.when(place > 0)
    def _():
        rim_copy.start()
    scanned = u_s[...] + carried
    drun = gather(dy_low * scanned - stepped_f * dxs_all, mapping)
    ssm_out = scanned + skip * values
    dgate[...] = (gg[...] * ssm_out * (gate_sig * (1.0 + gate * (1.0 - gate_sig)))).astype(bf16)
    gstep = gather(values * dxs_all, mapping)
    ones = jnp.ones((8, 128), bf16)
    high, low = split(gmem.astype(f32) * memory.astype(f32), 2)
    moved = nt(ones, high) + nt(ones, low)
    end = gather(jnp.sum(stepped_f * back, axis=0, keepdims=True) + jnp.zeros((8, 1), f32), mapping)
    end = end + gather(moved, mapping) * dec[rows - 1:rows, :]
    upper = (lax.broadcasted_iota(jnp.int32, (rows, rows), 1)
             >= lax.broadcasted_iota(jnp.int32, (rows, rows), 0)).astype(bf16)
    dlog = triangle_sum(upper, drun) + end[0:1, :]
    draw = (gstep - jnp.exp(heads_ref[1:2, :]) * dlog) * sigmoid(raw)
    draw_s[...] = draw.astype(bf16)
    dskip = gather(jnp.sum(grad_ssm * values, axis=0, keepdims=True) + jnp.zeros((8, 1), f32), mapping)
    dheads_ref[...] = jnp.zeros(dheads_ref.shape, f32)
    dheads_ref[0:1, :128] = jnp.sum(draw, axis=0, keepdims=True)
    dheads_ref[1:2, :128] = jnp.sum(dlog * log_decay, axis=0, keepdims=True)
    dheads_ref[2:3, :128] = dskip[0:1, :]
    for name in ("zx", "bc", "q", "kv"):
        loads[name].wait()

    for j in range(1, count):
        @pl.when(place + j < count)
        def _():
            kv_copies[j - 1].wait_recv()
    pump("two")
    own = pl.ds(pl.multiple_of(place * rows, rows), rows)
    total = acc[own, :]
    for j in range(1, count):
        total = total + dkv_in[(j - 1) * rows:j * rows, :].astype(f32)
    dkv[...] = total.astype(bf16)

    for i, chunk in enumerate(chunks):
        if i == len(chunks) - 1:
            @pl.when(place < count - 1)
            def _():
                rim_copy.wait_recv()
            dext[rows:rows + 8, :] += rim_in[...]
        dstack[chunk, :] = dext[8 + i * CHUNK:8 + (i + 1) * CHUNK, :].astype(bf16)
        two_out[chunk, :] = (
            nt(dgate[chunk, :], wzx_ref[:, :d_local]) + nt(dstack[chunk, :d_local], wzx_ref[:, d_local:])
            + nt(dstack[chunk, d_local:], wbc_ref[...]) + nt(draw_s[chunk, :], wdt_ref[...])
            + nt(dq[chunk, :], wq_ref[...]) + nt(dkv[chunk, :], wkv_ref[...])
        ).astype(bf16)
        copy = remote(two_out.at[chunk], two_in.at[chunk], two_send.at[i], two_recv.at[i], "head", partner)
        copy.start()
        two_copies.append(copy)

    gbc_out[:, model_width:] = jnp.transpose(jnp.concatenate(
        [dtaps_ref[:, d_local:], jnp.zeros((120, 2 * NS), f32)], axis=0)).astype(bf16)
    pump("mix")

    def mix_weights(block, slot):
        left = normed_ref[:, block]
        at = 0
        for right in (dgate[...], dstack[:, :d_local], dq[...], dkv[...], draw_s[...]):
            gblk[slot, :, at:at + right.shape[1]] = tn(left, right).astype(bf16)
            at += right.shape[1]
        left = branch[:, block]
        for right in (gated_ref[...], att_ref[...]):
            gblk[slot, :, at:at + right.shape[1]] = tn(left, right).astype(bf16)
            at += right.shape[1]
        gbc_out[:, block] = tn(dstack[:, d_local:], normed_ref[:, block]).astype(bf16)
    store_blocks(mix_weights, gblk, gmix_out, grad_sem)

    for i, chunk in enumerate(chunks):
        pump("last%d" % i)
        two_copies[i].wait_recv()
        grad = two_out[chunk, :].astype(f32) + two_in[chunk, :].astype(f32)
        moved, gain = norm_back(h_ref[chunk, :].astype(f32), gain_mix_ref[...], grad)
        gains_ref[0:1, :] += gain
        g_out[chunk, :] = gmid[chunk, :] + moved
    pump("end")
    for i in range(len(chunks)):
        one_copies[i].wait_send()
        two_copies[i].wait_send()

    @pl.when(place > 0)
    def _():
        rim_copy.wait_send()
        for copy in chain_copies:
            copy.wait_send()
    for j in range(1, count):
        @pl.when(place >= j)
        def _():
            kv_copies[j - 1].wait_send()


SCHEDULES = (
    {"own": False, "begin": ("start", "c0", "c1", "c2", "c3"), "ff0": ("a0", "a1", "a2", "a3"), "ff": ("d0", "d1"),
     "one0": ("d2",), "one1": ("d3",), "mix": ("b0", "b1"), "last0": ("e0", "e1", "e2", "e3", "b2"),
     "end": ("b3", "finish")},
    {"own": True, "ff": ("start",), "one0": ("a0", "a1"), "one1": ("a2", "a3"), "mix": ("b0",), "last0": ("b1", "b2"),
     "end": ("b3", "finish")},
)


def layer_backward(layer, grad, waiting, w, saved, context):
    dcol, dloc, drow = context
    rows, model_width = grad.shape
    heads = w["heads"]
    d_local = w["out"].shape[1]
    ff_local = w["down"].shape[1]
    q_width = w["q"].shape[2]
    width = d_local + 2 * NS
    count = lax.axis_size("seq")
    length = count * rows
    parts = rows // CHUNK
    mix_width = 3 * d_local + 2 * q_width + 256
    schedule = SCHEDULES[1 if waiting is None else 0]
    given = [] if waiting is None else list(waiting)
    outs = [
        ((rows, model_width), f32), ((model_width, 3 * ff_local), bf16), ((model_width, mix_width), bf16),
        ((2 * NS, model_width + 128), bf16), ((24, max(width, model_width)), f32),
    ]
    span = model_width // lax.axis_size("dp")
    if waiting is not None:
        outs.insert(0, ((span // count, 3 * ff_local), f32))
    outs.append(((span, 3 * ff_local if waiting is None else mix_width), bf16))
    full = (rows, model_width)
    state = (d_local, NS)
    names = ("hidden", "normed", "gate", "stack", "rim", "pre", "dt", "q", "kv", "att", "lse", "memory",
             "gated", "middle", "nff", "gu", "inner")

    def vm(shape, kind):
        return pltpu.VMEM(shape, kind)
    return pl.pallas_call(
        functools.partial(layer_backward_kernel, heads, layer, schedule),
        out_shape=[jax.ShapeDtypeStruct(shape, kind) for shape, kind in outs],
        in_specs=[VM] * 26 + [ANY] * (8 + len(given)),
        out_specs=[VM] * (len(outs) - 5) + [ANY, ANY] + [VM] * 3,
        scratch_shapes=[
            vm((ff_local, model_width), bf16), vm((model_width, 2 * max(d_local, ff_local)), bf16),
            vm((d_local, model_width), bf16), vm((q_width, model_width), bf16), vm((model_width, 2 * NS), bf16),
            vm((model_width, q_width), bf16), vm((model_width, 2 * HD), bf16),
            vm(full, bf16), vm((rows, 2 * ff_local), bf16), vm(full, bf16), vm(full, bf16), vm(full, bf16),
            vm(full, bf16), vm(full, f32), vm(full, bf16), vm((rows, d_local), f32), vm((rows, q_width), bf16),
            vm((rows, d_local), bf16), vm((rows, d_local), f32), vm((rows, d_local), f32),
            vm((rows, heads * rows), bf16),
            vm((rows, q_width // HD * length), bf16), vm((length, 2 * HD), f32), vm((length, 2 * HD), bf16),
            vm(((count - 1) * rows, 2 * HD), bf16), vm(state, bf16), vm(state, bf16), vm((8, width), f32),
            vm((rows + RIM, width), f32), vm((rows + 16, width), f32), vm((rows + 8, width), f32),
            vm((rows, d_local), bf16), vm((rows, width), bf16), vm((rows, q_width), bf16),
            vm((rows, 2 * HD), bf16), vm((rows, 128), bf16),
            DMA((8 + UNITS,)), DMA((parts,)), DMA((parts,)), DMA((parts,)), DMA((parts,)), DMA((heads // 2,)),
            DMA((heads // 2,)), DMA, DMA, DMA((count - 1,)), DMA((count - 1,)),
            vm((2, 128, max(3 * ff_local, mix_width)), bf16), DMA((2,)),
            *cross_scratch(UNITS, span, outs[-1][0][1]),
            *([] if waiting is None else
              [vm((UNITS, span, 3 * ff_local // UNITS), bf16), *line_scratch(UNITS, span, 3 * ff_local)]),
        ],
        compiler_params=pltpu.CompilerParams(
            vmem_limit_bytes=VMEM_LIMIT, collective_id=2 + layer, has_side_effects=True),
    )(grad, *[saved[name] for name in names], w["gain_mix"][layer], w["gain_ff"][layer], w["dt"][layer],
      w["taps"][layer], w["head_vals"][layer], dcol, dloc, drow, w["down"], saved["w_gu"], w["out"], w["o"],
      saved["w_zx"], w["bc"], w["q"], w["kv"], *given)


def on_device(hidden_in, segment_ids, gain_mix, w_zx, w_bc, w_dt, conv_x, conv_bc, ssm_head, w_q, w_kv,
              w_o, w_out, gain_ff, w_gu, w_down, cotangent):
    rows, model_width = hidden_in.shape
    taps_count = conv_x.shape[1]
    place = lax.axis_index("seq")
    context = (segment_ids,)
    layers = gain_mix.shape[0]
    heads = ssm_head.shape[2]
    d_local = w_zx.shape[3]
    w = dict(
        heads=heads,
        gain_mix=gain_mix[:, None].astype(f32),
        gain_ff=gain_ff[:, None].astype(f32),
        zx=w_zx,
        bc=w_bc,
        dt=jnp.pad(w_dt, ((0, 0), (0, 0), (0, 128 - heads))),
        q=w_q,
        kv=w_kv.reshape(layers, model_width, -1),
        o=w_o,
        out=w_out,
        gu=w_gu,
        down=w_down,
        taps=jnp.pad(jnp.concatenate([conv_x.reshape(layers, taps_count, -1), conv_bc], axis=2).astype(f32),
                     ((0, 0), (0, 8 - taps_count), (0, 0))),
        head_vals=jnp.pad(ssm_head, ((0, 0), (0, 5), (0, 128 - heads))),
    )
    hidden = hidden_in
    saved = []
    zx = None
    for l in range(layers):
        hidden, zx, context, kept = layer_forward(l, hidden, zx, w, context)
        saved.append(kept)
    block_out = hidden
    gradient = cotangent
    narrow, small = [None] * layers, [None] * layers
    waiting = None
    for l in reversed(range(layers)):
        *summed, gradient, ff_grads, mix_grads, narrow[l], small[l], half = layer_backward(
            l, gradient, waiting, w, saved[l], context)
        waiting = (mix_grads, half)
    g_bc = lax.psum_scatter(jnp.concatenate(narrow, axis=1), ("dp", "seq", "head"), scatter_dimension=0, tiled=True)
    small = [lax.psum(a, ("dp", "seq")) for a in small]
    shards = lax.axis_size("dp") * lax.axis_size("seq")
    shard = lax.axis_index("dp") * lax.axis_size("seq") + place
    ff_local = w_down.shape[1]
    q_width = w_q.shape[2]
    part = model_width // shards
    down, gu, zx, q, kv, dt, out, o = last_sum(
        (ff_grads, mix_grads), half, summed[0],
        ((ff_local, -ff_local), (-d_local, q_width, 128, 128, d_local, q_width)))
    down, out, o = (jnp.transpose(a, (0, 2, 1)) for a in (down, out, o))
    kv = kv.reshape(layers, part, 1, 128)
    dt = dt[:, :, :heads]
    g_bc = g_bc.astype(f32).reshape(g_bc.shape[0], layers, -1)
    w_bc_grad = jnp.transpose(g_bc[:, :, :model_width], (1, 2, 0))
    conv_bc_grad = jnp.transpose(g_bc[:, :, model_width:model_width + taps_count], (1, 2, 0))
    small = jnp.stack(small, axis=0)
    gain_a = lax.dynamic_slice_in_dim(small[:, 8, :model_width], shard * part, part, 1)
    gain_b = lax.dynamic_slice_in_dim(small[:, 9, :model_width], shard * part, part, 1)
    taps = small[:, :taps_count, :d_local].reshape(layers, taps_count, heads, -1)
    taps_part = taps.shape[3] // shards
    conv_x_grad = lax.dynamic_slice_in_dim(taps, shard * taps_part, taps_part, 3)
    head_grad = small[:, 16:19, :heads]
    return (block_out, gradient, gain_a, zx, w_bc_grad, dt, conv_x_grad, conv_bc_grad, head_grad, q, kv,
            o, out, gain_b, gu, down)


def solution(mesh):
    in_specs = (
        P(("dp", "seq"), None),
        P("dp", None),
        P(),
        P(None, None, None, "head"),
        P(),
        P(None, None, "head"),
        P(None, None, "head", None),
        P(),
        P(None, None, "head"),
        P(None, None, "head"),
        P(None, None, "head", None),
        P(None, "head", None),
        P(None, "head", None),
        P(),
        P(None, None, None, "head"),
        P(None, "head", None),
        P(("dp", "seq"), None),
    )
    out_specs = (
        P(("dp", "seq"), None),
        P(("dp", "seq"), None),
        P(None, ("dp", "seq")),
        P(None, ("dp", "seq"), None, "head"),
        P(None, None, ("dp", "seq", "head")),
        P(None, ("dp", "seq"), "head"),
        P(None, None, "head", ("dp", "seq")),
        P(None, None, ("dp", "seq", "head")),
        P(None, None, "head"),
        P(None, ("dp", "seq"), "head"),
        P(None, ("dp", "seq"), "head", None),
        P(None, "head", ("dp", "seq")),
        P(None, "head", ("dp", "seq")),
        P(None, ("dp", "seq")),
        P(None, ("dp", "seq"), None, "head"),
        P(None, "head", ("dp", "seq")),
    )
    return jax.shard_map(
        on_device, mesh=mesh, in_specs=in_specs, out_specs=out_specs, check_vma=False
    )
```

```python
import functools

import jax
import jax.numpy as jnp
from jax import lax
from jax.experimental import pallas as pl
from jax.experimental.pallas import tpu as pltpu
from jax.sharding import PartitionSpec as P

NS = 128
HD = 64
RIM = 16

norm_eps = 1e-05
masked_score = -1e30
bf16 = jnp.bfloat16
f32 = jnp.float32
VMEM_LIMIT = 63 * 1024 * 1024


def nn(left, right):
    return jnp.dot(left, right, preferred_element_type=f32)


def tn(left, right):
    return lax.dot_general(left, right, (((0,), (0,)), ((), ())), preferred_element_type=f32)


def nt(left, right):
    return lax.dot_general(left, right, (((1,), (1,)), ((), ())), preferred_element_type=f32)


def split(v, terms):
    parts = []
    for _ in range(terms):
        parts.append(v.astype(bf16))
        v = v - parts[-1].astype(f32)
    return parts


def sigmoid(v):
    return 0.5 * jnp.tanh(0.5 * v) + 0.5


def softplus(v):
    return jnp.maximum(v, 0.0) + jnp.log(1.0 + jnp.exp(-jnp.abs(v)))


def head_map(heads, width):
    rows = lax.rem(lax.broadcasted_iota(jnp.int32, (256, heads * width), 0), 128)
    columns = lax.broadcasted_iota(jnp.int32, (256, heads * width), 1)
    return (columns // width == rows).astype(bf16)


def spread(scalars, mapping):
    return nn(jnp.concatenate(split(scalars, 2), axis=1), mapping)


def spread_rows(scalars, mapping):
    return tn(mapping, jnp.concatenate(split(scalars, 2), axis=0))


def gather(columns, mapping):
    high, low = split(columns, 2)
    return nt(high, mapping[:128]) + nt(low, mapping[:128])


def triangle_sum(triangle, v):
    width = v.shape[1]
    sums = nn(triangle, jnp.concatenate(split(v, 3), axis=1))
    return sums[:, :width] + sums[:, width:2 * width] + sums[:, 2 * width:]


def rms_scaled(hidden, gain):
    return hidden * lax.rsqrt(jnp.mean(hidden * hidden, axis=-1, keepdims=True) + norm_eps) * gain


def ssm_scalars(dt_ref, heads_ref):
    rows = dt_ref.shape[0]
    raw = dt_ref[...] + heads_ref[0:1, :]
    step = softplus(raw)
    log_decay = -jnp.exp(heads_ref[1:2, :]) * step
    place_t = lax.broadcasted_iota(jnp.int32, (rows, rows), 0)
    place_s = lax.broadcasted_iota(jnp.int32, (rows, rows), 1)
    running = triangle_sum((place_s <= place_t).astype(bf16), log_decay)
    running_t = jnp.transpose(running)
    return raw, step, log_decay, running, running_t, place_t >= place_s


def score_mask(dcol_ref, drow_ref):
    rows, length = dcol_ref.shape[0], drow_ref.shape[1]
    query_pos = lax.broadcasted_iota(jnp.int32, (rows, length), 0) + lax.axis_index("seq") * rows
    key_pos = lax.broadcasted_iota(jnp.int32, (rows, length), 1)
    return (key_pos <= query_pos) & (dcol_ref[:, 0:1] == drow_ref[0:1, :])


MESH_ID = pl.DeviceIdType.MESH
CHUNK = 128


def remote(src, dst, send, recv, axis, target):
    return pltpu.make_async_remote_copy(
        src_ref=src, dst_ref=dst, send_sem=send, recv_sem=recv,
        device_id={axis: target}, device_id_type=MESH_ID,
    )


def meet(count, later_sends, extra=None):
    place = lax.axis_index("seq")
    barrier = pltpu.get_barrier_semaphore()
    for j in range(1, count if extra is None else 1):
        here = place - j if not later_sends else place + j

        @pl.when((here >= 0) & (here < count))
        def _():
            pl.semaphore_signal(barrier, inc=1, device_id={"seq": here}, device_id_type=MESH_ID)
    heads_axis = lax.axis_size("head")
    partner = lax.rem(lax.axis_index("head") + 1, heads_axis)
    pl.semaphore_signal(barrier, inc=1, device_id={"head": partner}, device_id_type=MESH_ID)
    waits = (place if later_sends else count - 1 - place) + 1
    if extra is not None:
        waits = extra() + 1
    pl.semaphore_wait(barrier, waits)
    return partner


VM = pl.BlockSpec(memory_space=pltpu.VMEM)
ANY = pl.BlockSpec(memory_space=pl.ANY)
DMA = pltpu.SemaphoreType.DMA
UNITS = 4


def add_rows(out, terms):
    rows = out.shape[0]
    size = min(64, rows)

    def one(i, carry):
        part = pl.ds(pl.multiple_of(i * size, size), size)
        total = terms[0][part, :].astype(f32)
        for term in terms[1:]:
            total = total + term[part, :].astype(f32)
        out[part, :] = total.astype(out.dtype)
        return carry
    lax.fori_loop(0, rows // size, one, 0)


def dp_spot():
    spot = lax.axis_index("dp")
    return lax.rem(spot, 2), spot // 2, lax.axis_size("dp") // 2


def greet_sums():
    barrier = pltpu.get_barrier_semaphore()
    core, group, others = dp_spot()
    count = lax.axis_size("seq")
    place = lax.axis_index("seq")
    targets = [{"dp": group * 2 + 1 - core}]
    targets += [{"dp": lax.rem(group + k, others) * 2 + core} for k in range(1, others)]
    targets += [{"seq": lax.rem(place + k, count)} for k in range(1, count)]
    for target in targets:
        pl.semaphore_signal(barrier, inc=1, device_id=target, device_id_type=MESH_ID)
    return len(targets)


class CrossSum:
    def __init__(self, ranges, buffers, sems):
        self.ranges = ranges
        self.own, self.first, self.second = buffers
        self.load_sem, self.first_send, self.first_recv, self.second_send, self.second_recv = sems
        self.core, self.group, self.others = dp_spot()
        self.loads, self.firsts, self.seconds = [], [], []

    def start(self):
        span = self.own.shape[2]
        for n, (grad, columns) in enumerate(self.ranges):
            self.firsts.append([])
            self.loads.append([])
            for g in range(self.others):
                theirs = pl.ds(pl.multiple_of((2 * g + 1 - self.core) * span, span), span)
                mine = pl.ds(pl.multiple_of((2 * g + self.core) * span, span), span)
                self.firsts[n].append(remote(
                    grad.at[theirs, columns], self.first.at[n, g], self.first_send.at[n, g],
                    self.first_recv.at[n, g], "dp", self.group * 2 + 1 - self.core))
                self.loads[n].append(pltpu.make_async_copy(
                    grad.at[mine, columns], self.own.at[n, g], self.load_sem.at[n, g]))
                self.firsts[n][g].start()
                self.loads[n][g].start()

    def step_a(self, n):
        for g in range(self.others):
            self.loads[n][g].wait()
            self.firsts[n][g].wait_recv()
        copies = []
        for k in range(1, self.others):
            peer = lax.rem(self.group + k, self.others)
            theirs = self.own.at[n, peer]
            add_rows(theirs, [theirs, self.first.at[n, peer]])
            copies.append(remote(
                theirs, self.second.at[n, k - 1], self.second_send.at[n, k - 1], self.second_recv.at[n, k - 1],
                "dp", peer * 2 + self.core))
            copies[-1].start()
        self.seconds.append(copies)

    def step_b(self, n, out):
        for copy in self.seconds[n]:
            copy.wait_recv()
        add_rows(out, [self.own.at[n, self.group], self.first.at[n, self.group]]
                 + [self.second.at[n, k] for k in range(self.others - 1)])

    def finish(self):
        for n in range(len(self.ranges)):
            for copy in self.firsts[n] + self.seconds[n]:
                copy.wait_send()


class Exchange:
    def __init__(self, array, received, send_sem, recv_sem, steps):
        self.array, self.received = array, received
        self.copies = [remote(array, received.at[i], send_sem.at[i], recv_sem.at[i], axis, target)
                       for i, (axis, target) in enumerate(steps)]

    def send(self, i):
        self.copies[i].start()

    def add(self, i):
        self.copies[i].wait_recv()
        self.copies[i].wait_send()
        self.array[...] = (self.array[...].astype(f32) + self.received[i].astype(f32)).astype(self.array.dtype)


def across(place, bit):
    step = 2 ** bit
    return place + step - 2 * step * lax.rem(lax.div(place, step), 2)


def bits(count):
    return range(count.bit_length() - 1)


class LineSum:
    def __init__(self, pieces, received, send_sem, recv_sem):
        self.pieces = pieces
        self.received, self.send_sem, self.recv_sem = received, send_sem, recv_sem
        self.count = lax.axis_size("seq")
        self.place = lax.axis_index("seq")
        self.shard = received.shape[2]
        self.copies = [[] for _ in pieces]

    def rows(self, shard):
        return pl.ds(pl.multiple_of(shard * self.shard, self.shard), self.shard)

    def pass_on(self, n, bit):
        step = 2 ** bit
        side = lax.rem(lax.div(self.place, step), 2)
        target = self.place + step - 2 * step * side
        low = lax.rem(target, 2 * step)
        copies = []
        slot = self.count - self.count // step
        for m in range(self.count // (2 * step)):
            copies.append(remote(
                self.pieces[n].at[self.rows(low + 2 * step * m)], self.received.at[n, slot + m],
                self.send_sem.at[n, slot + m], self.recv_sem.at[n, slot + m], "seq", target))
            copies[-1].start()
        self.copies[n].append(copies)

    def take_in(self, n, bit):
        step = 2 ** bit
        low = lax.rem(self.place, 2 * step)
        slot = self.count - self.count // step
        for m, copy in enumerate(self.copies[n][bit]):
            copy.wait_recv()
            rows = self.pieces[n].at[self.rows(low + 2 * step * m)]
            if 2 * step == self.count:
                return [rows, self.received.at[n, slot + m]]
            add_rows(rows, [rows, self.received.at[n, slot + m]])

    def step_c(self, n):
        self.pass_on(n, 0)

    def step_d(self, n):
        bit = 1
        while 2 ** bit < self.count:
            self.take_in(n, bit - 1)
            self.pass_on(n, bit)
            bit += 1

    def step_e(self, n, write):
        write(n, self.take_in(n, len(self.copies[n]) - 1))

    def finish(self):
        for steps in self.copies:
            for copies in steps:
                for copy in copies:
                    copy.wait_send()


def cut_columns(refs):
    ranges = []
    for ref in refs:
        size = ref.shape[1] // UNITS
        ranges += [(ref, pl.ds(u * size, size)) for u in range(UNITS)]
    return ranges


def cross_scratch(ranges, span, columns):
    others = lax.axis_size("dp") // 2
    size = columns // UNITS
    peers = max(others - 1, 1)
    return [
        pltpu.VMEM((ranges, others, span, size), bf16), pltpu.VMEM((ranges, others, span, size), bf16),
        pltpu.VMEM((ranges, peers, span, size), bf16), DMA((ranges, others)), DMA((ranges, others)),
        DMA((ranges, others)), DMA((ranges, peers)), DMA((ranges, peers)),
    ]


def line_scratch(ranges, span, columns):
    count = lax.axis_size("seq")
    return [pltpu.VMEM((ranges, count - 1, span // count, columns // UNITS), bf16),
            DMA((ranges, count - 1)), DMA((ranges, count - 1))]


CROSS_REFS = 8
LINE_REFS = 3


def last_sum_kernel(widths, *refs):
    grads, half, done, maps, small = refs[:2], refs[2], refs[3], refs[4:6], refs[6:8]
    kinds = len(widths[0]) + len(widths[1])
    outs = refs[8:8 + kinds]
    small_out, maps_out = refs[8 + kinds:10 + kinds]
    scratch, extra = refs[10 + kinds:-17], refs[-17:]
    place = lax.axis_index("seq")
    count = lax.axis_size("seq")
    core, group, peers = dp_spot()
    partner = {"head": lax.rem(lax.axis_index("head") + 1, lax.axis_size("head"))}
    pl.semaphore_signal(pltpu.get_barrier_semaphore(), inc=1, device_id=partner, device_id_type=MESH_ID)
    partners = greet_sums() + 1
    pl.semaphore_wait(pltpu.get_barrier_semaphore(), partners)
    (both, both_in, both_send, both_recv) = extra[:4]
    map_cross = CrossSum([(ref, pl.ds(0, ref.shape[1])) for ref in maps], extra[4:7], extra[7:12])
    map_part, map_rest = extra[12:14]
    rest_in, rest_send, rest_recv = extra[14:17]
    line_steps = [("seq", across(place, bit)) for bit in bits(count)]
    few = Exchange(both, both_in, both_send, both_recv,
                   [("dp", group * 2 + 1 - core)] + [("dp", across(group, bit) * 2 + core) for bit in bits(peers)]
                   + line_steps)
    span, shard = map_part.shape[1], map_rest.shape[1]
    rest = Exchange(map_rest, rest_in, rest_send, rest_recv, line_steps if shard == span else [])
    per_layer = small[0].shape[0]
    for l in range(2):
        both[l * per_layer:(l + 1) * per_layer, :] = small[l][...]
    few.send(0)
    map_cross.start()
    halves, early_half = scratch[:2]
    for n, (_, columns) in enumerate(cut_columns([half])):
        early_half[n] = half[:, columns]
    early = LineSum([early_half.at[n] for n in range(UNITS)], *scratch[2:5])
    cross = CrossSum(cut_columns(grads), scratch[5:8], scratch[8:13])
    total = len(cross.ranges)
    line = LineSum([halves.at[n] for n in range(total)], *scratch[13:])
    cross.start()
    few.add(0)
    few.send(1)
    for l in range(2):
        map_cross.step_a(l)
    for n in range(UNITS):
        early.step_c(n)

    def pass_few(i):
        few.add(i)
        if i + 1 < len(few.copies):
            few.send(i + 1)

    def take_maps():
        for l in range(2):
            map_cross.step_b(l, map_part.at[l])
        halve(0)

    def halve(bit):
        if shard == span:
            if bit == 0:
                map_rest[...] = map_part[...]
            rest.send(bit)
            return
        step = 2 ** bit
        low = lax.rem(across(place, bit), 2 * step)
        for m in range(count // (2 * step)):
            source = pl.ds(pl.multiple_of((low + 2 * step * m) * shard, shard), shard)
            halves_sent.append(remote(map_part.at[:, source], rest_in.at[len(halves_sent)],
                                      rest_send.at[len(halves_sent)], rest_recv.at[len(halves_sent)],
                                      "seq", across(place, bit)))
            halves_sent[-1].start()

    halves_sent = []
    halves_taken = []

    def join(bit):
        if shard == span:
            rest.add(bit)
        else:
            step = 2 ** bit
            low = lax.rem(place, 2 * step)
            for m in range(count // (2 * step)):
                slot = len(halves_taken)
                halves_sent[slot].wait_recv()
                mine = pl.ds(pl.multiple_of((low + 2 * step * m) * shard, shard), shard)
                map_part[:, mine] = (map_part[:, mine].astype(f32) + rest_in[slot].astype(f32)).astype(bf16)
                halves_taken.append(slot)
        if bit + 1 < count.bit_length() - 1:
            halve(bit + 1)
        else:
            if shard != span:
                map_rest[...] = map_part[:, pl.ds(pl.multiple_of(place * shard, shard), shard)]
            head_copy.start()

    last = rest_in.shape[0] - 1
    head_copy = remote(map_rest, rest_in.at[last], rest_send.at[last], rest_recv.at[last], "head", partner["head"])

    def end_maps():
        head_copy.wait_recv()
        maps_out[...] = map_rest[...].astype(f32) + rest_in[last].astype(f32)
    chores = [functools.partial(pass_few, i) for i in range(1, len(few.copies) - 2)]
    chores += [take_maps] + [functools.partial(pass_few, i) for i in range(len(few.copies) - 2, len(few.copies))]
    chores += [functools.partial(join, bit) for bit in bits(count)] + [end_maps]
    pieces = []
    which = 0
    for a in range(2):
        at = 0
        for width in widths[a]:
            if width < 0:
                pieces += [(a, at, -width, outs[which], 0), (a, at - width, -width, outs[which], 1)]
                at -= 2 * width
            else:
                pieces.append((a, at, width, outs[which], None))
                at += width
            which += 1

    def place_of(out, layer, side, columns):
        return out.at[layer, :, columns] if side is None else out.at[layer, :, side, columns]

    def write(layer, array, n, terms):
        size = terms[0].shape[1]
        begin = n % UNITS * size
        for a, at, width, out, side in pieces:
            low, high = max(at, begin), min(at + width, begin + size)
            if a == array and low < high:
                add_rows(place_of(out, layer, side, pl.ds(low - at, high - low)),
                         [term.at[:, pl.ds(low - begin, high - low)] for term in terms])

    def write_early(n, terms):
        write(1, 1, n, terms)

    def write_line(n, terms):
        write(0, n // UNITS, n, terms)
    for n in range(total):
        cross.step_a(n)
        if n < UNITS:
            early.step_d(n)
    for a, at, width, out, side in pieces:
        if a == 0:
            place_of(out, 1, side, pl.ds(0, width))[...] = done[:, at:at + width]
    for n in range(total + 2):
        if n < total:
            cross.step_b(n, halves.at[n])
            line.step_c(n)
        if 1 <= n <= total:
            line.step_d(n - 1)
        if n < UNITS:
            early.step_e(n, write_early)
        if n >= 2:
            line.step_e(n - 2, write_line)
        if chores:
            chores.pop(0)()
    for chore in chores:
        chore()
    small_out[...] = both[...]
    for copy in halves_sent + [head_copy]:
        copy.wait_send()
    map_cross.finish()
    early.finish()
    cross.finish()
    line.finish()


def last_sum(grads, half, done, maps, small, widths):
    columns = grads[0].shape[1]
    span = half.shape[0]
    shard = span // lax.axis_size("seq")
    total = 2 * UNITS
    count, others = lax.axis_size("seq"), lax.axis_size("dp") // 2
    both = (2 * small[0].shape[0], small[0].shape[1])
    steps = 1 + len(bits(others)) + len(bits(count))
    map_span = maps[0].shape[0] // lax.axis_size("dp")
    map_width = maps[0].shape[1]
    map_rows = map_span // count if map_span // count >= 16 else map_span
    slots = count if map_rows < map_span else len(bits(count)) + 1
    return pl.pallas_call(
        functools.partial(last_sum_kernel, widths),
        out_shape=[jax.ShapeDtypeStruct((2, shard, width) if width > 0 else (2, shard, 2, -width), f32)
                   for width in widths[0] + widths[1]]
        + [jax.ShapeDtypeStruct(shape, f32) for shape in (both, (2, map_rows, map_width))],
        in_specs=[ANY] * 2 + [VM] * 2 + [ANY] * 2 + [VM] * 2,
        out_specs=[VM] * (len(widths[0]) + len(widths[1]) + 2),
        scratch_shapes=[pltpu.VMEM((total, span, columns // UNITS), bf16),
                        pltpu.VMEM((UNITS, span, columns // UNITS), bf16), *line_scratch(UNITS, span, columns),
                        *cross_scratch(total, span, columns), *line_scratch(total, span, columns),
                        pltpu.VMEM(both, f32), pltpu.VMEM((steps, *both), f32), DMA((steps,)), DMA((steps,)),
                        *cross_scratch(2, map_span, map_width * UNITS),
                        pltpu.VMEM((2, map_span, map_width), bf16), pltpu.VMEM((2, map_rows, map_width), bf16),
                        pltpu.VMEM((slots, 2, map_rows, map_width), bf16), DMA((slots,)), DMA((slots,))],
        compiler_params=pltpu.CompilerParams(
            vmem_limit_bytes=VMEM_LIMIT, collective_id=9, has_side_effects=True),
        cost_estimate=pl.CostEstimate(flops=0, bytes_accessed=400 * 1024 * 1024, transcendentals=0),
    )(*grads, half, done, *maps, *small)


def unpack(pairs, out):
    def one(i, carry):
        rows = pl.ds(pl.multiple_of(i * 128, 128), 128)
        out[rows, :] = pairs[rows].reshape(128, out.shape[1])
        return carry
    lax.fori_loop(0, out.shape[0] // 128, one, 0)


def find_documents(seg_ref, dcol_ref, dloc_ref, drow_ref, column):
    place = lax.axis_index("seq")
    rows = dcol_ref.shape[0]
    drow_ref[...] = jnp.broadcast_to(seg_ref[...].astype(f32), drow_ref.shape)
    here = drow_ref[0:1, pl.ds(pl.multiple_of(place * rows, 128), rows)]
    dloc_ref[...] = jnp.broadcast_to(here, dloc_ref.shape)
    behind = drow_ref[0:1, pl.ds(pl.multiple_of(jnp.maximum(place * rows - 128, 0), 128), 128)]
    behind = jnp.where(place > 0, behind, -1.0)
    column[0:8, :] = jnp.transpose(jnp.broadcast_to(behind, (128, 128)))[120:, :]
    column[8:, :] = jnp.transpose(jnp.broadcast_to(here, (128, rows)))
    lane = lax.broadcasted_iota(jnp.int32, (rows, 128), 1)
    docs = column[8:, :]
    result = jnp.where(lane == 0, docs, 0.0)
    tests = [column[8 - k:8 - k + rows, :] for k in range(1, 4)] + [column[7:8, :], column[7 + rows:8 + rows, :]]
    for i, test in enumerate(tests):
        result = jnp.where(lane == i + 1, (docs == test).astype(f32), result)
    dcol_ref[...] = result


def layer_forward_kernel(heads, layer, layers, h_ref, gain_mix_ref, gain_ff_ref, wdt_ref,
                         taps_ref, heads_ref, *refs):
    refs = list(refs)
    seg_ref = refs.pop(0) if layer == 0 else None
    dcol_ref, dloc_ref, drow_ref = (None,) * 3 if layer == 0 else [refs.pop(0) for _ in range(3)]
    (wkv_hbm, wbc_hbm, zx_hbm, wq_hbm, wout_hbm, wo_hbm, gu_hbm, wdown_hbm) = refs[:8]
    refs = refs[8:]
    ready = layer > 0
    follows = layer + 1 < layers
    zx_ready = refs.pop(0) if ready else None
    (h_out, normed_ref, gate_ref, stack_ref, rim_ref, pre_ref, dt_ref, q_ref, kvall_ref,
     att_ref, lse_ref, mem_ref, gated_ref, middle_ref, nff_ref, gu_ref, inner_ref, gu_out) = refs[:18]
    refs = refs[18:]
    if not ready:
        dcol_ref, dloc_ref, drow_ref = [refs.pop(0) for _ in range(3)]
    zx_out = None if ready else refs.pop(0)
    zx_next = refs.pop(0) if follows else None
    column = refs.pop() if not ready else None
    (ext, y, wkv_ref, wbc_ref, wzx_ref, wq_ref, wo_ref, wout_ref, wgu_ref, wdown_ref, raw_zx, raw_gu,
     rim_in, kv_in, chain_in, chain_out, part_out, part_in, down_out, down_in,
     load_sem, kv_send, kv_recv, rim_send, rim_recv, chain_send, chain_recv,
     part_send, part_recv, down_send, down_recv) = refs
    rows = dt_ref.shape[0]
    d_local = gate_ref.shape[1]
    ff_local = inner_ref.shape[1]
    count = lax.axis_size("seq")
    place = lax.axis_index("seq")
    loads = {}
    plan = [("kv", wkv_hbm.at[layer], wkv_ref), ("bc", wbc_hbm.at[layer], wbc_ref)]
    plan.append(("zx", zx_ready, wzx_ref) if ready else ("zx", zx_hbm.at[layer], raw_zx))
    plan += [("q", wq_hbm.at[layer], wq_ref), ("out", wout_hbm.at[layer], wout_ref), ("o", wo_hbm.at[layer], wo_ref),
             ("gu", gu_hbm.at[layer], raw_gu), ("down", wdown_hbm.at[layer], wdown_ref)]
    later = [("gu_store", wgu_ref, gu_out)]
    if not ready:
        later.append(("zx_store", wzx_ref, zx_out))
    if follows:
        later += [("next", zx_hbm.at[layer + 1], raw_zx), ("next_store", wzx_ref, zx_next)]
    for name, src, dst in plan + later:
        loads[name] = pltpu.make_async_copy(src, dst, load_sem.at[len(loads)])
    for name, src, dst in plan:
        loads[name].start()
    partner = meet(count, False)

    if not ready:
        find_documents(seg_ref, dcol_ref, dloc_ref, drow_ref, column)
    normed_ref[...] = rms_scaled(h_ref[...].astype(f32), gain_mix_ref[...]).astype(bf16)
    normed = normed_ref[...]
    own = pl.ds(pl.multiple_of(place * rows, rows), rows)
    for j in range(count):
        @pl.when(j > place)
        def _():
            kv_in[j * rows:(j + 1) * rows, :] = jnp.zeros((rows, 2 * HD), bf16)
    loads["kv"].wait()
    kv_in[own, :] = nn(normed, wkv_ref[...]).astype(bf16)
    kv_copies = [
        remote(kv_in.at[own], kv_in.at[own], kv_send.at[j - 1], kv_recv.at[j - 1], "seq", place + j)
        for j in range(1, count)
    ]
    for j in range(1, count):
        @pl.when(place + j < count)
        def _():
            kv_copies[j - 1].start()
    loads["bc"].wait()
    stack_ref[:, d_local:] = nn(normed, wbc_ref[...]).astype(bf16)
    loads["zx"].wait()
    if not ready:
        unpack(raw_zx, wzx_ref)
        loads["zx_store"].start()
    if follows:
        loads["next"].start()
    stack_ref[:, :d_local] = nn(normed, wzx_ref[:, d_local:]).astype(bf16)
    rim_copy = remote(stack_ref.at[pl.ds(rows - RIM, RIM)], rim_in, rim_send, rim_recv, "seq", place + 1)

    @pl.when(place + 1 < count)
    def _():
        rim_copy.start()

    @pl.when(place == 0)
    def _():
        rim_in[...] = jnp.zeros(rim_in.shape, bf16)
        chain_in[...] = jnp.zeros(chain_in.shape, bf16)
    dt_ref[...] = nn(normed, wdt_ref[...]).astype(bf16).astype(f32)
    gate_ref[...] = nn(normed, wzx_ref[:, :d_local]).astype(bf16)
    loads["q"].wait()
    q_ref[...] = nn(normed, wq_ref[...]).astype(bf16)
    raw, step, log_decay, running, running_t, ordered = ssm_scalars(dt_ref, heads_ref)
    mapping = head_map(heads, d_local // heads)
    last = running[rows - 1:rows, :]
    fade = jnp.exp(last - running) * dcol_ref[:, 5:6]
    dec = jnp.exp(running) * dcol_ref[:, 4:5]
    ends = jnp.exp(running_t[:, rows - 1:rows]) * dcol_ref[rows - 1:rows, 4:5] + jnp.zeros((128, NS), f32)
    ends = spread_rows(ends, mapping)
    steps = spread(step, mapping)
    ext[RIM:, :] = stack_ref[...].astype(f32)

    @pl.when(place > 0)
    def _():
        rim_copy.wait_recv()
    rim_ref[...] = rim_in[...]
    ext[0:RIM, :] = rim_in[...].astype(f32)
    pre = ext[RIM:RIM + rows, :] * taps_ref[0:1, :]
    for k in range(1, 4):
        pre = pre + ext[RIM - k:RIM - k + rows, :] * dcol_ref[:, k:k + 1] * taps_ref[k:k + 1, :]
    pre_ref[...] = pre
    mixed = pre_ref[...] * sigmoid(pre_ref[...])
    values = mixed[:, :d_local]
    b_rows = mixed[:, d_local:d_local + NS].astype(bf16)
    c_rows = mixed[:, d_local + NS:].astype(bf16)
    stepped = values * steps
    state = tn((stepped * spread(fade, mapping)).astype(bf16), b_rows)
    y[...] = values * spread(heads_ref[2:3, :] + jnp.zeros((8, 128), f32), mapping)[0:1, :]
    linked = ordered & (dcol_ref[:, 0:1] == dloc_ref[0:1, :])
    cb = jnp.where(linked, nt(c_rows, b_rows), 0.0)
    stepped = stepped.astype(bf16)
    lane = lax.broadcasted_iota(jnp.int32, (rows, 128), 1)

    for j in range(1, count):
        @pl.when(place - j >= 0)
        def _():
            kv_copies[j - 1].wait_recv()
    allowed = score_mask(dcol_ref, drow_ref)
    keyvals = kv_in[...]
    kvall_ref[...] = keyvals
    keys, vals = keyvals[:, :HD], keyvals[:, HD:]
    totals = jnp.zeros((rows, 128), f32)
    pairs = heads // 2
    query_heads = q_ref.shape[1] // HD
    chain_copies = []
    for pair in range(pairs):
        span = slice(pair * 128, pair * 128 + 128)
        copy = remote(chain_out.at[pl.ds(pair * 128, 128)], chain_in.at[pl.ds(pair * 128, 128)],
                      chain_send.at[pair], chain_recv.at[pair], "seq", place + 1)
        chain_copies.append(copy)

        @pl.when(place > 0)
        def _():
            copy.wait_recv()
        chain_out[span, :] = (ends[span] * chain_in[span, :].astype(f32) + state[span]).astype(bf16)

        @pl.when(place + 1 < count)
        def _():
            copy.start()
        sides = []
        for h in (2 * pair, 2 * pair + 1):
            gap = running[:, h:h + 1] - running_t[h:h + 1, :]
            mixing = (jnp.exp(jnp.minimum(gap, 0.0)) * cb).astype(bf16)
            sides.append(nn(mixing, stepped[:, span]))
        y[:, span] += jnp.where(lane < 64, sides[0], sides[1])
        for h in range(query_heads * pair // pairs, query_heads * (pair + 1) // pairs):
            query = q_ref[:, h * HD:(h + 1) * HD] * jnp.asarray(HD ** -0.5, bf16)
            scores = jnp.where(allowed, nt(query, keys), masked_score)
            peak = jnp.max(scores, axis=1, keepdims=True)
            expo = jnp.exp(scores - peak)
            total = jnp.sum(expo, axis=1, keepdims=True)
            probs = (expo * (1.0 / total)).astype(bf16)
            att_ref[:, h * HD:(h + 1) * HD] = nn(probs, vals).astype(bf16)
            totals = jnp.where(lane == h, peak + jnp.log(total), totals)
    lse_ref[...] = totals
    mem_ref[...] = chain_in[...]
    decs = spread(dec, mapping)
    carried = decs * nt(c_rows, mem_ref[...])
    gate = gate_ref[...].astype(f32)
    gated_ref[...] = ((y[...] + carried) * (gate * sigmoid(gate))).astype(bf16)
    loads["out"].wait()
    loads["o"].wait()
    chunks = [pl.ds(begin, CHUNK) for begin in range(0, rows, CHUNK)]
    part_copies, down_copies = [], []
    for i, chunk in enumerate(chunks):
        part_out[chunk, :] = (nn(gated_ref[chunk, :], wout_ref[...])
                              + nn(att_ref[chunk, :], wo_ref[...])).astype(bf16)
        copy = remote(part_out.at[chunk], part_in.at[chunk], part_send.at[i], part_recv.at[i], "head", partner)
        copy.start()
        part_copies.append(copy)
    loads["gu"].wait()
    unpack(raw_gu, wgu_ref)
    loads["gu_store"].start()
    loads["down"].wait()
    for i, chunk in enumerate(chunks):
        part_copies[i].wait_recv()
        middle_ref[chunk, :] = h_ref[chunk, :].astype(f32) + (
            part_out[chunk, :].astype(f32) + part_in[chunk, :].astype(f32))
        nff_ref[chunk, :] = rms_scaled(middle_ref[chunk, :], gain_ff_ref[...]).astype(bf16)
        gu_ref[chunk, :] = nn(nff_ref[chunk, :], wgu_ref[...]).astype(bf16)
        gate = gu_ref[chunk, :ff_local].astype(f32)
        inner_ref[chunk, :] = (gate * sigmoid(gate) * gu_ref[chunk, ff_local:].astype(f32)).astype(bf16)
        down_out[chunk, :] = nn(inner_ref[chunk, :], wdown_ref[...]).astype(bf16)
        copy = remote(down_out.at[chunk], down_in.at[chunk], down_send.at[i], down_recv.at[i], "head", partner)
        copy.start()
        down_copies.append(copy)
    if not ready:
        loads["zx_store"].wait()
    if follows:
        loads["next"].wait()
        unpack(raw_zx, wzx_ref)
        loads["next_store"].start()
    for i, chunk in enumerate(chunks):
        down_copies[i].wait_recv()
        h_out[chunk, :] = (middle_ref[chunk, :] + (
            down_out[chunk, :].astype(f32) + down_in[chunk, :].astype(f32))).astype(bf16)
    loads["gu_store"].wait()
    if follows:
        loads["next_store"].wait()
    for i in range(len(chunks)):
        part_copies[i].wait_send()
        down_copies[i].wait_send()

    @pl.when(place + 1 < count)
    def _():
        rim_copy.wait_send()
        for copy in chain_copies:
            copy.wait_send()
    for j in range(1, count):
        @pl.when(place + j < count)
        def _():
            kv_copies[j - 1].wait_send()


def layer_forward(layer, hidden, zx, w, context):
    rows, model_width = hidden.shape
    heads = w["heads"]
    layers = w["out"].shape[0]
    d_local = w["out"].shape[1]
    ff_local = w["down"].shape[1]
    q_width = w["q"].shape[2]
    width = d_local + 2 * NS
    count = lax.axis_size("seq")
    length = count * rows
    parts = rows // CHUNK
    wide = ((model_width, 2 * d_local), bf16)
    outs = [
        ((rows, model_width), bf16), ((rows, model_width), bf16), ((rows, d_local), bf16), ((rows, width), bf16),
        ((RIM, width), bf16), ((rows, width), f32), ((rows, 128), f32), ((rows, q_width), bf16),
        ((length, 2 * HD), bf16), ((rows, q_width), bf16), ((rows, 128), f32), ((d_local, NS), bf16),
        ((rows, d_local), bf16), ((rows, model_width), f32), ((rows, model_width), bf16),
        ((rows, 2 * ff_local), bf16), ((rows, ff_local), bf16), ((model_width, 2 * ff_local), bf16),
    ]
    kept = len(outs) - 1
    documents = [((rows, 128), f32), ((8, rows), f32), ((8, length), f32)] if layer == 0 else []
    outs += documents
    outs += [wide] * ((layer == 0) + (layer + 1 < layers))
    full = (rows, model_width)
    given = [] if layer == 0 else [zx]
    result = pl.pallas_call(
        functools.partial(layer_forward_kernel, heads, layer, layers),
        out_shape=[jax.ShapeDtypeStruct(shape, kind) for shape, kind in outs],
        in_specs=[VM] * (6 + len(context)) + [ANY] * (8 + len(given)),
        out_specs=[VM] * kept + [ANY] + [VM] * len(documents) + [ANY] * (len(outs) - kept - 1 - len(documents)),
        scratch_shapes=[
            pltpu.VMEM((rows + RIM, width), f32), pltpu.VMEM((rows, d_local), f32),
            pltpu.VMEM((model_width, 2 * HD), bf16), pltpu.VMEM((model_width, 2 * NS), bf16),
            pltpu.VMEM((model_width, 2 * d_local), bf16), pltpu.VMEM((model_width, q_width), bf16),
            pltpu.VMEM((q_width, model_width), bf16), pltpu.VMEM((d_local, model_width), bf16),
            pltpu.VMEM((model_width, 2 * ff_local), bf16), pltpu.VMEM((ff_local, model_width), bf16),
            pltpu.VMEM((model_width, 2, d_local), bf16), pltpu.VMEM((model_width, 2, ff_local), bf16),
            pltpu.VMEM((RIM, width), bf16), pltpu.VMEM((length, 2 * HD), bf16),
            pltpu.VMEM((d_local, NS), bf16), pltpu.VMEM((d_local, NS), bf16),
            pltpu.VMEM(full, bf16), pltpu.VMEM(full, bf16), pltpu.VMEM(full, bf16), pltpu.VMEM(full, bf16),
            DMA((12,)), DMA((count - 1,)), DMA((count - 1,)), DMA, DMA, DMA((heads // 2,)), DMA((heads // 2,)),
            DMA((parts,)), DMA((parts,)), DMA((parts,)), DMA((parts,)),
            *([pltpu.VMEM((rows + 8, 128), f32)] if layer == 0 else []),
        ],
        compiler_params=pltpu.CompilerParams(
            vmem_limit_bytes=VMEM_LIMIT, collective_id=layer, has_side_effects=True),
    )(hidden, w["gain_mix"][layer], w["gain_ff"][layer], w["dt"][layer], w["taps"][layer], w["head_vals"][layer],
      *context, w["kv"], w["bc"], w["zx"], w["q"], w["out"], w["o"], w["gu"], w["down"], *given)
    names = ("out", "normed", "gate", "stack", "rim", "pre", "dt", "q", "kv", "att", "lse", "memory",
             "gated", "middle", "nff", "gu", "inner", "w_gu")
    saved = dict(zip(names, result))
    saved["hidden"] = hidden
    extra = list(result[len(names):])
    if layer == 0:
        context = [extra.pop(0) for _ in range(3)]
    saved["w_zx"] = extra.pop(0) if layer == 0 else zx
    return saved.pop("out"), (extra.pop(0) if extra else None), context, saved


def norm_back(hidden, gain, grad):
    inverse = lax.rsqrt(jnp.mean(hidden * hidden, axis=-1, keepdims=True) + norm_eps)
    scaled = grad * gain
    lean = jnp.mean(scaled * hidden, axis=-1, keepdims=True)
    grad_gain = jnp.sum(grad * hidden * inverse, axis=0, keepdims=True)
    return inverse * (scaled - hidden * (inverse * inverse * lean)), grad_gain


def store_blocks(compute, slots, out, sems):
    size = slots.shape[1]
    columns = out.shape[1]
    blocks = out.shape[0] // size

    def rows(i):
        return pl.ds(pl.multiple_of(i * size, size), size)

    def copy(i, slot):
        return pltpu.make_async_copy(slots.at[slot, :, pl.ds(0, columns)], out.at[rows(i)], sems.at[slot])

    def one(i, carry):
        slot = lax.rem(i, 2)

        @pl.when(i >= 2)
        def _():
            copy(i - 2, slot).wait()
        compute(rows(i), slot)
        copy(i, slot).start()
        return carry
    lax.fori_loop(0, blocks, one, 0)
    for i in range(max(0, blocks - 2), blocks):
        copy(i, i % 2).wait()


def layer_backward_kernel(heads, layer, schedule, grad_ref, h_ref, normed_ref, gate_ref, stack_ref, rim_ref, pre_ref, dt_ref,
                          q_ref, kv_ref, att_ref, lse_ref, mem_ref, gated_ref, middle_ref, nff_ref, gu_ref,
                          inner_ref, gain_mix_ref, gain_ff_ref, wdt_ref,
                          taps_ref, heads_ref, dcol_ref, dloc_ref, drow_ref,
                          wdown_hbm, wgu_hbm, wout_hbm, wo_hbm, wzx_hbm, wbc_hbm, wq_hbm, wkv_hbm, *refs):
    refs = list(refs)
    own_sum = schedule["own"]
    source = None if own_sum else refs.pop(0)
    half_in = None if own_sum else refs.pop(0)
    if not own_sum:
        line_refs, refs = refs[-LINE_REFS - 1:], refs[:-LINE_REFS - 1]
    cross_refs, refs = refs[-CROSS_REFS:], refs[:-CROSS_REFS]
    summed_ref = None if own_sum else refs.pop(0)
    (g_out, gff_out, gmix_out, gbc_out, small_ref, half_ref,
     wdown_ref, wide_ref, wout_ref, wo_ref, wbc_ref, wq_ref, wkv_ref,
     gff, dgu, one_out, one_in, two_out, two_in, gmid, branch, gg, datt, dy_s, dxs_s, u_s,
     decay_s, probs_s, acc, dkv_out, dkv_in, chain_in, chain_out, rim_in,
     ext, pad, dext, dgate, dstack, dq, dkv, draw_s,
     load_sem, one_send, one_recv, two_send, two_recv, chain_send, chain_recv,
     rim_send, rim_recv, kv_send, kv_recv, gblk, grad_sem) = refs
    rows = dt_ref.shape[0]
    d_local = gate_ref.shape[1]
    ff_local = inner_ref.shape[1]
    q_width = q_ref.shape[1]
    model_width = h_ref.shape[1]
    width = pre_ref.shape[1]
    length = kv_ref.shape[0]
    count = lax.axis_size("seq")
    place = lax.axis_index("seq")
    wgu_ref = wide_ref.at[:, pl.ds(0, 2 * ff_local)]
    wzx_ref = wide_ref.at[:, pl.ds(0, 2 * d_local)]
    loads = {}
    for name, src, dst in (
        ("down", wdown_hbm.at[layer], wdown_ref), ("gu", wgu_hbm, wgu_ref), ("out", wout_hbm.at[layer], wout_ref),
        ("o", wo_hbm.at[layer], wo_ref), ("bc", wbc_hbm.at[layer], wbc_ref), ("q", wq_hbm.at[layer], wq_ref),
        ("kv", wkv_hbm.at[layer], wkv_ref), ("zx", wzx_hbm, wzx_ref),
    ):
        loads[name] = pltpu.make_async_copy(src, dst, load_sem.at[len(loads)])
    for name in ("down", "gu", "out", "o", "bc", "q", "kv"):
        loads[name].start()
    partner = meet(count, True, greet_sums)
    cross = CrossSum(cut_columns([gff_out if own_sum else source]), cross_refs[:3], cross_refs[3:])
    ranges = [columns for _, columns in cut_columns([half_ref])]
    steps_of = {"a": cross.step_a, "b": lambda n: cross.step_b(n, half_ref.at[:, ranges[n]])}
    if not own_sum:
        fetches = [pltpu.make_async_copy(half_in.at[:, columns], line_refs[0].at[n], load_sem.at[len(loads) + n])
                   for n, (_, columns) in enumerate(cut_columns([half_in]))]
        for fetch in fetches:
            fetch.start()
        for fetch in fetches:
            fetch.wait()
        line = LineSum([line_refs[0].at[n] for n in range(UNITS)], *line_refs[1:])

        def write(n, terms):
            size = terms[0].shape[1]
            add_rows(summed_ref.at[:, pl.ds(n * size, size)], terms)
        steps_of.update({"c": line.step_c, "d": line.step_d, "e": lambda n: line.step_e(n, write)})

    def pump(spot):
        for step in schedule.get(spot, ()):
            if step == "start":
                cross.start()
            elif step == "finish":
                cross.finish()
                if not own_sum:
                    line.finish()
            else:
                steps_of[step[0]](int(step[1]))
    pump("begin")
    chunks = [pl.ds(begin, CHUNK) for begin in range(0, rows, CHUNK)]

    gff[...] = grad_ref[...].astype(bf16)
    loads["down"].wait()
    loads["gu"].wait()
    one_copies, two_copies = [], []
    for i, chunk in enumerate(chunks):
        grad_inner = nt(gff[chunk, :], wdown_ref[...])
        gate = gu_ref[chunk, :ff_local].astype(f32)
        up = gu_ref[chunk, ff_local:].astype(f32)
        sig = sigmoid(gate)
        dgu[chunk, :ff_local] = (grad_inner * up * (sig * (1.0 + gate * (1.0 - sig)))).astype(bf16)
        dgu[chunk, ff_local:] = (grad_inner * (gate * sig)).astype(bf16)
        one_out[chunk, :] = nt(dgu[chunk, :], wgu_ref[...]).astype(bf16)
        copy = remote(one_out.at[chunk], one_in.at[chunk], one_send.at[i], one_recv.at[i], "head", partner)
        copy.start()
        one_copies.append(copy)
    loads["zx"].start()

    @pl.when(place == count - 1)
    def _():
        rim_in[...] = jnp.zeros(rim_in.shape, f32)
        chain_in[...] = jnp.zeros(chain_in.shape, bf16)
    for j in range(1, count):
        @pl.when(place + j >= count)
        def _():
            dkv_in[(j - 1) * rows:j * rows, :] = jnp.zeros((rows, 2 * HD), bf16)

    pump("ff0")

    def ff_weights(block, slot):
        gblk[slot, :, :ff_local] = tn(gff[:, block], inner_ref[...]).astype(bf16)
        gblk[slot, :, ff_local:3 * ff_local] = tn(nff_ref[:, block], dgu[...]).astype(bf16)
    store_blocks(ff_weights, gblk, gff_out, grad_sem)
    pump("ff")

    raw, step, log_decay, running, running_t, ordered = ssm_scalars(dt_ref, heads_ref)
    mapping = head_map(heads, d_local // heads)
    last = running[rows - 1:rows, :]
    fade = spread(jnp.exp(last - running) * dcol_ref[:, 5:6], mapping)
    dec = jnp.exp(running) * dcol_ref[:, 4:5]
    decs = spread(dec, mapping)
    ends = jnp.exp(running_t[:, rows - 1:rows]) * dcol_ref[rows - 1:rows, 4:5] + jnp.zeros((128, NS), f32)
    ends = spread_rows(ends, mapping)
    steps = spread(step, mapping)
    skip = spread(heads_ref[2:3, :] + jnp.zeros((8, 128), f32), mapping)[0:1, :]
    pre_v = pre_ref[:, :d_local]
    values = pre_v * sigmoid(pre_v)
    pre_n = pre_ref[:, d_local:]
    maps = (pre_n * sigmoid(pre_n)).astype(bf16)
    b_rows, c_rows = maps[:, :NS], maps[:, NS:]
    stepped = (values * steps).astype(bf16)
    linked = ordered & (dcol_ref[:, 0:1] == dloc_ref[0:1, :])
    cb = jnp.where(linked, nt(c_rows, b_rows), 0.0)
    lane = lax.broadcasted_iota(jnp.int32, (rows, 128), 1)
    pairs = heads // 2
    for pair in range(pairs):
        span = slice(pair * 128, pair * 128 + 128)
        sides = []
        for h in (2 * pair, 2 * pair + 1):
            at = slice(h * rows, (h + 1) * rows)
            gap = running[:, h:h + 1] - running_t[h:h + 1, :]
            decay = jnp.exp(jnp.minimum(gap, 0.0))
            decay_s[:, at] = decay.astype(bf16)
            mixing = (decay_s[:, at].astype(f32) * cb).astype(bf16)
            sides.append(nn(mixing, stepped[:, span]))
        u_s[:, span] = jnp.where(lane < 64, sides[0], sides[1])
    allowed = score_mask(dcol_ref, drow_ref)
    keyvals = kv_ref[...]
    keys, vals = keyvals[:, :HD], keyvals[:, HD:]
    scale = jnp.asarray(HD ** -0.5, bf16)
    query_heads = q_width // HD
    for h in range(query_heads):
        query = q_ref[:, h * HD:(h + 1) * HD] * scale
        scores = jnp.where(allowed, nt(query, keys), masked_score)
        probs_s[:, h * length:(h + 1) * length] = jnp.exp(scores - lse_ref[:, h:h + 1]).astype(bf16)
    ext[0:RIM, :] = rim_ref[...].astype(f32)
    ext[RIM:, :] = stack_ref[...].astype(f32)
    gate = gate_ref[...].astype(f32)
    gate_sig = sigmoid(gate)
    gate_act = gate * gate_sig
    loads["out"].wait()
    loads["o"].wait()
    dtaps_ref = small_ref.at[pl.ds(0, 8)]
    gains_ref = small_ref.at[pl.ds(8, 8)]
    gains_ref[...] = jnp.zeros(gains_ref.shape, f32)
    for i, chunk in enumerate(chunks):
        pump("one%d" % i)
        one_copies[i].wait_recv()
        grad = one_out[chunk, :].astype(f32) + one_in[chunk, :].astype(f32)
        moved, gain = norm_back(middle_ref[chunk, :], gain_ff_ref[...], grad)
        gains_ref[1:2, :] += gain
        gmid[chunk, :] = grad_ref[chunk, :].astype(f32) + moved
        branch[chunk, :] = gmid[chunk, :].astype(bf16)
        gg[chunk, :] = nt(branch[chunk, :], wout_ref[...])
        datt[chunk, :] = nt(branch[chunk, :], wo_ref[...]).astype(bf16)
    grad_ssm = gg[...] * gate_act
    dy_s[...] = grad_ssm.astype(bf16)
    push = tn((grad_ssm * decs).astype(bf16), c_rows)
    dcb = jnp.zeros((rows, rows), f32)
    chain_copies = []
    for pair in range(pairs):
        pump("pair%d" % pair)
        span = slice(pair * 128, pair * 128 + 128)
        copy = remote(chain_out.at[pl.ds(pair * 128, 128)], chain_in.at[pl.ds(pair * 128, 128)],
                      chain_send.at[pair], chain_recv.at[pair], "seq", place - 1)
        chain_copies.append(copy)

        @pl.when(place < count - 1)
        def _():
            copy.wait_recv()
        chain_out[span, :] = (ends[span] * chain_in[span, :].astype(f32) + push[span]).astype(bf16)

        @pl.when(place > 0)
        def _():
            copy.start()
        stepped_p = stepped[:, span]
        dy_p = dy_s[:, span]
        dxs = []
        for side, h in enumerate((2 * pair, 2 * pair + 1)):
            at = slice(h * rows, (h + 1) * rows)
            decay = decay_s[:, at].astype(f32)
            dxs.append(tn((decay * cb).astype(bf16), dy_p))
            half = jnp.where((lane < 64) == (side == 0), dy_p, jnp.zeros_like(dy_p))
            dcb = dcb + nt(half, stepped_p) * decay
        dxs_s[:, span] = jnp.where(lane < 64, dxs[0], dxs[1])
        for h in range(query_heads * pair // pairs, query_heads * (pair + 1) // pairs):
            part = slice(h * HD, (h + 1) * HD)
            query = q_ref[:, part] * scale
            grad = datt[:, part]
            delta = jnp.sum(grad.astype(f32) * att_ref[:, part].astype(f32), axis=1, keepdims=True)
            probs = probs_s[:, h * length:(h + 1) * length]
            grad_scores = (probs.astype(f32) * (nt(grad, vals) - delta)).astype(bf16)
            dq[:, part] = (nn(grad_scores, keys) * HD ** -0.5).astype(bf16)
            dk = tn(grad_scores, query)
            dv = tn(probs, grad)
            if h == 0:
                acc[:, :HD] = dk
                acc[:, HD:] = dv
            else:
                acc[:, :HD] += dk
                acc[:, HD:] += dv
    dkv_out[...] = acc[...].astype(bf16)
    kv_copies = []
    for j in range(1, count):
        target = jnp.maximum(place - j, 0)
        theirs = pl.ds(pl.multiple_of(target * rows, rows), rows)
        copy = remote(dkv_out.at[theirs], dkv_in.at[pl.ds((j - 1) * rows, rows)], kv_send.at[j - 1],
                      kv_recv.at[j - 1], "seq", place - j)
        kv_copies.append(copy)

        @pl.when(place >= j)
        def _():
            copy.start()
    pump("post")
    memory = mem_ref[...]
    gmem = chain_in[...]
    carried = decs * nt(c_rows, memory)
    back = fade * nt(b_rows, gmem)
    dy_low = dy_s[...].astype(f32)
    stepped_f = stepped.astype(f32)
    dxs_all = dxs_s[...] + back
    dxs_s[...] = dxs_all
    dcb = jnp.where(linked, dcb, 0.0).astype(bf16)
    dc = nn(dcb, b_rows) + nn((dy_low * decs).astype(bf16), memory)
    db = tn(dcb, c_rows) + nn((stepped_f * fade).astype(bf16), gmem)
    dvalues = steps * dxs_all + skip * grad_ssm
    pad[0:8, :] = jnp.zeros((8, width), f32)
    pad[8 + rows:, :] = jnp.zeros((8, width), f32)
    sig = sigmoid(pre_v)
    pad[8:8 + rows, :d_local] = dvalues * (sig * (1.0 + pre_v * (1.0 - sig)))
    sig = sigmoid(pre_n)
    slope = sig * (1.0 + pre_n * (1.0 - sig))
    pad[8:8 + rows, d_local:d_local + NS] = db * slope[:, :NS]
    pad[8:8 + rows, d_local + NS:] = dc * slope[:, NS:]
    dpre = pad[8:8 + rows, :]
    dext[...] = pad[0:8 + rows, :] * taps_ref[0:1, :]
    dtaps_ref[...] = jnp.zeros((8, width), f32)
    dtaps_ref[0:1, :] = jnp.sum(dpre * ext[RIM:RIM + rows, :], axis=0, keepdims=True)
    for k in range(1, 4):
        masked = dpre * dcol_ref[:, k:k + 1]
        pad[8:8 + rows, :] = masked
        dtaps_ref[k:k + 1, :width] = jnp.sum(masked * ext[RIM - k:RIM - k + rows, :], axis=0, keepdims=True)
        dext[...] += pad[k:k + 8 + rows, :] * taps_ref[k:k + 1, :]
    rim_copy = remote(dext.at[pl.ds(0, 8)], rim_in, rim_send, rim_recv, "seq", place - 1)

    @pl.when(place > 0)
    def _():
        rim_copy.start()
    scanned = u_s[...] + carried
    drun = gather(dy_low * scanned - stepped_f * dxs_all, mapping)
    ssm_out = scanned + skip * values
    dgate[...] = (gg[...] * ssm_out * (gate_sig * (1.0 + gate * (1.0 - gate_sig)))).astype(bf16)
    gstep = gather(values * dxs_all, mapping)
    ones = jnp.ones((8, 128), bf16)
    high, low = split(gmem.astype(f32) * memory.astype(f32), 2)
    moved = nt(ones, high) + nt(ones, low)
    end = gather(jnp.sum(stepped_f * back, axis=0, keepdims=True) + jnp.zeros((8, 1), f32), mapping)
    end = end + gather(moved, mapping) * dec[rows - 1:rows, :]
    upper = (lax.broadcasted_iota(jnp.int32, (rows, rows), 1)
             >= lax.broadcasted_iota(jnp.int32, (rows, rows), 0)).astype(bf16)
    dlog = triangle_sum(upper, drun) + end[0:1, :]
    draw = (gstep - jnp.exp(heads_ref[1:2, :]) * dlog) * sigmoid(raw)
    draw_s[...] = draw.astype(bf16)
    dskip = gather(jnp.sum(grad_ssm * values, axis=0, keepdims=True) + jnp.zeros((8, 1), f32), mapping)
    small_ref[4:5, :128] = jnp.sum(draw, axis=0, keepdims=True)
    small_ref[5:6, :128] = jnp.sum(dlog * log_decay, axis=0, keepdims=True)
    small_ref[6:7, :128] = dskip[0:1, :]
    for name in ("zx", "bc", "q", "kv"):
        loads[name].wait()

    for j in range(1, count):
        @pl.when(place + j < count)
        def _():
            kv_copies[j - 1].wait_recv()
    pump("two")
    own = pl.ds(pl.multiple_of(place * rows, rows), rows)
    total = acc[own, :]
    for j in range(1, count):
        total = total + dkv_in[(j - 1) * rows:j * rows, :].astype(f32)
    dkv[...] = total.astype(bf16)

    for i, chunk in enumerate(chunks):
        if i == len(chunks) - 1:
            @pl.when(place < count - 1)
            def _():
                rim_copy.wait_recv()
            dext[rows:rows + 8, :] += rim_in[...]
        dstack[chunk, :] = dext[8 + i * CHUNK:8 + (i + 1) * CHUNK, :].astype(bf16)
        two_out[chunk, :] = (
            nt(dgate[chunk, :], wzx_ref[:, :d_local]) + nt(dstack[chunk, :d_local], wzx_ref[:, d_local:])
            + nt(dstack[chunk, d_local:], wbc_ref[...]) + nt(draw_s[chunk, :], wdt_ref[...])
            + nt(dq[chunk, :], wq_ref[...]) + nt(dkv[chunk, :], wkv_ref[...])
        ).astype(bf16)
        copy = remote(two_out.at[chunk], two_in.at[chunk], two_send.at[i], two_recv.at[i], "head", partner)
        copy.start()
        two_copies.append(copy)

    gbc_out[:, model_width:] = jnp.transpose(jnp.concatenate(
        [dtaps_ref[0:4, d_local:], jnp.zeros((124, 2 * NS), f32)], axis=0)).astype(bf16)
    pump("mix")

    def mix_weights(block, slot):
        left = normed_ref[:, block]
        at = 0
        for right in (dgate[...], dstack[:, :d_local], dq[...], dkv[...], draw_s[...]):
            gblk[slot, :, at:at + right.shape[1]] = tn(left, right).astype(bf16)
            at += right.shape[1]
        left = branch[:, block]
        for right in (gated_ref[...], att_ref[...]):
            gblk[slot, :, at:at + right.shape[1]] = tn(left, right).astype(bf16)
            at += right.shape[1]
        gbc_out[:, block] = tn(dstack[:, d_local:], normed_ref[:, block]).astype(bf16)
    store_blocks(mix_weights, gblk, gmix_out, grad_sem)

    for i, chunk in enumerate(chunks):
        pump("last%d" % i)
        two_copies[i].wait_recv()
        grad = two_out[chunk, :].astype(f32) + two_in[chunk, :].astype(f32)
        moved, gain = norm_back(h_ref[chunk, :].astype(f32), gain_mix_ref[...], grad)
        gains_ref[0:1, :] += gain
        g_out[chunk, :] = gmid[chunk, :] + moved
    pump("end")
    for i in range(len(chunks)):
        one_copies[i].wait_send()
        two_copies[i].wait_send()

    @pl.when(place > 0)
    def _():
        rim_copy.wait_send()
        for copy in chain_copies:
            copy.wait_send()
    for j in range(1, count):
        @pl.when(place >= j)
        def _():
            kv_copies[j - 1].wait_send()


SCHEDULES = (
    {"own": False, "begin": ("start", "c0", "c1", "c2", "c3"), "ff0": ("a0", "a1", "a2", "a3"), "ff": ("d0", "d1"),
     "one0": ("d2",), "one1": ("d3",), "mix": ("b0", "b1"), "last0": ("e0", "e1", "e2", "e3", "b2"),
     "end": ("b3", "finish")},
    {"own": True, "ff": ("start",), "one0": ("a0", "a1"), "one1": ("a2", "a3"), "mix": ("b0",), "last0": ("b1", "b2"),
     "end": ("b3", "finish")},
)


def layer_backward(layer, grad, waiting, w, saved, context):
    dcol, dloc, drow = context
    rows, model_width = grad.shape
    heads = w["heads"]
    d_local = w["out"].shape[1]
    ff_local = w["down"].shape[1]
    q_width = w["q"].shape[2]
    width = d_local + 2 * NS
    count = lax.axis_size("seq")
    length = count * rows
    parts = rows // CHUNK
    mix_width = 3 * d_local + 2 * q_width + 256
    schedule = SCHEDULES[1 if waiting is None else 0]
    given = [] if waiting is None else list(waiting)
    outs = [
        ((rows, model_width), f32), ((model_width, 3 * ff_local), bf16), ((model_width, mix_width), bf16),
        ((2 * NS, model_width + 128), bf16), ((16, max(width, model_width)), f32),
    ]
    span = model_width // lax.axis_size("dp")
    if waiting is not None:
        outs.insert(0, ((span // count, 3 * ff_local), f32))
    outs.append(((span, 3 * ff_local if waiting is None else mix_width), bf16))
    full = (rows, model_width)
    state = (d_local, NS)
    names = ("hidden", "normed", "gate", "stack", "rim", "pre", "dt", "q", "kv", "att", "lse", "memory",
             "gated", "middle", "nff", "gu", "inner")

    def vm(shape, kind):
        return pltpu.VMEM(shape, kind)
    return pl.pallas_call(
        functools.partial(layer_backward_kernel, heads, layer, schedule),
        out_shape=[jax.ShapeDtypeStruct(shape, kind) for shape, kind in outs],
        in_specs=[VM] * 26 + [ANY] * (8 + len(given)),
        out_specs=[VM] * (len(outs) - 5) + [ANY, ANY] + [VM] * 3,
        scratch_shapes=[
            vm((ff_local, model_width), bf16), vm((model_width, 2 * max(d_local, ff_local)), bf16),
            vm((d_local, model_width), bf16), vm((q_width, model_width), bf16), vm((model_width, 2 * NS), bf16),
            vm((model_width, q_width), bf16), vm((model_width, 2 * HD), bf16),
            vm(full, bf16), vm((rows, 2 * ff_local), bf16), vm(full, bf16), vm(full, bf16), vm(full, bf16),
            vm(full, bf16), vm(full, f32), vm(full, bf16), vm((rows, d_local), f32), vm((rows, q_width), bf16),
            vm((rows, d_local), bf16), vm((rows, d_local), f32), vm((rows, d_local), f32),
            vm((rows, heads * rows), bf16),
            vm((rows, q_width // HD * length), bf16), vm((length, 2 * HD), f32), vm((length, 2 * HD), bf16),
            vm(((count - 1) * rows, 2 * HD), bf16), vm(state, bf16), vm(state, bf16), vm((8, width), f32),
            vm((rows + RIM, width), f32), vm((rows + 16, width), f32), vm((rows + 8, width), f32),
            vm((rows, d_local), bf16), vm((rows, width), bf16), vm((rows, q_width), bf16),
            vm((rows, 2 * HD), bf16), vm((rows, 128), bf16),
            DMA((8 + UNITS,)), DMA((parts,)), DMA((parts,)), DMA((parts,)), DMA((parts,)), DMA((heads // 2,)),
            DMA((heads // 2,)), DMA, DMA, DMA((count - 1,)), DMA((count - 1,)),
            vm((2, 128, max(3 * ff_local, mix_width)), bf16), DMA((2,)),
            *cross_scratch(UNITS, span, outs[-1][0][1]),
            *([] if waiting is None else
              [vm((UNITS, span, 3 * ff_local // UNITS), bf16), *line_scratch(UNITS, span, 3 * ff_local)]),
        ],
        compiler_params=pltpu.CompilerParams(
            vmem_limit_bytes=VMEM_LIMIT, collective_id=2 + layer, has_side_effects=True),
    )(grad, *[saved[name] for name in names], w["gain_mix"][layer], w["gain_ff"][layer], w["dt"][layer],
      w["taps"][layer], w["head_vals"][layer], dcol, dloc, drow, w["down"], saved["w_gu"], w["out"], w["o"],
      saved["w_zx"], w["bc"], w["q"], w["kv"], *given)


def on_device(hidden_in, segment_ids, gain_mix, w_zx, w_bc, w_dt, conv_x, conv_bc, ssm_head, w_q, w_kv,
              w_o, w_out, gain_ff, w_gu, w_down, cotangent):
    rows, model_width = hidden_in.shape
    taps_count = conv_x.shape[1]
    place = lax.axis_index("seq")
    context = (segment_ids,)
    layers = gain_mix.shape[0]
    heads = ssm_head.shape[2]
    d_local = w_zx.shape[3]
    w = dict(
        heads=heads,
        gain_mix=gain_mix[:, None].astype(f32),
        gain_ff=gain_ff[:, None].astype(f32),
        zx=w_zx,
        bc=w_bc,
        dt=jnp.pad(w_dt, ((0, 0), (0, 0), (0, 128 - heads))),
        q=w_q,
        kv=w_kv.reshape(layers, model_width, -1),
        o=w_o,
        out=w_out,
        gu=w_gu,
        down=w_down,
        taps=jnp.pad(jnp.concatenate([conv_x.reshape(layers, taps_count, -1), conv_bc], axis=2).astype(f32),
                     ((0, 0), (0, 8 - taps_count), (0, 0))),
        head_vals=jnp.pad(ssm_head, ((0, 0), (0, 5), (0, 128 - heads))),
    )
    hidden = hidden_in
    saved = []
    zx = None
    for l in range(layers):
        hidden, zx, context, kept = layer_forward(l, hidden, zx, w, context)
        saved.append(kept)
    block_out = hidden
    gradient = cotangent
    narrow, small = [None] * layers, [None] * layers
    waiting = None
    for l in reversed(range(layers)):
        *summed, gradient, ff_grads, mix_grads, narrow[l], small[l], half = layer_backward(
            l, gradient, waiting, w, saved[l], context)
        waiting = (mix_grads, half)
    shards = lax.axis_size("dp") * lax.axis_size("seq")
    shard = lax.axis_index("dp") * lax.axis_size("seq") + place
    ff_local = w_down.shape[1]
    q_width = w_q.shape[2]
    part = model_width // shards
    down, gu, zx, q, kv, dt, out, o, small, g_bc = last_sum(
        (ff_grads, mix_grads), half, summed[0], narrow, small,
        ((ff_local, -ff_local), (-d_local, q_width, 128, 128, d_local, q_width)))
    down, out, o = (jnp.transpose(a, (0, 2, 1)) for a in (down, out, o))
    kv = kv.reshape(layers, part, 1, 128)
    dt = dt[:, :, :heads]
    own = 2 * NS // (shards * lax.axis_size("head"))
    spot = place * lax.axis_size("head") + lax.axis_index("head")
    g_bc = lax.dynamic_slice_in_dim(g_bc, lax.rem(spot * own, g_bc.shape[1]), own, 1)
    w_bc_grad = jnp.transpose(g_bc[:, :, :model_width], (0, 2, 1))
    conv_bc_grad = jnp.transpose(g_bc[:, :, model_width:model_width + taps_count], (0, 2, 1))
    small = small.reshape(layers, -1, small.shape[1])
    gain_a = lax.dynamic_slice_in_dim(small[:, 8, :model_width], shard * part, part, 1)
    gain_b = lax.dynamic_slice_in_dim(small[:, 9, :model_width], shard * part, part, 1)
    taps = small[:, :taps_count, :d_local].reshape(layers, taps_count, heads, -1)
    taps_part = taps.shape[3] // shards
    conv_x_grad = lax.dynamic_slice_in_dim(taps, shard * taps_part, taps_part, 3)
    head_grad = small[:, 4:7, :heads]
    return (block_out, gradient, gain_a, zx, w_bc_grad, dt, conv_x_grad, conv_bc_grad, head_grad, q, kv,
            o, out, gain_b, gu, down)


def solution(mesh):
    in_specs = (
        P(("dp", "seq"), None),
        P("dp", None),
        P(),
        P(None, None, None, "head"),
        P(),
        P(None, None, "head"),
        P(None, None, "head", None),
        P(),
        P(None, None, "head"),
        P(None, None, "head"),
        P(None, None, "head", None),
        P(None, "head", None),
        P(None, "head", None),
        P(),
        P(None, None, None, "head"),
        P(None, "head", None),
        P(("dp", "seq"), None),
    )
    out_specs = (
        P(("dp", "seq"), None),
        P(("dp", "seq"), None),
        P(None, ("dp", "seq")),
        P(None, ("dp", "seq"), None, "head"),
        P(None, None, ("dp", "seq", "head")),
        P(None, ("dp", "seq"), "head"),
        P(None, None, "head", ("dp", "seq")),
        P(None, None, ("dp", "seq", "head")),
        P(None, None, "head"),
        P(None, ("dp", "seq"), "head"),
        P(None, ("dp", "seq"), "head", None),
        P(None, "head", ("dp", "seq")),
        P(None, "head", ("dp", "seq")),
        P(None, ("dp", "seq")),
        P(None, ("dp", "seq"), None, "head"),
        P(None, "head", ("dp", "seq")),
    )
    return jax.shard_map(
        on_device, mesh=mesh, in_specs=in_specs, out_specs=out_specs, check_vma=False
    )
```

```python
import functools

import jax
import jax.numpy as jnp
from jax import lax
from jax.experimental import pallas as pl
from jax.experimental.pallas import tpu as pltpu
from jax.sharding import PartitionSpec as P

NS = 128
HD = 64
RIM = 16

norm_eps = 1e-05
masked_score = -1e30
bf16 = jnp.bfloat16
f32 = jnp.float32
VMEM_LIMIT = 63 * 1024 * 1024


def nn(left, right):
    return jnp.dot(left, right, preferred_element_type=f32)


def tn(left, right):
    return lax.dot_general(left, right, (((0,), (0,)), ((), ())), preferred_element_type=f32)


def nt(left, right):
    return lax.dot_general(left, right, (((1,), (1,)), ((), ())), preferred_element_type=f32)


def split(v, terms):
    parts = []
    for _ in range(terms):
        parts.append(v.astype(bf16))
        v = v - parts[-1].astype(f32)
    return parts


def sigmoid(v):
    return 0.5 * jnp.tanh(0.5 * v) + 0.5


def softplus(v):
    return jnp.maximum(v, 0.0) + jnp.log(1.0 + jnp.exp(-jnp.abs(v)))


def head_map(heads, width):
    rows = lax.rem(lax.broadcasted_iota(jnp.int32, (256, heads * width), 0), 128)
    columns = lax.broadcasted_iota(jnp.int32, (256, heads * width), 1)
    return (columns // width == rows).astype(bf16)


def spread(scalars, mapping):
    return nn(jnp.concatenate(split(scalars, 2), axis=1), mapping)


def spread_rows(scalars, mapping):
    return tn(mapping, jnp.concatenate(split(scalars, 2), axis=0))


def gather(columns, mapping):
    high, low = split(columns, 2)
    return nt(high, mapping[:128]) + nt(low, mapping[:128])


def triangle_sum(triangle, v):
    width = v.shape[1]
    sums = nn(triangle, jnp.concatenate(split(v, 3), axis=1))
    return sums[:, :width] + sums[:, width:2 * width] + sums[:, 2 * width:]


def rms_scaled(hidden, gain):
    return hidden * lax.rsqrt(jnp.mean(hidden * hidden, axis=-1, keepdims=True) + norm_eps) * gain


def ssm_scalars(dt_ref, heads_ref):
    rows = dt_ref.shape[0]
    raw = dt_ref[...] + heads_ref[0:1, :]
    step = softplus(raw)
    log_decay = -jnp.exp(heads_ref[1:2, :]) * step
    place_t = lax.broadcasted_iota(jnp.int32, (rows, rows), 0)
    place_s = lax.broadcasted_iota(jnp.int32, (rows, rows), 1)
    running = triangle_sum((place_s <= place_t).astype(bf16), log_decay)
    running_t = jnp.transpose(running)
    return raw, step, log_decay, running, running_t, place_t >= place_s


def score_mask(dcol_ref, drow_ref):
    rows, length = dcol_ref.shape[0], drow_ref.shape[1]
    query_pos = lax.broadcasted_iota(jnp.int32, (rows, length), 0) + lax.axis_index("seq") * rows
    key_pos = lax.broadcasted_iota(jnp.int32, (rows, length), 1)
    return (key_pos <= query_pos) & (dcol_ref[:, 0:1] == drow_ref[0:1, :])


MESH_ID = pl.DeviceIdType.MESH
CHUNK = 128


def remote(src, dst, send, recv, axis, target):
    return pltpu.make_async_remote_copy(
        src_ref=src, dst_ref=dst, send_sem=send, recv_sem=recv,
        device_id={axis: target}, device_id_type=MESH_ID,
    )


def meet(count, later_sends, extra=None):
    place = lax.axis_index("seq")
    barrier = pltpu.get_barrier_semaphore()
    for j in range(1, count if extra is None else 1):
        here = place - j if not later_sends else place + j

        @pl.when((here >= 0) & (here < count))
        def _():
            pl.semaphore_signal(barrier, inc=1, device_id={"seq": here}, device_id_type=MESH_ID)
    heads_axis = lax.axis_size("head")
    partner = lax.rem(lax.axis_index("head") + 1, heads_axis)
    pl.semaphore_signal(barrier, inc=1, device_id={"head": partner}, device_id_type=MESH_ID)
    waits = (place if later_sends else count - 1 - place) + 1
    if extra is not None:
        waits = extra() + 1
    pl.semaphore_wait(barrier, waits)
    return partner


VM = pl.BlockSpec(memory_space=pltpu.VMEM)
ANY = pl.BlockSpec(memory_space=pl.ANY)
DMA = pltpu.SemaphoreType.DMA
UNITS = 4
BEGUN = 2


def add_rows(out, terms):
    rows = out.shape[0]
    size = min(64, rows)

    def one(i, carry):
        part = pl.ds(pl.multiple_of(i * size, size), size)
        total = terms[0][part, :].astype(f32)
        for term in terms[1:]:
            total = total + term[part, :].astype(f32)
        out[part, :] = total.astype(out.dtype)
        return carry
    lax.fori_loop(0, rows // size, one, 0)


def dp_spot():
    spot = lax.axis_index("dp")
    return lax.rem(spot, 2), spot // 2, lax.axis_size("dp") // 2


def greet_sums():
    barrier = pltpu.get_barrier_semaphore()
    core, group, others = dp_spot()
    count = lax.axis_size("seq")
    place = lax.axis_index("seq")
    targets = [{"dp": group * 2 + 1 - core}]
    targets += [{"dp": lax.rem(group + k, others) * 2 + core} for k in range(1, others)]
    targets += [{"seq": lax.rem(place + k, count)} for k in range(1, count)]
    for target in targets:
        pl.semaphore_signal(barrier, inc=1, device_id=target, device_id_type=MESH_ID)
    return len(targets)


class CrossSum:
    def __init__(self, ranges, buffers, sems):
        self.ranges = ranges
        self.own, self.first, self.second = buffers
        self.load_sem, self.first_send, self.first_recv, self.second_send, self.second_recv = sems
        self.core, self.group, self.others = dp_spot()
        self.loads, self.firsts, self.seconds = [], [], []

    def start(self):
        span = self.own.shape[2]
        for n, (grad, columns) in enumerate(self.ranges):
            self.firsts.append([])
            self.loads.append([])
            for g in range(self.others):
                theirs = pl.ds(pl.multiple_of((2 * g + 1 - self.core) * span, span), span)
                mine = pl.ds(pl.multiple_of((2 * g + self.core) * span, span), span)
                self.firsts[n].append(remote(
                    grad.at[theirs, columns], self.first.at[n, g], self.first_send.at[n, g],
                    self.first_recv.at[n, g], "dp", self.group * 2 + 1 - self.core))
                self.loads[n].append(pltpu.make_async_copy(
                    grad.at[mine, columns], self.own.at[n, g], self.load_sem.at[n, g]))
                self.firsts[n][g].start()
                self.loads[n][g].start()

    def step_a(self, n):
        for g in range(self.others):
            self.loads[n][g].wait()
            self.firsts[n][g].wait_recv()
        copies = []
        for k in range(1, self.others):
            peer = lax.rem(self.group + k, self.others)
            theirs = self.own.at[n, peer]
            add_rows(theirs, [theirs, self.first.at[n, peer]])
            copies.append(remote(
                theirs, self.second.at[n, k - 1], self.second_send.at[n, k - 1], self.second_recv.at[n, k - 1],
                "dp", peer * 2 + self.core))
            copies[-1].start()
        self.seconds.append(copies)

    def step_b(self, n, out):
        for copy in self.seconds[n]:
            copy.wait_recv()
        add_rows(out, [self.own.at[n, self.group], self.first.at[n, self.group]]
                 + [self.second.at[n, k] for k in range(self.others - 1)])

    def finish(self):
        for n in range(len(self.ranges)):
            for copy in self.firsts[n] + self.seconds[n]:
                copy.wait_send()


class Exchange:
    def __init__(self, array, received, send_sem, recv_sem, steps):
        self.array, self.received = array, received
        self.copies = [remote(array, received.at[i], send_sem.at[i], recv_sem.at[i], axis, target)
                       for i, (axis, target) in enumerate(steps)]

    def send(self, i):
        self.copies[i].start()

    def add(self, i):
        self.copies[i].wait_recv()
        self.copies[i].wait_send()
        self.array[...] = (self.array[...].astype(f32) + self.received[i].astype(f32)).astype(self.array.dtype)


def across(place, bit):
    step = 2 ** bit
    return place + step - 2 * step * lax.rem(lax.div(place, step), 2)


def bits(count):
    return range(count.bit_length() - 1)


class LineSum:
    def __init__(self, pieces, received, send_sem, recv_sem, begun=0):
        self.pieces, self.begun = pieces, begun
        self.received, self.send_sem, self.recv_sem = received, send_sem, recv_sem
        self.count = lax.axis_size("seq")
        self.place = lax.axis_index("seq")
        self.shard = received.shape[2]
        self.copies = [{} for _ in pieces]

    def rows(self, shard):
        return pl.ds(pl.multiple_of(shard * self.shard, self.shard), self.shard)

    def pass_on(self, n, bit):
        step = 2 ** bit
        side = lax.rem(lax.div(self.place, step), 2)
        target = self.place + step - 2 * step * side
        low = lax.rem(target, 2 * step)
        copies = []
        slot = self.count - self.count // step
        for m in range(self.count // (2 * step)):
            copies.append(remote(
                self.pieces[n].at[self.rows(low + 2 * step * m)], self.received.at[n, slot + m],
                self.send_sem.at[n, slot + m], self.recv_sem.at[n, slot + m], "seq", target))
            copies[-1].start()
        self.copies[n][bit] = copies

    def take_in(self, n, bit):
        step = 2 ** bit
        low = lax.rem(self.place, 2 * step)
        slot = self.count - self.count // step
        for m, copy in enumerate(self.copies[n][bit]):
            copy.wait_recv()
            rows = self.pieces[n].at[self.rows(low + 2 * step * m)]
            if 2 * step == self.count:
                return [rows, self.received.at[n, slot + m]]
            add_rows(rows, [rows, self.received.at[n, slot + m]])

    def step_c(self, n):
        self.pass_on(n, 1 if n < self.begun else 0)

    def step_d(self, n):
        bit = 2 if n < self.begun else 1
        while 2 ** bit < self.count:
            self.take_in(n, bit - 1)
            self.pass_on(n, bit)
            bit += 1

    def step_e(self, n, write):
        write(n, self.take_in(n, max(self.copies[n])))

    def finish(self):
        for steps in self.copies:
            for copies in steps.values():
                for copy in copies:
                    copy.wait_send()


def cut_columns(refs):
    ranges = []
    for ref in refs:
        size = ref.shape[1] // UNITS
        ranges += [(ref, pl.ds(u * size, size)) for u in range(UNITS)]
    return ranges


def cross_scratch(ranges, span, columns):
    others = lax.axis_size("dp") // 2
    size = columns // UNITS
    peers = max(others - 1, 1)
    return [
        pltpu.VMEM((ranges, others, span, size), bf16), pltpu.VMEM((ranges, others, span, size), bf16),
        pltpu.VMEM((ranges, peers, span, size), bf16), DMA((ranges, others)), DMA((ranges, others)),
        DMA((ranges, others)), DMA((ranges, peers)), DMA((ranges, peers)),
    ]


def line_scratch(ranges, span, columns, slots=None):
    count = lax.axis_size("seq")
    slots = count - 1 if slots is None else slots
    return [pltpu.VMEM((ranges, slots, span // count, columns // UNITS), bf16),
            DMA((ranges, slots)), DMA((ranges, slots))]


CROSS_REFS = 8
LINE_REFS = 3


def last_sum_kernel(widths, *refs):
    grads, half, done, maps, small = refs[:2], refs[2], refs[3], refs[4:6], refs[6:8]
    kinds = len(widths[0]) + len(widths[1])
    outs = refs[8:8 + kinds]
    small_out, maps_out = refs[8 + kinds:10 + kinds]
    scratch, extra = refs[10 + kinds:-17], refs[-17:]
    place = lax.axis_index("seq")
    count = lax.axis_size("seq")
    core, group, peers = dp_spot()
    partner = {"head": lax.rem(lax.axis_index("head") + 1, lax.axis_size("head"))}
    pl.semaphore_signal(pltpu.get_barrier_semaphore(), inc=1, device_id=partner, device_id_type=MESH_ID)
    partners = greet_sums() + 1
    pl.semaphore_wait(pltpu.get_barrier_semaphore(), partners)
    (both, both_in, both_send, both_recv) = extra[:4]
    map_cross = CrossSum([(ref, pl.ds(0, ref.shape[1])) for ref in maps], extra[4:7], extra[7:12])
    map_part, map_rest = extra[12:14]
    rest_in, rest_send, rest_recv = extra[14:17]
    line_steps = [("seq", across(place, bit)) for bit in bits(count)]
    few = Exchange(both, both_in, both_send, both_recv,
                   [("dp", group * 2 + 1 - core)] + [("dp", across(group, bit) * 2 + core) for bit in bits(peers)]
                   + line_steps)
    span, shard = map_part.shape[1], map_rest.shape[1]
    rest = Exchange(map_rest, rest_in, rest_send, rest_recv, line_steps if shard == span else [])
    per_layer = small[0].shape[0]
    for l in range(2):
        both[l * per_layer:(l + 1) * per_layer, :] = small[l][...]
    few.send(0)
    map_cross.start()
    halves, early_half = scratch[:2]
    for n, (_, columns) in enumerate(cut_columns([half])):
        early_half[n] = half[:, columns]
    early = LineSum([early_half.at[n] for n in range(UNITS)], *scratch[2:5], begun=BEGUN)
    cross = CrossSum(cut_columns(grads), scratch[5:8], scratch[8:13])
    total = len(cross.ranges)
    line = LineSum([halves.at[n] for n in range(total)], *scratch[13:])
    cross.start()
    few.add(0)
    few.send(1)
    for l in range(2):
        map_cross.step_a(l)
    for n in range(UNITS):
        early.step_c(n)

    def pass_few(i):
        few.add(i)
        if i + 1 < len(few.copies):
            few.send(i + 1)

    def take_maps():
        for l in range(2):
            map_cross.step_b(l, map_part.at[l])
        halve(0)

    def halve(bit):
        if shard == span:
            if bit == 0:
                map_rest[...] = map_part[...]
            rest.send(bit)
            return
        step = 2 ** bit
        low = lax.rem(across(place, bit), 2 * step)
        for m in range(count // (2 * step)):
            source = pl.ds(pl.multiple_of((low + 2 * step * m) * shard, shard), shard)
            halves_sent.append(remote(map_part.at[:, source], rest_in.at[len(halves_sent)],
                                      rest_send.at[len(halves_sent)], rest_recv.at[len(halves_sent)],
                                      "seq", across(place, bit)))
            halves_sent[-1].start()

    halves_sent = []
    halves_taken = []

    def join(bit):
        if shard == span:
            rest.add(bit)
        else:
            step = 2 ** bit
            low = lax.rem(place, 2 * step)
            for m in range(count // (2 * step)):
                slot = len(halves_taken)
                halves_sent[slot].wait_recv()
                mine = pl.ds(pl.multiple_of((low + 2 * step * m) * shard, shard), shard)
                map_part[:, mine] = (map_part[:, mine].astype(f32) + rest_in[slot].astype(f32)).astype(bf16)
                halves_taken.append(slot)
        if bit + 1 < count.bit_length() - 1:
            halve(bit + 1)
        else:
            if shard != span:
                map_rest[...] = map_part[:, pl.ds(pl.multiple_of(place * shard, shard), shard)]
            head_copy.start()

    last = rest_in.shape[0] - 1
    head_copy = remote(map_rest, rest_in.at[last], rest_send.at[last], rest_recv.at[last], "head", partner["head"])

    def end_maps():
        head_copy.wait_recv()
        maps_out[...] = map_rest[...].astype(f32) + rest_in[last].astype(f32)
    chores = [functools.partial(pass_few, i) for i in range(1, len(few.copies) - 2)]
    chores += [take_maps] + [functools.partial(pass_few, i) for i in range(len(few.copies) - 2, len(few.copies))]
    chores += [functools.partial(join, bit) for bit in bits(count)] + [end_maps]
    pieces = []
    which = 0
    for a in range(2):
        at = 0
        for width in widths[a]:
            if width < 0:
                pieces += [(a, at, -width, outs[which], 0), (a, at - width, -width, outs[which], 1)]
                at -= 2 * width
            else:
                pieces.append((a, at, width, outs[which], None))
                at += width
            which += 1

    def place_of(out, layer, side, columns):
        return out.at[layer, :, columns] if side is None else out.at[layer, :, side, columns]

    def write(layer, array, n, terms):
        size = terms[0].shape[1]
        begin = n % UNITS * size
        for a, at, width, out, side in pieces:
            low, high = max(at, begin), min(at + width, begin + size)
            if a == array and low < high:
                add_rows(place_of(out, layer, side, pl.ds(low - at, high - low)),
                         [term.at[:, pl.ds(low - begin, high - low)] for term in terms])

    def write_early(n, terms):
        write(1, 1, n, terms)

    def write_line(n, terms):
        write(0, n // UNITS, n, terms)
    for n in range(total):
        cross.step_a(n)
        if n < UNITS:
            early.step_d(n)
    for a, at, width, out, side in pieces:
        if a == 0:
            place_of(out, 1, side, pl.ds(0, width))[...] = done[:, at:at + width]
    for n in range(total + 2):
        if n < total:
            cross.step_b(n, halves.at[n])
            line.step_c(n)
        if 1 <= n <= total:
            line.step_d(n - 1)
        if n < UNITS:
            early.step_e(n, write_early)
        if n >= 2:
            line.step_e(n - 2, write_line)
        if chores:
            chores.pop(0)()
    for chore in chores:
        chore()
    small_out[...] = both[...]
    for copy in halves_sent + [head_copy]:
        copy.wait_send()
    map_cross.finish()
    early.finish()
    cross.finish()
    line.finish()


def last_sum(grads, half, done, maps, small, widths):
    columns = grads[0].shape[1]
    span = half.shape[0]
    shard = span // lax.axis_size("seq")
    total = 2 * UNITS
    count, others = lax.axis_size("seq"), lax.axis_size("dp") // 2
    both = (2 * small[0].shape[0], small[0].shape[1])
    steps = 1 + len(bits(others)) + len(bits(count))
    map_span = maps[0].shape[0] // lax.axis_size("dp")
    map_width = maps[0].shape[1]
    map_rows = map_span // count if map_span // count >= 16 else map_span
    slots = count if map_rows < map_span else len(bits(count)) + 1
    return pl.pallas_call(
        functools.partial(last_sum_kernel, widths),
        out_shape=[jax.ShapeDtypeStruct((2, shard, width) if width > 0 else (2, shard, 2, -width), f32)
                   for width in widths[0] + widths[1]]
        + [jax.ShapeDtypeStruct(shape, f32) for shape in (both, (2, map_rows, map_width))],
        in_specs=[ANY] * 2 + [VM] * 2 + [ANY] * 2 + [VM] * 2,
        out_specs=[VM] * (len(widths[0]) + len(widths[1]) + 2),
        scratch_shapes=[pltpu.VMEM((total, span, columns // UNITS), bf16),
                        pltpu.VMEM((UNITS, span, columns // UNITS), bf16), *line_scratch(UNITS, span, columns),
                        *cross_scratch(total, span, columns), *line_scratch(total, span, columns),
                        pltpu.VMEM(both, f32), pltpu.VMEM((steps, *both), f32), DMA((steps,)), DMA((steps,)),
                        *cross_scratch(2, map_span, map_width * UNITS),
                        pltpu.VMEM((2, map_span, map_width), bf16), pltpu.VMEM((2, map_rows, map_width), bf16),
                        pltpu.VMEM((slots, 2, map_rows, map_width), bf16), DMA((slots,)), DMA((slots,))],
        compiler_params=pltpu.CompilerParams(
            vmem_limit_bytes=VMEM_LIMIT, collective_id=9, has_side_effects=True),
        cost_estimate=pl.CostEstimate(flops=0, bytes_accessed=400 * 1024 * 1024, transcendentals=0),
    )(*grads, half, done, *maps, *small)


def unpack(pairs, out):
    def one(i, carry):
        rows = pl.ds(pl.multiple_of(i * 128, 128), 128)
        out[rows, :] = pairs[rows].reshape(128, out.shape[1])
        return carry
    lax.fori_loop(0, out.shape[0] // 128, one, 0)


def find_documents(seg_ref, dcol_ref, dloc_ref, drow_ref, column):
    place = lax.axis_index("seq")
    rows = dcol_ref.shape[0]
    drow_ref[...] = jnp.broadcast_to(seg_ref[...].astype(f32), drow_ref.shape)
    here = drow_ref[0:1, pl.ds(pl.multiple_of(place * rows, 128), rows)]
    dloc_ref[...] = jnp.broadcast_to(here, dloc_ref.shape)
    behind = drow_ref[0:1, pl.ds(pl.multiple_of(jnp.maximum(place * rows - 128, 0), 128), 128)]
    behind = jnp.where(place > 0, behind, -1.0)
    column[0:8, :] = jnp.transpose(jnp.broadcast_to(behind, (128, 128)))[120:, :]
    column[8:, :] = jnp.transpose(jnp.broadcast_to(here, (128, rows)))
    lane = lax.broadcasted_iota(jnp.int32, (rows, 128), 1)
    docs = column[8:, :]
    result = jnp.where(lane == 0, docs, 0.0)
    tests = [column[8 - k:8 - k + rows, :] for k in range(1, 4)] + [column[7:8, :], column[7 + rows:8 + rows, :]]
    for i, test in enumerate(tests):
        result = jnp.where(lane == i + 1, (docs == test).astype(f32), result)
    dcol_ref[...] = result


def layer_forward_kernel(heads, layer, layers, h_ref, gain_mix_ref, gain_ff_ref, wdt_ref,
                         taps_ref, heads_ref, *refs):
    refs = list(refs)
    seg_ref = refs.pop(0) if layer == 0 else None
    dcol_ref, dloc_ref, drow_ref = (None,) * 3 if layer == 0 else [refs.pop(0) for _ in range(3)]
    (wkv_hbm, wbc_hbm, zx_hbm, wq_hbm, wout_hbm, wo_hbm, gu_hbm, wdown_hbm) = refs[:8]
    refs = refs[8:]
    ready = layer > 0
    follows = layer + 1 < layers
    zx_ready = refs.pop(0) if ready else None
    (h_out, normed_ref, gate_ref, stack_ref, rim_ref, pre_ref, dt_ref, q_ref, kvall_ref,
     att_ref, lse_ref, mem_ref, gated_ref, middle_ref, nff_ref, gu_ref, inner_ref, gu_out) = refs[:18]
    refs = refs[18:]
    if not ready:
        dcol_ref, dloc_ref, drow_ref = [refs.pop(0) for _ in range(3)]
    zx_out = None if ready else refs.pop(0)
    zx_next = refs.pop(0) if follows else None
    column = refs.pop() if not ready else None
    (ext, y, wkv_ref, wbc_ref, wzx_ref, wq_ref, wo_ref, wout_ref, wgu_ref, wdown_ref, raw_zx, raw_gu,
     rim_in, kv_in, chain_in, chain_out, part_out, part_in, down_out, down_in,
     load_sem, kv_send, kv_recv, rim_send, rim_recv, chain_send, chain_recv,
     part_send, part_recv, down_send, down_recv) = refs
    rows = dt_ref.shape[0]
    d_local = gate_ref.shape[1]
    ff_local = inner_ref.shape[1]
    count = lax.axis_size("seq")
    place = lax.axis_index("seq")
    loads = {}
    plan = [("kv", wkv_hbm.at[layer], wkv_ref), ("bc", wbc_hbm.at[layer], wbc_ref)]
    plan.append(("zx", zx_ready, wzx_ref) if ready else ("zx", zx_hbm.at[layer], raw_zx))
    plan += [("q", wq_hbm.at[layer], wq_ref), ("out", wout_hbm.at[layer], wout_ref), ("o", wo_hbm.at[layer], wo_ref),
             ("gu", gu_hbm.at[layer], raw_gu), ("down", wdown_hbm.at[layer], wdown_ref)]
    later = [("gu_store", wgu_ref, gu_out)]
    if not ready:
        later.append(("zx_store", wzx_ref, zx_out))
    if follows:
        later += [("next", zx_hbm.at[layer + 1], raw_zx), ("next_store", wzx_ref, zx_next)]
    for name, src, dst in plan + later:
        loads[name] = pltpu.make_async_copy(src, dst, load_sem.at[len(loads)])
    for name, src, dst in plan:
        loads[name].start()
    partner = meet(count, False)

    if not ready:
        find_documents(seg_ref, dcol_ref, dloc_ref, drow_ref, column)
    normed_ref[...] = rms_scaled(h_ref[...].astype(f32), gain_mix_ref[...]).astype(bf16)
    normed = normed_ref[...]
    own = pl.ds(pl.multiple_of(place * rows, rows), rows)
    for j in range(count):
        @pl.when(j > place)
        def _():
            kv_in[j * rows:(j + 1) * rows, :] = jnp.zeros((rows, 2 * HD), bf16)
    loads["kv"].wait()
    kv_in[own, :] = nn(normed, wkv_ref[...]).astype(bf16)
    kv_copies = [
        remote(kv_in.at[own], kv_in.at[own], kv_send.at[j - 1], kv_recv.at[j - 1], "seq", place + j)
        for j in range(1, count)
    ]
    for j in range(1, count):
        @pl.when(place + j < count)
        def _():
            kv_copies[j - 1].start()
    loads["bc"].wait()
    stack_ref[:, d_local:] = nn(normed, wbc_ref[...]).astype(bf16)
    loads["zx"].wait()
    if not ready:
        unpack(raw_zx, wzx_ref)
        loads["zx_store"].start()
    if follows:
        loads["next"].start()
    stack_ref[:, :d_local] = nn(normed, wzx_ref[:, d_local:]).astype(bf16)
    rim_copy = remote(stack_ref.at[pl.ds(rows - RIM, RIM)], rim_in, rim_send, rim_recv, "seq", place + 1)

    @pl.when(place + 1 < count)
    def _():
        rim_copy.start()

    @pl.when(place == 0)
    def _():
        rim_in[...] = jnp.zeros(rim_in.shape, bf16)
        chain_in[...] = jnp.zeros(chain_in.shape, bf16)
    dt_ref[...] = nn(normed, wdt_ref[...]).astype(bf16).astype(f32)
    gate_ref[...] = nn(normed, wzx_ref[:, :d_local]).astype(bf16)
    loads["q"].wait()
    q_ref[...] = nn(normed, wq_ref[...]).astype(bf16)
    raw, step, log_decay, running, running_t, ordered = ssm_scalars(dt_ref, heads_ref)
    mapping = head_map(heads, d_local // heads)
    last = running[rows - 1:rows, :]
    fade = jnp.exp(last - running) * dcol_ref[:, 5:6]
    dec = jnp.exp(running) * dcol_ref[:, 4:5]
    ends = jnp.exp(running_t[:, rows - 1:rows]) * dcol_ref[rows - 1:rows, 4:5] + jnp.zeros((128, NS), f32)
    ends = spread_rows(ends, mapping)
    steps = spread(step, mapping)
    ext[RIM:, :] = stack_ref[...].astype(f32)

    @pl.when(place > 0)
    def _():
        rim_copy.wait_recv()
    rim_ref[...] = rim_in[...]
    ext[0:RIM, :] = rim_in[...].astype(f32)
    pre = ext[RIM:RIM + rows, :] * taps_ref[0:1, :]
    for k in range(1, 4):
        pre = pre + ext[RIM - k:RIM - k + rows, :] * dcol_ref[:, k:k + 1] * taps_ref[k:k + 1, :]
    pre_ref[...] = pre
    mixed = pre_ref[...] * sigmoid(pre_ref[...])
    values = mixed[:, :d_local]
    b_rows = mixed[:, d_local:d_local + NS].astype(bf16)
    c_rows = mixed[:, d_local + NS:].astype(bf16)
    stepped = values * steps
    state = tn((stepped * spread(fade, mapping)).astype(bf16), b_rows)
    y[...] = values * spread(heads_ref[2:3, :] + jnp.zeros((8, 128), f32), mapping)[0:1, :]
    linked = ordered & (dcol_ref[:, 0:1] == dloc_ref[0:1, :])
    cb = jnp.where(linked, nt(c_rows, b_rows), 0.0)
    stepped = stepped.astype(bf16)
    lane = lax.broadcasted_iota(jnp.int32, (rows, 128), 1)

    for j in range(1, count):
        @pl.when(place - j >= 0)
        def _():
            kv_copies[j - 1].wait_recv()
    allowed = score_mask(dcol_ref, drow_ref)
    keyvals = kv_in[...]
    kvall_ref[...] = keyvals
    keys, vals = keyvals[:, :HD], keyvals[:, HD:]
    totals = jnp.zeros((rows, 128), f32)
    pairs = heads // 2
    query_heads = q_ref.shape[1] // HD
    chain_copies = []
    for pair in range(pairs):
        span = slice(pair * 128, pair * 128 + 128)
        copy = remote(chain_out.at[pl.ds(pair * 128, 128)], chain_in.at[pl.ds(pair * 128, 128)],
                      chain_send.at[pair], chain_recv.at[pair], "seq", place + 1)
        chain_copies.append(copy)

        @pl.when(place > 0)
        def _():
            copy.wait_recv()
        chain_out[span, :] = (ends[span] * chain_in[span, :].astype(f32) + state[span]).astype(bf16)

        @pl.when(place + 1 < count)
        def _():
            copy.start()
        sides = []
        for h in (2 * pair, 2 * pair + 1):
            gap = running[:, h:h + 1] - running_t[h:h + 1, :]
            mixing = (jnp.exp(jnp.minimum(gap, 0.0)) * cb).astype(bf16)
            sides.append(nn(mixing, stepped[:, span]))
        y[:, span] += jnp.where(lane < 64, sides[0], sides[1])
        for h in range(query_heads * pair // pairs, query_heads * (pair + 1) // pairs):
            query = q_ref[:, h * HD:(h + 1) * HD] * jnp.asarray(HD ** -0.5, bf16)
            scores = jnp.where(allowed, nt(query, keys), masked_score)
            peak = jnp.max(scores, axis=1, keepdims=True)
            expo = jnp.exp(scores - peak)
            total = jnp.sum(expo, axis=1, keepdims=True)
            probs = (expo * (1.0 / total)).astype(bf16)
            att_ref[:, h * HD:(h + 1) * HD] = nn(probs, vals).astype(bf16)
            totals = jnp.where(lane == h, peak + jnp.log(total), totals)
    lse_ref[...] = totals
    mem_ref[...] = chain_in[...]
    decs = spread(dec, mapping)
    carried = decs * nt(c_rows, mem_ref[...])
    gate = gate_ref[...].astype(f32)
    gated_ref[...] = ((y[...] + carried) * (gate * sigmoid(gate))).astype(bf16)
    loads["out"].wait()
    loads["o"].wait()
    chunks = [pl.ds(begin, CHUNK) for begin in range(0, rows, CHUNK)]
    part_copies, down_copies = [], []
    for i, chunk in enumerate(chunks):
        part_out[chunk, :] = (nn(gated_ref[chunk, :], wout_ref[...])
                              + nn(att_ref[chunk, :], wo_ref[...])).astype(bf16)
        copy = remote(part_out.at[chunk], part_in.at[chunk], part_send.at[i], part_recv.at[i], "head", partner)
        copy.start()
        part_copies.append(copy)
    loads["gu"].wait()
    unpack(raw_gu, wgu_ref)
    loads["gu_store"].start()
    loads["down"].wait()
    for i, chunk in enumerate(chunks):
        part_copies[i].wait_recv()
        middle_ref[chunk, :] = h_ref[chunk, :].astype(f32) + (
            part_out[chunk, :].astype(f32) + part_in[chunk, :].astype(f32))
        nff_ref[chunk, :] = rms_scaled(middle_ref[chunk, :], gain_ff_ref[...]).astype(bf16)
        gu_ref[chunk, :] = nn(nff_ref[chunk, :], wgu_ref[...]).astype(bf16)
        gate = gu_ref[chunk, :ff_local].astype(f32)
        inner_ref[chunk, :] = (gate * sigmoid(gate) * gu_ref[chunk, ff_local:].astype(f32)).astype(bf16)
        down_out[chunk, :] = nn(inner_ref[chunk, :], wdown_ref[...]).astype(bf16)
        copy = remote(down_out.at[chunk], down_in.at[chunk], down_send.at[i], down_recv.at[i], "head", partner)
        copy.start()
        down_copies.append(copy)
    if not ready:
        loads["zx_store"].wait()
    if follows:
        loads["next"].wait()
        unpack(raw_zx, wzx_ref)
        loads["next_store"].start()
    for i, chunk in enumerate(chunks):
        down_copies[i].wait_recv()
        h_out[chunk, :] = (middle_ref[chunk, :] + (
            down_out[chunk, :].astype(f32) + down_in[chunk, :].astype(f32))).astype(bf16)
    loads["gu_store"].wait()
    if follows:
        loads["next_store"].wait()
    for i in range(len(chunks)):
        part_copies[i].wait_send()
        down_copies[i].wait_send()

    @pl.when(place + 1 < count)
    def _():
        rim_copy.wait_send()
        for copy in chain_copies:
            copy.wait_send()
    for j in range(1, count):
        @pl.when(place + j < count)
        def _():
            kv_copies[j - 1].wait_send()


def layer_forward(layer, hidden, zx, w, context):
    rows, model_width = hidden.shape
    heads = w["heads"]
    layers = w["out"].shape[0]
    d_local = w["out"].shape[1]
    ff_local = w["down"].shape[1]
    q_width = w["q"].shape[2]
    width = d_local + 2 * NS
    count = lax.axis_size("seq")
    length = count * rows
    parts = rows // CHUNK
    wide = ((model_width, 2 * d_local), bf16)
    outs = [
        ((rows, model_width), bf16), ((rows, model_width), bf16), ((rows, d_local), bf16), ((rows, width), bf16),
        ((RIM, width), bf16), ((rows, width), f32), ((rows, 128), f32), ((rows, q_width), bf16),
        ((length, 2 * HD), bf16), ((rows, q_width), bf16), ((rows, 128), f32), ((d_local, NS), bf16),
        ((rows, d_local), bf16), ((rows, model_width), f32), ((rows, model_width), bf16),
        ((rows, 2 * ff_local), bf16), ((rows, ff_local), bf16), ((model_width, 2 * ff_local), bf16),
    ]
    kept = len(outs) - 1
    documents = [((rows, 128), f32), ((8, rows), f32), ((8, length), f32)] if layer == 0 else []
    outs += documents
    outs += [wide] * ((layer == 0) + (layer + 1 < layers))
    full = (rows, model_width)
    given = [] if layer == 0 else [zx]
    result = pl.pallas_call(
        functools.partial(layer_forward_kernel, heads, layer, layers),
        out_shape=[jax.ShapeDtypeStruct(shape, kind) for shape, kind in outs],
        in_specs=[VM] * (6 + len(context)) + [ANY] * (8 + len(given)),
        out_specs=[VM] * kept + [ANY] + [VM] * len(documents) + [ANY] * (len(outs) - kept - 1 - len(documents)),
        scratch_shapes=[
            pltpu.VMEM((rows + RIM, width), f32), pltpu.VMEM((rows, d_local), f32),
            pltpu.VMEM((model_width, 2 * HD), bf16), pltpu.VMEM((model_width, 2 * NS), bf16),
            pltpu.VMEM((model_width, 2 * d_local), bf16), pltpu.VMEM((model_width, q_width), bf16),
            pltpu.VMEM((q_width, model_width), bf16), pltpu.VMEM((d_local, model_width), bf16),
            pltpu.VMEM((model_width, 2 * ff_local), bf16), pltpu.VMEM((ff_local, model_width), bf16),
            pltpu.VMEM((model_width, 2, d_local), bf16), pltpu.VMEM((model_width, 2, ff_local), bf16),
            pltpu.VMEM((RIM, width), bf16), pltpu.VMEM((length, 2 * HD), bf16),
            pltpu.VMEM((d_local, NS), bf16), pltpu.VMEM((d_local, NS), bf16),
            pltpu.VMEM(full, bf16), pltpu.VMEM(full, bf16), pltpu.VMEM(full, bf16), pltpu.VMEM(full, bf16),
            DMA((12,)), DMA((count - 1,)), DMA((count - 1,)), DMA, DMA, DMA((heads // 2,)), DMA((heads // 2,)),
            DMA((parts,)), DMA((parts,)), DMA((parts,)), DMA((parts,)),
            *([pltpu.VMEM((rows + 8, 128), f32)] if layer == 0 else []),
        ],
        compiler_params=pltpu.CompilerParams(
            vmem_limit_bytes=VMEM_LIMIT, collective_id=layer, has_side_effects=True),
    )(hidden, w["gain_mix"][layer], w["gain_ff"][layer], w["dt"][layer], w["taps"][layer], w["head_vals"][layer],
      *context, w["kv"], w["bc"], w["zx"], w["q"], w["out"], w["o"], w["gu"], w["down"], *given)
    names = ("out", "normed", "gate", "stack", "rim", "pre", "dt", "q", "kv", "att", "lse", "memory",
             "gated", "middle", "nff", "gu", "inner", "w_gu")
    saved = dict(zip(names, result))
    saved["hidden"] = hidden
    extra = list(result[len(names):])
    if layer == 0:
        context = [extra.pop(0) for _ in range(3)]
    saved["w_zx"] = extra.pop(0) if layer == 0 else zx
    return saved.pop("out"), (extra.pop(0) if extra else None), context, saved


def norm_back(hidden, gain, grad):
    inverse = lax.rsqrt(jnp.mean(hidden * hidden, axis=-1, keepdims=True) + norm_eps)
    scaled = grad * gain
    lean = jnp.mean(scaled * hidden, axis=-1, keepdims=True)
    grad_gain = jnp.sum(grad * hidden * inverse, axis=0, keepdims=True)
    return inverse * (scaled - hidden * (inverse * inverse * lean)), grad_gain


def store_blocks(compute, slots, out, sems):
    size = slots.shape[1]
    columns = out.shape[1]
    blocks = out.shape[0] // size

    def rows(i):
        return pl.ds(pl.multiple_of(i * size, size), size)

    def copy(i, slot):
        return pltpu.make_async_copy(slots.at[slot, :, pl.ds(0, columns)], out.at[rows(i)], sems.at[slot])

    def one(i, carry):
        slot = lax.rem(i, 2)

        @pl.when(i >= 2)
        def _():
            copy(i - 2, slot).wait()
        compute(rows(i), slot)
        copy(i, slot).start()
        return carry
    lax.fori_loop(0, blocks, one, 0)
    for i in range(max(0, blocks - 2), blocks):
        copy(i, i % 2).wait()


def layer_backward_kernel(heads, layer, schedule, grad_ref, h_ref, normed_ref, gate_ref, stack_ref, rim_ref, pre_ref, dt_ref,
                          q_ref, kv_ref, att_ref, lse_ref, mem_ref, gated_ref, middle_ref, nff_ref, gu_ref,
                          inner_ref, gain_mix_ref, gain_ff_ref, wdt_ref,
                          taps_ref, heads_ref, dcol_ref, dloc_ref, drow_ref,
                          wdown_hbm, wgu_hbm, wout_hbm, wo_hbm, wzx_hbm, wbc_hbm, wq_hbm, wkv_hbm, *refs):
    refs = list(refs)
    own_sum = schedule["own"]
    source = None if own_sum else refs.pop(0)
    half_in = None if own_sum else refs.pop(0)
    if not own_sum:
        next_refs, refs = refs[-LINE_REFS:], refs[:-LINE_REFS]
        line_refs, refs = refs[-LINE_REFS - 1:], refs[:-LINE_REFS - 1]
    cross_refs, refs = refs[-CROSS_REFS:], refs[:-CROSS_REFS]
    summed_ref = None if own_sum else refs.pop(0)
    (g_out, gff_out, gmix_out, gbc_out, small_ref, half_ref,
     wdown_ref, wide_ref, wout_ref, wo_ref, wbc_ref, wq_ref, wkv_ref,
     gff, dgu, one_out, one_in, two_out, two_in, gmid, branch, gg, datt, dy_s, dxs_s, u_s,
     decay_s, probs_s, acc, dkv_out, dkv_in, chain_in, chain_out, rim_in,
     ext, pad, dext, dgate, dstack, dq, dkv, draw_s,
     load_sem, one_send, one_recv, two_send, two_recv, chain_send, chain_recv,
     rim_send, rim_recv, kv_send, kv_recv, gblk, grad_sem) = refs
    rows = dt_ref.shape[0]
    d_local = gate_ref.shape[1]
    ff_local = inner_ref.shape[1]
    q_width = q_ref.shape[1]
    model_width = h_ref.shape[1]
    width = pre_ref.shape[1]
    length = kv_ref.shape[0]
    count = lax.axis_size("seq")
    place = lax.axis_index("seq")
    wgu_ref = wide_ref.at[:, pl.ds(0, 2 * ff_local)]
    wzx_ref = wide_ref.at[:, pl.ds(0, 2 * d_local)]
    loads = {}
    for name, src, dst in (
        ("down", wdown_hbm.at[layer], wdown_ref), ("gu", wgu_hbm, wgu_ref), ("out", wout_hbm.at[layer], wout_ref),
        ("o", wo_hbm.at[layer], wo_ref), ("bc", wbc_hbm.at[layer], wbc_ref), ("q", wq_hbm.at[layer], wq_ref),
        ("kv", wkv_hbm.at[layer], wkv_ref), ("zx", wzx_hbm, wzx_ref),
    ):
        loads[name] = pltpu.make_async_copy(src, dst, load_sem.at[len(loads)])
    for name in ("down", "gu", "out", "o", "bc", "q", "kv"):
        loads[name].start()
    partner = meet(count, True, greet_sums)
    cross = CrossSum(cut_columns([gff_out if own_sum else source]), cross_refs[:3], cross_refs[3:])
    ranges = [columns for _, columns in cut_columns([half_ref])]
    steps_of = {"a": cross.step_a, "b": lambda n: cross.step_b(n, half_ref.at[:, ranges[n]])}
    if not own_sum:
        fetches = [pltpu.make_async_copy(half_in.at[:, columns], line_refs[0].at[n], load_sem.at[len(loads) + n])
                   for n, (_, columns) in enumerate(cut_columns([half_in]))]
        for fetch in fetches:
            fetch.start()
        for fetch in fetches:
            fetch.wait()
        line = LineSum([line_refs[0].at[n] for n in range(UNITS)], *line_refs[1:])

        def write(n, terms):
            size = terms[0].shape[1]
            add_rows(summed_ref.at[:, pl.ds(n * size, size)], terms)
        follow = LineSum([half_ref.at[:, columns] for columns in ranges[:BEGUN]], *next_refs)
        steps_of.update({"f": follow.step_c, "g": lambda n: follow.take_in(n, 0)})
        steps_of.update({"c": line.step_c, "d": line.step_d, "e": lambda n: line.step_e(n, write)})

    def pump(spot):
        for step in schedule.get(spot, ()):
            if step == "start":
                cross.start()
            elif step == "finish":
                cross.finish()
                if not own_sum:
                    line.finish()
                    follow.finish()
            else:
                steps_of[step[0]](int(step[1]))
    pump("begin")
    chunks = [pl.ds(begin, CHUNK) for begin in range(0, rows, CHUNK)]

    gff[...] = grad_ref[...].astype(bf16)
    loads["down"].wait()
    loads["gu"].wait()
    one_copies, two_copies = [], []
    for i, chunk in enumerate(chunks):
        grad_inner = nt(gff[chunk, :], wdown_ref[...])
        gate = gu_ref[chunk, :ff_local].astype(f32)
        up = gu_ref[chunk, ff_local:].astype(f32)
        sig = sigmoid(gate)
        dgu[chunk, :ff_local] = (grad_inner * up * (sig * (1.0 + gate * (1.0 - sig)))).astype(bf16)
        dgu[chunk, ff_local:] = (grad_inner * (gate * sig)).astype(bf16)
        one_out[chunk, :] = nt(dgu[chunk, :], wgu_ref[...]).astype(bf16)
        copy = remote(one_out.at[chunk], one_in.at[chunk], one_send.at[i], one_recv.at[i], "head", partner)
        copy.start()
        one_copies.append(copy)
    loads["zx"].start()

    @pl.when(place == count - 1)
    def _():
        rim_in[...] = jnp.zeros(rim_in.shape, f32)
        chain_in[...] = jnp.zeros(chain_in.shape, bf16)
    for j in range(1, count):
        @pl.when(place + j >= count)
        def _():
            dkv_in[(j - 1) * rows:j * rows, :] = jnp.zeros((rows, 2 * HD), bf16)

    pump("ff0")

    def ff_weights(block, slot):
        gblk[slot, :, :ff_local] = tn(gff[:, block], inner_ref[...]).astype(bf16)
        gblk[slot, :, ff_local:3 * ff_local] = tn(nff_ref[:, block], dgu[...]).astype(bf16)
    store_blocks(ff_weights, gblk, gff_out, grad_sem)
    pump("ff")

    raw, step, log_decay, running, running_t, ordered = ssm_scalars(dt_ref, heads_ref)
    mapping = head_map(heads, d_local // heads)
    last = running[rows - 1:rows, :]
    fade = spread(jnp.exp(last - running) * dcol_ref[:, 5:6], mapping)
    dec = jnp.exp(running) * dcol_ref[:, 4:5]
    decs = spread(dec, mapping)
    ends = jnp.exp(running_t[:, rows - 1:rows]) * dcol_ref[rows - 1:rows, 4:5] + jnp.zeros((128, NS), f32)
    ends = spread_rows(ends, mapping)
    steps = spread(step, mapping)
    skip = spread(heads_ref[2:3, :] + jnp.zeros((8, 128), f32), mapping)[0:1, :]
    pre_v = pre_ref[:, :d_local]
    values = pre_v * sigmoid(pre_v)
    pre_n = pre_ref[:, d_local:]
    maps = (pre_n * sigmoid(pre_n)).astype(bf16)
    b_rows, c_rows = maps[:, :NS], maps[:, NS:]
    stepped = (values * steps).astype(bf16)
    linked = ordered & (dcol_ref[:, 0:1] == dloc_ref[0:1, :])
    cb = jnp.where(linked, nt(c_rows, b_rows), 0.0)
    lane = lax.broadcasted_iota(jnp.int32, (rows, 128), 1)
    pairs = heads // 2
    for pair in range(pairs):
        span = slice(pair * 128, pair * 128 + 128)
        sides = []
        for h in (2 * pair, 2 * pair + 1):
            at = slice(h * rows, (h + 1) * rows)
            gap = running[:, h:h + 1] - running_t[h:h + 1, :]
            decay = jnp.exp(jnp.minimum(gap, 0.0))
            decay_s[:, at] = decay.astype(bf16)
            mixing = (decay_s[:, at].astype(f32) * cb).astype(bf16)
            sides.append(nn(mixing, stepped[:, span]))
        u_s[:, span] = jnp.where(lane < 64, sides[0], sides[1])
    allowed = score_mask(dcol_ref, drow_ref)
    keyvals = kv_ref[...]
    keys, vals = keyvals[:, :HD], keyvals[:, HD:]
    scale = jnp.asarray(HD ** -0.5, bf16)
    query_heads = q_width // HD
    for h in range(query_heads):
        query = q_ref[:, h * HD:(h + 1) * HD] * scale
        scores = jnp.where(allowed, nt(query, keys), masked_score)
        probs_s[:, h * length:(h + 1) * length] = jnp.exp(scores - lse_ref[:, h:h + 1]).astype(bf16)
    ext[0:RIM, :] = rim_ref[...].astype(f32)
    ext[RIM:, :] = stack_ref[...].astype(f32)
    gate = gate_ref[...].astype(f32)
    gate_sig = sigmoid(gate)
    gate_act = gate * gate_sig
    loads["out"].wait()
    loads["o"].wait()
    dtaps_ref = small_ref.at[pl.ds(0, 8)]
    gains_ref = small_ref.at[pl.ds(8, 8)]
    gains_ref[...] = jnp.zeros(gains_ref.shape, f32)
    for i, chunk in enumerate(chunks):
        pump("one%d" % i)
        one_copies[i].wait_recv()
        grad = one_out[chunk, :].astype(f32) + one_in[chunk, :].astype(f32)
        moved, gain = norm_back(middle_ref[chunk, :], gain_ff_ref[...], grad)
        gains_ref[1:2, :] += gain
        gmid[chunk, :] = grad_ref[chunk, :].astype(f32) + moved
        branch[chunk, :] = gmid[chunk, :].astype(bf16)
        gg[chunk, :] = nt(branch[chunk, :], wout_ref[...])
        datt[chunk, :] = nt(branch[chunk, :], wo_ref[...]).astype(bf16)
    grad_ssm = gg[...] * gate_act
    dy_s[...] = grad_ssm.astype(bf16)
    push = tn((grad_ssm * decs).astype(bf16), c_rows)
    dcb = jnp.zeros((rows, rows), f32)
    chain_copies = []
    for pair in range(pairs):
        pump("pair%d" % pair)
        span = slice(pair * 128, pair * 128 + 128)
        copy = remote(chain_out.at[pl.ds(pair * 128, 128)], chain_in.at[pl.ds(pair * 128, 128)],
                      chain_send.at[pair], chain_recv.at[pair], "seq", place - 1)
        chain_copies.append(copy)

        @pl.when(place < count - 1)
        def _():
            copy.wait_recv()
        chain_out[span, :] = (ends[span] * chain_in[span, :].astype(f32) + push[span]).astype(bf16)

        @pl.when(place > 0)
        def _():
            copy.start()
        stepped_p = stepped[:, span]
        dy_p = dy_s[:, span]
        dxs = []
        for side, h in enumerate((2 * pair, 2 * pair + 1)):
            at = slice(h * rows, (h + 1) * rows)
            decay = decay_s[:, at].astype(f32)
            dxs.append(tn((decay * cb).astype(bf16), dy_p))
            half = jnp.where((lane < 64) == (side == 0), dy_p, jnp.zeros_like(dy_p))
            dcb = dcb + nt(half, stepped_p) * decay
        dxs_s[:, span] = jnp.where(lane < 64, dxs[0], dxs[1])
        for h in range(query_heads * pair // pairs, query_heads * (pair + 1) // pairs):
            part = slice(h * HD, (h + 1) * HD)
            query = q_ref[:, part] * scale
            grad = datt[:, part]
            delta = jnp.sum(grad.astype(f32) * att_ref[:, part].astype(f32), axis=1, keepdims=True)
            probs = probs_s[:, h * length:(h + 1) * length]
            grad_scores = (probs.astype(f32) * (nt(grad, vals) - delta)).astype(bf16)
            dq[:, part] = (nn(grad_scores, keys) * HD ** -0.5).astype(bf16)
            dk = tn(grad_scores, query)
            dv = tn(probs, grad)
            if h == 0:
                acc[:, :HD] = dk
                acc[:, HD:] = dv
            else:
                acc[:, :HD] += dk
                acc[:, HD:] += dv
    dkv_out[...] = acc[...].astype(bf16)
    kv_copies = []
    for j in range(1, count):
        target = jnp.maximum(place - j, 0)
        theirs = pl.ds(pl.multiple_of(target * rows, rows), rows)
        copy = remote(dkv_out.at[theirs], dkv_in.at[pl.ds((j - 1) * rows, rows)], kv_send.at[j - 1],
                      kv_recv.at[j - 1], "seq", place - j)
        kv_copies.append(copy)

        @pl.when(place >= j)
        def _():
            copy.start()
    pump("post")
    memory = mem_ref[...]
    gmem = chain_in[...]
    carried = decs * nt(c_rows, memory)
    back = fade * nt(b_rows, gmem)
    dy_low = dy_s[...].astype(f32)
    stepped_f = stepped.astype(f32)
    dxs_all = dxs_s[...] + back
    dxs_s[...] = dxs_all
    dcb = jnp.where(linked, dcb, 0.0).astype(bf16)
    dc = nn(dcb, b_rows) + nn((dy_low * decs).astype(bf16), memory)
    db = tn(dcb, c_rows) + nn((stepped_f * fade).astype(bf16), gmem)
    dvalues = steps * dxs_all + skip * grad_ssm
    pad[0:8, :] = jnp.zeros((8, width), f32)
    pad[8 + rows:, :] = jnp.zeros((8, width), f32)
    sig = sigmoid(pre_v)
    pad[8:8 + rows, :d_local] = dvalues * (sig * (1.0 + pre_v * (1.0 - sig)))
    sig = sigmoid(pre_n)
    slope = sig * (1.0 + pre_n * (1.0 - sig))
    pad[8:8 + rows, d_local:d_local + NS] = db * slope[:, :NS]
    pad[8:8 + rows, d_local + NS:] = dc * slope[:, NS:]
    dpre = pad[8:8 + rows, :]
    dext[...] = pad[0:8 + rows, :] * taps_ref[0:1, :]
    dtaps_ref[...] = jnp.zeros((8, width), f32)
    dtaps_ref[0:1, :] = jnp.sum(dpre * ext[RIM:RIM + rows, :], axis=0, keepdims=True)
    for k in range(1, 4):
        masked = dpre * dcol_ref[:, k:k + 1]
        pad[8:8 + rows, :] = masked
        dtaps_ref[k:k + 1, :width] = jnp.sum(masked * ext[RIM - k:RIM - k + rows, :], axis=0, keepdims=True)
        dext[...] += pad[k:k + 8 + rows, :] * taps_ref[k:k + 1, :]
    rim_copy = remote(dext.at[pl.ds(0, 8)], rim_in, rim_send, rim_recv, "seq", place - 1)

    @pl.when(place > 0)
    def _():
        rim_copy.start()
    scanned = u_s[...] + carried
    drun = gather(dy_low * scanned - stepped_f * dxs_all, mapping)
    ssm_out = scanned + skip * values
    dgate[...] = (gg[...] * ssm_out * (gate_sig * (1.0 + gate * (1.0 - gate_sig)))).astype(bf16)
    gstep = gather(values * dxs_all, mapping)
    ones = jnp.ones((8, 128), bf16)
    high, low = split(gmem.astype(f32) * memory.astype(f32), 2)
    moved = nt(ones, high) + nt(ones, low)
    end = gather(jnp.sum(stepped_f * back, axis=0, keepdims=True) + jnp.zeros((8, 1), f32), mapping)
    end = end + gather(moved, mapping) * dec[rows - 1:rows, :]
    upper = (lax.broadcasted_iota(jnp.int32, (rows, rows), 1)
             >= lax.broadcasted_iota(jnp.int32, (rows, rows), 0)).astype(bf16)
    dlog = triangle_sum(upper, drun) + end[0:1, :]
    draw = (gstep - jnp.exp(heads_ref[1:2, :]) * dlog) * sigmoid(raw)
    draw_s[...] = draw.astype(bf16)
    dskip = gather(jnp.sum(grad_ssm * values, axis=0, keepdims=True) + jnp.zeros((8, 1), f32), mapping)
    small_ref[4:5, :128] = jnp.sum(draw, axis=0, keepdims=True)
    small_ref[5:6, :128] = jnp.sum(dlog * log_decay, axis=0, keepdims=True)
    small_ref[6:7, :128] = dskip[0:1, :]
    for name in ("zx", "bc", "q", "kv"):
        loads[name].wait()

    for j in range(1, count):
        @pl.when(place + j < count)
        def _():
            kv_copies[j - 1].wait_recv()
    pump("two")
    own = pl.ds(pl.multiple_of(place * rows, rows), rows)
    total = acc[own, :]
    for j in range(1, count):
        total = total + dkv_in[(j - 1) * rows:j * rows, :].astype(f32)
    dkv[...] = total.astype(bf16)

    for i, chunk in enumerate(chunks):
        if i == len(chunks) - 1:
            @pl.when(place < count - 1)
            def _():
                rim_copy.wait_recv()
            dext[rows:rows + 8, :] += rim_in[...]
        dstack[chunk, :] = dext[8 + i * CHUNK:8 + (i + 1) * CHUNK, :].astype(bf16)
        two_out[chunk, :] = (
            nt(dgate[chunk, :], wzx_ref[:, :d_local]) + nt(dstack[chunk, :d_local], wzx_ref[:, d_local:])
            + nt(dstack[chunk, d_local:], wbc_ref[...]) + nt(draw_s[chunk, :], wdt_ref[...])
            + nt(dq[chunk, :], wq_ref[...]) + nt(dkv[chunk, :], wkv_ref[...])
        ).astype(bf16)
        copy = remote(two_out.at[chunk], two_in.at[chunk], two_send.at[i], two_recv.at[i], "head", partner)
        copy.start()
        two_copies.append(copy)

    gbc_out[:, model_width:] = jnp.transpose(jnp.concatenate(
        [dtaps_ref[0:4, d_local:], jnp.zeros((124, 2 * NS), f32)], axis=0)).astype(bf16)
    pump("mix")

    def mix_weights(block, slot):
        left = normed_ref[:, block]
        at = 0
        for right in (dgate[...], dstack[:, :d_local], dq[...], dkv[...], draw_s[...]):
            gblk[slot, :, at:at + right.shape[1]] = tn(left, right).astype(bf16)
            at += right.shape[1]
        left = branch[:, block]
        for right in (gated_ref[...], att_ref[...]):
            gblk[slot, :, at:at + right.shape[1]] = tn(left, right).astype(bf16)
            at += right.shape[1]
        gbc_out[:, block] = tn(dstack[:, d_local:], normed_ref[:, block]).astype(bf16)
    store_blocks(mix_weights, gblk, gmix_out, grad_sem)

    for i, chunk in enumerate(chunks):
        pump("last%d" % i)
        two_copies[i].wait_recv()
        grad = two_out[chunk, :].astype(f32) + two_in[chunk, :].astype(f32)
        moved, gain = norm_back(h_ref[chunk, :].astype(f32), gain_mix_ref[...], grad)
        gains_ref[0:1, :] += gain
        g_out[chunk, :] = gmid[chunk, :] + moved
    pump("end")
    for i in range(len(chunks)):
        one_copies[i].wait_send()
        two_copies[i].wait_send()

    @pl.when(place > 0)
    def _():
        rim_copy.wait_send()
        for copy in chain_copies:
            copy.wait_send()
    for j in range(1, count):
        @pl.when(place >= j)
        def _():
            kv_copies[j - 1].wait_send()


SCHEDULES = (
    {"own": False, "begin": ("start", "c0", "c1", "c2", "c3"), "ff0": ("a0", "a1", "a2", "a3"), "ff": ("d0", "d1"),
     "one0": ("d2",), "one1": ("d3",), "post": ("b0", "b1"), "two": ("f0", "f1"), "mix": ("b2",),
     "last0": ("e0", "e1", "e2", "e3"), "last1": ("b3",), "end": ("g0", "g1", "finish")},
    {"own": True, "ff": ("start",), "one0": ("a0", "a1"), "one1": ("a2", "a3"), "mix": ("b0",), "last0": ("b1", "b2"),
     "end": ("b3", "finish")},
)


def layer_backward(layer, grad, waiting, w, saved, context):
    dcol, dloc, drow = context
    rows, model_width = grad.shape
    heads = w["heads"]
    d_local = w["out"].shape[1]
    ff_local = w["down"].shape[1]
    q_width = w["q"].shape[2]
    width = d_local + 2 * NS
    count = lax.axis_size("seq")
    length = count * rows
    parts = rows // CHUNK
    mix_width = 3 * d_local + 2 * q_width + 256
    schedule = SCHEDULES[1 if waiting is None else 0]
    given = [] if waiting is None else list(waiting)
    outs = [
        ((rows, model_width), f32), ((model_width, 3 * ff_local), bf16), ((model_width, mix_width), bf16),
        ((2 * NS, model_width + 128), bf16), ((16, max(width, model_width)), f32),
    ]
    span = model_width // lax.axis_size("dp")
    if waiting is not None:
        outs.insert(0, ((span // count, 3 * ff_local), f32))
    outs.append(((span, 3 * ff_local if waiting is None else mix_width), bf16))
    full = (rows, model_width)
    state = (d_local, NS)
    names = ("hidden", "normed", "gate", "stack", "rim", "pre", "dt", "q", "kv", "att", "lse", "memory",
             "gated", "middle", "nff", "gu", "inner")

    def vm(shape, kind):
        return pltpu.VMEM(shape, kind)
    return pl.pallas_call(
        functools.partial(layer_backward_kernel, heads, layer, schedule),
        out_shape=[jax.ShapeDtypeStruct(shape, kind) for shape, kind in outs],
        in_specs=[VM] * 26 + [ANY] * (8 + len(given)),
        out_specs=[VM] * (len(outs) - 5) + [ANY, ANY] + [VM] * 3,
        scratch_shapes=[
            vm((ff_local, model_width), bf16), vm((model_width, 2 * max(d_local, ff_local)), bf16),
            vm((d_local, model_width), bf16), vm((q_width, model_width), bf16), vm((model_width, 2 * NS), bf16),
            vm((model_width, q_width), bf16), vm((model_width, 2 * HD), bf16),
            vm(full, bf16), vm((rows, 2 * ff_local), bf16), vm(full, bf16), vm(full, bf16), vm(full, bf16),
            vm(full, bf16), vm(full, f32), vm(full, bf16), vm((rows, d_local), f32), vm((rows, q_width), bf16),
            vm((rows, d_local), bf16), vm((rows, d_local), f32), vm((rows, d_local), f32),
            vm((rows, heads * rows), bf16),
            vm((rows, q_width // HD * length), bf16), vm((length, 2 * HD), f32), vm((length, 2 * HD), bf16),
            vm(((count - 1) * rows, 2 * HD), bf16), vm(state, bf16), vm(state, bf16), vm((8, width), f32),
            vm((rows + RIM, width), f32), vm((rows + 16, width), f32), vm((rows + 8, width), f32),
            vm((rows, d_local), bf16), vm((rows, width), bf16), vm((rows, q_width), bf16),
            vm((rows, 2 * HD), bf16), vm((rows, 128), bf16),
            DMA((8 + UNITS,)), DMA((parts,)), DMA((parts,)), DMA((parts,)), DMA((parts,)), DMA((heads // 2,)),
            DMA((heads // 2,)), DMA, DMA, DMA((count - 1,)), DMA((count - 1,)),
            vm((2, 128, max(3 * ff_local, mix_width)), bf16), DMA((2,)),
            *cross_scratch(UNITS, span, outs[-1][0][1]),
            *([] if waiting is None else
              [vm((UNITS, span, 3 * ff_local // UNITS), bf16), *line_scratch(UNITS, span, 3 * ff_local),
               *line_scratch(BEGUN, span, mix_width, count // 2)]),
        ],
        compiler_params=pltpu.CompilerParams(
            vmem_limit_bytes=VMEM_LIMIT, collective_id=2 + layer, has_side_effects=True),
    )(grad, *[saved[name] for name in names], w["gain_mix"][layer], w["gain_ff"][layer], w["dt"][layer],
      w["taps"][layer], w["head_vals"][layer], dcol, dloc, drow, w["down"], saved["w_gu"], w["out"], w["o"],
      saved["w_zx"], w["bc"], w["q"], w["kv"], *given)


def on_device(hidden_in, segment_ids, gain_mix, w_zx, w_bc, w_dt, conv_x, conv_bc, ssm_head, w_q, w_kv,
              w_o, w_out, gain_ff, w_gu, w_down, cotangent):
    rows, model_width = hidden_in.shape
    taps_count = conv_x.shape[1]
    place = lax.axis_index("seq")
    context = (segment_ids,)
    layers = gain_mix.shape[0]
    heads = ssm_head.shape[2]
    d_local = w_zx.shape[3]
    w = dict(
        heads=heads,
        gain_mix=gain_mix[:, None].astype(f32),
        gain_ff=gain_ff[:, None].astype(f32),
        zx=w_zx,
        bc=w_bc,
        dt=jnp.pad(w_dt, ((0, 0), (0, 0), (0, 128 - heads))),
        q=w_q,
        kv=w_kv.reshape(layers, model_width, -1),
        o=w_o,
        out=w_out,
        gu=w_gu,
        down=w_down,
        taps=jnp.pad(jnp.concatenate([conv_x.reshape(layers, taps_count, -1), conv_bc], axis=2).astype(f32),
                     ((0, 0), (0, 8 - taps_count), (0, 0))),
        head_vals=jnp.pad(ssm_head, ((0, 0), (0, 5), (0, 128 - heads))),
    )
    hidden = hidden_in
    saved = []
    zx = None
    for l in range(layers):
        hidden, zx, context, kept = layer_forward(l, hidden, zx, w, context)
        saved.append(kept)
    block_out = hidden
    gradient = cotangent
    narrow, small = [None] * layers, [None] * layers
    waiting = None
    for l in reversed(range(layers)):
        *summed, gradient, ff_grads, mix_grads, narrow[l], small[l], half = layer_backward(
            l, gradient, waiting, w, saved[l], context)
        waiting = (mix_grads, half)
    shards = lax.axis_size("dp") * lax.axis_size("seq")
    shard = lax.axis_index("dp") * lax.axis_size("seq") + place
    ff_local = w_down.shape[1]
    q_width = w_q.shape[2]
    part = model_width // shards
    down, gu, zx, q, kv, dt, out, o, small, g_bc = last_sum(
        (ff_grads, mix_grads), half, summed[0], narrow, small,
        ((ff_local, -ff_local), (-d_local, q_width, 128, 128, d_local, q_width)))
    down, out, o = (jnp.transpose(a, (0, 2, 1)) for a in (down, out, o))
    kv = kv.reshape(layers, part, 1, 128)
    dt = dt[:, :, :heads]
    own = 2 * NS // (shards * lax.axis_size("head"))
    spot = place * lax.axis_size("head") + lax.axis_index("head")
    g_bc = lax.dynamic_slice_in_dim(g_bc, lax.rem(spot * own, g_bc.shape[1]), own, 1)
    w_bc_grad = jnp.transpose(g_bc[:, :, :model_width], (0, 2, 1))
    conv_bc_grad = jnp.transpose(g_bc[:, :, model_width:model_width + taps_count], (0, 2, 1))
    small = small.reshape(layers, -1, small.shape[1])
    gain_a = lax.dynamic_slice_in_dim(small[:, 8, :model_width], shard * part, part, 1)
    gain_b = lax.dynamic_slice_in_dim(small[:, 9, :model_width], shard * part, part, 1)
    taps = small[:, :taps_count, :d_local].reshape(layers, taps_count, heads, -1)
    taps_part = taps.shape[3] // shards
    conv_x_grad = lax.dynamic_slice_in_dim(taps, shard * taps_part, taps_part, 3)
    head_grad = small[:, 4:7, :heads]
    return (block_out, gradient, gain_a, zx, w_bc_grad, dt, conv_x_grad, conv_bc_grad, head_grad, q, kv,
            o, out, gain_b, gu, down)


def solution(mesh):
    in_specs = (
        P(("dp", "seq"), None),
        P("dp", None),
        P(),
        P(None, None, None, "head"),
        P(),
        P(None, None, "head"),
        P(None, None, "head", None),
        P(),
        P(None, None, "head"),
        P(None, None, "head"),
        P(None, None, "head", None),
        P(None, "head", None),
        P(None, "head", None),
        P(),
        P(None, None, None, "head"),
        P(None, "head", None),
        P(("dp", "seq"), None),
    )
    out_specs = (
        P(("dp", "seq"), None),
        P(("dp", "seq"), None),
        P(None, ("dp", "seq")),
        P(None, ("dp", "seq"), None, "head"),
        P(None, None, ("dp", "seq", "head")),
        P(None, ("dp", "seq"), "head"),
        P(None, None, "head", ("dp", "seq")),
        P(None, None, ("dp", "seq", "head")),
        P(None, None, "head"),
        P(None, ("dp", "seq"), "head"),
        P(None, ("dp", "seq"), "head", None),
        P(None, "head", ("dp", "seq")),
        P(None, "head", ("dp", "seq")),
        P(None, ("dp", "seq")),
        P(None, ("dp", "seq"), None, "head"),
        P(None, "head", ("dp", "seq")),
    )
    return jax.shard_map(
        on_device, mesh=mesh, in_specs=in_specs, out_specs=out_specs, check_vma=False
    )
```

```python
import functools

import jax
import jax.numpy as jnp
from jax import lax
from jax.experimental import pallas as pl
from jax.experimental.pallas import tpu as pltpu
from jax.sharding import PartitionSpec as P

NS = 128
HD = 64
RIM = 16

norm_eps = 1e-05
masked_score = -1e30
bf16 = jnp.bfloat16
f32 = jnp.float32
VMEM_LIMIT = 63 * 1024 * 1024


def nn(left, right):
    return jnp.dot(left, right, preferred_element_type=f32)


def tn(left, right):
    return lax.dot_general(left, right, (((0,), (0,)), ((), ())), preferred_element_type=f32)


def nt(left, right):
    return lax.dot_general(left, right, (((1,), (1,)), ((), ())), preferred_element_type=f32)


def split(v, terms):
    parts = []
    for _ in range(terms):
        parts.append(v.astype(bf16))
        v = v - parts[-1].astype(f32)
    return parts


def sigmoid(v):
    return 0.5 * jnp.tanh(0.5 * v) + 0.5


def softplus(v):
    return jnp.maximum(v, 0.0) + jnp.log(1.0 + jnp.exp(-jnp.abs(v)))


def head_map(heads, width):
    rows = lax.rem(lax.broadcasted_iota(jnp.int32, (256, heads * width), 0), 128)
    columns = lax.broadcasted_iota(jnp.int32, (256, heads * width), 1)
    return (columns // width == rows).astype(bf16)


def spread(scalars, mapping):
    return nn(jnp.concatenate(split(scalars, 2), axis=1), mapping)


def spread_rows(scalars, mapping):
    return tn(mapping, jnp.concatenate(split(scalars, 2), axis=0))


def gather(columns, mapping):
    high, low = split(columns, 2)
    return nt(high, mapping[:128]) + nt(low, mapping[:128])


def triangle_sum(triangle, v):
    width = v.shape[1]
    sums = nn(triangle, jnp.concatenate(split(v, 3), axis=1))
    return sums[:, :width] + sums[:, width:2 * width] + sums[:, 2 * width:]


def rms_scaled(hidden, gain):
    return hidden * lax.rsqrt(jnp.mean(hidden * hidden, axis=-1, keepdims=True) + norm_eps) * gain


def ssm_scalars(dt_ref, heads_ref):
    rows = dt_ref.shape[0]
    raw = dt_ref[...] + heads_ref[0:1, :]
    step = softplus(raw)
    log_decay = -jnp.exp(heads_ref[1:2, :]) * step
    place_t = lax.broadcasted_iota(jnp.int32, (rows, rows), 0)
    place_s = lax.broadcasted_iota(jnp.int32, (rows, rows), 1)
    running = triangle_sum((place_s <= place_t).astype(bf16), log_decay)
    running_t = jnp.transpose(running)
    return raw, step, log_decay, running, running_t, place_t >= place_s


def score_mask(dcol_ref, drow_ref):
    rows, length = dcol_ref.shape[0], drow_ref.shape[1]
    query_pos = lax.broadcasted_iota(jnp.int32, (rows, length), 0) + lax.axis_index("seq") * rows
    key_pos = lax.broadcasted_iota(jnp.int32, (rows, length), 1)
    return (key_pos <= query_pos) & (dcol_ref[:, 0:1] == drow_ref[0:1, :])


MESH_ID = pl.DeviceIdType.MESH
CHUNK = 128


def remote(src, dst, send, recv, axis, target):
    return pltpu.make_async_remote_copy(
        src_ref=src, dst_ref=dst, send_sem=send, recv_sem=recv,
        device_id={axis: target}, device_id_type=MESH_ID,
    )


def meet(count, later_sends, extra=None):
    place = lax.axis_index("seq")
    barrier = pltpu.get_barrier_semaphore()
    for j in range(1, count if extra is None else 1):
        here = place - j if not later_sends else place + j

        @pl.when((here >= 0) & (here < count))
        def _():
            pl.semaphore_signal(barrier, inc=1, device_id={"seq": here}, device_id_type=MESH_ID)
    heads_axis = lax.axis_size("head")
    partner = lax.rem(lax.axis_index("head") + 1, heads_axis)
    pl.semaphore_signal(barrier, inc=1, device_id={"head": partner}, device_id_type=MESH_ID)
    waits = (place if later_sends else count - 1 - place) + 1
    if extra is not None:
        waits = extra() + 1
    pl.semaphore_wait(barrier, waits)
    return partner


VM = pl.BlockSpec(memory_space=pltpu.VMEM)
ANY = pl.BlockSpec(memory_space=pl.ANY)
DMA = pltpu.SemaphoreType.DMA
UNITS = 4
LAST_UNITS = 8
BEGUN = 2


def add_rows(out, terms):
    rows = out.shape[0]
    size = min(64, rows)

    def one(i, carry):
        part = pl.ds(pl.multiple_of(i * size, size), size)
        total = terms[0][part, :].astype(f32)
        for term in terms[1:]:
            total = total + term[part, :].astype(f32)
        out[part, :] = total.astype(out.dtype)
        return carry
    lax.fori_loop(0, rows // size, one, 0)


def dp_spot():
    spot = lax.axis_index("dp")
    return lax.rem(spot, 2), spot // 2, lax.axis_size("dp") // 2


def greet_sums():
    barrier = pltpu.get_barrier_semaphore()
    core, group, others = dp_spot()
    count = lax.axis_size("seq")
    place = lax.axis_index("seq")
    targets = [{"dp": group * 2 + 1 - core}]
    targets += [{"dp": lax.rem(group + k, others) * 2 + core} for k in range(1, others)]
    targets += [{"seq": lax.rem(place + k, count)} for k in range(1, count)]
    for target in targets:
        pl.semaphore_signal(barrier, inc=1, device_id=target, device_id_type=MESH_ID)
    return len(targets)


class CrossSum:
    def __init__(self, ranges, buffers, sems):
        self.ranges = ranges
        self.own, self.first, self.second = buffers
        self.load_sem, self.first_send, self.first_recv, self.second_send, self.second_recv = sems
        self.core, self.group, self.others = dp_spot()
        self.loads, self.firsts, self.seconds = [], [], []

    def start(self):
        span = self.own.shape[2]
        for n, (grad, columns) in enumerate(self.ranges):
            self.firsts.append([])
            self.loads.append([])
            for g in range(self.others):
                theirs = pl.ds(pl.multiple_of((2 * g + 1 - self.core) * span, span), span)
                mine = pl.ds(pl.multiple_of((2 * g + self.core) * span, span), span)
                self.firsts[n].append(remote(
                    grad.at[theirs, columns], self.first.at[n, g], self.first_send.at[n, g],
                    self.first_recv.at[n, g], "dp", self.group * 2 + 1 - self.core))
                self.loads[n].append(pltpu.make_async_copy(
                    grad.at[mine, columns], self.own.at[n, g], self.load_sem.at[n, g]))
                self.firsts[n][g].start()
                self.loads[n][g].start()

    def step_a(self, n):
        for g in range(self.others):
            self.loads[n][g].wait()
            self.firsts[n][g].wait_recv()
        copies = []
        for k in range(1, self.others):
            peer = lax.rem(self.group + k, self.others)
            theirs = self.own.at[n, peer]
            add_rows(theirs, [theirs, self.first.at[n, peer]])
            copies.append(remote(
                theirs, self.second.at[n, k - 1], self.second_send.at[n, k - 1], self.second_recv.at[n, k - 1],
                "dp", peer * 2 + self.core))
            copies[-1].start()
        self.seconds.append(copies)

    def step_b(self, n, out):
        for copy in self.seconds[n]:
            copy.wait_recv()
        add_rows(out, [self.own.at[n, self.group], self.first.at[n, self.group]]
                 + [self.second.at[n, k] for k in range(self.others - 1)])

    def finish(self):
        for n in range(len(self.ranges)):
            for copy in self.firsts[n] + self.seconds[n]:
                copy.wait_send()


class Exchange:
    def __init__(self, array, received, send_sem, recv_sem, steps):
        self.array, self.received = array, received
        self.copies = [remote(array, received.at[i], send_sem.at[i], recv_sem.at[i], axis, target)
                       for i, (axis, target) in enumerate(steps)]

    def send(self, i):
        self.copies[i].start()

    def add(self, i):
        self.copies[i].wait_recv()
        self.copies[i].wait_send()
        self.array[...] = (self.array[...].astype(f32) + self.received[i].astype(f32)).astype(self.array.dtype)


def across(place, bit):
    step = 2 ** bit
    return place + step - 2 * step * lax.rem(lax.div(place, step), 2)


def bits(count):
    return range(count.bit_length() - 1)


class LineSum:
    def __init__(self, pieces, received, send_sem, recv_sem, begun=0):
        self.pieces, self.begun = pieces, begun
        self.received, self.send_sem, self.recv_sem = received, send_sem, recv_sem
        self.count = lax.axis_size("seq")
        self.place = lax.axis_index("seq")
        self.shard = received.shape[2]
        self.copies = [{} for _ in pieces]

    def rows(self, shard):
        return pl.ds(pl.multiple_of(shard * self.shard, self.shard), self.shard)

    def pass_on(self, n, bit):
        step = 2 ** bit
        side = lax.rem(lax.div(self.place, step), 2)
        target = self.place + step - 2 * step * side
        low = lax.rem(target, 2 * step)
        copies = []
        slot = self.count - self.count // step
        for m in range(self.count // (2 * step)):
            copies.append(remote(
                self.pieces[n].at[self.rows(low + 2 * step * m)], self.received.at[n, slot + m],
                self.send_sem.at[n, slot + m], self.recv_sem.at[n, slot + m], "seq", target))
            copies[-1].start()
        self.copies[n][bit] = copies

    def take_in(self, n, bit):
        step = 2 ** bit
        low = lax.rem(self.place, 2 * step)
        slot = self.count - self.count // step
        for m, copy in enumerate(self.copies[n][bit]):
            copy.wait_recv()
            rows = self.pieces[n].at[self.rows(low + 2 * step * m)]
            if 2 * step == self.count:
                return [rows, self.received.at[n, slot + m]]
            add_rows(rows, [rows, self.received.at[n, slot + m]])

    def step_c(self, n):
        self.pass_on(n, 1 if n < self.begun else 0)

    def step_d(self, n):
        bit = 2 if n < self.begun else 1
        while 2 ** bit < self.count:
            self.take_in(n, bit - 1)
            self.pass_on(n, bit)
            bit += 1

    def step_e(self, n, write):
        write(n, self.take_in(n, max(self.copies[n])))

    def finish(self):
        for steps in self.copies:
            for copies in steps.values():
                for copy in copies:
                    copy.wait_send()


def cut_columns(refs, units=UNITS):
    ranges = []
    for ref in refs:
        size = ref.shape[1] // units
        ranges += [(ref, pl.ds(u * size, size)) for u in range(units)]
    return ranges


def cross_scratch(ranges, span, columns, units=UNITS):
    others = lax.axis_size("dp") // 2
    size = columns // units
    peers = max(others - 1, 1)
    return [
        pltpu.VMEM((ranges, others, span, size), bf16), pltpu.VMEM((ranges, others, span, size), bf16),
        pltpu.VMEM((ranges, peers, span, size), bf16), DMA((ranges, others)), DMA((ranges, others)),
        DMA((ranges, others)), DMA((ranges, peers)), DMA((ranges, peers)),
    ]


def line_scratch(ranges, span, columns, slots=None, units=UNITS):
    count = lax.axis_size("seq")
    slots = count - 1 if slots is None else slots
    return [pltpu.VMEM((ranges, slots, span // count, columns // units), bf16),
            DMA((ranges, slots)), DMA((ranges, slots))]


CROSS_REFS = 8
LINE_REFS = 3


def last_sum_kernel(widths, *refs):
    grads, half, done, maps, small = refs[:2], refs[2], refs[3], refs[4:6], refs[6:8]
    kinds = len(widths[0]) + len(widths[1])
    outs = refs[8:8 + kinds]
    small_out, maps_out = refs[8 + kinds:10 + kinds]
    scratch, extra = refs[10 + kinds:-17], refs[-17:]
    place = lax.axis_index("seq")
    count = lax.axis_size("seq")
    core, group, peers = dp_spot()
    partner = {"head": lax.rem(lax.axis_index("head") + 1, lax.axis_size("head"))}
    pl.semaphore_signal(pltpu.get_barrier_semaphore(), inc=1, device_id=partner, device_id_type=MESH_ID)
    partners = greet_sums() + 1
    pl.semaphore_wait(pltpu.get_barrier_semaphore(), partners)
    (both, both_in, both_send, both_recv) = extra[:4]
    map_cross = CrossSum([(ref, pl.ds(0, ref.shape[1])) for ref in maps], extra[4:7], extra[7:12])
    map_part, map_rest = extra[12:14]
    rest_in, rest_send, rest_recv = extra[14:17]
    line_steps = [("seq", across(place, bit)) for bit in bits(count)]
    few = Exchange(both, both_in, both_send, both_recv,
                   [("dp", group * 2 + 1 - core)] + [("dp", across(group, bit) * 2 + core) for bit in bits(peers)]
                   + line_steps)
    span, shard = map_part.shape[1], map_rest.shape[1]
    rest = Exchange(map_rest, rest_in, rest_send, rest_recv, line_steps if shard == span else [])
    per_layer = small[0].shape[0]
    for l in range(2):
        both[l * per_layer:(l + 1) * per_layer, :] = small[l][...]
    few.send(0)
    map_cross.start()
    halves, early_half = scratch[:2]
    for n, (_, columns) in enumerate(cut_columns([half], LAST_UNITS)):
        early_half[n] = half[:, columns]
    early = LineSum([early_half.at[n] for n in range(LAST_UNITS)], *scratch[2:5], begun=BEGUN * LAST_UNITS // UNITS)
    cross = CrossSum(cut_columns(grads, LAST_UNITS), scratch[5:8], scratch[8:13])
    total = len(cross.ranges)
    line = LineSum([halves.at[n] for n in range(total)], *scratch[13:])
    cross.start()
    few.add(0)
    few.send(1)
    for l in range(2):
        map_cross.step_a(l)
    for n in range(LAST_UNITS):
        early.step_c(n)

    def pass_few(i):
        few.add(i)
        if i + 1 < len(few.copies):
            few.send(i + 1)

    def take_maps():
        for l in range(2):
            map_cross.step_b(l, map_part.at[l])
        halve(0)

    def halve(bit):
        if shard == span:
            if bit == 0:
                map_rest[...] = map_part[...]
            rest.send(bit)
            return
        step = 2 ** bit
        low = lax.rem(across(place, bit), 2 * step)
        for m in range(count // (2 * step)):
            source = pl.ds(pl.multiple_of((low + 2 * step * m) * shard, shard), shard)
            halves_sent.append(remote(map_part.at[:, source], rest_in.at[len(halves_sent)],
                                      rest_send.at[len(halves_sent)], rest_recv.at[len(halves_sent)],
                                      "seq", across(place, bit)))
            halves_sent[-1].start()

    halves_sent = []
    halves_taken = []

    def join(bit):
        if shard == span:
            rest.add(bit)
        else:
            step = 2 ** bit
            low = lax.rem(place, 2 * step)
            for m in range(count // (2 * step)):
                slot = len(halves_taken)
                halves_sent[slot].wait_recv()
                mine = pl.ds(pl.multiple_of((low + 2 * step * m) * shard, shard), shard)
                map_part[:, mine] = (map_part[:, mine].astype(f32) + rest_in[slot].astype(f32)).astype(bf16)
                halves_taken.append(slot)
        if bit + 1 < count.bit_length() - 1:
            halve(bit + 1)
        else:
            if shard != span:
                map_rest[...] = map_part[:, pl.ds(pl.multiple_of(place * shard, shard), shard)]
            head_copy.start()

    last = rest_in.shape[0] - 1
    head_copy = remote(map_rest, rest_in.at[last], rest_send.at[last], rest_recv.at[last], "head", partner["head"])

    def end_maps():
        head_copy.wait_recv()
        maps_out[...] = map_rest[...].astype(f32) + rest_in[last].astype(f32)
    chores = [functools.partial(pass_few, i) for i in range(1, len(few.copies) - 2)]
    chores += [take_maps] + [functools.partial(pass_few, i) for i in range(len(few.copies) - 2, len(few.copies))]
    chores += [functools.partial(join, bit) for bit in bits(count)] + [end_maps]
    pieces = []
    which = 0
    for a in range(2):
        at = 0
        for width in widths[a]:
            if width < 0:
                pieces += [(a, at, -width, outs[which], 0), (a, at - width, -width, outs[which], 1)]
                at -= 2 * width
            else:
                pieces.append((a, at, width, outs[which], None))
                at += width
            which += 1

    def place_of(out, layer, side, columns):
        return out.at[layer, :, columns] if side is None else out.at[layer, :, side, columns]

    def write(layer, array, n, terms):
        size = terms[0].shape[1]
        begin = n % LAST_UNITS * size
        for a, at, width, out, side in pieces:
            low, high = max(at, begin), min(at + width, begin + size)
            if a == array and low < high:
                add_rows(place_of(out, layer, side, pl.ds(low - at, high - low)),
                         [term.at[:, pl.ds(low - begin, high - low)] for term in terms])

    def write_early(n, terms):
        write(1, 1, n, terms)

    def write_line(n, terms):
        write(0, n // LAST_UNITS, n, terms)
    for n in range(total):
        cross.step_a(n)
        if n < LAST_UNITS:
            early.step_d(n)
    for a, at, width, out, side in pieces:
        if a == 0:
            place_of(out, 1, side, pl.ds(0, width))[...] = done[:, at:at + width]
    for n in range(total + 2):
        if n < total:
            cross.step_b(n, halves.at[n])
            line.step_c(n)
        if 1 <= n <= total:
            line.step_d(n - 1)
        if n < LAST_UNITS:
            early.step_e(n, write_early)
        if n >= 2:
            line.step_e(n - 2, write_line)
        if chores:
            chores.pop(0)()
    for chore in chores:
        chore()
    small_out[...] = both[...]
    for copy in halves_sent + [head_copy]:
        copy.wait_send()
    map_cross.finish()
    early.finish()
    cross.finish()
    line.finish()


def last_sum(grads, half, done, maps, small, widths):
    columns = grads[0].shape[1]
    span = half.shape[0]
    shard = span // lax.axis_size("seq")
    total = 2 * LAST_UNITS
    count, others = lax.axis_size("seq"), lax.axis_size("dp") // 2
    both = (2 * small[0].shape[0], small[0].shape[1])
    steps = 1 + len(bits(others)) + len(bits(count))
    map_span = maps[0].shape[0] // lax.axis_size("dp")
    map_width = maps[0].shape[1]
    map_rows = map_span // count if map_span // count >= 16 else map_span
    slots = count if map_rows < map_span else len(bits(count)) + 1
    return pl.pallas_call(
        functools.partial(last_sum_kernel, widths),
        out_shape=[jax.ShapeDtypeStruct((2, shard, width) if width > 0 else (2, shard, 2, -width), f32)
                   for width in widths[0] + widths[1]]
        + [jax.ShapeDtypeStruct(shape, f32) for shape in (both, (2, map_rows, map_width))],
        in_specs=[ANY] * 2 + [VM] * 2 + [ANY] * 2 + [VM] * 2,
        out_specs=[VM] * (len(widths[0]) + len(widths[1]) + 2),
        scratch_shapes=[pltpu.VMEM((total, span, columns // LAST_UNITS), bf16),
                        pltpu.VMEM((LAST_UNITS, span, columns // LAST_UNITS), bf16), *line_scratch(LAST_UNITS, span, columns, None, LAST_UNITS),
                        *cross_scratch(total, span, columns, LAST_UNITS), *line_scratch(total, span, columns, None, LAST_UNITS),
                        pltpu.VMEM(both, f32), pltpu.VMEM((steps, *both), f32), DMA((steps,)), DMA((steps,)),
                        *cross_scratch(2, map_span, map_width, 1),
                        pltpu.VMEM((2, map_span, map_width), bf16), pltpu.VMEM((2, map_rows, map_width), bf16),
                        pltpu.VMEM((slots, 2, map_rows, map_width), bf16), DMA((slots,)), DMA((slots,))],
        compiler_params=pltpu.CompilerParams(
            vmem_limit_bytes=VMEM_LIMIT, collective_id=9, has_side_effects=True),
        cost_estimate=pl.CostEstimate(flops=0, bytes_accessed=400 * 1024 * 1024, transcendentals=0),
    )(*grads, half, done, *maps, *small)


def unpack(pairs, out):
    def one(i, carry):
        rows = pl.ds(pl.multiple_of(i * 128, 128), 128)
        out[rows, :] = pairs[rows].reshape(128, out.shape[1])
        return carry
    lax.fori_loop(0, out.shape[0] // 128, one, 0)


def find_documents(seg_ref, dcol_ref, dloc_ref, drow_ref, column):
    place = lax.axis_index("seq")
    rows = dcol_ref.shape[0]
    drow_ref[...] = jnp.broadcast_to(seg_ref[...].astype(f32), drow_ref.shape)
    here = drow_ref[0:1, pl.ds(pl.multiple_of(place * rows, 128), rows)]
    dloc_ref[...] = jnp.broadcast_to(here, dloc_ref.shape)
    behind = drow_ref[0:1, pl.ds(pl.multiple_of(jnp.maximum(place * rows - 128, 0), 128), 128)]
    behind = jnp.where(place > 0, behind, -1.0)
    column[0:8, :] = jnp.transpose(jnp.broadcast_to(behind, (128, 128)))[120:, :]
    column[8:, :] = jnp.transpose(jnp.broadcast_to(here, (128, rows)))
    lane = lax.broadcasted_iota(jnp.int32, (rows, 128), 1)
    docs = column[8:, :]
    result = jnp.where(lane == 0, docs, 0.0)
    tests = [column[8 - k:8 - k + rows, :] for k in range(1, 4)] + [column[7:8, :], column[7 + rows:8 + rows, :]]
    for i, test in enumerate(tests):
        result = jnp.where(lane == i + 1, (docs == test).astype(f32), result)
    dcol_ref[...] = result


def layer_forward_kernel(heads, layer, layers, h_ref, gain_mix_ref, gain_ff_ref, wdt_ref,
                         taps_ref, heads_ref, *refs):
    refs = list(refs)
    seg_ref = refs.pop(0) if layer == 0 else None
    dcol_ref, dloc_ref, drow_ref = (None,) * 3 if layer == 0 else [refs.pop(0) for _ in range(3)]
    (wkv_hbm, wbc_hbm, zx_hbm, wq_hbm, wout_hbm, wo_hbm, gu_hbm, wdown_hbm) = refs[:8]
    refs = refs[8:]
    ready = layer > 0
    follows = layer + 1 < layers
    zx_ready = refs.pop(0) if ready else None
    (h_out, normed_ref, gate_ref, stack_ref, rim_ref, pre_ref, dt_ref, q_ref, kvall_ref,
     att_ref, lse_ref, mem_ref, gated_ref, middle_ref, nff_ref, gu_ref, inner_ref, gu_out) = refs[:18]
    refs = refs[18:]
    if not ready:
        dcol_ref, dloc_ref, drow_ref = [refs.pop(0) for _ in range(3)]
    zx_out = None if ready else refs.pop(0)
    zx_next = refs.pop(0) if follows else None
    column = refs.pop() if not ready else None
    (ext, y, wkv_ref, wbc_ref, wzx_ref, wq_ref, wo_ref, wout_ref, wgu_ref, wdown_ref, raw_zx, raw_gu,
     rim_in, kv_in, chain_in, chain_out, part_out, part_in, down_out, down_in,
     load_sem, kv_send, kv_recv, rim_send, rim_recv, chain_send, chain_recv,
     part_send, part_recv, down_send, down_recv) = refs
    rows = dt_ref.shape[0]
    d_local = gate_ref.shape[1]
    ff_local = inner_ref.shape[1]
    count = lax.axis_size("seq")
    place = lax.axis_index("seq")
    loads = {}
    plan = [("kv", wkv_hbm.at[layer], wkv_ref), ("bc", wbc_hbm.at[layer], wbc_ref)]
    plan.append(("zx", zx_ready, wzx_ref) if ready else ("zx", zx_hbm.at[layer], raw_zx))
    plan += [("q", wq_hbm.at[layer], wq_ref), ("out", wout_hbm.at[layer], wout_ref), ("o", wo_hbm.at[layer], wo_ref),
             ("gu", gu_hbm.at[layer], raw_gu), ("down", wdown_hbm.at[layer], wdown_ref)]
    later = [("gu_store", wgu_ref, gu_out)]
    if not ready:
        later.append(("zx_store", wzx_ref, zx_out))
    if follows:
        later += [("next", zx_hbm.at[layer + 1], raw_zx), ("next_store", wzx_ref, zx_next)]
    for name, src, dst in plan + later:
        loads[name] = pltpu.make_async_copy(src, dst, load_sem.at[len(loads)])
    for name, src, dst in plan:
        loads[name].start()
    partner = meet(count, False)

    if not ready:
        find_documents(seg_ref, dcol_ref, dloc_ref, drow_ref, column)
    normed_ref[...] = rms_scaled(h_ref[...].astype(f32), gain_mix_ref[...]).astype(bf16)
    normed = normed_ref[...]
    own = pl.ds(pl.multiple_of(place * rows, rows), rows)
    for j in range(count):
        @pl.when(j > place)
        def _():
            kv_in[j * rows:(j + 1) * rows, :] = jnp.zeros((rows, 2 * HD), bf16)
    loads["kv"].wait()
    kv_in[own, :] = nn(normed, wkv_ref[...]).astype(bf16)
    kv_copies = [
        remote(kv_in.at[own], kv_in.at[own], kv_send.at[j - 1], kv_recv.at[j - 1], "seq", place + j)
        for j in range(1, count)
    ]
    for j in range(1, count):
        @pl.when(place + j < count)
        def _():
            kv_copies[j - 1].start()
    loads["bc"].wait()
    stack_ref[:, d_local:] = nn(normed, wbc_ref[...]).astype(bf16)
    loads["zx"].wait()
    if not ready:
        unpack(raw_zx, wzx_ref)
        loads["zx_store"].start()
    if follows:
        loads["next"].start()
    stack_ref[:, :d_local] = nn(normed, wzx_ref[:, d_local:]).astype(bf16)
    rim_copy = remote(stack_ref.at[pl.ds(rows - RIM, RIM)], rim_in, rim_send, rim_recv, "seq", place + 1)

    @pl.when(place + 1 < count)
    def _():
        rim_copy.start()

    @pl.when(place == 0)
    def _():
        rim_in[...] = jnp.zeros(rim_in.shape, bf16)
        chain_in[...] = jnp.zeros(chain_in.shape, bf16)
    dt_ref[...] = nn(normed, wdt_ref[...]).astype(bf16).astype(f32)
    gate_ref[...] = nn(normed, wzx_ref[:, :d_local]).astype(bf16)
    loads["q"].wait()
    q_ref[...] = nn(normed, wq_ref[...]).astype(bf16)
    raw, step, log_decay, running, running_t, ordered = ssm_scalars(dt_ref, heads_ref)
    mapping = head_map(heads, d_local // heads)
    last = running[rows - 1:rows, :]
    fade = jnp.exp(last - running) * dcol_ref[:, 5:6]
    dec = jnp.exp(running) * dcol_ref[:, 4:5]
    ends = jnp.exp(running_t[:, rows - 1:rows]) * dcol_ref[rows - 1:rows, 4:5] + jnp.zeros((128, NS), f32)
    ends = spread_rows(ends, mapping)
    steps = spread(step, mapping)
    ext[RIM:, :] = stack_ref[...].astype(f32)

    @pl.when(place > 0)
    def _():
        rim_copy.wait_recv()
    rim_ref[...] = rim_in[...]
    ext[0:RIM, :] = rim_in[...].astype(f32)
    pre = ext[RIM:RIM + rows, :] * taps_ref[0:1, :]
    for k in range(1, 4):
        pre = pre + ext[RIM - k:RIM - k + rows, :] * dcol_ref[:, k:k + 1] * taps_ref[k:k + 1, :]
    pre_ref[...] = pre
    mixed = pre_ref[...] * sigmoid(pre_ref[...])
    values = mixed[:, :d_local]
    b_rows = mixed[:, d_local:d_local + NS].astype(bf16)
    c_rows = mixed[:, d_local + NS:].astype(bf16)
    stepped = values * steps
    state = tn((stepped * spread(fade, mapping)).astype(bf16), b_rows)
    y[...] = values * spread(heads_ref[2:3, :] + jnp.zeros((8, 128), f32), mapping)[0:1, :]
    linked = ordered & (dcol_ref[:, 0:1] == dloc_ref[0:1, :])
    cb = jnp.where(linked, nt(c_rows, b_rows), 0.0)
    stepped = stepped.astype(bf16)
    lane = lax.broadcasted_iota(jnp.int32, (rows, 128), 1)

    for j in range(1, count):
        @pl.when(place - j >= 0)
        def _():
            kv_copies[j - 1].wait_recv()
    allowed = score_mask(dcol_ref, drow_ref)
    keyvals = kv_in[...]
    kvall_ref[...] = keyvals
    keys, vals = keyvals[:, :HD], keyvals[:, HD:]
    totals = jnp.zeros((rows, 128), f32)
    pairs = heads // 2
    query_heads = q_ref.shape[1] // HD
    chain_copies = []
    for pair in range(pairs):
        span = slice(pair * 128, pair * 128 + 128)
        copy = remote(chain_out.at[pl.ds(pair * 128, 128)], chain_in.at[pl.ds(pair * 128, 128)],
                      chain_send.at[pair], chain_recv.at[pair], "seq", place + 1)
        chain_copies.append(copy)

        @pl.when(place > 0)
        def _():
            copy.wait_recv()
        chain_out[span, :] = (ends[span] * chain_in[span, :].astype(f32) + state[span]).astype(bf16)

        @pl.when(place + 1 < count)
        def _():
            copy.start()
        sides = []
        for h in (2 * pair, 2 * pair + 1):
            gap = running[:, h:h + 1] - running_t[h:h + 1, :]
            mixing = (jnp.exp(jnp.minimum(gap, 0.0)) * cb).astype(bf16)
            sides.append(nn(mixing, stepped[:, span]))
        y[:, span] += jnp.where(lane < 64, sides[0], sides[1])
        for h in range(query_heads * pair // pairs, query_heads * (pair + 1) // pairs):
            query = q_ref[:, h * HD:(h + 1) * HD] * jnp.asarray(HD ** -0.5, bf16)
            scores = jnp.where(allowed, nt(query, keys), masked_score)
            peak = jnp.max(scores, axis=1, keepdims=True)
            expo = jnp.exp(scores - peak)
            total = jnp.sum(expo, axis=1, keepdims=True)
            probs = (expo * (1.0 / total)).astype(bf16)
            att_ref[:, h * HD:(h + 1) * HD] = nn(probs, vals).astype(bf16)
            totals = jnp.where(lane == h, peak + jnp.log(total), totals)
    lse_ref[...] = totals
    mem_ref[...] = chain_in[...]
    decs = spread(dec, mapping)
    carried = decs * nt(c_rows, mem_ref[...])
    gate = gate_ref[...].astype(f32)
    gated_ref[...] = ((y[...] + carried) * (gate * sigmoid(gate))).astype(bf16)
    loads["out"].wait()
    loads["o"].wait()
    chunks = [pl.ds(begin, CHUNK) for begin in range(0, rows, CHUNK)]
    part_copies, down_copies = [], []
    for i, chunk in enumerate(chunks):
        part_out[chunk, :] = (nn(gated_ref[chunk, :], wout_ref[...])
                              + nn(att_ref[chunk, :], wo_ref[...])).astype(bf16)
        copy = remote(part_out.at[chunk], part_in.at[chunk], part_send.at[i], part_recv.at[i], "head", partner)
        copy.start()
        part_copies.append(copy)
    loads["gu"].wait()
    unpack(raw_gu, wgu_ref)
    loads["gu_store"].start()
    loads["down"].wait()
    for i, chunk in enumerate(chunks):
        part_copies[i].wait_recv()
        middle_ref[chunk, :] = h_ref[chunk, :].astype(f32) + (
            part_out[chunk, :].astype(f32) + part_in[chunk, :].astype(f32))
        nff_ref[chunk, :] = rms_scaled(middle_ref[chunk, :], gain_ff_ref[...]).astype(bf16)
        gu_ref[chunk, :] = nn(nff_ref[chunk, :], wgu_ref[...]).astype(bf16)
        gate = gu_ref[chunk, :ff_local].astype(f32)
        inner_ref[chunk, :] = (gate * sigmoid(gate) * gu_ref[chunk, ff_local:].astype(f32)).astype(bf16)
        down_out[chunk, :] = nn(inner_ref[chunk, :], wdown_ref[...]).astype(bf16)
        copy = remote(down_out.at[chunk], down_in.at[chunk], down_send.at[i], down_recv.at[i], "head", partner)
        copy.start()
        down_copies.append(copy)
    if not ready:
        loads["zx_store"].wait()
    if follows:
        loads["next"].wait()
        unpack(raw_zx, wzx_ref)
        loads["next_store"].start()
    for i, chunk in enumerate(chunks):
        down_copies[i].wait_recv()
        h_out[chunk, :] = (middle_ref[chunk, :] + (
            down_out[chunk, :].astype(f32) + down_in[chunk, :].astype(f32))).astype(bf16)
    loads["gu_store"].wait()
    if follows:
        loads["next_store"].wait()
    for i in range(len(chunks)):
        part_copies[i].wait_send()
        down_copies[i].wait_send()

    @pl.when(place + 1 < count)
    def _():
        rim_copy.wait_send()
        for copy in chain_copies:
            copy.wait_send()
    for j in range(1, count):
        @pl.when(place + j < count)
        def _():
            kv_copies[j - 1].wait_send()


def layer_forward(layer, hidden, zx, w, context):
    rows, model_width = hidden.shape
    heads = w["heads"]
    layers = w["out"].shape[0]
    d_local = w["out"].shape[1]
    ff_local = w["down"].shape[1]
    q_width = w["q"].shape[2]
    width = d_local + 2 * NS
    count = lax.axis_size("seq")
    length = count * rows
    parts = rows // CHUNK
    wide = ((model_width, 2 * d_local), bf16)
    outs = [
        ((rows, model_width), bf16), ((rows, model_width), bf16), ((rows, d_local), bf16), ((rows, width), bf16),
        ((RIM, width), bf16), ((rows, width), f32), ((rows, 128), f32), ((rows, q_width), bf16),
        ((length, 2 * HD), bf16), ((rows, q_width), bf16), ((rows, 128), f32), ((d_local, NS), bf16),
        ((rows, d_local), bf16), ((rows, model_width), f32), ((rows, model_width), bf16),
        ((rows, 2 * ff_local), bf16), ((rows, ff_local), bf16), ((model_width, 2 * ff_local), bf16),
    ]
    kept = len(outs) - 1
    documents = [((rows, 128), f32), ((8, rows), f32), ((8, length), f32)] if layer == 0 else []
    outs += documents
    outs += [wide] * ((layer == 0) + (layer + 1 < layers))
    full = (rows, model_width)
    given = [] if layer == 0 else [zx]
    result = pl.pallas_call(
        functools.partial(layer_forward_kernel, heads, layer, layers),
        out_shape=[jax.ShapeDtypeStruct(shape, kind) for shape, kind in outs],
        in_specs=[VM] * (6 + len(context)) + [ANY] * (8 + len(given)),
        out_specs=[VM] * kept + [ANY] + [VM] * len(documents) + [ANY] * (len(outs) - kept - 1 - len(documents)),
        scratch_shapes=[
            pltpu.VMEM((rows + RIM, width), f32), pltpu.VMEM((rows, d_local), f32),
            pltpu.VMEM((model_width, 2 * HD), bf16), pltpu.VMEM((model_width, 2 * NS), bf16),
            pltpu.VMEM((model_width, 2 * d_local), bf16), pltpu.VMEM((model_width, q_width), bf16),
            pltpu.VMEM((q_width, model_width), bf16), pltpu.VMEM((d_local, model_width), bf16),
            pltpu.VMEM((model_width, 2 * ff_local), bf16), pltpu.VMEM((ff_local, model_width), bf16),
            pltpu.VMEM((model_width, 2, d_local), bf16), pltpu.VMEM((model_width, 2, ff_local), bf16),
            pltpu.VMEM((RIM, width), bf16), pltpu.VMEM((length, 2 * HD), bf16),
            pltpu.VMEM((d_local, NS), bf16), pltpu.VMEM((d_local, NS), bf16),
            pltpu.VMEM(full, bf16), pltpu.VMEM(full, bf16), pltpu.VMEM(full, bf16), pltpu.VMEM(full, bf16),
            DMA((12,)), DMA((count - 1,)), DMA((count - 1,)), DMA, DMA, DMA((heads // 2,)), DMA((heads // 2,)),
            DMA((parts,)), DMA((parts,)), DMA((parts,)), DMA((parts,)),
            *([pltpu.VMEM((rows + 8, 128), f32)] if layer == 0 else []),
        ],
        compiler_params=pltpu.CompilerParams(
            vmem_limit_bytes=VMEM_LIMIT, collective_id=layer, has_side_effects=True),
    )(hidden, w["gain_mix"][layer], w["gain_ff"][layer], w["dt"][layer], w["taps"][layer], w["head_vals"][layer],
      *context, w["kv"], w["bc"], w["zx"], w["q"], w["out"], w["o"], w["gu"], w["down"], *given)
    names = ("out", "normed", "gate", "stack", "rim", "pre", "dt", "q", "kv", "att", "lse", "memory",
             "gated", "middle", "nff", "gu", "inner", "w_gu")
    saved = dict(zip(names, result))
    saved["hidden"] = hidden
    extra = list(result[len(names):])
    if layer == 0:
        context = [extra.pop(0) for _ in range(3)]
    saved["w_zx"] = extra.pop(0) if layer == 0 else zx
    return saved.pop("out"), (extra.pop(0) if extra else None), context, saved


def norm_back(hidden, gain, grad):
    inverse = lax.rsqrt(jnp.mean(hidden * hidden, axis=-1, keepdims=True) + norm_eps)
    scaled = grad * gain
    lean = jnp.mean(scaled * hidden, axis=-1, keepdims=True)
    grad_gain = jnp.sum(grad * hidden * inverse, axis=0, keepdims=True)
    return inverse * (scaled - hidden * (inverse * inverse * lean)), grad_gain


def store_blocks(compute, slots, out, sems):
    size = slots.shape[1]
    columns = out.shape[1]
    blocks = out.shape[0] // size

    def rows(i):
        return pl.ds(pl.multiple_of(i * size, size), size)

    def copy(i, slot):
        return pltpu.make_async_copy(slots.at[slot, :, pl.ds(0, columns)], out.at[rows(i)], sems.at[slot])

    def one(i, carry):
        slot = lax.rem(i, 2)

        @pl.when(i >= 2)
        def _():
            copy(i - 2, slot).wait()
        compute(rows(i), slot)
        copy(i, slot).start()
        return carry
    lax.fori_loop(0, blocks, one, 0)
    for i in range(max(0, blocks - 2), blocks):
        copy(i, i % 2).wait()


def layer_backward_kernel(heads, layer, schedule, grad_ref, h_ref, normed_ref, gate_ref, stack_ref, rim_ref, pre_ref, dt_ref,
                          q_ref, kv_ref, att_ref, lse_ref, mem_ref, gated_ref, middle_ref, nff_ref, gu_ref,
                          inner_ref, gain_mix_ref, gain_ff_ref, wdt_ref,
                          taps_ref, heads_ref, dcol_ref, dloc_ref, drow_ref,
                          wdown_hbm, wgu_hbm, wout_hbm, wo_hbm, wzx_hbm, wbc_hbm, wq_hbm, wkv_hbm, *refs):
    refs = list(refs)
    own_sum = schedule["own"]
    source = None if own_sum else refs.pop(0)
    half_in = None if own_sum else refs.pop(0)
    if not own_sum:
        next_refs, refs = refs[-LINE_REFS:], refs[:-LINE_REFS]
        line_refs, refs = refs[-LINE_REFS - 1:], refs[:-LINE_REFS - 1]
    cross_refs, refs = refs[-CROSS_REFS:], refs[:-CROSS_REFS]
    summed_ref = None if own_sum else refs.pop(0)
    (g_out, gff_out, gmix_out, gbc_out, small_ref, half_ref,
     wdown_ref, wide_ref, wout_ref, wo_ref, wbc_ref, wq_ref, wkv_ref,
     gff, dgu, one_out, one_in, two_out, two_in, gmid, branch, gg, datt, dy_s, dxs_s, u_s,
     decay_s, probs_s, acc, dkv_out, dkv_in, chain_in, chain_out, rim_in,
     ext, pad, dext, dgate, dstack, dq, dkv, draw_s,
     load_sem, one_send, one_recv, two_send, two_recv, chain_send, chain_recv,
     rim_send, rim_recv, kv_send, kv_recv, gblk, grad_sem) = refs
    rows = dt_ref.shape[0]
    d_local = gate_ref.shape[1]
    ff_local = inner_ref.shape[1]
    q_width = q_ref.shape[1]
    model_width = h_ref.shape[1]
    width = pre_ref.shape[1]
    length = kv_ref.shape[0]
    count = lax.axis_size("seq")
    place = lax.axis_index("seq")
    wgu_ref = wide_ref.at[:, pl.ds(0, 2 * ff_local)]
    wzx_ref = wide_ref.at[:, pl.ds(0, 2 * d_local)]
    loads = {}
    for name, src, dst in (
        ("down", wdown_hbm.at[layer], wdown_ref), ("gu", wgu_hbm, wgu_ref), ("out", wout_hbm.at[layer], wout_ref),
        ("o", wo_hbm.at[layer], wo_ref), ("bc", wbc_hbm.at[layer], wbc_ref), ("q", wq_hbm.at[layer], wq_ref),
        ("kv", wkv_hbm.at[layer], wkv_ref), ("zx", wzx_hbm, wzx_ref),
    ):
        loads[name] = pltpu.make_async_copy(src, dst, load_sem.at[len(loads)])
    for name in ("down", "gu", "out", "o", "bc", "q", "kv"):
        loads[name].start()
    partner = meet(count, True, greet_sums)
    cross = CrossSum(cut_columns([gff_out if own_sum else source]), cross_refs[:3], cross_refs[3:])
    ranges = [columns for _, columns in cut_columns([half_ref])]
    steps_of = {"a": cross.step_a, "b": lambda n: cross.step_b(n, half_ref.at[:, ranges[n]])}
    if not own_sum:
        fetches = [pltpu.make_async_copy(half_in.at[:, columns], line_refs[0].at[n], load_sem.at[len(loads) + n])
                   for n, (_, columns) in enumerate(cut_columns([half_in]))]
        for fetch in fetches:
            fetch.start()
        for fetch in fetches:
            fetch.wait()
        line = LineSum([line_refs[0].at[n] for n in range(UNITS)], *line_refs[1:])

        def write(n, terms):
            size = terms[0].shape[1]
            add_rows(summed_ref.at[:, pl.ds(n * size, size)], terms)
        follow = LineSum([half_ref.at[:, columns] for columns in ranges[:BEGUN]], *next_refs)
        steps_of.update({"f": follow.step_c, "g": lambda n: follow.take_in(n, 0)})
        steps_of.update({"c": line.step_c, "d": line.step_d, "e": lambda n: line.step_e(n, write)})

    def pump(spot):
        for step in schedule.get(spot, ()):
            if step == "start":
                cross.start()
            elif step == "finish":
                cross.finish()
                if not own_sum:
                    line.finish()
                    follow.finish()
            else:
                steps_of[step[0]](int(step[1]))
    pump("begin")
    chunks = [pl.ds(begin, CHUNK) for begin in range(0, rows, CHUNK)]

    gff[...] = grad_ref[...].astype(bf16)
    loads["down"].wait()
    loads["gu"].wait()
    one_copies, two_copies = [], []
    for i, chunk in enumerate(chunks):
        grad_inner = nt(gff[chunk, :], wdown_ref[...])
        gate = gu_ref[chunk, :ff_local].astype(f32)
        up = gu_ref[chunk, ff_local:].astype(f32)
        sig = sigmoid(gate)
        dgu[chunk, :ff_local] = (grad_inner * up * (sig * (1.0 + gate * (1.0 - sig)))).astype(bf16)
        dgu[chunk, ff_local:] = (grad_inner * (gate * sig)).astype(bf16)
        one_out[chunk, :] = nt(dgu[chunk, :], wgu_ref[...]).astype(bf16)
        copy = remote(one_out.at[chunk], one_in.at[chunk], one_send.at[i], one_recv.at[i], "head", partner)
        copy.start()
        one_copies.append(copy)
    loads["zx"].start()

    @pl.when(place == count - 1)
    def _():
        rim_in[...] = jnp.zeros(rim_in.shape, f32)
        chain_in[...] = jnp.zeros(chain_in.shape, bf16)
    for j in range(1, count):
        @pl.when(place + j >= count)
        def _():
            dkv_in[(j - 1) * rows:j * rows, :] = jnp.zeros((rows, 2 * HD), bf16)

    pump("ff0")

    def ff_weights(block, slot):
        gblk[slot, :, :ff_local] = tn(gff[:, block], inner_ref[...]).astype(bf16)
        gblk[slot, :, ff_local:3 * ff_local] = tn(nff_ref[:, block], dgu[...]).astype(bf16)
    store_blocks(ff_weights, gblk, gff_out, grad_sem)
    pump("ff")

    raw, step, log_decay, running, running_t, ordered = ssm_scalars(dt_ref, heads_ref)
    mapping = head_map(heads, d_local // heads)
    last = running[rows - 1:rows, :]
    fade = spread(jnp.exp(last - running) * dcol_ref[:, 5:6], mapping)
    dec = jnp.exp(running) * dcol_ref[:, 4:5]
    decs = spread(dec, mapping)
    ends = jnp.exp(running_t[:, rows - 1:rows]) * dcol_ref[rows - 1:rows, 4:5] + jnp.zeros((128, NS), f32)
    ends = spread_rows(ends, mapping)
    steps = spread(step, mapping)
    skip = spread(heads_ref[2:3, :] + jnp.zeros((8, 128), f32), mapping)[0:1, :]
    pre_v = pre_ref[:, :d_local]
    values = pre_v * sigmoid(pre_v)
    pre_n = pre_ref[:, d_local:]
    maps = (pre_n * sigmoid(pre_n)).astype(bf16)
    b_rows, c_rows = maps[:, :NS], maps[:, NS:]
    stepped = (values * steps).astype(bf16)
    linked = ordered & (dcol_ref[:, 0:1] == dloc_ref[0:1, :])
    cb = jnp.where(linked, nt(c_rows, b_rows), 0.0)
    lane = lax.broadcasted_iota(jnp.int32, (rows, 128), 1)
    pairs = heads // 2
    for pair in range(pairs):
        span = slice(pair * 128, pair * 128 + 128)
        sides = []
        for h in (2 * pair, 2 * pair + 1):
            at = slice(h * rows, (h + 1) * rows)
            gap = running[:, h:h + 1] - running_t[h:h + 1, :]
            decay = jnp.exp(jnp.minimum(gap, 0.0))
            decay_s[:, at] = decay.astype(bf16)
            mixing = (decay_s[:, at].astype(f32) * cb).astype(bf16)
            sides.append(nn(mixing, stepped[:, span]))
        u_s[:, span] = jnp.where(lane < 64, sides[0], sides[1])
    allowed = score_mask(dcol_ref, drow_ref)
    keyvals = kv_ref[...]
    keys, vals = keyvals[:, :HD], keyvals[:, HD:]
    scale = jnp.asarray(HD ** -0.5, bf16)
    query_heads = q_width // HD
    for h in range(query_heads):
        query = q_ref[:, h * HD:(h + 1) * HD] * scale
        scores = jnp.where(allowed, nt(query, keys), masked_score)
        probs_s[:, h * length:(h + 1) * length] = jnp.exp(scores - lse_ref[:, h:h + 1]).astype(bf16)
    ext[0:RIM, :] = rim_ref[...].astype(f32)
    ext[RIM:, :] = stack_ref[...].astype(f32)
    gate = gate_ref[...].astype(f32)
    gate_sig = sigmoid(gate)
    gate_act = gate * gate_sig
    loads["out"].wait()
    loads["o"].wait()
    dtaps_ref = small_ref.at[pl.ds(0, 8)]
    gains_ref = small_ref.at[pl.ds(8, 8)]
    gains_ref[...] = jnp.zeros(gains_ref.shape, f32)
    for i, chunk in enumerate(chunks):
        pump("one%d" % i)
        one_copies[i].wait_recv()
        grad = one_out[chunk, :].astype(f32) + one_in[chunk, :].astype(f32)
        moved, gain = norm_back(middle_ref[chunk, :], gain_ff_ref[...], grad)
        gains_ref[1:2, :] += gain
        gmid[chunk, :] = grad_ref[chunk, :].astype(f32) + moved
        branch[chunk, :] = gmid[chunk, :].astype(bf16)
        gg[chunk, :] = nt(branch[chunk, :], wout_ref[...])
        datt[chunk, :] = nt(branch[chunk, :], wo_ref[...]).astype(bf16)
    grad_ssm = gg[...] * gate_act
    dy_s[...] = grad_ssm.astype(bf16)
    push = tn((grad_ssm * decs).astype(bf16), c_rows)
    dcb = jnp.zeros((rows, rows), f32)
    chain_copies = []
    for pair in range(pairs):
        pump("pair%d" % pair)
        span = slice(pair * 128, pair * 128 + 128)
        copy = remote(chain_out.at[pl.ds(pair * 128, 128)], chain_in.at[pl.ds(pair * 128, 128)],
                      chain_send.at[pair], chain_recv.at[pair], "seq", place - 1)
        chain_copies.append(copy)

        @pl.when(place < count - 1)
        def _():
            copy.wait_recv()
        chain_out[span, :] = (ends[span] * chain_in[span, :].astype(f32) + push[span]).astype(bf16)

        @pl.when(place > 0)
        def _():
            copy.start()
        stepped_p = stepped[:, span]
        dy_p = dy_s[:, span]
        dxs = []
        for side, h in enumerate((2 * pair, 2 * pair + 1)):
            at = slice(h * rows, (h + 1) * rows)
            decay = decay_s[:, at].astype(f32)
            dxs.append(tn((decay * cb).astype(bf16), dy_p))
            half = jnp.where((lane < 64) == (side == 0), dy_p, jnp.zeros_like(dy_p))
            dcb = dcb + nt(half, stepped_p) * decay
        dxs_s[:, span] = jnp.where(lane < 64, dxs[0], dxs[1])
        for h in range(query_heads * pair // pairs, query_heads * (pair + 1) // pairs):
            part = slice(h * HD, (h + 1) * HD)
            query = q_ref[:, part] * scale
            grad = datt[:, part]
            delta = jnp.sum(grad.astype(f32) * att_ref[:, part].astype(f32), axis=1, keepdims=True)
            probs = probs_s[:, h * length:(h + 1) * length]
            grad_scores = (probs.astype(f32) * (nt(grad, vals) - delta)).astype(bf16)
            dq[:, part] = (nn(grad_scores, keys) * HD ** -0.5).astype(bf16)
            dk = tn(grad_scores, query)
            dv = tn(probs, grad)
            if h == 0:
                acc[:, :HD] = dk
                acc[:, HD:] = dv
            else:
                acc[:, :HD] += dk
                acc[:, HD:] += dv
    dkv_out[...] = acc[...].astype(bf16)
    kv_copies = []
    for j in range(1, count):
        target = jnp.maximum(place - j, 0)
        theirs = pl.ds(pl.multiple_of(target * rows, rows), rows)
        copy = remote(dkv_out.at[theirs], dkv_in.at[pl.ds((j - 1) * rows, rows)], kv_send.at[j - 1],
                      kv_recv.at[j - 1], "seq", place - j)
        kv_copies.append(copy)

        @pl.when(place >= j)
        def _():
            copy.start()
    pump("post")
    memory = mem_ref[...]
    gmem = chain_in[...]
    carried = decs * nt(c_rows, memory)
    back = fade * nt(b_rows, gmem)
    dy_low = dy_s[...].astype(f32)
    stepped_f = stepped.astype(f32)
    dxs_all = dxs_s[...] + back
    dxs_s[...] = dxs_all
    dcb = jnp.where(linked, dcb, 0.0).astype(bf16)
    dc = nn(dcb, b_rows) + nn((dy_low * decs).astype(bf16), memory)
    db = tn(dcb, c_rows) + nn((stepped_f * fade).astype(bf16), gmem)
    dvalues = steps * dxs_all + skip * grad_ssm
    pad[0:8, :] = jnp.zeros((8, width), f32)
    pad[8 + rows:, :] = jnp.zeros((8, width), f32)
    sig = sigmoid(pre_v)
    pad[8:8 + rows, :d_local] = dvalues * (sig * (1.0 + pre_v * (1.0 - sig)))
    sig = sigmoid(pre_n)
    slope = sig * (1.0 + pre_n * (1.0 - sig))
    pad[8:8 + rows, d_local:d_local + NS] = db * slope[:, :NS]
    pad[8:8 + rows, d_local + NS:] = dc * slope[:, NS:]
    dpre = pad[8:8 + rows, :]
    dext[...] = pad[0:8 + rows, :] * taps_ref[0:1, :]
    dtaps_ref[...] = jnp.zeros((8, width), f32)
    dtaps_ref[0:1, :] = jnp.sum(dpre * ext[RIM:RIM + rows, :], axis=0, keepdims=True)
    for k in range(1, 4):
        masked = dpre * dcol_ref[:, k:k + 1]
        pad[8:8 + rows, :] = masked
        dtaps_ref[k:k + 1, :width] = jnp.sum(masked * ext[RIM - k:RIM - k + rows, :], axis=0, keepdims=True)
        dext[...] += pad[k:k + 8 + rows, :] * taps_ref[k:k + 1, :]
    rim_copy = remote(dext.at[pl.ds(0, 8)], rim_in, rim_send, rim_recv, "seq", place - 1)

    @pl.when(place > 0)
    def _():
        rim_copy.start()
    scanned = u_s[...] + carried
    drun = gather(dy_low * scanned - stepped_f * dxs_all, mapping)
    ssm_out = scanned + skip * values
    dgate[...] = (gg[...] * ssm_out * (gate_sig * (1.0 + gate * (1.0 - gate_sig)))).astype(bf16)
    gstep = gather(values * dxs_all, mapping)
    ones = jnp.ones((8, 128), bf16)
    high, low = split(gmem.astype(f32) * memory.astype(f32), 2)
    moved = nt(ones, high) + nt(ones, low)
    end = gather(jnp.sum(stepped_f * back, axis=0, keepdims=True) + jnp.zeros((8, 1), f32), mapping)
    end = end + gather(moved, mapping) * dec[rows - 1:rows, :]
    upper = (lax.broadcasted_iota(jnp.int32, (rows, rows), 1)
             >= lax.broadcasted_iota(jnp.int32, (rows, rows), 0)).astype(bf16)
    dlog = triangle_sum(upper, drun) + end[0:1, :]
    draw = (gstep - jnp.exp(heads_ref[1:2, :]) * dlog) * sigmoid(raw)
    draw_s[...] = draw.astype(bf16)
    dskip = gather(jnp.sum(grad_ssm * values, axis=0, keepdims=True) + jnp.zeros((8, 1), f32), mapping)
    small_ref[4:5, :128] = jnp.sum(draw, axis=0, keepdims=True)
    small_ref[5:6, :128] = jnp.sum(dlog * log_decay, axis=0, keepdims=True)
    small_ref[6:7, :128] = dskip[0:1, :]
    for name in ("zx", "bc", "q", "kv"):
        loads[name].wait()

    for j in range(1, count):
        @pl.when(place + j < count)
        def _():
            kv_copies[j - 1].wait_recv()
    pump("two")
    own = pl.ds(pl.multiple_of(place * rows, rows), rows)
    total = acc[own, :]
    for j in range(1, count):
        total = total + dkv_in[(j - 1) * rows:j * rows, :].astype(f32)
    dkv[...] = total.astype(bf16)

    for i, chunk in enumerate(chunks):
        if i == len(chunks) - 1:
            @pl.when(place < count - 1)
            def _():
                rim_copy.wait_recv()
            dext[rows:rows + 8, :] += rim_in[...]
        dstack[chunk, :] = dext[8 + i * CHUNK:8 + (i + 1) * CHUNK, :].astype(bf16)
        two_out[chunk, :] = (
            nt(dgate[chunk, :], wzx_ref[:, :d_local]) + nt(dstack[chunk, :d_local], wzx_ref[:, d_local:])
            + nt(dstack[chunk, d_local:], wbc_ref[...]) + nt(draw_s[chunk, :], wdt_ref[...])
            + nt(dq[chunk, :], wq_ref[...]) + nt(dkv[chunk, :], wkv_ref[...])
        ).astype(bf16)
        copy = remote(two_out.at[chunk], two_in.at[chunk], two_send.at[i], two_recv.at[i], "head", partner)
        copy.start()
        two_copies.append(copy)

    gbc_out[:, model_width:] = jnp.transpose(jnp.concatenate(
        [dtaps_ref[0:4, d_local:], jnp.zeros((124, 2 * NS), f32)], axis=0)).astype(bf16)
    pump("mix")

    def mix_weights(block, slot):
        left = normed_ref[:, block]
        at = 0
        for right in (dgate[...], dstack[:, :d_local], dq[...], dkv[...], draw_s[...]):
            gblk[slot, :, at:at + right.shape[1]] = tn(left, right).astype(bf16)
            at += right.shape[1]
        left = branch[:, block]
        for right in (gated_ref[...], att_ref[...]):
            gblk[slot, :, at:at + right.shape[1]] = tn(left, right).astype(bf16)
            at += right.shape[1]
        gbc_out[:, block] = tn(dstack[:, d_local:], normed_ref[:, block]).astype(bf16)
    store_blocks(mix_weights, gblk, gmix_out, grad_sem)

    for i, chunk in enumerate(chunks):
        pump("last%d" % i)
        two_copies[i].wait_recv()
        grad = two_out[chunk, :].astype(f32) + two_in[chunk, :].astype(f32)
        moved, gain = norm_back(h_ref[chunk, :].astype(f32), gain_mix_ref[...], grad)
        gains_ref[0:1, :] += gain
        g_out[chunk, :] = gmid[chunk, :] + moved
    pump("end")
    for i in range(len(chunks)):
        one_copies[i].wait_send()
        two_copies[i].wait_send()

    @pl.when(place > 0)
    def _():
        rim_copy.wait_send()
        for copy in chain_copies:
            copy.wait_send()
    for j in range(1, count):
        @pl.when(place >= j)
        def _():
            kv_copies[j - 1].wait_send()


SCHEDULES = (
    {"own": False, "begin": ("start", "c0", "c1", "c2", "c3"), "ff0": ("a0", "a1", "a2", "a3"), "ff": ("d0", "d1"),
     "one0": ("d2",), "one1": ("d3",), "post": ("b0", "b1"), "two": ("f0", "f1"), "mix": ("b2",),
     "last0": ("e0", "e1", "e2", "e3"), "last1": ("b3",), "end": ("g0", "g1", "finish")},
    {"own": True, "ff": ("start",), "one0": ("a0", "a1"), "one1": ("a2", "a3"), "mix": ("b0",), "last0": ("b1", "b2"),
     "end": ("b3", "finish")},
)


def layer_backward(layer, grad, waiting, w, saved, context):
    dcol, dloc, drow = context
    rows, model_width = grad.shape
    heads = w["heads"]
    d_local = w["out"].shape[1]
    ff_local = w["down"].shape[1]
    q_width = w["q"].shape[2]
    width = d_local + 2 * NS
    count = lax.axis_size("seq")
    length = count * rows
    parts = rows // CHUNK
    mix_width = 3 * d_local + 2 * q_width + 256
    schedule = SCHEDULES[1 if waiting is None else 0]
    given = [] if waiting is None else list(waiting)
    outs = [
        ((rows, model_width), f32), ((model_width, 3 * ff_local), bf16), ((model_width, mix_width), bf16),
        ((2 * NS, model_width + 128), bf16), ((16, max(width, model_width)), f32),
    ]
    span = model_width // lax.axis_size("dp")
    if waiting is not None:
        outs.insert(0, ((span // count, 3 * ff_local), f32))
    outs.append(((span, 3 * ff_local if waiting is None else mix_width), bf16))
    full = (rows, model_width)
    state = (d_local, NS)
    names = ("hidden", "normed", "gate", "stack", "rim", "pre", "dt", "q", "kv", "att", "lse", "memory",
             "gated", "middle", "nff", "gu", "inner")

    def vm(shape, kind):
        return pltpu.VMEM(shape, kind)
    return pl.pallas_call(
        functools.partial(layer_backward_kernel, heads, layer, schedule),
        out_shape=[jax.ShapeDtypeStruct(shape, kind) for shape, kind in outs],
        in_specs=[VM] * 26 + [ANY] * (8 + len(given)),
        out_specs=[VM] * (len(outs) - 5) + [ANY, ANY] + [VM] * 3,
        scratch_shapes=[
            vm((ff_local, model_width), bf16), vm((model_width, 2 * max(d_local, ff_local)), bf16),
            vm((d_local, model_width), bf16), vm((q_width, model_width), bf16), vm((model_width, 2 * NS), bf16),
            vm((model_width, q_width), bf16), vm((model_width, 2 * HD), bf16),
            vm(full, bf16), vm((rows, 2 * ff_local), bf16), vm(full, bf16), vm(full, bf16), vm(full, bf16),
            vm(full, bf16), vm(full, f32), vm(full, bf16), vm((rows, d_local), f32), vm((rows, q_width), bf16),
            vm((rows, d_local), bf16), vm((rows, d_local), f32), vm((rows, d_local), f32),
            vm((rows, heads * rows), bf16),
            vm((rows, q_width // HD * length), bf16), vm((length, 2 * HD), f32), vm((length, 2 * HD), bf16),
            vm(((count - 1) * rows, 2 * HD), bf16), vm(state, bf16), vm(state, bf16), vm((8, width), f32),
            vm((rows + RIM, width), f32), vm((rows + 16, width), f32), vm((rows + 8, width), f32),
            vm((rows, d_local), bf16), vm((rows, width), bf16), vm((rows, q_width), bf16),
            vm((rows, 2 * HD), bf16), vm((rows, 128), bf16),
            DMA((8 + UNITS,)), DMA((parts,)), DMA((parts,)), DMA((parts,)), DMA((parts,)), DMA((heads // 2,)),
            DMA((heads // 2,)), DMA, DMA, DMA((count - 1,)), DMA((count - 1,)),
            vm((2, 128, max(3 * ff_local, mix_width)), bf16), DMA((2,)),
            *cross_scratch(UNITS, span, outs[-1][0][1]),
            *([] if waiting is None else
              [vm((UNITS, span, 3 * ff_local // UNITS), bf16), *line_scratch(UNITS, span, 3 * ff_local),
               *line_scratch(BEGUN, span, mix_width, count // 2)]),
        ],
        compiler_params=pltpu.CompilerParams(
            vmem_limit_bytes=VMEM_LIMIT, collective_id=2 + layer, has_side_effects=True),
    )(grad, *[saved[name] for name in names], w["gain_mix"][layer], w["gain_ff"][layer], w["dt"][layer],
      w["taps"][layer], w["head_vals"][layer], dcol, dloc, drow, w["down"], saved["w_gu"], w["out"], w["o"],
      saved["w_zx"], w["bc"], w["q"], w["kv"], *given)


def on_device(hidden_in, segment_ids, gain_mix, w_zx, w_bc, w_dt, conv_x, conv_bc, ssm_head, w_q, w_kv,
              w_o, w_out, gain_ff, w_gu, w_down, cotangent):
    rows, model_width = hidden_in.shape
    taps_count = conv_x.shape[1]
    place = lax.axis_index("seq")
    context = (segment_ids,)
    layers = gain_mix.shape[0]
    heads = ssm_head.shape[2]
    d_local = w_zx.shape[3]
    w = dict(
        heads=heads,
        gain_mix=gain_mix[:, None].astype(f32),
        gain_ff=gain_ff[:, None].astype(f32),
        zx=w_zx,
        bc=w_bc,
        dt=jnp.pad(w_dt, ((0, 0), (0, 0), (0, 128 - heads))),
        q=w_q,
        kv=w_kv.reshape(layers, model_width, -1),
        o=w_o,
        out=w_out,
        gu=w_gu,
        down=w_down,
        taps=jnp.pad(jnp.concatenate([conv_x.reshape(layers, taps_count, -1), conv_bc], axis=2).astype(f32),
                     ((0, 0), (0, 8 - taps_count), (0, 0))),
        head_vals=jnp.pad(ssm_head, ((0, 0), (0, 5), (0, 128 - heads))),
    )
    hidden = hidden_in
    saved = []
    zx = None
    for l in range(layers):
        hidden, zx, context, kept = layer_forward(l, hidden, zx, w, context)
        saved.append(kept)
    block_out = hidden
    gradient = cotangent
    narrow, small = [None] * layers, [None] * layers
    waiting = None
    for l in reversed(range(layers)):
        *summed, gradient, ff_grads, mix_grads, narrow[l], small[l], half = layer_backward(
            l, gradient, waiting, w, saved[l], context)
        waiting = (mix_grads, half)
    shards = lax.axis_size("dp") * lax.axis_size("seq")
    shard = lax.axis_index("dp") * lax.axis_size("seq") + place
    ff_local = w_down.shape[1]
    q_width = w_q.shape[2]
    part = model_width // shards
    down, gu, zx, q, kv, dt, out, o, small, g_bc = last_sum(
        (ff_grads, mix_grads), half, summed[0], narrow, small,
        ((ff_local, -ff_local), (-d_local, q_width, 128, 128, d_local, q_width)))
    down, out, o = (jnp.transpose(a, (0, 2, 1)) for a in (down, out, o))
    kv = kv.reshape(layers, part, 1, 128)
    dt = dt[:, :, :heads]
    own = 2 * NS // (shards * lax.axis_size("head"))
    spot = place * lax.axis_size("head") + lax.axis_index("head")
    g_bc = lax.dynamic_slice_in_dim(g_bc, lax.rem(spot * own, g_bc.shape[1]), own, 1)
    w_bc_grad = jnp.transpose(g_bc[:, :, :model_width], (0, 2, 1))
    conv_bc_grad = jnp.transpose(g_bc[:, :, model_width:model_width + taps_count], (0, 2, 1))
    small = small.reshape(layers, -1, small.shape[1])
    gain_a = lax.dynamic_slice_in_dim(small[:, 8, :model_width], shard * part, part, 1)
    gain_b = lax.dynamic_slice_in_dim(small[:, 9, :model_width], shard * part, part, 1)
    taps = small[:, :taps_count, :d_local].reshape(layers, taps_count, heads, -1)
    taps_part = taps.shape[3] // shards
    conv_x_grad = lax.dynamic_slice_in_dim(taps, shard * taps_part, taps_part, 3)
    head_grad = small[:, 4:7, :heads]
    return (block_out, gradient, gain_a, zx, w_bc_grad, dt, conv_x_grad, conv_bc_grad, head_grad, q, kv,
            o, out, gain_b, gu, down)


def solution(mesh):
    in_specs = (
        P(("dp", "seq"), None),
        P("dp", None),
        P(),
        P(None, None, None, "head"),
        P(),
        P(None, None, "head"),
        P(None, None, "head", None),
        P(),
        P(None, None, "head"),
        P(None, None, "head"),
        P(None, None, "head", None),
        P(None, "head", None),
        P(None, "head", None),
        P(),
        P(None, None, None, "head"),
        P(None, "head", None),
        P(("dp", "seq"), None),
    )
    out_specs = (
        P(("dp", "seq"), None),
        P(("dp", "seq"), None),
        P(None, ("dp", "seq")),
        P(None, ("dp", "seq"), None, "head"),
        P(None, None, ("dp", "seq", "head")),
        P(None, ("dp", "seq"), "head"),
        P(None, None, "head", ("dp", "seq")),
        P(None, None, ("dp", "seq", "head")),
        P(None, None, "head"),
        P(None, ("dp", "seq"), "head"),
        P(None, ("dp", "seq"), "head", None),
        P(None, "head", ("dp", "seq")),
        P(None, "head", ("dp", "seq")),
        P(None, ("dp", "seq")),
        P(None, ("dp", "seq"), None, "head"),
        P(None, "head", ("dp", "seq")),
    )
    return jax.shard_map(
        on_device, mesh=mesh, in_specs=in_specs, out_specs=out_specs, check_vma=False
    )
```
